32 devices in a mesh: section: 2 (over core), dp: 16 (over z, y, x).
Axes of the slice: x: 2, y: 2, z: 4, core: 2. Of those that a mesh axis runs over, the one named last changes fastest.
Arguments:
- frames: bfloat16 [16, 1024, 80], P('dp'), may hold values from -6 to 6
- targets: int32 [16, 1024], P('dp'), may hold values from 0 to 1023
- lengths: int32 [16], P('dp'), may hold values from 128 to 1024, as said below
- w_attn: float32 [2, 512, 1536], P('section', 'dp'), may hold values from -0.25 to 0.25
- w_out: float32 [2, 512, 512], P('section', 'dp'), may hold values from -0.75 to 0.75
- w_pos: float32 [2, 512, 512], P('section', 'dp'), may hold values from -0.25 to 0.25
- w_up: float32 [2, 512, 2048], P('section', 'dp'), may hold values from -0.25 to 0.25
- w_down: float32 [2, 2048, 512], P('section', 'dp'), may hold values from -0.125 to 0.125
- layer_vecs: float32 [2, 4, 512], P('section', None, 'dp'), may hold values from -1.5 to 3.125
- w_in: float32 [80, 512], P(None, 'dp'), may hold values from -0.625 to 0.625
- w_head: float32 [512, 1024], P('dp'), may hold values from -0.25 to 0.25
- gain_final: float32 [512], P('dp'), may hold values from 0.4 to 3.125
- moment_attn: float32 [2, 512, 1536], P('section', 'dp'), may hold values from -4.7683716e-06 to 4.7683716e-06
- moment_out: float32 [2, 512, 512], P('section', 'dp'), may hold values from -4.7683716e-06 to 4.7683716e-06
- moment_pos: float32 [2, 512, 512], P('section', 'dp'), may hold values from -4.7683716e-06 to 4.7683716e-06
- moment_up: float32 [2, 512, 2048], P('section', 'dp'), may hold values from -4.7683716e-06 to 4.7683716e-06
- moment_down: float32 [2, 2048, 512], P('section', 'dp'), may hold values from -4.7683716e-06 to 4.7683716e-06
- moment_vecs: float32 [2, 4, 512], P('section', None, 'dp'), may hold values from -1.9073486e-05 to 1.9073486e-05
- moment_in: float32 [80, 512], P(None, 'dp'), may hold values from -4.7683716e-06 to 4.7683716e-06
- moment_head: float32 [512, 1024], P('dp'), may hold values from -4.7683716e-06 to 4.7683716e-06
- moment_final: float32 [512], P('dp'), may hold values from -1.9073486e-05 to 1.9073486e-05
- second_attn: float32 [2, 512, 1536], P('section', 'dp'), may hold values from 5.4159446e-14 to 2.1663778e-13
- second_out: float32 [2, 512, 512], P('section', 'dp'), may hold values from 5.4159446e-14 to 2.1663778e-13
- second_pos: float32 [2, 512, 512], P('section', 'dp'), may hold values from 2.7079722e-15 to 1.0831889e-14
- second_up: float32 [2, 512, 2048], P('section', 'dp'), may hold values from 5.4159446e-14 to 2.1663778e-13
- second_down: float32 [2, 2048, 512], P('section', 'dp'), may hold values from 5.4159446e-14 to 2.1663778e-13
- second_vecs: float32 [2, 4, 512], P('section', None, 'dp'), may hold values from 8.6655113e-13 to 3.4662045e-12
- second_in: float32 [80, 512], P(None, 'dp'), may hold values from 5.4159446e-14 to 2.1663778e-13
- second_head: float32 [512, 1024], P('dp'), may hold values from 5.4159446e-14 to 2.1663778e-13
- second_final: float32 [512], P('dp'), may hold values from 8.6655113e-13 to 3.4662045e-12
Outputs:
- new_attn: float32 [2, 512, 1536], P('section', 'dp')
- new_out: float32 [2, 512, 512], P('section', 'dp')
- new_pos: float32 [2, 512, 512], P('section', 'dp')
- new_up: float32 [2, 512, 2048], P('section', 'dp')
- new_down: float32 [2, 2048, 512], P('section', 'dp')
- new_vecs: float32 [2, 4, 512], P('section', None, 'dp')
- new_in: float32 [80, 512], P(None, 'dp')
- new_head: float32 [512, 1024], P('dp')
- new_final: float32 [512], P('dp')
- new_moment_attn: float32 [2, 512, 1536], P('section', 'dp')
- new_moment_out: float32 [2, 512, 512], P('section', 'dp')
- new_moment_pos: float32 [2, 512, 512], P('section', 'dp')
- new_moment_up: float32 [2, 512, 2048], P('section', 'dp')
- new_moment_down: float32 [2, 2048, 512], P('section', 'dp')
- new_moment_vecs: float32 [2, 4, 512], P('section', None, 'dp')
- new_moment_in: float32 [80, 512], P(None, 'dp')
- new_moment_head: float32 [512, 1024], P('dp')
- new_moment_final: float32 [512], P('dp')
- new_second_attn: float32 [2, 512, 1536], P('section', 'dp')
- new_second_out: float32 [2, 512, 512], P('section', 'dp')
- new_second_pos: float32 [2, 512, 512], P('section', 'dp')
- new_second_up: float32 [2, 512, 2048], P('section', 'dp')
- new_second_down: float32 [2, 2048, 512], P('section', 'dp')
- new_second_vecs: float32 [2, 4, 512], P('section', None, 'dp')
- new_second_in: float32 [80, 512], P(None, 'dp')
- new_second_head: float32 [512, 1024], P('dp')
- new_second_final: float32 [512], P('dp')
- grad_norm: float32 [], replicated
- loss_sum: float32 [], replicated
The draws below stay inside these ranges and needn't reach their ends.
Inputs may be any that keep to these rules, and one draw needn't show every extreme that they name: `lengths`: one stream has exactly 1024 valid frames.
All inputs are finite; a program needn't handle non-finite values.
Results may differ from the reference program's by a relative error of at most 0.012.
The reference program's roundings to bfloat16 on the way count: a program that leaves them out, or rounds other values in their place, can miss the bound.
Values may be sent and summed in bfloat16 or wider, within the bound.
No kernel may reach another device: no remote copies, remote signals or barrier semaphores. Data moves between devices by JAX's collectives and lax.ppermute only.
A program may use at most 192 MiB of HBM per device.

```python
import math
import jax
import jax.numpy as jnp
import numpy as np
from jax import lax

D = 512
HEADS = 8
HEAD_DIM = 64
FF = 2048
CODES = 1024
FEATS = 80
MEM = 256
SEG = 512
SEGS = 2
STEP = 10
LAYERS = 2
FRAMES = 1024
STREAMS = 16
NPARAM = 7385600


def rising_gains(key, shape, length):
    rise = 3.0
    bottom = 0.6
    ramp = bottom * rise ** (jnp.arange(length, dtype=jnp.float32) / (length - 1))
    return ramp * jax.random.uniform(key, shape, jnp.float32, 0.8, 1.25)


def draw_layer_vecs(key, part):
    key = jax.random.fold_in(key, 11)
    first_key, second_key = jax.random.split(key)
    gains = rising_gains(first_key, (LAYERS, 2, D), D)
    biases = 0.5 * jnp.clip(jax.random.normal(second_key, (LAYERS, 2, D), jnp.float32), -3.0, 3.0)
    return jnp.concatenate([gains, biases], 1)


def draw_gain_final(key, part):
    key = jax.random.fold_in(key, 12)
    return rising_gains(key, (D,), D)


def draw_lengths(key, part):
    key = jax.random.fold_in(key, 13)
    first_key, second_key = jax.random.split(key)
    base = jax.random.randint(first_key, (STREAMS,), SEG // 4, FRAMES + 1, jnp.int32)
    chosen = jax.random.randint(second_key, (), 0, STREAMS, jnp.int32)
    return jnp.where(jnp.arange(STREAMS, dtype=jnp.int32) == chosen, FRAMES, base).astype(jnp.int32)


def set_ends(values, key, smallest, top_value):
    index_at = [jax.random.randint(jax.random.fold_in(key, axis), (), 0, length) for axis, length in enumerate(values.shape)]
    widest = values.shape.index(max(values.shape))
    next_to = index_at[:widest] + [(index_at[widest] + 1) % values.shape[widest]] + index_at[widest + 1:]
    return values.at[tuple(index_at)].set(smallest).at[tuple(next_to)].set(top_value)


def block_scale(stream_key, extent, cuts, smallest, top_value):
    def one(axis_at, parts):
        heights = jax.random.uniform(jax.random.fold_in(jax.random.fold_in(stream_key, 6), axis_at), (parts,), jnp.float32, smallest / len(cuts), top_value / len(cuts))
        return jnp.repeat(jnp.exp(heights), extent[axis_at] // parts).reshape((-1,) + (1,) * (len(extent) - axis_at - 1))

    level = one(*cuts[0])
    for cut in cuts[1:]:
        level = level * one(*cut)
    return level


def cumulative_ranks(amount, skew):
    loads = [(1 << 20) // math.isqrt(rank ** skew) + 1 for rank in range(1, amount + 1)]
    scale = 1 + sum(loads) // (1 << 30)
    return np.cumsum(np.array([max(1, weight // scale) for weight in loads]))


def skewed_ids(key, shape, number_of, lean):
    table = cumulative_ranks(number_of, lean)
    pick = jax.random.randint(jax.random.fold_in(key, 1), shape, 0, int(table[number_of - 1]))
    grade = jnp.searchsorted(jnp.asarray(table, jnp.int32), pick, side="right")
    return jax.random.permutation(jax.random.fold_in(key, 2), number_of)[grade].astype(jnp.int32)


def normal_values(rng, shape, deviation, most, cuts=(), held_as=jnp.bfloat16):
    drawn = jax.random.normal(rng, shape, jnp.float32) * deviation
    if len(cuts) > 0:
        drawn = block_scale(rng, shape, cuts, -0.22, 0.18) * drawn
    return jnp.clip(drawn, min=-most, max=most).astype(held_as)


def setup_inputs(seed: int = 0) -> dict:
    seeds = jax.random.split(jax.random.key(seed), 31)
    return {
        "frames": normal_values(seeds[0], (STREAMS, FRAMES, FEATS), 1.0, 6.0, ((0, 16),)),
        "targets": set_ends(skewed_ids(seeds[1], (STREAMS, FRAMES), CODES, 2), jax.random.fold_in(seeds[1], 3), 0, CODES - 1).astype(jnp.int32),
        "lengths": draw_lengths(jax.random.fold_in(seeds[30], 71), 0),
        "w_attn": normal_values(seeds[3], (LAYERS, D, 3 * D), D ** -0.5, 0.25, ((0, 2), (1, 16)), jnp.float32),
        "w_out": normal_values(seeds[4], (LAYERS, D, D), (D // 8) ** -0.5, 0.75, ((0, 2), (1, 16)), jnp.float32),
        "w_pos": normal_values(seeds[5], (LAYERS, D, D), D ** -0.5, 0.25, ((0, 2), (1, 16)), jnp.float32),
        "w_up": normal_values(seeds[6], (LAYERS, D, FF), D ** -0.5, 0.25, ((0, 2), (1, 16)), jnp.float32),
        "w_down": normal_values(seeds[7], (LAYERS, FF, D), FF ** -0.5, 0.125, ((0, 2), (1, 16)), jnp.float32),
        "layer_vecs": draw_layer_vecs(jax.random.fold_in(seeds[30], 71), 0),
        "w_in": normal_values(seeds[9], (FEATS, D), FEATS ** -0.5, 0.625, ((1, 16),), jnp.float32),
        "w_head": normal_values(seeds[10], (D, CODES), D ** -0.5, 0.25, ((0, 16),), jnp.float32),
        "gain_final": draw_gain_final(jax.random.fold_in(seeds[30], 71), 0),
        "moment_attn": normal_values(seeds[12], (LAYERS, D, 3 * D), (0.0022 / NPARAM ** 0.5), 4.76837158203125e-06, ((0, 2), (1, 16)), jnp.float32),
        "moment_out": normal_values(seeds[13], (LAYERS, D, D), (0.0022 / NPARAM ** 0.5), 4.76837158203125e-06, ((0, 2), (1, 16)), jnp.float32),
        "moment_pos": normal_values(seeds[14], (LAYERS, D, D), (0.0022 / NPARAM ** 0.5), 4.76837158203125e-06, ((0, 2), (1, 16)), jnp.float32),
        "moment_up": normal_values(seeds[15], (LAYERS, D, FF), (0.0022 / NPARAM ** 0.5), 4.76837158203125e-06, ((0, 2), (1, 16)), jnp.float32),
        "moment_down": normal_values(seeds[16], (LAYERS, FF, D), (0.0022 / NPARAM ** 0.5), 4.76837158203125e-06, ((0, 2), (1, 16)), jnp.float32),
        "moment_vecs": normal_values(seeds[17], (LAYERS, 4, D), (0.0088 / NPARAM ** 0.5), 1.9073486328125e-05, ((0, 2), (2, 16)), jnp.float32),
        "moment_in": normal_values(seeds[18], (FEATS, D), (0.0022 / NPARAM ** 0.5), 4.76837158203125e-06, ((1, 16),), jnp.float32),
        "moment_head": normal_values(seeds[19], (D, CODES), (0.0022 / NPARAM ** 0.5), 4.76837158203125e-06, ((0, 16),), jnp.float32),
        "moment_final": normal_values(seeds[20], (D,), (0.0088 / NPARAM ** 0.5), 1.9073486328125e-05, ((0, 16),), jnp.float32),
        "second_attn": jnp.clip(jnp.exp(math.log(2.166377835585362e-13) - 1.3862944 * jax.random.uniform(seeds[21], (LAYERS, D, 3 * D), jnp.float32) ** block_scale(seeds[21], (LAYERS, D, 3 * D), ((0, 2), (1, 16)), -0.2, 0.2)), 5.415944588963405e-14, 2.166377835585362e-13),
        "second_out": jnp.clip(jnp.exp(math.log(2.166377835585362e-13) - 1.3862944 * jax.random.uniform(seeds[22], (LAYERS, D, D), jnp.float32) ** block_scale(seeds[22], (LAYERS, D, D), ((0, 2), (1, 16)), -0.2, 0.2)), 5.415944588963405e-14, 2.166377835585362e-13),
        "second_pos": jnp.clip(jnp.exp(math.log(1.0831888669707041e-14) - 1.3862944 * jax.random.uniform(seeds[23], (LAYERS, D, D), jnp.float32) ** block_scale(seeds[23], (LAYERS, D, D), ((0, 2), (1, 16)), -0.2, 0.2)), 2.7079721674267603e-15, 1.0831888669707041e-14),
        "second_up": jnp.clip(jnp.exp(math.log(2.166377835585362e-13) - 1.3862944 * jax.random.uniform(seeds[24], (LAYERS, D, FF), jnp.float32) ** block_scale(seeds[24], (LAYERS, D, FF), ((0, 2), (1, 16)), -0.2, 0.2)), 5.415944588963405e-14, 2.166377835585362e-13),
        "second_down": jnp.clip(jnp.exp(math.log(2.166377835585362e-13) - 1.3862944 * jax.random.uniform(seeds[25], (LAYERS, FF, D), jnp.float32) ** block_scale(seeds[25], (LAYERS, FF, D), ((0, 2), (1, 16)), -0.2, 0.2)), 5.415944588963405e-14, 2.166377835585362e-13),
        "second_vecs": jnp.clip(jnp.exp(math.log(3.466204536936579e-12) - 1.3862944 * jax.random.uniform(seeds[26], (LAYERS, 4, D), jnp.float32) ** block_scale(seeds[26], (LAYERS, 4, D), ((0, 2), (2, 16)), -0.2, 0.2)), 8.665511342341448e-13, 3.466204536936579e-12),
        "second_in": jnp.clip(jnp.exp(math.log(2.166377835585362e-13) - 1.3862944 * jax.random.uniform(seeds[27], (FEATS, D), jnp.float32) ** block_scale(seeds[27], (FEATS, D), ((1, 16),), -0.2, 0.2)), 5.415944588963405e-14, 2.166377835585362e-13),
        "second_head": jnp.clip(jnp.exp(math.log(2.166377835585362e-13) - 1.3862944 * jax.random.uniform(seeds[28], (D, CODES), jnp.float32) ** block_scale(seeds[28], (D, CODES), ((0, 16),), -0.2, 0.2)), 5.415944588963405e-14, 2.166377835585362e-13),
        "second_final": jnp.clip(jnp.exp(math.log(3.466204536936579e-12) - 1.3862944 * jax.random.uniform(seeds[29], (D,), jnp.float32) ** block_scale(seeds[29], (D,), ((0, 16),), -0.2, 0.2)), 8.665511342341448e-13, 3.466204536936579e-12),
    }


NEG = -1e+30
CLIP = 0.02

@jax.custom_vjp
def low(v):
    return lax.optimization_barrier(v.astype(jnp.bfloat16)).astype(jnp.float32)

@jax.custom_vjp
def low_back(v):
    return v

def low_keep(v):
    return (low(v), None)

def low_pass(kept, grad):
    return (grad,)

def back_keep(v):
    return (v, None)

def back_low(kept, grad):
    return (low(grad),)
low.defvjp(low_keep, low_pass)
low_back.defvjp(back_keep, back_low)

def mult(left, right):
    return jnp.dot(left, right, precision=lax.Precision.HIGHEST)

def einmul(form, left, right):
    return jnp.einsum(form, left, right, precision=lax.Precision.HIGHEST)

def norm_gain(values, gain):
    center = values - lax.optimization_barrier(jnp.mean(values, -1, keepdims=True))
    spread = lax.optimization_barrier(jnp.mean(center * center, -1, keepdims=True))
    return center * lax.rsqrt(spread + 1e-05) * gain

def sinus_table():
    count = MEM + SEG
    where_at = (count - 1 - jnp.arange(count, dtype=jnp.int32)).astype(jnp.float32)[:, None]
    freqs = jnp.exp(-jnp.log(10000.0) * (2.0 * jnp.arange(D // 2, dtype=jnp.int32).astype(jnp.float32) / D))
    angles = where_at * freqs[None, :]
    return jnp.concatenate([jnp.sin(angles), jnp.cos(angles)], 1)

def key_mask(segment, length):
    rows = jnp.arange(SEG, dtype=jnp.int32)[:, None]
    joint = jnp.arange(MEM + SEG, dtype=jnp.int32)[None, :]
    segment = jnp.asarray(segment, jnp.int32)
    spot = jnp.where(joint < MEM, (segment - 1) * SEG + SEG - MEM + joint, segment * SEG + joint - MEM)
    return (spot < length) & ((joint >= MEM) | (segment >= 1)) & (joint <= MEM + rows)

def row_weight(segment, length):
    spot = jnp.asarray(segment, jnp.int32) * SEG + jnp.arange(SEG, dtype=jnp.int32)
    return (spot < length).astype(jnp.float32) / length.astype(jnp.float32)

def skew(block):
    count, rows, cols = block.shape
    lead = rows - 1
    flat = jnp.pad(block, ((0, 0), (0, 0), (0, 1))).reshape(count, rows * (cols + 1))
    return flat[:, lead:lead + rows * cols].reshape(count, rows, cols)

def layer(hidden, memory, segment, length, w_attn, w_out, w_pos, w_up, w_down, vectors, table):
    joined = jnp.concatenate([memory, hidden], 0)
    normed = low(norm_gain(joined, vectors[0]))
    query = low_back(mult(normed[MEM:], w_attn[:, :D]))
    key_val = low_back(mult(normed, w_attn[:, D:]))
    count = MEM + SEG
    keys = low(key_val[:, :D]).reshape(count, HEADS, HEAD_DIM)
    values = low(key_val[:, D:]).reshape(count, HEADS, HEAD_DIM)
    query_u = low(query + vectors[2]).reshape(SEG, HEADS, HEAD_DIM)
    query_v = low(query + vectors[3]).reshape(SEG, HEADS, HEAD_DIM)
    rel = low(low_back(mult(table, w_pos))).reshape(count, HEADS, HEAD_DIM)
    content = low_back(einmul('ihd,jhd->hij', query_u, keys))
    position = skew(low_back(einmul('ihd,jhd->hij', query_v, rel)))
    mask = key_mask(segment, length)
    scores = jnp.where(mask[None], (content + position) * HEAD_DIM ** (-0.5), NEG)
    probs = low(jax.nn.softmax(scores, -1))
    attended = low(low_back(einmul('hij,jhd->ihd', probs, values)).reshape(SEG, D))
    mixed = hidden + low_back(mult(attended, w_out))
    normed_two = low(norm_gain(mixed, vectors[1]))
    inner = low_back(mult(normed_two, w_up))
    return mixed + low_back(mult(low(jax.nn.gelu(inner)), w_down))

def segment_pass(rounded, frame_rows, target_rows, memories, segment, length, table):
    w_attn, w_out, w_pos, w_up, w_down, vectors, w_in, w_head, gain_final = rounded
    hidden = low_back(mult(frame_rows, w_in))
    inputs = []
    for level in range(LAYERS):
        inputs.append(hidden)
        hidden = layer(hidden, memories[level], segment, length, w_attn[level], w_out[level], w_pos[level], w_up[level], w_down[level], vectors[level], table)
    final = low(norm_gain(hidden, gain_final))
    logits = low_back(mult(final, w_head))
    top = lax.optimization_barrier(jnp.max(logits, -1, keepdims=True))
    log_total = top[:, 0] + jnp.log(lax.optimization_barrier(jnp.sum(jnp.exp(logits - top), -1)))
    picked = jnp.take_along_axis(logits, target_rows[:, None], 1)[:, 0]
    return (jnp.sum((log_total - picked) * row_weight(segment, length)), inputs)

def run(weights, frame_rows, target_rows, length, memories, table):
    rounded = tuple((low(item) for item in weights))
    total = jnp.zeros((), jnp.float32)
    all_inputs = []
    for segment in range(SEGS):
        if memories is None:
            if segment == 0:
                seg_mem = [jnp.zeros((MEM, D), jnp.float32) for level in range(LAYERS)]
            else:
                seg_mem = [item[SEG - MEM:] for item in all_inputs[-1]]
        else:
            seg_mem = memories[segment]
        term, inputs = segment_pass(rounded, frame_rows[segment * SEG:(segment + 1) * SEG], target_rows[segment * SEG:(segment + 1) * SEG], seg_mem, segment, length, table)
        total = total + term
        all_inputs.append(inputs)
    return (total, all_inputs)

def adam_step(weight, grad, first, second, rate, decay, factor):
    grad = grad * factor
    first = 0.9 * first + 0.1 * grad
    second = 0.999 * second + 0.001 * grad * grad
    ratio = first / (1.0 - 0.9 ** STEP) / (jnp.sqrt(second / (1.0 - 0.999 ** STEP)) + 1e-08)
    return (weight - rate * (ratio + decay * weight), first, second)

def reference(frames, targets, lengths, w_attn, w_out, w_pos, w_up, w_down, layer_vecs, w_in, w_head, gain_final, moment_attn, moment_out, moment_pos, moment_up, moment_down, moment_vecs, moment_in, moment_head, moment_final, second_attn, second_out, second_pos, second_up, second_down, second_vecs, second_in, second_head, second_final):
    params = (w_attn, w_out, w_pos, w_up, w_down, layer_vecs, w_in, w_head, gain_final)
    table = low(sinus_table())
    frame_all = frames.astype(jnp.float32)

    def one_stream(carry, items):
        grad_acc, loss_acc = carry
        frame_rows, target_rows, length = items
        unused, inputs = run(params, frame_rows, target_rows, length, None, table)
        memories = [[jnp.zeros((MEM, D), jnp.float32) for level in range(LAYERS)]]
        for segment in range(1, SEGS):
            memories.append([item[SEG - MEM:] for item in inputs[segment - 1]])
        total, pullback, extra = jax.vjp(lambda weights: run(weights, frame_rows, target_rows, length, memories, table), params, has_aux=True)
        grads = pullback(jnp.ones_like(total) / STREAMS)[0]
        return ((tuple((a + b for a, b in zip(grad_acc, grads))), loss_acc + total), None)
    start = (tuple((jnp.zeros_like(item) for item in params)), jnp.zeros((), jnp.float32))
    (grads, loss_sum), unused = lax.scan(one_stream, start, (frame_all, targets, lengths))
    squares = jnp.zeros((), jnp.float32)
    for item in grads:
        squares = squares + jnp.sum(item * item)
    grad_norm = jnp.sqrt(squares)
    factor = jnp.minimum(1.0, CLIP / (grad_norm + 1e-06))
    firsts = (moment_attn, moment_out, moment_pos, moment_up, moment_down, moment_vecs, moment_in, moment_head, moment_final)
    seconds = (second_attn, second_out, second_pos, second_up, second_down, second_vecs, second_in, second_head, second_final)
    news, moms, sqs = ([], [], [])
    for index in range(9):
        vector = index in (5, 8)
        rate = 0.3 if vector else 0.03
        decay = 0.0 if vector else 0.01
        weight, first, second = adam_step(params[index], grads[index], firsts[index], seconds[index], rate, decay, factor)
        news.append(weight)
        moms.append(first)
        sqs.append(second)
    return (news[0], news[1], news[2], news[3], news[4], news[5], news[6], news[7], news[8], moms[0], moms[1], moms[2], moms[3], moms[4], moms[5], moms[6], moms[7], moms[8], sqs[0], sqs[1], sqs[2], sqs[3], sqs[4], sqs[5], sqs[6], sqs[7], sqs[8], grad_norm, loss_sum)
```

```python
import functools

import jax
import jax.numpy as jnp
from jax import lax
from jax.experimental import pallas as pl
from jax.experimental.pallas import tpu as pltpu
from jax.sharding import PartitionSpec as P

D = 512
FF = 2048
CODES = 1024
FEATS = 80
MEM = 256
SEG = 512
SEGS = 2
STEP = 10
ROWS = MEM + SEG
BLOCK = 128
PAIRS = 4
WIDE = 18 * BLOCK
GROUPS = 16
NEG = -1e30
CLIP = 0.02
SCALE = 0.125
F32 = jnp.float32
BF16 = jnp.bfloat16
SPANS = tuple((MEM + BLOCK * (b + 1) for b in range(4)))
STARTS = tuple((sum(SPANS[:b]) for b in range(4)))
VMEM_LIMIT = 56 * 1024 * 1024


def nn(left, right):
    return jnp.dot(left, right, preferred_element_type=F32)


def nt(left, right):
    return lax.dot_general(left, right, (((1,), (1,)), ((), ())), preferred_element_type=F32)


def tn(left, right):
    return lax.dot_general(left, right, (((0,), (0,)), ((), ())), preferred_element_type=F32)


def norm_parts(values):
    center = values - jnp.mean(values, -1, keepdims=True)
    spread = jnp.mean(center * center, -1, keepdims=True)
    inverse = lax.rsqrt(spread + 1e-05)
    return center * inverse, inverse


def norm_back(unit, inverse, gain, grad):
    scaled = grad * gain
    first = jnp.mean(scaled, -1, keepdims=True)
    second = jnp.mean(scaled * unit, -1, keepdims=True)
    return inverse * (scaled - first - unit * second), jnp.sum(grad * unit, 0, keepdims=True)


def group_of(bits, spot, place, half):
    code = jnp.int32(0)
    for index, (low, high) in enumerate(zip(bits[0], bits[1])):
        bit = lax.rem(lax.div(spot, 1 << index), 2)
        code = code + bit * jnp.where(half == 0, low, high)
    return jnp.bitwise_xor(place, code)


def copies(bits, place, half, pieces, units, rows, sem, outward):
    count = GROUPS // len(pieces)
    for index, slab in enumerate(pieces):

        def one(spot, carry):
            group = group_of(bits, index * count + spot, place, half)
            for whole, first in units:
                there = whole.at[pl.ds(pl.multiple_of((group * 2 + half) * rows, rows), rows), :]
                here = slab.at[spot, pl.ds(first, rows), pl.ds(0, whole.shape[1])]
                if outward:
                    pltpu.make_async_copy(there, here, sem).start()
                else:
                    pltpu.make_async_copy(here, there, sem).start()
            return carry

        lax.fori_loop(0, count, one, 0)


def tri_mask():
    row = lax.broadcasted_iota(jnp.int32, (2 * BLOCK, BLOCK), 0)
    col = lax.broadcasted_iota(jnp.int32, (2 * BLOCK, BLOCK), 1)
    return col <= lax.rem(row, BLOCK)


def stack_heads(part):
    col = lax.broadcasted_iota(jnp.int32, part.shape, 1)
    zero = jnp.zeros_like(part)
    return jnp.concatenate(
        [jnp.where(col < 64, part, zero), jnp.where(col < 64, zero, part)], 0
    )


def pick_heads(both):
    col = lax.broadcasted_iota(jnp.int32, (BLOCK, BLOCK), 1)
    return jnp.where(col < 64, both[:BLOCK], both[BLOCK:])


def lanes(pair):
    return pl.ds(pl.multiple_of(pair * BLOCK, BLOCK), BLOCK)


def attn_forward(bits, base, *refs):
    first_layer = base == 0
    if first_layer:
        (scalars, frames, own_low, own_high, other_low, other_high, table, mixed, joined, normed,
         query_u, query_v, keys, values, rel, probs, attended, weights, vecs, sem, small,
         small_sem) = refs
    else:
        (scalars, memory, hidden, vecs, own_low, own_high, other_low, other_high, table, mixed,
         joined, normed, query_u, query_v, keys, values, rel, probs, attended, weights, sem) = refs
    place, half, length, segment = scalars[0], scalars[1], scalars[2], scalars[3]
    both = ((half, (own_low, own_high)), (1 - half, (other_low, other_high)))
    if first_layer:
        for which, pieces in both:
            copies(bits, place, which, pieces, [(small, 80)], 16, small_sem, False)
    units = [(weights.at[u], 16 * u) for u in range(5)]
    for which, pieces in both:
        copies(bits, place, which, pieces, units, 16, sem, False)
    if first_layer:
        pltpu.make_async_copy(small, small, small_sem).wait()
        vecs[...] = jnp.transpose(small[...].astype(F32))[80:96]
        for b in range(3):
            rows = pl.ds(256 * b, 256)
            joined[rows, :] = nt(frames[rows, :], small[...])
    else:
        joined[0:MEM, :] = memory[...]
        joined[MEM:, :] = hidden[...]
    gain = vecs[base : base + 1, :]
    bias_u = vecs[base + 2 : base + 3, :]
    bias_v = vecs[base + 3 : base + 4, :]
    for b in range(3):
        rows = pl.ds(256 * b, 256)
        unit, unused = norm_parts(joined[rows, :])
        normed[rows, :] = (unit * gain).astype(BF16)
    pltpu.make_async_copy(weights, weights, sem).wait()
    for b in range(3):
        rows = pl.ds(256 * b, 256)
        part = normed[rows, :]
        keys[rows, :] = nn(part, weights[1]).astype(BF16)
        values[rows, :] = nn(part, weights[2]).astype(BF16)
        rel[rows, :] = nn(table[rows, :], weights[4]).astype(BF16)
        if b > 0:
            query = nn(part, weights[0])
            back = pl.ds(256 * (b - 1), 256)
            query_u[back, :] = (query + bias_u).astype(BF16)
            query_v[back, :] = (query + bias_v).astype(BF16)
    spot = lax.broadcasted_iota(jnp.int32, (1, ROWS), 1)
    where_at = segment * SEG + spot - MEM
    allowed = (where_at < length) & ((spot >= MEM) | (segment >= 1))
    bias = jnp.where(allowed, 0.0, NEG)
    triangle = tri_mask()

    def one_pair(pair, carry):
        lane = lanes(pair)
        for b, span in enumerate(SPANS):
            rows = pl.ds(BLOCK * b, BLOCK)
            stack_u = stack_heads(query_u[rows, lane]) * SCALE
            stack_v = stack_heads(query_v[rows, lane]) * SCALE
            content = nt(stack_u, keys[0:span, lane])
            full = nt(stack_v, rel[ROWS - span : ROWS, lane])
            position = jnp.concatenate(
                [
                    pltpu.roll(full[:BLOCK], span - BLOCK + 1, 1, stride=1, stride_axis=0),
                    pltpu.roll(full[BLOCK:], span - BLOCK + 1, 1, stride=1, stride_axis=0),
                ],
                0,
            )
            score = content + position + bias[:, :span]
            score = jnp.concatenate(
                [score[:, : span - BLOCK], jnp.where(triangle, score[:, span - BLOCK :], NEG)], 1
            )
            top = jnp.max(score, -1, keepdims=True)
            expo = jnp.exp(score - top)
            total = jnp.sum(expo, -1, keepdims=True)
            prob = (expo * (1.0 / total)).astype(BF16)
            probs[pair, :, STARTS[b] : STARTS[b] + span] = prob
            attended[rows, lane] = pick_heads(nn(prob, values[0:span, lane])).astype(BF16)
        return carry

    lax.fori_loop(0, PAIRS, one_pair, 0)
    for b in range(2):
        rows = pl.ds(256 * b, 256)
        mixed[rows, :] = joined[pl.ds(MEM + 256 * b, 256), :] + nn(attended[rows, :], weights[3])


def attn_backward(bits, base, *refs):
    last_kernel = base == 0
    (scalars, grad_mixed, joined, normed, query_u, query_v, keys, values, rel, probs, attended,
     weights, vecs, table) = refs[:14]
    if last_kernel:
        (frames, gain_two, vecs_one, gain_two_one, gain_final, keep, send) = refs[14:21]
        (staged_small, small_sem) = refs[-2:]
        rest = refs[21:-2]
    else:
        (keep, send, grad_hidden, grad_vecs) = refs[14:18]
        rest = refs[18:]
    (flip, grad_att, acc_keys, acc_values, acc_rel, grad_qu, grad_qv, staged, smalls, sem) = rest
    place, half = scalars[0], scalars[1]
    row = lax.broadcasted_iota(jnp.int32, (2 * BLOCK, 2 * BLOCK), 0)
    col = lax.broadcasted_iota(jnp.int32, (2 * BLOCK, 2 * BLOCK), 1)
    back = (row // BLOCK) * BLOCK + BLOCK - 1 - lax.rem(row, BLOCK)
    flip[...] = (col == back).astype(F32).astype(BF16)
    grad_mixed_b = grad_mixed[...].astype(BF16)
    staged[3] = tn(attended[...], grad_mixed_b).astype(BF16)
    grad_att[...] = nt(grad_mixed_b, weights[3]).astype(BF16)

    def one_pair(pair, carry):
        lane = lanes(pair)
        for b in (3, 2, 1, 0):
            span = SPANS[b]
            rows = pl.ds(BLOCK * b, BLOCK)
            stack_u = stack_heads(query_u[rows, lane]) * SCALE
            stack_v = nn(flip[...], stack_heads(query_v[rows, lane]) * SCALE).astype(BF16)
            stack_g = stack_heads(grad_att[rows, lane])
            prob_b = probs[pair, :, STARTS[b] : STARTS[b] + span]
            prob = prob_b.astype(F32)
            grad_prob = nt(stack_g, values[0:span, lane])
            inner = jnp.sum(prob * grad_prob, -1, keepdims=True)
            grad_score = (prob * (grad_prob - inner)).astype(BF16)
            turned = nn(flip[...], grad_score)
            grad_full = jnp.concatenate(
                [
                    pltpu.roll(turned[:BLOCK], 0, 1, stride=1, stride_axis=0),
                    pltpu.roll(turned[BLOCK:], 0, 1, stride=1, stride_axis=0),
                ],
                0,
            ).astype(BF16)
            grad_qu[rows, lane] = pick_heads(nn(grad_score, keys[0:span, lane])) * SCALE
            grad_qv[rows, lane] = pick_heads(nn(grad_full, rel[ROWS - span : ROWS, lane])) * SCALE
            part_keys = tn(stack_u, grad_score)
            part_values = tn(stack_g, prob_b)
            part_rel = tn(stack_v, grad_full)
            if b == 3:
                acc_keys[lane, :] = part_keys
                acc_values[lane, :] = part_values
                acc_rel[lane, :] = part_rel
            else:
                acc_keys[lane, 0:span] += part_keys
                acc_values[lane, 0:span] += part_values
                acc_rel[lane, ROWS - span : ROWS] += part_rel
        return carry

    lax.fori_loop(0, PAIRS, one_pair, 0)
    sum_u = jnp.sum(grad_qu[...], 0, keepdims=True)
    sum_v = jnp.sum(grad_qv[...], 0, keepdims=True)
    flip_one = flip[0:BLOCK, 0:BLOCK]
    turned = []
    for b in range(4):
        rows = pl.ds(BLOCK * b, BLOCK)
        part = grad_qv[rows, :]
        high = part.astype(BF16)
        low = (part - high.astype(F32)).astype(BF16)
        turned.append((grad_qu[rows, :] + nn(flip_one, high) + nn(flip_one, low)).astype(BF16))
    grad_query = jnp.concatenate(turned, 0)
    grad_keys = jnp.transpose(acc_keys[...]).astype(BF16)
    grad_values = jnp.transpose(acc_values[...]).astype(BF16)
    grad_rel = jnp.transpose(acc_rel[...]).astype(BF16)
    staged[0] = tn(normed[MEM:, :], grad_query).astype(BF16)
    staged[1] = tn(normed[...], grad_keys).astype(BF16)
    staged[2] = tn(normed[...], grad_values).astype(BF16)
    staged[4] = tn(table[...], grad_rel).astype(BF16)
    units = [(staged.at[u], 16 * u) for u in range(5)]
    copies(bits, place, half, (keep,), units, 16, sem, True)
    copies(bits, place, 1 - half, (send,), units, 16, sem, True)
    gain = vecs[base : base + 1, :]
    grad_normed = nt(grad_keys, weights[1]) + nt(grad_values, weights[2])
    unit, inverse = norm_parts(joined[0:MEM, :])
    unused, grad_gain = norm_back(unit, inverse, gain, grad_normed[0:MEM])
    unit, inverse = norm_parts(joined[MEM:, :])
    grad_here = grad_normed[MEM:] + nt(grad_query, weights[0])
    grad_joined, grad_gain_here = norm_back(unit, inverse, gain, grad_here)
    grad_gain = grad_gain + grad_gain_here
    grad_in = grad_mixed[...] + grad_joined
    if last_kernel:
        entry = tn(frames[MEM:, :], grad_in.astype(BF16))
        smalls[...] = entry
        smalls[80:81, :] = grad_gain
        smalls[81:82, :] = gain_two[0:1, :]
        smalls[82:83, :] = sum_u
        smalls[83:84, :] = sum_v
        smalls[84:88, :] = vecs_one[0:4, :]
        smalls[85:86, :] = gain_two_one[0:1, :]
        smalls[88:89, :] = gain_final[0:1, :]
        staged_small[...] = jnp.zeros_like(staged_small)
        staged_small[:, 0:BLOCK] = jnp.transpose(smalls[...]).astype(BF16)
        units = [(staged_small, 80)]
        copies(bits, place, half, (keep,), units, 16, small_sem, True)
        copies(bits, place, 1 - half, (send,), units, 16, small_sem, True)
        pltpu.make_async_copy(staged_small, staged_small, small_sem).wait()
    else:
        grad_hidden[...] = grad_in
        grad_vecs[...] = jnp.zeros_like(grad_vecs)
        grad_vecs[0:1, :] = grad_gain
        grad_vecs[2:3, :] = sum_u
        grad_vecs[3:4, :] = sum_v
    pltpu.make_async_copy(staged, staged, sem).wait()


def feed_forward(bits, base, scalars, mixed, vecs, own_low, own_high, other_low, other_high, output, normed, active, slope, up, down, sem):
    place, half = scalars[0], scalars[1]
    ups = [(up.at[u], 16 * u) for u in range(4)]
    downs = [(down, 64)]
    for which, pieces in ((half, (own_low, own_high)), (1 - half, (other_low, other_high))):
        copies(bits, place, which, pieces, ups, 16, sem.at[0], False)
        copies(bits, place, which, pieces, downs, 64, sem.at[1], False)
    gain = vecs[base + 1 : base + 2, :]
    for b in range(2):
        rows = pl.ds(256 * b, 256)
        unit, unused = norm_parts(mixed[rows, :])
        normed[rows, :] = (unit * gain).astype(BF16)
    pltpu.make_async_copy(up, up, sem.at[0]).wait()
    for b in range(2):
        rows = pl.ds(256 * b, 256)
        for u in range(4):
            inner = nn(normed[rows, :], up[u])
            square = inner * inner
            bent = jnp.tanh(0.7978845608028654 * (inner + 0.044715 * (square * inner)))
            part = 0.5 * (1.0 + bent)
            active[rows, 512 * u : 512 * (u + 1)] = (inner * part).astype(BF16)
            slope[rows, 512 * u : 512 * (u + 1)] = (
                part
                + (0.5 * inner)
                * (1.0 - bent * bent)
                * (0.7978845608028654 * (1.0 + (3 * 0.044715) * square))
            ).astype(BF16)
    pltpu.make_async_copy(down, down, sem.at[1]).wait()
    for b in range(2):
        rows = pl.ds(256 * b, 256)
        output[rows, :] = mixed[rows, :] + nn(active[rows, :], down[...])


def feed_backward(bits, base, scalars, grad_out, mixed, vecs, normed, active, slope, up, down,
                  keep, send, grad_mixed, grad_gain, grad_inner, staged_up, staged_down, sem):
    place, half = scalars[0], scalars[1]
    grad_y = grad_out[...].astype(BF16)
    for u in range(4):
        cols = slice(512 * u, 512 * (u + 1))
        part = nt(grad_y, down[cols, :])
        grad_inner[:, cols] = (part * slope[:, cols].astype(F32)).astype(BF16)
        staged_down[cols, :] = tn(active[:, cols], grad_y).astype(BF16)
        staged_up[u] = tn(normed[...], grad_inner[:, cols]).astype(BF16)
    ups = [(staged_up.at[u], 16 * u) for u in range(4)]
    downs = [(staged_down, 64)]
    for which, pieces in ((half, (keep,)), (1 - half, (send,))):
        copies(bits, place, which, pieces, ups, 16, sem.at[0], True)
        copies(bits, place, which, pieces, downs, 64, sem.at[1], True)
    grad_normed = nt(grad_inner[:, 0:512], up[0])
    for u in range(1, 4):
        grad_normed = grad_normed + nt(grad_inner[:, 512 * u : 512 * (u + 1)], up[u])
    unit, inverse = norm_parts(mixed[...])
    grad_here, gains = norm_back(unit, inverse, vecs[base + 1 : base + 2, :], grad_normed)
    grad_mixed[...] = grad_out[...] + grad_here
    grad_gain[...] = jnp.broadcast_to(gains, grad_gain.shape)
    pltpu.make_async_copy(staged_up, staged_up, sem.at[0]).wait()
    pltpu.make_async_copy(staged_down, staged_down, sem.at[1]).wait()


def head_pass(bits, streams, scalars, output, targets, vecs, own_low, own_high, other_low, other_high,
              keep, send, grad_out, grad_gain, loss, table, final, grad_logits, staged, sem):
    place, half, length, segment = scalars[0], scalars[1], scalars[2], scalars[3]
    units = [(table.at[u], 128 + 16 * u) for u in range(2)]
    copies(bits, place, half, (own_low, own_high), units, 16, sem, False)
    copies(bits, place, 1 - half, (other_low, other_high), units, 16, sem, False)
    pltpu.make_async_copy(table, table, sem).wait()
    size = length.astype(F32)
    gain = vecs[8:9, :]
    gains = jnp.zeros((1, D), F32)
    terms = jnp.zeros((1, 1), F32)
    for b in range(2):
        rows = pl.ds(256 * b, 256)
        unit, inverse = norm_parts(output[rows, :])
        fin = (unit * gain).astype(BF16)
        final[rows, :] = fin
        logits = jnp.concatenate([nn(fin, table[0]), nn(fin, table[1])], 1)
        top = jnp.max(logits, -1, keepdims=True)
        expo = jnp.exp(logits - top)
        total = jnp.sum(expo, -1, keepdims=True)
        picks = lax.broadcasted_iota(jnp.int32, logits.shape, 1) == targets[rows, :]
        picked = jnp.sum(jnp.where(picks, logits, 0.0), -1, keepdims=True)
        spot = segment * SEG + 256 * b + lax.broadcasted_iota(jnp.int32, (256, 1), 0)
        weight = jnp.where(spot < length, 1.0 / size, 0.0)
        terms = terms + jnp.sum((top + jnp.log(total) - picked) * weight, keepdims=True)
        grad = (expo * (1.0 / total) - jnp.where(picks, 1.0, 0.0)) * (weight * (1.0 / streams))
        grad_b = grad.astype(BF16)
        grad_logits[rows, :] = grad_b
        grad_final = nt(grad_b[:, 0:512], table[0]) + nt(grad_b[:, 512:1024], table[1])
        grad_here, gain_here = norm_back(unit, inverse, gain, grad_final)
        grad_out[rows, :] = grad_here
        gains = gains + gain_here
    for u in range(2):
        staged[u] = tn(final[...], grad_logits[:, 512 * u : 512 * (u + 1)]).astype(BF16)
    units = [(staged.at[u], 16 * u) for u in range(2)]
    copies(bits, place, half, (keep,), units, 16, sem, True)
    copies(bits, place, 1 - half, (send,), units, 16, sem, True)
    grad_gain[...] = jnp.broadcast_to(gains, grad_gain.shape)
    loss[...] = jnp.broadcast_to(terms, loss.shape)
    pltpu.make_async_copy(staged, staged, sem).wait()


VMEM = pl.BlockSpec(memory_space=pltpu.VMEM)
ANY = pl.BlockSpec(memory_space=pl.ANY)
SMEM = pl.BlockSpec(memory_space=pltpu.SMEM)


def shape(*dims, dtype=F32):
    return jax.ShapeDtypeStruct(dims, dtype)


def call(body, name, ins, outs, out_specs, scratch, flops):
    return pl.pallas_call(
        body,
        name=name,
        in_specs=ins,
        out_shape=outs,
        out_specs=out_specs,
        scratch_shapes=scratch,
        compiler_params=pltpu.CompilerParams(vmem_limit_bytes=VMEM_LIMIT),
        cost_estimate=pl.CostEstimate(flops=flops, bytes_accessed=1 << 23, transcendentals=0),
    )


SAVED = (
    shape(ROWS, D),
    shape(ROWS, D, dtype=BF16),
    shape(SEG, D, dtype=BF16),
    shape(SEG, D, dtype=BF16),
    shape(ROWS, D, dtype=BF16),
    shape(ROWS, D, dtype=BF16),
    shape(ROWS, D, dtype=BF16),
    shape(PAIRS, 2 * BLOCK, WIDE, dtype=BF16),
    shape(SEG, D, dtype=BF16),
    shape(5, D, D, dtype=BF16),
)


def run_attn_forward_first(bits, scalars, frames, pieces, table):
    outs = (shape(SEG, D),) + SAVED + (shape(16, D),)
    result = call(
        functools.partial(attn_forward, bits, 0),
        "attn_forward_first",
        [SMEM, VMEM, ANY, ANY, ANY, ANY, VMEM],
        outs,
        [VMEM] * len(outs),
        [pltpu.SemaphoreType.DMA, pltpu.VMEM((D, BLOCK), BF16), pltpu.SemaphoreType.DMA],
        5_000_000_000,
    )(scalars, frames, *pieces, table)
    return result[0], result[1:11], result[11]


def run_attn_forward(bits, scalars, memory, hidden, vecs, pieces, table):
    outs = (shape(SEG, D),) + SAVED
    result = call(
        functools.partial(attn_forward, bits, 4),
        "attn_forward",
        [SMEM, VMEM, VMEM, VMEM, ANY, ANY, ANY, ANY, VMEM],
        outs,
        [VMEM] * len(outs),
        [pltpu.SemaphoreType.DMA],
        5_000_000_000,
    )(scalars, memory, hidden, vecs, *pieces, table)
    return result[0], result[1:11]


ATTN_SCRATCH = [
    pltpu.VMEM((2 * BLOCK, 2 * BLOCK), BF16),
    pltpu.VMEM((SEG, D), BF16),
    pltpu.VMEM((D, ROWS), F32),
    pltpu.VMEM((D, ROWS), F32),
    pltpu.VMEM((D, ROWS), F32),
    pltpu.VMEM((SEG, D), F32),
    pltpu.VMEM((SEG, D), F32),
    pltpu.VMEM((5, D, D), BF16),
    pltpu.VMEM((BLOCK, D), F32),
    pltpu.SemaphoreType.DMA,
]


def run_attn_backward(bits, scalars, grad_mixed, saved, vecs, table):
    return call(
        functools.partial(attn_backward, bits, 4),
        "attn_backward",
        [SMEM] + [VMEM] * 13,
        (shape(GROUPS, 80, D, dtype=BF16), shape(GROUPS, 80, D, dtype=BF16), shape(SEG, D), shape(8, D)),
        [ANY, ANY, VMEM, VMEM],
        ATTN_SCRATCH,
        10_000_000_000,
    )(scalars, grad_mixed, *saved, vecs, table)


def run_attn_backward_last(bits, scalars, grad_mixed, saved, vecs, table, frames, *small_grads):
    return call(
        functools.partial(attn_backward, bits, 0),
        "attn_backward_last",
        [SMEM] + [VMEM] * 18,
        (shape(GROUPS, 96, D, dtype=BF16), shape(GROUPS, 96, D, dtype=BF16)),
        [ANY, ANY],
        ATTN_SCRATCH + [pltpu.VMEM((D, D), BF16), pltpu.SemaphoreType.DMA],
        10_000_000_000,
    )(scalars, grad_mixed, *saved, vecs, table, frames, *small_grads)


def run_feed_forward(bits, base, scalars, mixed, vecs, pieces):
    outs = (
        shape(SEG, D),
        shape(SEG, D, dtype=BF16),
        shape(SEG, FF, dtype=BF16),
        shape(SEG, FF, dtype=BF16),
        shape(4, D, D, dtype=BF16),
        shape(FF, D, dtype=BF16),
    )
    result = call(
        functools.partial(feed_forward, bits, base),
        "feed_forward",
        [SMEM, VMEM, VMEM, ANY, ANY, ANY, ANY],
        outs,
        [VMEM] * len(outs),
        [pltpu.SemaphoreType.DMA((2,))],
        4_000_000_000,
    )(scalars, mixed, vecs, *pieces)
    return result[0], result[1:]


def run_feed_backward(bits, base, scalars, grad_out, mixed, vecs, saved):
    return call(
        functools.partial(feed_backward, bits, base),
        "feed_backward",
        [SMEM] + [VMEM] * 8,
        (shape(GROUPS, 128, D, dtype=BF16), shape(GROUPS, 128, D, dtype=BF16), shape(SEG, D), shape(8, D)),
        [ANY, ANY, VMEM, VMEM],
        [
            pltpu.VMEM((SEG, FF), BF16),
            pltpu.VMEM((4, D, D), BF16),
            pltpu.VMEM((FF, D), BF16),
            pltpu.SemaphoreType.DMA((2,)),
        ],
        8_000_000_000,
    )(scalars, grad_out, mixed, vecs, *saved)


def run_head(bits, streams, scalars, output, targets, vecs, pieces):
    return call(
        functools.partial(head_pass, bits, streams),
        "head",
        [SMEM, VMEM, VMEM, VMEM, ANY, ANY, ANY, ANY],
        (
            shape(GROUPS, 32, D, dtype=BF16),
            shape(GROUPS, 32, D, dtype=BF16),
            shape(SEG, D),
            shape(8, D),
            shape(8, 128),
        ),
        [ANY, ANY, VMEM, VMEM, VMEM],
        [
            pltpu.VMEM((2, D, D), BF16),
            pltpu.VMEM((SEG, D), BF16),
            pltpu.VMEM((SEG, CODES), BF16),
            pltpu.VMEM((2, D, D), BF16),
            pltpu.SemaphoreType.DMA,
        ],
        2_000_000_000,
    )(scalars, output, targets, vecs, *pieces)


def spread(value, bits):
    count = lax.axis_size("dp")
    pairs = [
        (half * count + i, half * count + (i ^ bit)) for half, bit in enumerate(bits) for i in range(count)
    ]
    return lax.ppermute(value, ("section", "dp"), pairs)


def swap(value):
    return lax.ppermute(value, "section", [(0, 1), (1, 0)])


def gather_pieces(mine, bits):
    low = mine[None]
    steps = list(zip(*bits))
    for pair in steps[:-1]:
        low = jnp.concatenate([low, spread(low, pair)], 0)
    high = spread(low, steps[-1])
    return (low, high, swap(low), swap(high))


def reduce_pieces(keep, send, bits):
    total = keep.astype(F32) + swap(send).astype(F32)
    for pair in reversed(list(zip(*bits))):
        count = total.shape[0] // 2
        total = total[:count] + spread(total[count:].astype(BF16), pair).astype(F32)
    return total[0]


def add_up(value, bits):
    value = value + swap(value)
    for low, unused in zip(*bits):
        value = value + spread(value, (low, low))
    return value


def lanes_of(block):
    return [block[:, D * u : D * (u + 1)] for u in range(block.shape[1] // D)]


def sinus_table():
    where_at = (ROWS - 1 - jnp.arange(ROWS, dtype=jnp.int32)).astype(F32)[:, None]
    freqs = jnp.exp(-jnp.log(10000.0) * (2.0 * jnp.arange(D // 2, dtype=jnp.int32).astype(F32) / D))
    angles = where_at * freqs[None, :]
    return jnp.concatenate([jnp.sin(angles), jnp.cos(angles)], 1).astype(BF16)


def small_rows(w_in, vecs, gain, section):
    blank = jnp.zeros_like(vecs)
    return jnp.concatenate(
        [
            w_in,
            jnp.where(section == 0, vecs, blank),
            jnp.where(section == 0, blank, vecs),
            gain[None],
            jnp.zeros((BLOCK - 89, gain.shape[0]), vecs.dtype),
        ],
        0,
    )


def pack_shards(section, w_attn, w_out, w_pos, w_up, w_down, layer_vecs, w_in, w_head, gain_final):
    attn = lanes_of(w_attn[0]) + [w_out[0], w_pos[0]]
    ups = lanes_of(w_up[0])
    heads = lanes_of(w_head)
    small = small_rows(w_in, layer_vecs[0], gain_final, section)
    mark = lax.broadcasted_iota(jnp.int32, small.shape, 0)
    vecs_only = jnp.where((mark >= FEATS) & (mark < FEATS + 8), small, 0.0)
    small, vecs_only = (
        jnp.pad(jnp.transpose(item), ((0, 0), (0, D - BLOCK))) for item in (small, vecs_only)
    )

    def half_of(half, tail):
        rows = slice(16 * half, 16 * half + 16)
        return jnp.concatenate(
            [item[rows] for item in attn]
            + [item[rows] for item in ups]
            + [w_down[0, 64 * half : 64 * half + 64], tail[rows]],
            0,
        ).astype(BF16)

    first = section == 0
    kept = jnp.where(first, half_of(0, small), half_of(1, small))
    got = swap(jnp.where(first, half_of(1, vecs_only), half_of(0, vecs_only)))
    zero = jnp.where(first, kept, got)
    one = jnp.where(first, got, kept)
    head = jnp.where(
        first,
        jnp.concatenate([item[:16] for item in heads], 0),
        jnp.concatenate([item[16:] for item in heads], 0),
    ).astype(BF16)
    return (
        jnp.concatenate([zero[:80], kept[208:] + got[208:]], 0),
        zero[80:208],
        one[:80],
        jnp.concatenate([one[80:208], head], 0),
    )


def halves(whole, rows):
    return whole.reshape(GROUPS, 2, rows, whole.shape[1]).transpose(1, 0, 2, 3)


def gather_whole(section, w_attn, w_out, w_pos, w_up, w_down, layer_vecs, w_in, w_head, gain_final):
    def over(value, axis):
        return lax.all_gather(value.astype(BF16), "dp", axis=axis, tiled=True)

    def layers(value):
        return lax.all_gather(over(value[0], 0), "section", axis=0)

    attn, out, pos, up, down = (layers(item) for item in (w_attn, w_out, w_pos, w_up, w_down))
    vecs = lax.all_gather(over(layer_vecs[0], 1), "section", axis=0)
    small = jnp.concatenate(
        [over(w_in, 1), vecs[0], vecs[1], over(gain_final, 0)[None], jnp.zeros((BLOCK - 89, D), BF16)], 0
    )
    small = jnp.pad(jnp.transpose(small), ((0, 0), (0, D - BLOCK)))
    head = over(w_head, 0)

    def pieces(units):
        both = jnp.concatenate([halves(item, item.shape[0] // 32) for item in units], 2)
        own = lax.dynamic_index_in_dim(both, section, 0, keepdims=False)
        other = lax.dynamic_index_in_dim(both, 1 - section, 0, keepdims=False)
        return (own[:8], own[8:], other[:8], other[8:])

    return (
        pieces(lanes_of(attn[0]) + [out[0], pos[0], small]),
        pieces(lanes_of(up[0]) + [down[0]]),
        pieces(lanes_of(attn[1]) + [out[1], pos[1]]),
        pieces(lanes_of(up[1]) + [down[1]] + lanes_of(head)),
    )


def own_grads(section, attn_zero, feed_zero, attn_one, feed_one, head):
    first = section == 0
    zero = jnp.concatenate([attn_zero[:80], feed_zero], 0)
    one = jnp.concatenate([attn_one, feed_one], 0)
    both = jnp.concatenate([head, attn_zero[80:96]], 0)
    kept = jnp.concatenate([jnp.where(first, zero, one), both], 0)
    got = swap(jnp.concatenate([jnp.where(first, one, zero), both], 0))
    low = jnp.where(first, kept, got)
    high = jnp.where(first, got, kept)

    def unit(start, rows):
        return jnp.concatenate([low[start : start + rows], high[start : start + rows]], 0)

    small = jnp.transpose(unit(240, 16)[:, :BLOCK])
    return (
        jnp.concatenate([unit(16 * u, 16) for u in range(3)], 1),
        unit(48, 16),
        unit(64, 16),
        jnp.concatenate([unit(80 + 16 * u, 16) for u in range(4)], 1),
        unit(144, 64),
        jnp.where(first, small[80:84], small[84:88]),
        small[:80],
        jnp.concatenate([unit(208 + 16 * u, 16) for u in range(2)], 1),
        small[88],
    )


def whole_grads(section, sums):
    count = lax.axis_size("dp")
    place = lax.axis_index("dp")
    both = [lax.all_gather(lax.psum(item, "dp"), "section", axis=0) for item in sums]

    def unit(index, start, rows):
        item = both[index][:, :, start : start + rows]
        return item.transpose(1, 0, 2, 3).reshape(GROUPS * 2 * rows, D)

    def layer(attn, feed):
        return (
            jnp.concatenate([unit(attn, 16 * u, 16) for u in range(3)], 1),
            unit(attn, 48, 16),
            unit(attn, 64, 16),
            jnp.concatenate([unit(feed, 16 * u, 16) for u in range(4)], 1),
            unit(feed, 64, 64),
        )

    small = jnp.transpose(unit(0, 80, 16)[:, :BLOCK])
    zero = layer(0, 1) + (small[80:84],)
    one = layer(2, 3) + (small[84:88],)
    ends = (small[:80], jnp.concatenate([unit(4, 16 * u, 16) for u in range(2)], 1), small[88])
    squares = sum((jnp.sum(item * item) for item in zero + one + ends))
    dims = (0, 0, 0, 0, 0, 1, 1, 0, 0)
    grads = tuple((jnp.where(section == 0, a, b) for a, b in zip(zero, one))) + ends
    return squares, tuple(
        (
            lax.dynamic_slice_in_dim(item, place * (item.shape[dim] // count), item.shape[dim] // count, dim)
            for item, dim in zip(grads, dims)
        )
    )


def adam_step(weight, grad, first, second, rate, decay, factor):
    grad = grad * factor
    first = 0.9 * first + 0.1 * grad
    second = 0.999 * second + 0.001 * grad * grad
    ratio = first / (1.0 - 0.9**STEP) / (jnp.sqrt(second / (1.0 - 0.999**STEP)) + 1e-08)
    return (weight - rate * (ratio + decay * weight), first, second)


def local(frames, targets, lengths, *state):
    params, firsts, seconds = (state[:9], state[9:18], state[18:])
    section = lax.axis_index("section")
    streams = lax.axis_size("dp")
    ringed = streams == GROUPS
    if ringed:
        bits = ((4, 8, 1, 2), (4, 8, 2, 1))
        place = lax.axis_index("dp")
        chunks = [gather_pieces(item, bits) for item in pack_shards(section, *params)]
    else:
        bits = ((1, 2, 4, 8), (1, 2, 4, 8))
        place = jnp.int32(0)
        chunks = gather_whole(section, *params)
    length = lengths[0]
    scalars = jnp.stack([place, section, length, section]).astype(jnp.int32)
    table = sinus_table()
    rows = lax.dynamic_slice_in_dim(
        jnp.pad(frames[0], ((MEM, 0), (0, BLOCK - FEATS))), section * SEG, ROWS, 0
    )
    codes = lax.dynamic_slice_in_dim(targets[0], section * SEG, SEG, 0)[:, None]

    mixed_zero, saved_zero, vecs = run_attn_forward_first(bits, scalars, rows, chunks[0], table)
    out_zero, fed_zero = run_feed_forward(bits, 0, scalars, mixed_zero, vecs, chunks[1])
    memory = lax.ppermute(out_zero[SEG - MEM :], "section", [(0, 1)])
    mixed_one, saved_one = run_attn_forward(bits, scalars, memory, out_zero, vecs, chunks[2], table)
    out_one, fed_one = run_feed_forward(bits, 4, scalars, mixed_one, vecs, chunks[3])
    head_keep, head_send, grad, gain_final, loss = run_head(
        bits, streams, scalars, out_one, codes, vecs, chunks[3]
    )
    feed_keep, feed_send, grad, gain_one = run_feed_backward(bits, 4, scalars, grad, mixed_one, vecs, fed_one)
    attn_keep, attn_send, grad, vecs_one = run_attn_backward(bits, scalars, grad, saved_one, vecs, table)
    feed_keep_zero, feed_send_zero, grad, gain_zero = run_feed_backward(
        bits, 0, scalars, grad, mixed_zero, vecs, fed_zero
    )
    attn_keep_zero, attn_send_zero = run_attn_backward_last(
        bits, scalars, grad, saved_zero, vecs, table, rows, gain_zero, vecs_one, gain_one, gain_final
    )
    pairs = (
        (attn_keep_zero, attn_send_zero),
        (feed_keep_zero, feed_send_zero),
        (attn_keep, attn_send),
        (feed_keep, feed_send),
        (head_keep, head_send),
    )
    if ringed:
        sums = [reduce_pieces(keep, send, bits) for keep, send in pairs]
        grads = own_grads(section, *sums)
        squares = sum((jnp.sum(item * item) for item in sums))
        total = add_up(jnp.stack([squares, loss[0, 0]])[None], bits)
        squares, loss_sum = total[0, 0], total[0, 1]
    else:
        sums = [keep.astype(F32) + swap(send).astype(F32) for keep, send in pairs]
        squares, grads = whole_grads(section, sums)
        loss_sum = lax.psum(loss[0, 0], ("section", "dp"))
    grad_norm = jnp.sqrt(squares)
    factor = jnp.minimum(1.0, CLIP / (grad_norm + 1e-06))
    results = []
    for index in range(9):
        vector = index in (5, 8)
        grad = grads[index][None] if index < 6 else grads[index]
        results.append(
            adam_step(
                params[index],
                grad,
                firsts[index],
                seconds[index],
                0.3 if vector else 0.03,
                0.0 if vector else 0.01,
                factor,
            )
        )
    news, moms, sqs = zip(*results)
    return (*news, *moms, *sqs, grad_norm, loss_sum)


def solution(mesh):
    weights = (
        P("section", "dp", None),
        P("section", "dp", None),
        P("section", "dp", None),
        P("section", "dp", None),
        P("section", "dp", None),
        P("section", None, "dp"),
        P(None, "dp"),
        P("dp", None),
        P("dp"),
    )
    return jax.shard_map(
        local,
        mesh=mesh,
        in_specs=(P("dp", None, None), P("dp", None), P("dp")) + weights * 3,
        out_specs=weights * 3 + (P(), P()),
        check_vma=False,
    )
```

```python
import functools

import jax
import jax.numpy as jnp
from jax import lax
from jax.experimental import pallas as pl
from jax.experimental.pallas import tpu as pltpu
from jax.sharding import PartitionSpec as P

D = 512
FF = 2048
CODES = 1024
FEATS = 80
MEM = 256
SEG = 512
SEGS = 2
STEP = 10
ROWS = MEM + SEG
BLOCK = 128
PAIRS = 4
WIDE = 18 * BLOCK
GROUPS = 16
IN_ORDER = ((1, 2, 4, 8), (1, 2, 4, 8))
NEG = -1e30
CLIP = 0.02
SCALE = 0.125
F32 = jnp.float32
BF16 = jnp.bfloat16
SPANS = tuple((MEM + BLOCK * (b + 1) for b in range(4)))
STARTS = tuple((sum(SPANS[:b]) for b in range(4)))
VMEM_LIMIT = 56 * 1024 * 1024


def nn(left, right):
    return jnp.dot(left, right, preferred_element_type=F32)


def nt(left, right):
    return lax.dot_general(left, right, (((1,), (1,)), ((), ())), preferred_element_type=F32)


def tn(left, right):
    return lax.dot_general(left, right, (((0,), (0,)), ((), ())), preferred_element_type=F32)


def norm_parts(values):
    center = values - jnp.mean(values, -1, keepdims=True)
    spread = jnp.mean(center * center, -1, keepdims=True)
    inverse = lax.rsqrt(spread + 1e-05)
    return center * inverse, inverse


def norm_back(unit, inverse, gain, grad):
    scaled = grad * gain
    first = jnp.mean(scaled, -1, keepdims=True)
    second = jnp.mean(scaled * unit, -1, keepdims=True)
    return inverse * (scaled - first - unit * second), jnp.sum(grad * unit, 0, keepdims=True)


def group_of(bits, spot, place, half):
    if bits == IN_ORDER:
        return spot
    code = jnp.int32(0)
    for index, (low, high) in enumerate(zip(bits[0], bits[1])):
        bit = lax.rem(lax.div(spot, 1 << index), 2)
        code = code + bit * jnp.where(half == 0, low, high)
    return jnp.bitwise_xor(place, code)


def copies(bits, place, half, pieces, units, rows, sem, outward):
    count = GROUPS // len(pieces)
    for index, slab in enumerate(pieces):

        def one(spot, carry):
            group = group_of(bits, index * count + spot, place, half)
            for whole, first in units:
                there = whole.at[pl.ds(pl.multiple_of((group * 2 + half) * rows, rows), rows), :]
                here = slab.at[spot, pl.ds(first, rows), pl.ds(0, whole.shape[1])]
                if outward:
                    pltpu.make_async_copy(there, here, sem).start()
                else:
                    pltpu.make_async_copy(here, there, sem).start()
            return carry

        lax.fori_loop(0, count, one, 0)


def fetch(source, target, sem):
    copy = pltpu.make_async_copy(source, target, sem)
    copy.start()
    return copy


def arrived(buffer, sem):
    pltpu.make_async_copy(buffer, buffer, sem).wait()


def tri_mask():
    row = lax.broadcasted_iota(jnp.int32, (2 * BLOCK, BLOCK), 0)
    col = lax.broadcasted_iota(jnp.int32, (2 * BLOCK, BLOCK), 1)
    return col <= lax.rem(row, BLOCK)


def stack_heads(part):
    col = lax.broadcasted_iota(jnp.int32, part.shape, 1)
    zero = jnp.zeros_like(part)
    return jnp.concatenate(
        [jnp.where(col < 64, part, zero), jnp.where(col < 64, zero, part)], 0
    )


def pick_heads(both):
    col = lax.broadcasted_iota(jnp.int32, (BLOCK, BLOCK), 1)
    return jnp.where(col < 64, both[:BLOCK], both[BLOCK:])


def shift(both, amount):
    return jnp.concatenate(
        [pltpu.roll(part, amount, 1, stride=1, stride_axis=0) for part in (both[:BLOCK], both[BLOCK:])], 0
    )


def masked(score, triangle, first):
    return jnp.concatenate([score[:, :first], jnp.where(triangle, score[:, first:], NEG)], 1)


def lanes(pair):
    return pl.ds(pl.multiple_of(pair * BLOCK, BLOCK), BLOCK)


def project(bits, base, *refs):
    first_layer = base == 0
    if first_layer:
        (scalars, frames, own_low, own_high, other_low, other_high, table) = refs[:7]
        (normed, query_u, query_v, keys, values, rel, weights_o, hidden, vecs, small_o) = refs[7:17]
        (weights, in_sem, out_sem, joined, small, small_sem) = refs[17:]
    else:
        (scalars, memory, hidden, vecs, own_low, own_high, other_low, other_high, table) = refs[:9]
        (normed, query_u, query_v, keys, values, rel, weights_o) = refs[9:16]
        (weights, in_sem, out_sem) = refs[16:]
    place, half = scalars[0], scalars[1]
    both = ((half, (own_low, own_high)), (1 - half, (other_low, other_high)))
    if first_layer:
        for which, pieces in both:
            copies(bits, place, which, pieces, [(small, 64)], 16, small_sem, False)
    units = [(weights.at[u], 16 * u) for u in range(4)]
    for which, pieces in both:
        copies(bits, place, which, pieces, units, 16, in_sem, False)
    if first_layer:
        arrived(small, small_sem)
        small_out = fetch(small, small_o, out_sem.at[1])
        vecs[...] = jnp.transpose(small[...].astype(F32))[80:96]
        for b in range(3):
            rows = pl.ds(256 * b, 256)
            joined[rows, :] = nt(frames[rows, :], small[...])
        hidden[...] = joined[MEM:, :]
        sources = [joined.at[pl.ds(256 * b, 256)] for b in range(3)]
    else:
        sources = [memory, hidden.at[pl.ds(0, 256)], hidden.at[pl.ds(256, 256)]]
    gain = vecs[base : base + 1, :]
    bias_u = vecs[base + 2 : base + 3, :]
    bias_v = vecs[base + 3 : base + 4, :]
    arrived(weights, in_sem)
    weights_out = fetch(weights, weights_o, out_sem.at[0])
    rel[...] = nn(table[...], weights[3]).astype(BF16)
    for b in range(3):
        unit, unused = norm_parts(sources[b][...])
        normed[pl.ds(256 * b, 256), :] = (unit * gain).astype(BF16)
    keys[...] = nn(normed[...], weights[1]).astype(BF16)
    values[...] = nn(normed[...], weights[2]).astype(BF16)
    query = nn(normed[MEM:, :], weights[0])
    query_u[...] = (query + bias_u).astype(BF16)
    query_v[...] = (query + bias_v).astype(BF16)
    weights_out.wait()
    if first_layer:
        small_out.wait()


def attend(scalars, query_u_h, query_v_h, keys_h, values_h, rel_h, attended, probs_o,
           query_u, query_v, keys, values, rel, probs, pair_sem, out_sem):
    length, segment = scalars[2], scalars[3]

    def parts(pair):
        lane = lanes(pair)
        return [
            pltpu.make_async_copy(there.at[:, lane], here.at[:, lane], pair_sem.at[pair, index])
            for index, (there, here) in enumerate(
                ((query_u_h, query_u), (query_v_h, query_v), (keys_h, keys), (values_h, values), (rel_h, rel))
            )
        ]

    for pair in range(PAIRS):
        for copy in parts(pair):
            copy.start()
    spot = lax.broadcasted_iota(jnp.int32, (1, ROWS), 1)
    where_at = segment * SEG + spot - MEM
    allowed = (where_at < length) & ((spot >= MEM) | (segment >= 1))
    bias = jnp.where(allowed, 0.0, NEG)
    triangle = tri_mask()

    def two_pairs(step, carry):
        tiles = [(2 * step + one, b) for one in range(2) for b in range(4)]
        for one in range(2):
            for copy in parts(2 * step + one):
                copy.wait()
        full = [
            nt(stack_heads(query_v[BLOCK * b : BLOCK * (b + 1), lanes(pair)]) * SCALE,
               rel[ROWS - SPANS[b] : ROWS, lanes(pair)])
            for pair, b in tiles
        ]
        content = [
            nt(stack_heads(query_u[BLOCK * b : BLOCK * (b + 1), lanes(pair)]) * SCALE,
               keys[0 : SPANS[b], lanes(pair)])
            for pair, b in tiles
        ]
        full = [shift(item, SPANS[b] - BLOCK + 1) for item, (pair, b) in zip(full, tiles)]
        score = [
            masked(one + two + bias[:, : SPANS[b]], triangle, SPANS[b] - BLOCK)
            for one, two, (pair, b) in zip(content, full, tiles)
        ]
        top = [jnp.max(item, -1, keepdims=True) for item in score]
        expo = [jnp.exp(item - most) for item, most in zip(score, top)]
        total = [jnp.sum(item, -1, keepdims=True) for item in expo]
        prob = [(item * (1.0 / most)).astype(BF16) for item, most in zip(expo, total)]
        for item, (pair, b) in zip(prob, tiles):
            probs[pair, :, STARTS[b] : STARTS[b] + SPANS[b]] = item
        for one in range(2):
            pair = 2 * step + one
            pltpu.make_async_copy(probs.at[pair], probs_o.at[pair], out_sem.at[pair]).start()
        found = [nn(item, values[0 : SPANS[b], lanes(pair)]) for item, (pair, b) in zip(prob, tiles)]
        for item, (pair, b) in zip(found, tiles):
            attended[BLOCK * b : BLOCK * (b + 1), lanes(pair)] = pick_heads(item).astype(BF16)
        return carry

    lax.fori_loop(0, PAIRS // 2, two_pairs, 0)
    for pair in range(PAIRS):
        pltpu.make_async_copy(probs.at[pair], probs_o.at[pair], out_sem.at[pair]).wait()


def attend_back(bits, second, *refs):
    (scalars, grad_att, normed, table, query_u_h, query_v_h, keys_h, values_h, rel_h, probs_h) = refs[:10]
    rest = refs[10:]
    if second:
        staged_h = rest[0]
        rest = rest[1:]
        (keep, send) = rest[4:6]
        sums, rest = rest[3], rest[:3] + rest[6:]
    else:
        (staged, sums) = rest[3:5]
        rest = rest[:3] + rest[5:]
    (grad_query, grad_keys, grad_values,
     query_u, query_v, keys, values, rel, probs, flip, acc_keys, acc_values, acc_rel,
     grad_qu, grad_qv, pair_sem) = rest[:16]
    first_pair = 2 if second else 0

    def parts(pair):
        lane, here = lanes(pair + first_pair), lanes(pair)
        moves = [(probs_h.at[pair + first_pair], probs.at[pair])]
        for there, target in (
            (query_u_h, query_u), (query_v_h, query_v), (keys_h, keys), (values_h, values), (rel_h, rel)
        ):
            moves.append((there.at[:, lane], target.at[:, here]))
        return [
            pltpu.make_async_copy(there, target, pair_sem.at[pair, index])
            for index, (there, target) in enumerate(moves)
        ]

    for pair in range(2):
        for copy in parts(pair):
            copy.start()
    if second:
        staged, sem, staged_sem = rest[16:]
        staged_copy = fetch(staged_h, staged.at[:, :, pl.ds(0, 256)], staged_sem)
    row = lax.broadcasted_iota(jnp.int32, (2 * BLOCK, 2 * BLOCK), 0)
    col = lax.broadcasted_iota(jnp.int32, (2 * BLOCK, 2 * BLOCK), 1)
    back = (row // BLOCK) * BLOCK + BLOCK - 1 - lax.rem(row, BLOCK)
    flip[...] = (col == back).astype(F32).astype(BF16)

    def one_pair(pair, carry):
        lane = lanes(pair)
        for copy in parts(pair):
            copy.wait()
        order = (3, 2, 1, 0)
        flipped = flip[...]
        stack_g = [
            stack_heads(grad_att[BLOCK * b : BLOCK * (b + 1), lanes(pair + first_pair)]) for b in order
        ]
        stack_u = [stack_heads(query_u[BLOCK * b : BLOCK * (b + 1), lane]) * SCALE for b in order]
        stack_v = [
            nn(flipped, stack_heads(query_v[BLOCK * b : BLOCK * (b + 1), lane]) * SCALE).astype(BF16)
            for b in order
        ]
        prob_b = [probs[pair, :, STARTS[b] : STARTS[b] + SPANS[b]] for b in order]
        grad_prob = [nt(one, values[0 : SPANS[b], lane]) for one, b in zip(stack_g, order)]
        part_values = [tn(one, two) for one, two in zip(stack_g, prob_b)]
        prob = [item.astype(F32) for item in prob_b]
        inner = [jnp.sum(one * two, -1, keepdims=True) for one, two in zip(prob, grad_prob)]
        grad_score = [
            (one * (two - three)).astype(BF16) for one, two, three in zip(prob, grad_prob, inner)
        ]
        turned = [nn(flipped, item) for item in grad_score]
        found_u = [nn(item, keys[0 : SPANS[b], lane]) for item, b in zip(grad_score, order)]
        part_keys = [tn(one, two) for one, two in zip(stack_u, grad_score)]
        grad_full = [shift(item, 0).astype(BF16) for item in turned]
        found_v = [nn(item, rel[ROWS - SPANS[b] : ROWS, lane]) for item, b in zip(grad_full, order)]
        part_rel = [tn(one, two) for one, two in zip(stack_v, grad_full)]
        for index, b in enumerate(order):
            span = SPANS[b]
            rows = pl.ds(BLOCK * b, BLOCK)
            grad_qu[rows, lane] = pick_heads(found_u[index]) * SCALE
            grad_qv[rows, lane] = pick_heads(found_v[index]) * SCALE
            if b == 3:
                acc_keys[lane, :] = part_keys[index]
                acc_values[lane, :] = part_values[index]
                acc_rel[lane, :] = part_rel[index]
            else:
                acc_keys[lane, 0:span] += part_keys[index]
                acc_values[lane, 0:span] += part_values[index]
                acc_rel[lane, ROWS - span : ROWS] += part_rel[index]
        return carry

    lax.fori_loop(0, 2, one_pair, 0)
    grad_keys[...] = jnp.transpose(acc_keys[...]).astype(BF16)
    grad_values[...] = jnp.transpose(acc_values[...]).astype(BF16)
    grad_rel = jnp.transpose(acc_rel[...]).astype(BF16)
    sums[...] = jnp.zeros_like(sums)
    sums[2:3, :] = jnp.sum(grad_qu[...], 0, keepdims=True)
    sums[3:4, :] = jnp.sum(grad_qv[...], 0, keepdims=True)
    flip_one = flip[0:BLOCK, 0:BLOCK]
    for b in range(4):
        rows = pl.ds(BLOCK * b, BLOCK)
        part = grad_qv[rows, :]
        high = part.astype(BF16)
        low = (part - high.astype(F32)).astype(BF16)
        grad_query[rows, :] = (grad_qu[rows, :] + nn(flip_one, high) + nn(flip_one, low)).astype(BF16)
    cols = slice(256, 512) if second else slice(None)
    staged[1, :, cols] = tn(normed[...], grad_keys[...]).astype(BF16)
    staged[2, :, cols] = tn(normed[...], grad_values[...]).astype(BF16)
    staged[3, :, cols] = tn(table[...], grad_rel).astype(BF16)
    staged[0, :, cols] = tn(normed[MEM:, :], grad_query[...]).astype(BF16)
    if second:
        staged_copy.wait()
        place, half = scalars[0], scalars[1]
        units = [(staged.at[u], 16 * u) for u in range(4)]
        copies(bits, place, half, (keep,), units, 16, sem, True)
        copies(bits, place, 1 - half, (send,), units, 16, sem, True)
        arrived(staged, sem)


def input_grads(bits, base, *refs):
    last_kernel = base == 0
    (scalars, weights, query_a, keys_a, values_a, sums_a, query_b, keys_b, values_b, sums_b, grad_mixed, vecs) = refs[:12]
    if last_kernel:
        (frames, small, gain_two, vecs_one, gain_two_one, gain_final, keep, send, joined, smalls, staged, sem) = refs[12:]
        joined[...] = nt(frames[...], small[...])
        before, here, first = joined, joined, MEM
    else:
        (memory, hidden, grad_hidden, grad_vecs) = refs[12:]
        before, here, first = memory, hidden, 0
    place, half = scalars[0], scalars[1]
    gain = vecs[base : base + 1, :]
    left, right = slice(0, 256), slice(256, 512)
    grad_keys = (
        nt(keys_a[...], weights[1, :, left])
        + nt(keys_b[...], weights[1, :, right])
        + nt(values_a[...], weights[2, :, left])
        + nt(values_b[...], weights[2, :, right])
    )
    grad_query = nt(query_a[...], weights[0, :, left]) + nt(query_b[...], weights[0, :, right])
    unit, inverse = norm_parts(before[0:MEM, :])
    grad_gain = jnp.sum(grad_keys[0:MEM] * unit, 0, keepdims=True)
    unit, inverse = norm_parts(here[first : first + SEG, :])
    grad_joined, gains = norm_back(unit, inverse, gain, grad_keys[MEM:] + grad_query)
    grad_gain = grad_gain + gains
    grad_in = grad_mixed[...] + grad_joined
    if last_kernel:
        smalls[...] = tn(frames[MEM:, :], grad_in.astype(BF16))
        smalls[80:81, :] = grad_gain
        smalls[81:82, :] = gain_two[0:1, :]
        smalls[82:84, left] = sums_a[2:4, :]
        smalls[82:84, right] = sums_b[2:4, :]
        smalls[84:88, :] = vecs_one[0:4, :]
        smalls[85:86, :] = gain_two_one[0:1, :]
        smalls[88:89, :] = gain_final[0:1, :]
        staged[...] = jnp.zeros_like(staged)
        staged[:, 0:BLOCK] = jnp.transpose(smalls[...]).astype(BF16)
        units = [(staged, 0)]
        copies(bits, place, half, (keep,), units, 16, sem, True)
        copies(bits, place, 1 - half, (send,), units, 16, sem, True)
        arrived(staged, sem)
    else:
        grad_hidden[...] = grad_in
        grad_vecs[:, left] = sums_a[...]
        grad_vecs[:, right] = sums_b[...]
        grad_vecs[0:1, :] = grad_gain


def feed_weights(bits, place, both, up, down, out, sem):
    for index, (units, rows) in enumerate(
        (([(out, 128)], 16), ([(up.at[u], 16 * u) for u in range(4)], 16), ([(down, 64)], 64))
    ):
        for which, pieces in both:
            copies(bits, place, which, pieces, units, rows, sem.at[index], False)


def feed_grads_out(bits, place, half, keep, send, up, down, out, sem):
    ups = [(up.at[u], 16 * u) for u in range(4)]
    for which, pieces in ((half, (keep,)), (1 - half, (send,))):
        copies(bits, place, which, pieces, ups, 16, sem.at[0], True)
        copies(bits, place, which, pieces, [(down, 64)], 64, sem.at[1], True)
        copies(bits, place, which, pieces, [(out, 128)], 16, sem.at[2], True)


def feed_mixed(residual, attended, out, gain, mixed, normed):
    mixed[...] = residual[...] + nn(attended[...], out[...])
    for b in range(2):
        rows = pl.ds(256 * b, 256)
        unit, unused = norm_parts(mixed[rows, :])
        normed[rows, :] = (unit * gain).astype(BF16)


def feed_inner(normed, up, active, slope):
    later = nn(normed[...], up[0])
    for u in range(4):
        inner = later
        if u < 3:
            later = nn(normed[...], up[u + 1])
        square = inner * inner
        bent = jnp.tanh(0.7978845608028654 * (inner + 0.044715 * (square * inner)))
        half = 0.5 * (1.0 + bent)
        active[:, 512 * u : 512 * (u + 1)] = (inner * half).astype(BF16)
        slope[:, 512 * u : 512 * (u + 1)] = (
            half
            + (0.5 * inner)
            * (1.0 - bent * bent)
            * (0.7978845608028654 * (1.0 + (3 * 0.044715) * square))
        ).astype(BF16)


def feed_output(mixed, active, down, output):
    output[...] = mixed[...] + nn(active[...], down[...])


def feed_forward(bits, base, scalars, residual, attended, vecs, own_low, own_high, other_low, other_high,
                 output, mixed, memory, normed_o, active_o, slope_o, up_o, down_o, out_o,
                 normed, active, slope, up, down, out, sem, out_sem):
    place, half = scalars[0], scalars[1]
    both = ((half, (own_low, own_high)), (1 - half, (other_low, other_high)))
    feed_weights(bits, place, both, up, down, out, sem)
    arrived(out, sem.at[0])
    outs = [fetch(out, out_o, out_sem.at[5])]
    feed_mixed(residual, attended, out, vecs[base + 1 : base + 2, :], mixed, normed)
    outs.append(fetch(normed, normed_o, out_sem.at[0]))
    arrived(up, sem.at[1])
    outs.append(fetch(up, up_o, out_sem.at[1]))
    feed_inner(normed, up, active, slope)
    outs.append(fetch(active, active_o, out_sem.at[2]))
    outs.append(fetch(slope, slope_o, out_sem.at[3]))
    arrived(down, sem.at[2])
    outs.append(fetch(down, down_o, out_sem.at[4]))
    feed_output(mixed, active, down, output)
    memory[...] = output[SEG - MEM :, :]
    for copy in outs:
        copy.wait()


def feed_back(base, grad_out, mixed, vecs, attended, normed, active, slope, up, down, out,
              grad_mixed, grad_att, grad_gain, grad_inner, staged_up, staged_down, staged_out):
    grad_y = grad_out[...].astype(BF16)
    later = nt(grad_y, down[0:512, :])
    grad_normed = jnp.zeros((SEG, D), F32)
    for u in range(4):
        cols = slice(512 * u, 512 * (u + 1))
        part = later
        if u < 3:
            later = nt(grad_y, down[512 * (u + 1) : 512 * (u + 2), :])
        staged_down[cols, :] = tn(active[:, cols], grad_y).astype(BF16)
        grad_inner[:, cols] = (part * slope[:, cols].astype(F32)).astype(BF16)
        grad_normed = grad_normed + nt(grad_inner[:, cols], up[u])
        staged_up[u] = tn(normed[...], grad_inner[:, cols]).astype(BF16)
    unit, inverse = norm_parts(mixed[...])
    grad_here, gains = norm_back(unit, inverse, vecs[base + 1 : base + 2, :], grad_normed)
    grad = grad_out[...] + grad_here
    grad_mixed[...] = grad
    grad_b = grad.astype(BF16)
    grad_att[...] = nt(grad_b, out[...]).astype(BF16)
    staged_out[...] = tn(attended[...], grad_b).astype(BF16)
    grad_gain[...] = jnp.broadcast_to(gains, grad_gain.shape)


def feed_backward(bits, base, scalars, grad_out, mixed, vecs, attended,
                  normed_h, active_h, slope_h, up_h, down_h, out_h,
                  keep, send, grad_mixed, grad_att, grad_gain,
                  normed, active, slope, up, down, out, grad_inner, staged_up, staged_down, staged_out,
                  in_sem, sem):
    moves = [
        fetch(there, here, in_sem.at[index])
        for index, (there, here) in enumerate(
            ((down_h, down), (slope_h, slope), (active_h, active), (normed_h, normed), (up_h, up), (out_h, out))
        )
    ]
    for copy in moves:
        copy.wait()
    feed_back(base, grad_out, mixed, vecs, attended, normed, active, slope, up, down, out,
              grad_mixed, grad_att, grad_gain, grad_inner, staged_up, staged_down, staged_out)
    feed_grads_out(bits, scalars[0], scalars[1], keep, send, staged_up, staged_down, staged_out, sem)
    arrived(staged_up, sem.at[0])
    arrived(staged_down, sem.at[1])
    arrived(staged_out, sem.at[2])


def top_kernel(bits, streams, scalars, residual, attended, targets, vecs, own_low, own_high, other_low, other_high,
               keep, send, grad_mixed, grad_att, grad_gain, final_gain, loss,
               normed, active, slope, up, down, out, mixed, output, grad_out, table, final, grad_logits, staged,
               grad_inner, staged_up, staged_down, staged_out, head_sem, sem, out_sem):
    place, half, length, segment = scalars[0], scalars[1], scalars[2], scalars[3]
    both = ((half, (own_low, own_high)), (1 - half, (other_low, other_high)))
    feed_weights(bits, place, both, up, down, out, sem)
    units = [(table.at[u], 144 + 16 * u) for u in range(2)]
    for which, pieces in both:
        copies(bits, place, which, pieces, units, 16, head_sem, False)
    arrived(out, sem.at[0])
    feed_mixed(residual, attended, out, vecs[5:6, :], mixed, normed)
    arrived(up, sem.at[1])
    feed_inner(normed, up, active, slope)
    arrived(down, sem.at[2])
    feed_output(mixed, active, down, output)
    arrived(table, head_sem)
    size = length.astype(F32)
    codes = jnp.transpose(jnp.broadcast_to(targets[...].astype(F32), (BLOCK, SEG))).astype(jnp.int32)
    gain = vecs[8:9, :]
    gains = jnp.zeros((1, D), F32)
    terms = jnp.zeros((1, 1), F32)
    for b in range(2):
        rows = pl.ds(256 * b, 256)
        unit, inverse = norm_parts(output[rows, :])
        fin = (unit * gain).astype(BF16)
        final[rows, :] = fin
        logits = jnp.concatenate([nn(fin, table[0]), nn(fin, table[1])], 1)
        top = jnp.max(logits, -1, keepdims=True)
        expo = jnp.exp(logits - top)
        total = jnp.sum(expo, -1, keepdims=True)
        picks = lax.broadcasted_iota(jnp.int32, logits.shape, 1) == codes[256 * b : 256 * (b + 1), 0:1]
        picked = jnp.sum(jnp.where(picks, logits, 0.0), -1, keepdims=True)
        spot = segment * SEG + 256 * b + lax.broadcasted_iota(jnp.int32, (256, 1), 0)
        weight = jnp.where(spot < length, 1.0 / size, 0.0)
        terms = terms + jnp.sum((top + jnp.log(total) - picked) * weight, keepdims=True)
        grad = (expo * (1.0 / total) - jnp.where(picks, 1.0, 0.0)) * (weight * (1.0 / streams))
        grad_b = grad.astype(BF16)
        grad_logits[rows, :] = grad_b
        grad_final = nt(grad_b[:, 0:512], table[0]) + nt(grad_b[:, 512:1024], table[1])
        grad_here, gain_here = norm_back(unit, inverse, gain, grad_final)
        grad_out[rows, :] = grad_here
        gains = gains + gain_here
    for u in range(2):
        staged[u] = tn(final[...], grad_logits[:, 512 * u : 512 * (u + 1)]).astype(BF16)
    units = [(staged.at[u], 144 + 16 * u) for u in range(2)]
    copies(bits, place, half, (keep,), units, 16, head_sem, True)
    copies(bits, place, 1 - half, (send,), units, 16, head_sem, True)
    final_gain[...] = jnp.broadcast_to(gains, final_gain.shape)
    loss[...] = jnp.broadcast_to(terms, loss.shape)
    feed_back(4, grad_out, mixed, vecs, attended, normed, active, slope, up, down, out,
              grad_mixed, grad_att, grad_gain, grad_inner, staged_up, staged_down, staged_out)
    feed_grads_out(bits, place, half, keep, send, staged_up, staged_down, staged_out, out_sem)
    arrived(staged, head_sem)
    arrived(staged_up, out_sem.at[0])
    arrived(staged_down, out_sem.at[1])
    arrived(staged_out, out_sem.at[2])


def finish(counts, *refs):
    scalars, loss = refs[0], refs[1]
    total_count = sum(counts)
    sources = refs[2 : 2 + total_count]
    kept, sent, total = refs[2 + total_count : 5 + total_count]
    buffers, sem = refs[5 + total_count : -1], refs[-1]
    moves = [fetch(there.at[0], here, sem.at[index]) for index, (there, here) in enumerate(zip(sources, buffers))]
    for copy in moves:
        copy.wait()
    sums = []
    start = 0
    for count in counts:
        item = buffers[start][...].astype(F32)
        for other in buffers[start + 1 : start + count]:
            item = item + other[...].astype(F32)
        sums.append(item)
        start += count
    attn_zero, feed_zero, attn_one, feed_one, small = sums[0], sums[1], sums[2], sums[3], sums[4]
    merged = sums[5]
    attn_zero = attn_zero + merged[0:64]
    small = small + merged[64:80]
    first = scalars[1] == 0
    lone = jnp.zeros((1, 1), F32)
    for zero, one, rows, begin in ((attn_zero, attn_one, 64, 0), (feed_zero, feed_one[0:144], 144, 64)):
        kept[begin : begin + rows, :] = jnp.where(first, zero, one)
        sent[begin : begin + rows, :] = jnp.where(first, one, zero)
        lone = lone + jnp.sum(zero * zero + one * one, keepdims=True)
    head = feed_one[144:176]
    lone = lone + jnp.sum(head * head, keepdims=True) + jnp.sum(small * small, keepdims=True)
    for target in (kept, sent):
        target[208:240, :] = head
        target[240:256, :] = small
    column = lax.broadcasted_iota(jnp.int32, (8, 128), 1)
    total[...] = jnp.where(column == 0, lone, 0.0) + jnp.where(column == 1, loss[...], 0.0)


def adam_step(weight, grad, first, second, rate, decay, factor):
    grad = grad * factor
    first = 0.9 * first + 0.1 * grad
    second = 0.999 * second + 0.001 * grad * grad
    ratio = first / (1.0 - 0.9**STEP) / (jnp.sqrt(second / (1.0 - 0.999**STEP)) + 1e-08)
    return (weight - rate * (ratio + decay * weight), first, second)


def update(scalars, total, kept, got, *refs):
    ins, outs, small = refs[:27], refs[27:56], refs[56]
    first = scalars[1] == 0
    squares = jnp.sum(total[0:1, 0:1], keepdims=True)
    norm = jnp.sqrt(squares)
    outs[27][...] = norm
    outs[28][...] = total[0:1, 1:2]
    factor = jnp.minimum(1.0, CLIP / (norm + 1e-06))

    def half_of(half, start, rows):
        here, there = kept[start : start + rows, :], got[start : start + rows, :]
        return jnp.where(first == (half == 0), here, there)

    def apply(index, spot, grad, rate, decay):
        results = adam_step(
            ins[index][spot], grad, ins[9 + index][spot], ins[18 + index][spot], rate, decay, factor
        )
        for which, result in enumerate(results):
            outs[9 * which + index][spot] = result

    for half in range(2):
        rows = slice(16 * half, 16 * half + 16)
        for u in range(3):
            apply(0, (0, rows, slice(D * u, D * (u + 1))), half_of(half, 16 * u, 16), 0.03, 0.01)
        apply(1, (0, rows, slice(None)), half_of(half, 192, 16), 0.03, 0.01)
        apply(2, (0, rows, slice(None)), half_of(half, 48, 16), 0.03, 0.01)
        for u in range(4):
            apply(3, (0, rows, slice(D * u, D * (u + 1))), half_of(half, 64 + 16 * u, 16), 0.03, 0.01)
        apply(4, (0, slice(64 * half, 64 * half + 64), slice(None)), half_of(half, 128, 64), 0.03, 0.01)
        for u in range(2):
            apply(7, (rows, slice(D * u, D * (u + 1))), half_of(half, 208 + 16 * u, 16), 0.03, 0.01)
        small[rows, :] = half_of(half, 240, 16)[:, 0:BLOCK]
    small[32:, :] = jnp.zeros((BLOCK - 32, BLOCK), F32)
    turned = jnp.transpose(small[...])
    apply(6, (slice(None), slice(None)), small[0:32, 0:FEATS], 0.03, 0.01)
    vecs = jnp.where(first, turned[80:84, 0:32], turned[84:88, 0:32])
    apply(5, (0, slice(None), slice(None)), vecs, 0.3, 0.0)
    apply(8, (slice(None), slice(None)), turned[88:89, 0:32], 0.3, 0.0)


def pack_shards(scalars, attn, out, pos, up, down, vecs, w_in, head, gain, kept, sent, codes, small):
    half, section = scalars[1], scalars[3]
    small[...] = jnp.zeros_like(small)
    small[88:89, 0:32] = gain[...]
    small[pl.ds(FEATS + 4 * section, 4), 0:32] = vecs[0]
    turned = jnp.transpose(small[...])[0:32]
    turned = jnp.concatenate([w_in[...], turned[:, FEATS:]], 1)
    column = lax.broadcasted_iota(jnp.int32, turned.shape, 1)
    shared = (column < FEATS) | (column == 88)
    for which, target in ((half, kept), (1 - half, sent)):
        rows = pl.ds(pl.multiple_of(16 * which, 16), 16)
        for u in range(3):
            target[16 * u : 16 * u + 16, :] = attn[0, rows, D * u : D * (u + 1)].astype(BF16)
        target[48:64, :] = pos[0, rows, :].astype(BF16)
        for u in range(4):
            target[64 + 16 * u : 80 + 16 * u, :] = up[0, rows, D * u : D * (u + 1)].astype(BF16)
        target[128:192, :] = down[0, pl.ds(pl.multiple_of(64 * which, 64), 64), :].astype(BF16)
        target[192:208, :] = out[0, rows, :].astype(BF16)
        tail = jnp.where(half == 0, turned[0:16], turned[16:32])
        if target is sent:
            tail = jnp.where(half == 0, turned[16:32], turned[0:16])
            tail = jnp.where(shared[0:16], 0.0, tail)
        target[208:224, :] = jnp.zeros((16, D), BF16)
        target[208:224, 0:BLOCK] = tail.astype(BF16)
    rows = pl.ds(pl.multiple_of(16 * half, 16), 16)
    for u in range(2):
        codes[16 * u : 16 * u + 16, :] = head[rows, D * u : D * (u + 1)].astype(BF16)


VMEM = pl.BlockSpec(memory_space=pltpu.VMEM)
ANY = pl.BlockSpec(memory_space=pl.ANY)
SMEM = pl.BlockSpec(memory_space=pltpu.SMEM)
DMA = pltpu.SemaphoreType.DMA


def shape(*dims, dtype=F32):
    return jax.ShapeDtypeStruct(dims, dtype)


def half_shape(*dims):
    return jax.ShapeDtypeStruct(dims, BF16)


def held(*dims):
    return pltpu.VMEM(dims, BF16)


def wide(*dims):
    return pltpu.VMEM(dims, F32)


def call(body, name, ins, outs, out_specs, scratch, micros, limit=VMEM_LIMIT):
    return pl.pallas_call(
        body,
        name=name,
        in_specs=ins,
        out_shape=outs,
        out_specs=out_specs,
        scratch_shapes=scratch,
        compiler_params=pltpu.CompilerParams(vmem_limit_bytes=limit),
        cost_estimate=pl.CostEstimate(flops=micros * 1_150_000_000, bytes_accessed=1 << 20, transcendentals=0),
    )


PROJECT_OUT = (
    half_shape(ROWS, D), half_shape(SEG, D), half_shape(SEG, D), half_shape(ROWS, D),
    half_shape(ROWS, D), half_shape(ROWS, D), half_shape(4, D, D),
)
PROJECT_HELD = [held(4, D, D), DMA, DMA((2,))]


def run_project_first(bits, scalars, frames, pieces, table):
    result = call(
        functools.partial(project, bits, 0),
        "project_first",
        [SMEM, VMEM, ANY, ANY, ANY, ANY, VMEM],
        PROJECT_OUT + (shape(SEG, D), shape(16, D), half_shape(D, BLOCK)),
        [VMEM] * 6 + [ANY, VMEM, VMEM, ANY],
        PROJECT_HELD + [wide(ROWS, D), held(D, BLOCK), DMA],
        6,
    )(scalars, frames, *pieces, table)
    return result[:7], *result[7:]


def run_project(bits, scalars, memory, hidden, vecs, pieces, table):
    return call(
        functools.partial(project, bits, 4),
        "project",
        [SMEM, VMEM, VMEM, VMEM, ANY, ANY, ANY, ANY, VMEM],
        PROJECT_OUT,
        [VMEM] * 6 + [ANY],
        PROJECT_HELD,
        6,
    )(scalars, memory, hidden, vecs, *pieces, table)


PAIR_HELD = [held(SEG, D), held(SEG, D), held(ROWS, D), held(ROWS, D), held(ROWS, D), held(PAIRS, 2 * BLOCK, WIDE)]


def run_attend(scalars, projected):
    return call(
        attend,
        "attend",
        [SMEM] + [ANY] * 5,
        (half_shape(SEG, D), half_shape(PAIRS, 2 * BLOCK, WIDE)),
        [VMEM, ANY],
        PAIR_HELD + [DMA((PAIRS, 5)), DMA((PAIRS,))],
        13,
    )(scalars, *projected[1:6])


HALF_HELD = [
    held(SEG, 256), held(SEG, 256), held(ROWS, 256), held(ROWS, 256), held(ROWS, 256),
    held(2, 2 * BLOCK, WIDE), held(2 * BLOCK, 2 * BLOCK),
    wide(256, ROWS), wide(256, ROWS), wide(256, ROWS), wide(SEG, 256), wide(SEG, 256), DMA((2, 6)),
]
HALF_OUT = (half_shape(SEG, 256), half_shape(ROWS, 256), half_shape(ROWS, 256))


def run_attend_back(bits, scalars, grad_att, projected, table, probs):
    result = call(
        functools.partial(attend_back, bits, False),
        "attend_back",
        [SMEM] + [VMEM] * 3 + [ANY] * 6,
        HALF_OUT + (half_shape(4, D, 256), shape(8, 256)),
        [VMEM] * 5,
        HALF_HELD,
        9,
    )(scalars, grad_att, projected[0], table, *projected[1:6], probs)
    return (*result[:3], result[4]), result[3]


def run_attend_back_rest(bits, scalars, grad_att, projected, table, probs, staged):
    result = call(
        functools.partial(attend_back, bits, True),
        "attend_back_rest",
        [SMEM] + [VMEM] * 3 + [ANY] * 7,
        HALF_OUT + (shape(8, 256), half_shape(GROUPS, 64, D), half_shape(GROUPS, 64, D)),
        [VMEM] * 4 + [ANY] * 2,
        HALF_HELD + [held(4, D, D), DMA, DMA],
        10,
    )(scalars, grad_att, projected[0], table, *projected[1:6], probs, staged)
    return result[:4], result[4], result[5]


def run_input_grads(bits, scalars, weights, grads, grad_mixed, vecs, memory, hidden):
    return call(
        functools.partial(input_grads, bits, 4),
        "input_grads",
        [SMEM] + [VMEM] * 13,
        (shape(SEG, D), shape(8, D)),
        [VMEM] * 2,
        [],
        5,
    )(scalars, weights, *grads, grad_mixed, vecs, memory, hidden)


def run_input_grads_last(bits, scalars, weights, grads, grad_mixed, vecs, frames, small, *small_grads):
    return call(
        functools.partial(input_grads, bits, 0),
        "input_grads_last",
        [SMEM] + [VMEM] * 17,
        (half_shape(GROUPS, 16, D), half_shape(GROUPS, 16, D)),
        [ANY] * 2,
        [wide(ROWS, D), wide(BLOCK, D), held(D, D), DMA],
        5,
    )(scalars, weights, *grads, grad_mixed, vecs, frames, small, *small_grads)


FEED_HELD = [held(SEG, D), held(SEG, FF), held(SEG, FF), held(4, D, D), held(FF, D), held(D, D)]
BACK_HELD = [held(SEG, FF), held(4, D, D), held(FF, D), held(D, D)]


def run_feed_forward(bits, base, scalars, residual, attended, vecs, pieces):
    result = call(
        functools.partial(feed_forward, bits, base),
        "feed_forward",
        [SMEM, VMEM, VMEM, VMEM, ANY, ANY, ANY, ANY],
        (shape(SEG, D), shape(SEG, D), shape(MEM, D), half_shape(SEG, D), half_shape(SEG, FF), half_shape(SEG, FF),
         half_shape(4, D, D), half_shape(FF, D), half_shape(D, D)),
        [VMEM] * 3 + [ANY] * 6,
        FEED_HELD + [DMA((3,)), DMA((6,))],
        9,
    )(scalars, residual, attended, vecs, *pieces)
    return result[0], result[1], result[2], result[3:]


def run_feed_backward(bits, base, scalars, grad_out, mixed, vecs, attended, saved):
    return call(
        functools.partial(feed_backward, bits, base),
        "feed_backward",
        [SMEM] + [VMEM] * 4 + [ANY] * 6,
        (half_shape(GROUPS, 144, D), half_shape(GROUPS, 144, D), shape(SEG, D), half_shape(SEG, D), shape(8, D)),
        [ANY, ANY, VMEM, VMEM, VMEM],
        FEED_HELD + BACK_HELD + [DMA((6,)), DMA((3,))],
        13,
    )(scalars, grad_out, mixed, vecs, attended, *saved)


def run_top(bits, streams, scalars, residual, attended, targets, vecs, pieces):
    return call(
        functools.partial(top_kernel, bits, streams),
        "top_kernel",
        [SMEM, VMEM, VMEM, VMEM, VMEM, ANY, ANY, ANY, ANY],
        (
            half_shape(GROUPS, 176, D), half_shape(GROUPS, 176, D),
            shape(SEG, D), half_shape(SEG, D), shape(8, D), shape(8, D), shape(8, 128),
        ),
        [ANY] * 2 + [VMEM] * 5,
        FEED_HELD
        + [wide(SEG, D), wide(SEG, D), wide(SEG, D), held(2, D, D), held(SEG, D), held(SEG, CODES), held(2, D, D)]
        + BACK_HELD
        + [DMA, DMA((3,)), DMA((3,))],
        21,
    )(scalars, residual, attended, targets, vecs, *pieces)


def run_finish(scalars, loss, *sums):
    counts = tuple((len(item) for item in sums))
    flat = [item for group in sums for item in group]
    return call(
        functools.partial(finish, counts),
        "finish",
        [SMEM, VMEM] + [ANY] * len(flat),
        (shape(256, D), shape(256, D), shape(8, 128)),
        [VMEM] * 3,
        [pltpu.VMEM(item.shape[1:], item.dtype) for item in flat] + [DMA((len(flat),))],
        3,
    )(scalars, loss, *flat)


def run_update(scalars, total, kept, got, state):
    flat = [item[None] if item.ndim == 1 else item for item in state]
    for index in (6, 15, 24):
        flat[index] = jnp.transpose(flat[index])
    result = call(
        update,
        "update",
        [SMEM] + [VMEM] * 30,
        tuple((shape(*item.shape) for item in flat)) + (shape(1, 1), shape(1, 1)),
        [VMEM] * 29,
        [wide(BLOCK, BLOCK)],
        5,
    )(scalars, total, kept, got, *flat)
    result = list(result)
    for index in (6, 15, 24):
        result[index] = jnp.transpose(result[index])
    return [item.reshape(old.shape) for item, old in zip(result, state)] + [result[27][0, 0], result[28][0, 0]]


def run_pack(scalars, w_attn, w_out, w_pos, w_up, w_down, layer_vecs, w_in, w_head, gain_final):
    return call(
        pack_shards,
        "pack_shards",
        [SMEM] + [VMEM] * 9,
        (half_shape(224, D), half_shape(224, D), half_shape(32, D)),
        [VMEM] * 3,
        [wide(BLOCK, BLOCK)],
        3,
    )(scalars, w_attn, w_out, w_pos, w_up, w_down, layer_vecs, jnp.transpose(w_in), w_head, gain_final[None])


def spread(value, bits):
    count = lax.axis_size("dp")
    pairs = [
        (half * count + i, half * count + (i ^ bit)) for half, bit in enumerate(bits) for i in range(count)
    ]
    return lax.ppermute(value, ("section", "dp"), pairs)


def swap(value):
    return lax.ppermute(value, "section", [(0, 1), (1, 0)])


def fence(*values):
    return lax.optimization_barrier(values)


def joined(low, got):
    return jnp.concatenate([low, got], 0)


def part(sources, first, last):
    total = sources[0][first:last].astype(F32)
    for item in sources[1:]:
        total = total + item[first:last].astype(F32)
    return total


def shrink(sources, pair):
    count = sources[-1].shape[0]
    return spread(part(sources, count // 2, count).astype(BF16), pair)


def add_up(value, bits):
    value = value + swap(value)
    steps = [low for low, unused in zip(*bits)]
    for one, two in zip(steps[0::2], steps[1::2]):
        first, second, third = (spread(value, (step, step)) for step in (one, two, one + two))
        value = (value + first) + (second + third)
    return value


def lanes_of(block):
    return [block[:, D * u : D * (u + 1)] for u in range(block.shape[1] // D)]


def sinus_table():
    where_at = (ROWS - 1 - jnp.arange(ROWS, dtype=jnp.int32)).astype(F32)[:, None]
    freqs = jnp.exp(-jnp.log(10000.0) * (2.0 * jnp.arange(D // 2, dtype=jnp.int32).astype(F32) / D))
    angles = where_at * freqs[None, :]
    return jnp.concatenate([jnp.sin(angles), jnp.cos(angles)], 1).astype(BF16)


def split_shards(section, scalars, params):
    kept, sent, head = run_pack(scalars, *params)
    got = swap(sent)
    first = section == 0
    zero = jnp.where(first, kept, got)
    one = jnp.where(first, got, kept)
    return (
        jnp.concatenate([zero[:64], kept[208:] + got[208:]], 0),
        zero[64:208],
        one[:64],
        jnp.concatenate([one[64:208], head], 0),
    )


def halves(whole, rows):
    return whole.reshape(GROUPS, 2, rows, whole.shape[1]).transpose(1, 0, 2, 3)


def gather_whole(section, w_attn, w_out, w_pos, w_up, w_down, layer_vecs, w_in, w_head, gain_final):
    def over(value, axis):
        return lax.all_gather(value.astype(BF16), "dp", axis=axis, tiled=True)

    def layers(value):
        return lax.all_gather(over(value[0], 0), "section", axis=0)

    attn, out, pos, up, down = (layers(item) for item in (w_attn, w_out, w_pos, w_up, w_down))
    vecs = lax.all_gather(over(layer_vecs[0], 1), "section", axis=0)
    small = jnp.concatenate(
        [over(w_in, 1), vecs[0], vecs[1], over(gain_final, 0)[None], jnp.zeros((BLOCK - 89, D), BF16)], 0
    )
    small = jnp.pad(jnp.transpose(small), ((0, 0), (0, D - BLOCK)))
    head = over(w_head, 0)

    def pieces(units):
        both = jnp.concatenate([halves(item, item.shape[0] // 32) for item in units], 2)
        own = lax.dynamic_index_in_dim(both, section, 0, keepdims=False)
        other = lax.dynamic_index_in_dim(both, 1 - section, 0, keepdims=False)
        return (own[:8], own[8:], other[:8], other[8:])

    return (
        pieces(lanes_of(attn[0]) + [pos[0], small]),
        pieces(lanes_of(up[0]) + [down[0], out[0]]),
        pieces(lanes_of(attn[1]) + [pos[1]]),
        pieces(lanes_of(up[1]) + [down[1], out[1]] + lanes_of(head)),
    )


def whole_grads(section, sums):
    count = lax.axis_size("dp")
    place = lax.axis_index("dp")
    attn_zero, feed_zero, attn_one, feed_one, small = (
        lax.all_gather(lax.psum(item, "dp"), "section", axis=0) for item in sums
    )

    def unit(both, start, rows):
        item = both[:, :, start : start + rows]
        return item.transpose(1, 0, 2, 3).reshape(GROUPS * 2 * rows, both.shape[3])

    def layer(attn, feed):
        return (
            jnp.concatenate([unit(attn, 16 * u, 16) for u in range(3)], 1),
            unit(feed, 128, 16),
            unit(attn, 48, 16),
            jnp.concatenate([unit(feed, 16 * u, 16) for u in range(4)], 1),
            unit(feed, 64, 64),
        )

    small = jnp.transpose(unit(small, 0, 16))
    zero = layer(attn_zero, feed_zero) + (small[80:84],)
    one = layer(attn_one, feed_one) + (small[84:88],)
    ends = (small[:80], jnp.concatenate([unit(feed_one, 144 + 16 * u, 16) for u in range(2)], 1), small[88])
    squares = sum((jnp.sum(item * item) for item in zero + one + ends))
    dims = (0, 0, 0, 0, 0, 1, 1, 0, 0)
    grads = tuple((jnp.where(section == 0, a, b) for a, b in zip(zero, one))) + ends
    return squares, tuple(
        (
            lax.dynamic_slice_in_dim(item, place * (item.shape[dim] // count), item.shape[dim] // count, dim)
            for item, dim in zip(grads, dims)
        )
    )


def local(frames, targets, lengths, *state):
    params, firsts, seconds = (state[:9], state[9:18], state[18:])
    section = lax.axis_index("section")
    streams = lax.axis_size("dp")
    ringed = streams == GROUPS
    place = lax.axis_index("dp") if ringed else jnp.int32(0)
    length = lengths[0]
    scalars = jnp.stack([place, section, length, section]).astype(jnp.int32)
    table = sinus_table()
    rows = lax.dynamic_slice_in_dim(
        jnp.pad(frames[0], ((MEM, 0), (0, BLOCK - FEATS))), section * SEG, ROWS, 0
    )
    codes = lax.dynamic_slice_in_dim(targets, section * SEG, SEG, 1)
    if ringed:
        bits = ((8, 4, 1, 2), (8, 4, 2, 1))
        far, near, side, last = zip(*bits)
        zero, one, two, three = (item[None] for item in split_shards(section, scalars, params))
        zero, got = fence(zero, spread(zero, far))
        zero = joined(zero, got)
        one_got = spread(one, far)
        zero, got = fence(zero, spread(zero, near))
        zero = joined(zero, got)
        one = joined(one, one_got)
        two_got = spread(two, far)
        one_got = spread(one, near)
        zero, got = fence(zero, spread(zero, side))
        zero = joined(zero, got)
        high = spread(zero, last)
        swapped = swap(zero)
        high, one, one_got, two, two_got, swapped, rows, table, codes = fence(
            high, one, one_got, two, two_got, swapped, rows, table, codes
        )
        chunk = (zero, high, swapped, swap(high))
        one, two = joined(one, one_got), joined(two, two_got)
        one_got, two_got, three_got = spread(one, side), spread(two, near), spread(three, far)
    else:
        bits = IN_ORDER
        chunk, chunk_one, chunk_two, chunk_three = gather_whole(section, *params)

    saved_zero, hidden_zero, vecs, small = run_project_first(bits, scalars, rows, chunk, table)
    if ringed:
        saved_zero, one_got, two_got = fence(saved_zero, one_got, two_got)
        one, two = joined(one, one_got), joined(two, two_got)
        one_got, two_got, swapped = spread(one, last), spread(two, side), swap(one)
    attended_zero, probs_zero = run_attend(scalars, saved_zero)
    if ringed:
        attended_zero, one_got, two_got, three_got, swapped = fence(
            attended_zero, one_got, two_got, three_got, swapped
        )
        chunk = (one, one_got, swapped, swap(one_got))
        two, three = joined(two, two_got), joined(three, three_got)
        two_got, three_got, swapped = spread(two, last), spread(three, near), swap(two)
    else:
        chunk = chunk_one
    out_zero, mixed_zero, memory, fed_zero = run_feed_forward(bits, 0, scalars, hidden_zero, attended_zero, vecs, chunk)
    if ringed:
        out_zero, memory, two_got, three_got, swapped = fence(out_zero, memory, two_got, three_got, swapped)
        chunk = (two, two_got, swapped, swap(two_got))
        three = joined(three, three_got)
        three_got = spread(three, side)
    else:
        chunk = chunk_two
    memory = lax.ppermute(memory, "section", [(0, 1)])
    saved_one = run_project(bits, scalars, memory, out_zero, vecs, chunk, table)
    if ringed:
        saved_one, three_got = fence(saved_one, three_got)
        three = joined(three, three_got)
        three_got, swapped = spread(three, last), swap(three)
    attended_one, probs_one = run_attend(scalars, saved_one)
    if ringed:
        attended_one, three_got, swapped = fence(attended_one, three_got, swapped)
        chunk = (three, three_got, swapped, swap(three_got))
    else:
        chunk = chunk_three
    keep_a, send_a, grad, grad_att, gain_one, gain_final, loss = run_top(
        bits, streams, scalars, out_zero, attended_one, codes, vecs, chunk
    )
    if ringed:
        grad_att, keep_a, send_a = fence(grad_att, keep_a, send_a)
        got_a = swap(send_a)
    grads_a, staged = run_attend_back(bits, scalars, grad_att, saved_one, table, probs_one)
    if ringed:
        grads_a, staged, got_a = fence(grads_a, staged, got_a)
        sum_a = [keep_a, got_a]
        got_a = shrink(sum_a, last)
    grads_b, keep_b, send_b = run_attend_back_rest(
        bits, scalars, grad_att, saved_one, table, probs_one, staged
    )
    if ringed:
        grads_b, keep_b, send_b = fence(grads_b, keep_b, send_b)
        got_b = swap(send_b)
    grad, vecs_one = run_input_grads(
        bits, scalars, saved_one[6], (*grads_a, *grads_b), grad, vecs, memory, out_zero
    )
    if ringed:
        grad, got_a, got_b = fence(grad, got_a, got_b)
        sum_a.append(got_a)
        sum_b = [keep_b, got_b]
        got_a, got_b = shrink(sum_a, side), shrink(sum_b, last)
    keep_c, send_c, grad, grad_att, gain_zero = run_feed_backward(
        bits, 0, scalars, grad, mixed_zero, vecs, attended_zero, fed_zero
    )
    if ringed:
        grad_att, got_a, got_b, keep_c, send_c = fence(grad_att, got_a, got_b, keep_c, send_c)
        sum_a.append(got_a)
        sum_b.append(got_b)
        got_a, got_b, got_c = shrink(sum_a, near), shrink(sum_b, side), swap(send_c)
    grads_a, staged = run_attend_back(bits, scalars, grad_att, saved_zero, table, probs_zero)
    if ringed:
        grads_a, staged, got_a, got_b, got_c = fence(grads_a, staged, got_a, got_b, got_c)
        sum_a.append(got_a)
        sum_b.append(got_b)
        sum_c = [keep_c, got_c]
        got_c, got_a, got_b = shrink(sum_c, last), shrink(sum_a, far), shrink(sum_b, near)
    grads_b, keep_d, send_d = run_attend_back_rest(
        bits, scalars, grad_att, saved_zero, table, probs_zero, staged
    )
    if ringed:
        grads_b, keep_d, send_d, got_a, got_b, got_c = fence(grads_b, keep_d, send_d, got_a, got_b, got_c)
        sum_a.append(got_a)
        sum_b.append(got_b)
        sum_c.append(got_c)
        got_d, got_c, got_b = swap(send_d), shrink(sum_c, side), shrink(sum_b, far)
    keep_e, send_e = run_input_grads_last(
        bits, scalars, saved_zero[6], (*grads_a, *grads_b), grad, vecs, rows, small,
        gain_zero, vecs_one, gain_one, gain_final,
    )
    if not ringed:
        pairs = ((keep_d, send_d), (keep_c, send_c), (keep_b, send_b), (keep_a, send_a), (keep_e, send_e))
        sums = [keep.astype(F32) + swap(send).astype(F32) for keep, send in pairs]
        squares, grads = whole_grads(section, sums)
        grad_norm = jnp.sqrt(squares)
        loss_sum = lax.psum(loss[0, 0], ("section", "dp"))
        factor = jnp.minimum(1.0, CLIP / (grad_norm + 1e-06))
        results = []
        for index in range(9):
            rate, decay = (0.3, 0.0) if index in (5, 8) else (0.03, 0.01)
            grad = grads[index][None] if index < 6 else grads[index]
            results.append(
                adam_step(params[index], grad, firsts[index], seconds[index], rate, decay, factor)
            )
        news, moms, sqs = zip(*results)
        return (*news, *moms, *sqs, grad_norm, loss_sum)
    keep_e, send_e, got_b, got_c, got_d = fence(keep_e, send_e, got_b, got_c, got_d)
    sum_b.append(got_b)
    sum_c.append(got_c)
    sum_d, sum_e, merged = [keep_d, got_d], [keep_e, swap(send_e)], []

    def shrink_ends(pair):
        count = GROUPS >> (len(merged) + 1)
        total = jnp.concatenate([part(sum_d, count, 2 * count), part(sum_e, count, 2 * count)], 1)
        if merged:
            total = total + part(merged, count, 2 * count)
        return spread(total.astype(BF16), pair)

    got, got_c = shrink_ends(last), shrink(sum_c, near)
    got, got_c = fence(got, got_c)
    merged.append(got)
    sum_c.append(got_c)
    got, got_c = shrink_ends(side), shrink(sum_c, far)
    got, got_c = fence(got, got_c)
    merged.append(got)
    sum_c.append(got_c)
    merged.append(shrink_ends(near))
    merged.append(shrink_ends(far))
    kept, sent, total = run_finish(scalars, loss, sum_d, sum_c, sum_b, sum_a, sum_e, merged)
    got = swap(sent)
    return tuple(run_update(scalars, add_up(total, bits), kept, got, state))


def solution(mesh):
    weights = (
        P("section", "dp", None),
        P("section", "dp", None),
        P("section", "dp", None),
        P("section", "dp", None),
        P("section", "dp", None),
        P("section", None, "dp"),
        P(None, "dp"),
        P("dp", None),
        P("dp"),
    )
    return jax.shard_map(
        local,
        mesh=mesh,
        in_specs=(P("dp", None, None), P("dp", None), P("dp")) + weights * 3,
        out_specs=weights * 3 + (P(), P()),
        check_vma=False,
    )
```

```python
import functools

import jax
import jax.numpy as jnp
from jax import lax
from jax.experimental import pallas as pl
from jax.experimental.pallas import tpu as pltpu
from jax.sharding import PartitionSpec as P

D = 512
FF = 2048
CODES = 1024
FEATS = 80
MEM = 256
SEG = 512
SEGS = 2
STEP = 10
ROWS = MEM + SEG
BLOCK = 128
PAIRS = 4
WIDE = 18 * BLOCK
GROUPS = 16
QUERY_U_AT, QUERY_V_AT, KEYS_AT, VALUES_AT, REL_AT, WEIGHTS_AT, SMALL_AT = 768, 1280, 1792, 2560, 3328, 4096, 6144
ACTIVE_AT, SLOPE_AT, UP_AT, DOWN_AT, OUT_AT = 512, 2560, 4608, 6656, 8704
KEPT_ROWS = 16384
KEPT_PAIRS = 14
IN_ORDER = ((1, 2, 4, 8), (1, 2, 4, 8))
NEG = -1e30
CLIP = 0.02
SCALE = 0.125
F32 = jnp.float32
BF16 = jnp.bfloat16
SPANS = tuple((MEM + BLOCK * (b + 1) for b in range(4)))
STARTS = tuple((sum(SPANS[:b]) for b in range(4)))


def nn(left, right):
    return jnp.dot(left, right, preferred_element_type=F32)


def nt(left, right):
    return lax.dot_general(left, right, (((1,), (1,)), ((), ())), preferred_element_type=F32)


def tn(left, right):
    return lax.dot_general(left, right, (((0,), (0,)), ((), ())), preferred_element_type=F32)


def norm_parts(values):
    center = values - jnp.mean(values, -1, keepdims=True)
    spread = jnp.mean(center * center, -1, keepdims=True)
    inverse = lax.rsqrt(spread + 1e-05)
    return center * inverse, inverse


def norm_back(unit, inverse, gain, grad):
    scaled = grad * gain
    first = jnp.mean(scaled, -1, keepdims=True)
    second = jnp.mean(scaled * unit, -1, keepdims=True)
    return inverse * (scaled - first - unit * second), jnp.sum(grad * unit, 0, keepdims=True)


def group_of(bits, spot, place, half):
    if bits == IN_ORDER:
        return spot
    code = jnp.int32(0)
    for index, (low, high) in enumerate(zip(bits[0], bits[1])):
        bit = lax.rem(lax.div(spot, 1 << index), 2)
        code = code + bit * jnp.where(half == 0, low, high)
    return jnp.bitwise_xor(place, code)


def copies(bits, place, half, pieces, units, rows, sem, outward):
    count = GROUPS // len(pieces)
    for index, slab in enumerate(pieces):

        def one(spot, carry):
            group = group_of(bits, index * count + spot, place, half)
            for whole, first in units:
                there = whole.at[pl.ds(pl.multiple_of((group * 2 + half) * rows, rows), rows), :]
                here = slab.at[spot, pl.ds(first, rows), pl.ds(0, whole.shape[1])]
                if outward:
                    pltpu.make_async_copy(there, here, sem).start()
                else:
                    pltpu.make_async_copy(here, there, sem).start()
            return carry

        lax.fori_loop(0, count, one, 0)


def fetch(source, target, sem):
    copy = pltpu.make_async_copy(source, target, sem)
    copy.start()
    return copy


def arrived(buffer, sem):
    pltpu.make_async_copy(buffer, buffer, sem).wait()


def tri_mask():
    row = lax.broadcasted_iota(jnp.int32, (2 * BLOCK, BLOCK), 0)
    col = lax.broadcasted_iota(jnp.int32, (2 * BLOCK, BLOCK), 1)
    return col <= lax.rem(row, BLOCK)


def stack_heads(part):
    col = lax.broadcasted_iota(jnp.int32, part.shape, 1)
    zero = jnp.zeros_like(part)
    return jnp.concatenate(
        [jnp.where(col < 64, part, zero), jnp.where(col < 64, zero, part)], 0
    )


def pick_heads(both):
    col = lax.broadcasted_iota(jnp.int32, (BLOCK, BLOCK), 1)
    return jnp.where(col < 64, both[:BLOCK], both[BLOCK:])


def shift(both, amount):
    return jnp.concatenate(
        [pltpu.roll(part, amount, 1, stride=1, stride_axis=0) for part in (both[:BLOCK], both[BLOCK:])], 0
    )


def masked(score, triangle, first):
    return jnp.concatenate([score[:, :first], jnp.where(triangle, score[:, first:], NEG)], 1)


def lanes(pair):
    return pl.ds(pl.multiple_of(pair * BLOCK, BLOCK), BLOCK)


def project(bits, base, *refs):
    first_layer = base == 0
    if first_layer:
        (scalars, frames, own_low, own_high, other_low, other_high, table) = refs[:7]
        (query_u, query_v, keys, values, rel, hidden, vecs, saved) = refs[7:15]
        (normed, weights, in_sem, out_sem, joined, small, small_sem) = refs[15:]
    else:
        (scalars, memory, hidden, vecs, own_low, own_high, other_low, other_high, table) = refs[:9]
        (query_u, query_v, keys, values, rel, saved) = refs[9:15]
        (normed, weights, in_sem, out_sem) = refs[15:]
    place, half = scalars[0], scalars[1]
    both = ((half, (own_low, own_high)), (1 - half, (other_low, other_high)))
    if first_layer:
        for which, pieces in both:
            copies(bits, place, which, pieces, [(small, 64)], 16, small_sem, False)
    units = [(weights.at[u], 16 * u) for u in range(4)]
    for which, pieces in both:
        copies(bits, place, which, pieces, units, 16, in_sem, False)
    if first_layer:
        arrived(small, small_sem)
        small_out = fetch(small, saved.at[pl.ds(SMALL_AT, D), pl.ds(0, BLOCK)], out_sem.at[7])
        vecs[...] = jnp.transpose(small[...].astype(F32))[80:96]
        for b in range(3):
            rows = pl.ds(256 * b, 256)
            joined[rows, :] = nt(frames[rows, :], small[...])
        hidden[...] = joined[MEM:, :]
        sources = [joined.at[pl.ds(256 * b, 256)] for b in range(3)]
    else:
        sources = [memory, hidden.at[pl.ds(0, 256)], hidden.at[pl.ds(256, 256)]]
    gain = vecs[base : base + 1, :]
    bias_u = vecs[base + 2 : base + 3, :]
    bias_v = vecs[base + 3 : base + 4, :]
    arrived(weights, in_sem)
    outs = [fetch(weights.at[u], saved.at[pl.ds(WEIGHTS_AT + D * u, D)], out_sem.at[8 + u]) for u in range(4)]
    rel[...] = nn(table[...], weights[3]).astype(BF16)
    outs.append(fetch(rel, saved.at[pl.ds(REL_AT, ROWS)], out_sem.at[5]))
    for b in range(3):
        unit, unused = norm_parts(sources[b][...])
        normed[pl.ds(256 * b, 256), :] = (unit * gain).astype(BF16)
    outs.append(fetch(normed, saved.at[pl.ds(0, ROWS)], out_sem.at[0]))
    keys[...] = nn(normed[...], weights[1]).astype(BF16)
    outs.append(fetch(keys, saved.at[pl.ds(KEYS_AT, ROWS)], out_sem.at[3]))
    values[...] = nn(normed[...], weights[2]).astype(BF16)
    outs.append(fetch(values, saved.at[pl.ds(VALUES_AT, ROWS)], out_sem.at[4]))
    query = nn(normed[MEM:, :], weights[0])
    query_u[...] = (query + bias_u).astype(BF16)
    query_v[...] = (query + bias_v).astype(BF16)
    outs.append(fetch(query_u, saved.at[pl.ds(QUERY_U_AT, SEG)], out_sem.at[1]))
    outs.append(fetch(query_v, saved.at[pl.ds(QUERY_V_AT, SEG)], out_sem.at[2]))
    if first_layer:
        outs.append(small_out)
    for copy in outs:
        copy.wait()


def attend(scalars, query_u, query_v, keys, values, rel, attended, probs_o, probs, out_sem):
    length, segment = scalars[2], scalars[3]
    spot = lax.broadcasted_iota(jnp.int32, (1, ROWS), 1)
    where_at = segment * SEG + spot - MEM
    allowed = (where_at < length) & ((spot >= MEM) | (segment >= 1))
    bias = jnp.where(allowed, 0.0, NEG)
    triangle = tri_mask()

    def two_pairs(step, carry):
        tiles = [(2 * step + one, b) for one in range(2) for b in range(4)]
        full = [
            nt(stack_heads(query_v[BLOCK * b : BLOCK * (b + 1), lanes(pair)]) * SCALE,
               rel[ROWS - SPANS[b] : ROWS, lanes(pair)])
            for pair, b in tiles
        ]
        content = [
            nt(stack_heads(query_u[BLOCK * b : BLOCK * (b + 1), lanes(pair)]) * SCALE,
               keys[0 : SPANS[b], lanes(pair)])
            for pair, b in tiles
        ]
        full = [shift(item, SPANS[b] - BLOCK + 1) for item, (pair, b) in zip(full, tiles)]
        score = [
            masked(one + two + bias[:, : SPANS[b]], triangle, SPANS[b] - BLOCK)
            for one, two, (pair, b) in zip(content, full, tiles)
        ]
        top = [jnp.max(item, -1, keepdims=True) for item in score]
        expo = [jnp.exp(item - most) for item, most in zip(score, top)]
        total = [jnp.sum(item, -1, keepdims=True) for item in expo]
        prob = [(item * (1.0 / most)).astype(BF16) for item, most in zip(expo, total)]
        for item, (pair, b) in zip(prob, tiles):
            probs[pair, :, STARTS[b] : STARTS[b] + SPANS[b]] = item
        for one in range(2):
            pair = 2 * step + one
            pltpu.make_async_copy(probs.at[pair], probs_o.at[pair], out_sem.at[pair]).start()
        found = [nn(item, values[0 : SPANS[b], lanes(pair)]) for item, (pair, b) in zip(prob, tiles)]
        for item, (pair, b) in zip(found, tiles):
            attended[BLOCK * b : BLOCK * (b + 1), lanes(pair)] = pick_heads(item).astype(BF16)
        return carry

    lax.fori_loop(0, PAIRS // 2, two_pairs, 0)
    outs = [
        fetch(attended.at[pl.ds(256 * b, 256)], probs_o.at[PAIRS + b, :, pl.ds(0, D)], out_sem.at[PAIRS + b])
        for b in range(2)
    ]
    for pair in range(PAIRS):
        pltpu.make_async_copy(probs.at[pair], probs_o.at[pair], out_sem.at[pair]).wait()
    for copy in outs:
        copy.wait()


def attend_back(bits, second, *refs):
    (scalars, grad_att, table_h, saved, probs_h) = refs[:5]
    normed, table, late_sem = refs[-3:]
    rest = refs[5:-3]
    query_u_h, query_v_h, keys_h, values_h, rel_h = (
        saved.at[pl.ds(first, rows)]
        for first, rows in (
            (QUERY_U_AT, SEG), (QUERY_V_AT, SEG), (KEYS_AT, ROWS), (VALUES_AT, ROWS), (REL_AT, ROWS)
        )
    )
    if second:
        staged_h = rest[0]
        rest = rest[1:]
        (keep, send) = rest[4:6]
        sums, rest = rest[3], rest[:3] + rest[6:]
    else:
        (staged, sums) = rest[3:5]
        rest = rest[:3] + rest[5:]
    (grad_query, grad_keys, grad_values,
     query_u, query_v, keys, values, rel, probs, flip, acc_keys, acc_values, acc_rel,
     grad_qu, grad_qv, pair_sem) = rest[:16]
    first_pair = 2 if second else 0

    def parts(pair):
        lane, here = lanes(pair + first_pair), lanes(pair)
        moves = [(probs_h.at[pair + first_pair], probs.at[pair])]
        for there, target in (
            (query_u_h, query_u), (query_v_h, query_v), (keys_h, keys), (values_h, values), (rel_h, rel)
        ):
            moves.append((there.at[:, lane], target.at[:, here]))
        return [
            pltpu.make_async_copy(there, target, pair_sem.at[pair, index])
            for index, (there, target) in enumerate(moves)
        ]

    for pair in range(2):
        for copy in parts(pair):
            copy.start()
    late = [fetch(saved.at[pl.ds(0, ROWS)], normed, late_sem.at[0]), fetch(table_h, table, late_sem.at[1])]
    if second:
        staged, sem = rest[16:]
        staged[:, :, 0:256] = staged_h[...]
    row = lax.broadcasted_iota(jnp.int32, (2 * BLOCK, 2 * BLOCK), 0)
    col = lax.broadcasted_iota(jnp.int32, (2 * BLOCK, 2 * BLOCK), 1)
    back = (row // BLOCK) * BLOCK + BLOCK - 1 - lax.rem(row, BLOCK)
    flip[...] = (col == back).astype(F32).astype(BF16)

    def one_pair(pair, carry):
        lane = lanes(pair)
        for copy in parts(pair):
            copy.wait()
        order = (3, 2, 1, 0)
        flipped = flip[...]
        stack_g = [
            stack_heads(grad_att[BLOCK * b : BLOCK * (b + 1), lanes(pair + first_pair)]) for b in order
        ]
        stack_u = [stack_heads(query_u[BLOCK * b : BLOCK * (b + 1), lane]) * SCALE for b in order]
        stack_v = [
            nn(flipped, stack_heads(query_v[BLOCK * b : BLOCK * (b + 1), lane]) * SCALE).astype(BF16)
            for b in order
        ]
        prob_b = [probs[pair, :, STARTS[b] : STARTS[b] + SPANS[b]] for b in order]
        grad_prob = [nt(one, values[0 : SPANS[b], lane]) for one, b in zip(stack_g, order)]
        part_values = [tn(one, two) for one, two in zip(stack_g, prob_b)]
        prob = [item.astype(F32) for item in prob_b]
        inner = [jnp.sum(one * two, -1, keepdims=True) for one, two in zip(prob, grad_prob)]
        grad_score = [
            (one * (two - three)).astype(BF16) for one, two, three in zip(prob, grad_prob, inner)
        ]
        turned = [nn(flipped, item) for item in grad_score]
        found_u = [nn(item, keys[0 : SPANS[b], lane]) for item, b in zip(grad_score, order)]
        part_keys = [tn(one, two) for one, two in zip(stack_u, grad_score)]
        grad_full = [shift(item, 0).astype(BF16) for item in turned]
        found_v = [nn(item, rel[ROWS - SPANS[b] : ROWS, lane]) for item, b in zip(grad_full, order)]
        part_rel = [tn(one, two) for one, two in zip(stack_v, grad_full)]
        for index, b in enumerate(order):
            span = SPANS[b]
            rows = pl.ds(BLOCK * b, BLOCK)
            grad_qu[rows, lane] = pick_heads(found_u[index]) * SCALE
            grad_qv[rows, lane] = pick_heads(found_v[index]) * SCALE
            if b == 3:
                acc_keys[lane, :] = part_keys[index]
                acc_values[lane, :] = part_values[index]
                acc_rel[lane, :] = part_rel[index]
            else:
                acc_keys[lane, 0:span] += part_keys[index]
                acc_values[lane, 0:span] += part_values[index]
                acc_rel[lane, ROWS - span : ROWS] += part_rel[index]
        return carry

    lax.fori_loop(0, 2, one_pair, 0)
    grad_keys[...] = jnp.transpose(acc_keys[...]).astype(BF16)
    grad_values[...] = jnp.transpose(acc_values[...]).astype(BF16)
    grad_rel = jnp.transpose(acc_rel[...]).astype(BF16)
    sums[...] = jnp.zeros_like(sums)
    sums[2:3, :] = jnp.sum(grad_qu[...], 0, keepdims=True)
    sums[3:4, :] = jnp.sum(grad_qv[...], 0, keepdims=True)
    flip_one = flip[0:BLOCK, 0:BLOCK]
    for b in range(4):
        rows = pl.ds(BLOCK * b, BLOCK)
        part = grad_qv[rows, :]
        high = part.astype(BF16)
        low = (part - high.astype(F32)).astype(BF16)
        grad_query[rows, :] = (grad_qu[rows, :] + nn(flip_one, high) + nn(flip_one, low)).astype(BF16)
    for copy in late:
        copy.wait()
    cols = slice(256, 512) if second else slice(None)
    staged[1, :, cols] = tn(normed[...], grad_keys[...]).astype(BF16)
    staged[2, :, cols] = tn(normed[...], grad_values[...]).astype(BF16)
    staged[3, :, cols] = tn(table[...], grad_rel).astype(BF16)
    staged[0, :, cols] = tn(normed[MEM:, :], grad_query[...]).astype(BF16)
    if second:
        place, half = scalars[0], scalars[1]
        units = [(staged.at[u], 16 * u) for u in range(4)]
        copies(bits, place, half, (keep,), units, 16, sem, True)
        copies(bits, place, 1 - half, (send,), units, 16, sem, True)
        arrived(staged, sem)


def input_grads(bits, base, *refs):
    last_kernel = base == 0
    weights, weights_sem = refs[-2:]
    refs = refs[:-2]
    weights_copies = [
        fetch(refs[1].at[pl.ds(WEIGHTS_AT + D * u, D)], weights.at[u], weights_sem.at[u]) for u in range(3)
    ]
    (scalars, saved, query_a, keys_a, values_a, sums_a, query_b, keys_b, values_b, sums_b, grad_mixed, vecs) = refs[:12]
    if last_kernel:
        (frames, gain_two, vecs_one, gain_two_one, gain_final, keep, send,
         joined, smalls, staged, sem, small, small_sem) = refs[12:]
        fetch(saved.at[pl.ds(SMALL_AT, D), pl.ds(0, BLOCK)], small, small_sem).wait()
        joined[...] = nt(frames[...], small[...])
        before, here, first = joined, joined, MEM
    else:
        (memory, hidden, grad_hidden, grad_vecs) = refs[12:]
        before, here, first = memory, hidden, 0
    place, half = scalars[0], scalars[1]
    gain = vecs[base : base + 1, :]
    left, right = slice(0, 256), slice(256, 512)
    for copy in weights_copies:
        copy.wait()
    grad_keys = (
        nt(keys_a[...], weights[1, :, left])
        + nt(keys_b[...], weights[1, :, right])
        + nt(values_a[...], weights[2, :, left])
        + nt(values_b[...], weights[2, :, right])
    )
    grad_query = nt(query_a[...], weights[0, :, left]) + nt(query_b[...], weights[0, :, right])
    unit, inverse = norm_parts(before[0:MEM, :])
    grad_gain = jnp.sum(grad_keys[0:MEM] * unit, 0, keepdims=True)
    unit, inverse = norm_parts(here[first : first + SEG, :])
    grad_joined, gains = norm_back(unit, inverse, gain, grad_keys[MEM:] + grad_query)
    grad_gain = grad_gain + gains
    grad_in = grad_mixed[...] + grad_joined
    if last_kernel:
        smalls[...] = tn(frames[MEM:, :], grad_in.astype(BF16))
        smalls[80:81, :] = grad_gain
        smalls[81:82, :] = gain_two[0:1, :]
        smalls[82:84, left] = sums_a[2:4, :]
        smalls[82:84, right] = sums_b[2:4, :]
        smalls[84:88, :] = vecs_one[0:4, :]
        smalls[85:86, :] = gain_two_one[0:1, :]
        smalls[88:89, :] = gain_final[0:1, :]
        staged[...] = jnp.zeros_like(staged)
        staged[:, 0:BLOCK] = jnp.transpose(smalls[...]).astype(BF16)
        units = [(staged, 0)]
        copies(bits, place, half, (keep,), units, 16, sem, True)
        copies(bits, place, 1 - half, (send,), units, 16, sem, True)
        arrived(staged, sem)
    else:
        grad_hidden[...] = grad_in
        grad_vecs[:, left] = sums_a[...]
        grad_vecs[:, right] = sums_b[...]
        grad_vecs[0:1, :] = grad_gain


def feed_weights(bits, place, both, up, down, out, sem):
    for index, (units, rows) in enumerate(
        (([(out, 128)], 16), ([(up.at[u], 16 * u) for u in range(4)], 16), ([(down, 64)], 64))
    ):
        for which, pieces in both:
            copies(bits, place, which, pieces, units, rows, sem.at[index], False)


def feed_grads_out(bits, place, half, keep, send, up, down, out, sem):
    ups = [(up.at[u], 16 * u) for u in range(4)]
    for which, pieces in ((half, (keep,)), (1 - half, (send,))):
        copies(bits, place, which, pieces, ups, 16, sem.at[0], True)
        copies(bits, place, which, pieces, [(down, 64)], 64, sem.at[1], True)
        copies(bits, place, which, pieces, [(out, 128)], 16, sem.at[2], True)


def feed_mixed(residual, attended, out, gain, mixed, normed):
    mixed[...] = residual[...] + nn(attended[...], out[...])
    for b in range(2):
        rows = pl.ds(256 * b, 256)
        unit, unused = norm_parts(mixed[rows, :])
        normed[rows, :] = (unit * gain).astype(BF16)


def feed_inner(normed, up, active, slope):
    later = nn(normed[...], up[0])
    for u in range(4):
        inner = later
        if u < 3:
            later = nn(normed[...], up[u + 1])
        square = inner * inner
        bent = jnp.tanh(0.7978845608028654 * (inner + 0.044715 * (square * inner)))
        half = 0.5 * (1.0 + bent)
        active[:, 512 * u : 512 * (u + 1)] = (inner * half).astype(BF16)
        slope[:, 512 * u : 512 * (u + 1)] = (
            half
            + (0.5 * inner)
            * (1.0 - bent * bent)
            * (0.7978845608028654 * (1.0 + (3 * 0.044715) * square))
        ).astype(BF16)


def feed_output(mixed, active, down, output):
    output[...] = mixed[...] + nn(active[...], down[...])


def feed_forward(bits, base, scalars, residual, attended, vecs, own_low, own_high, other_low, other_high,
                 output, memory, mixed_o, saved,
                 mixed, normed, active, slope, up, down, out, sem, out_sem):
    place, half = scalars[0], scalars[1]
    both = ((half, (own_low, own_high)), (1 - half, (other_low, other_high)))
    feed_weights(bits, place, both, up, down, out, sem)
    arrived(out, sem.at[0])
    outs = [fetch(out, saved.at[pl.ds(OUT_AT, D)], out_sem.at[0])]
    feed_mixed(residual, attended, out, vecs[base + 1 : base + 2, :], mixed, normed)
    outs.append(fetch(normed, saved.at[pl.ds(0, SEG)], out_sem.at[1]))
    outs.append(fetch(mixed, mixed_o, out_sem.at[2]))
    arrived(up, sem.at[1])
    outs += [fetch(up.at[u], saved.at[pl.ds(UP_AT + D * u, D)], out_sem.at[4 + u]) for u in range(4)]
    feed_inner(normed, up, active, slope)
    for u in range(4):
        cols = pl.ds(D * u, D)
        outs.append(fetch(active.at[:, cols], saved.at[pl.ds(ACTIVE_AT + D * u, D)], out_sem.at[8 + u]))
        outs.append(fetch(slope.at[:, cols], saved.at[pl.ds(SLOPE_AT + D * u, D)], out_sem.at[12 + u]))
    arrived(down, sem.at[2])
    outs.append(fetch(down, saved.at[pl.ds(DOWN_AT, FF)], out_sem.at[3]))
    feed_output(mixed, active, down, output)
    memory[...] = output[SEG - MEM :, :]
    for copy in outs:
        copy.wait()


def feed_back(moves, base, grad_out, mixed, vecs, attended, normed, active, slope, up, down, out,
              grad_mixed, grad_att, grad_gain, grad_inner, staged_up, staged_down, staged_out):
    grad_y = grad_out[...].astype(BF16)
    for copy in moves[:1]:
        copy.wait()
    later = nt(grad_y, down[0:512, :])
    for copy in moves[1:10]:
        copy.wait()
    grad_normed = jnp.zeros((SEG, D), F32)
    for u in range(4):
        cols = slice(512 * u, 512 * (u + 1))
        part = later
        if u < 3:
            later = nt(grad_y, down[512 * (u + 1) : 512 * (u + 2), :])
        staged_down[cols, :] = tn(active[:, cols], grad_y).astype(BF16)
        grad_inner[:, cols] = (part * slope[:, cols].astype(F32)).astype(BF16)
        for copy in moves[10 + u : 11 + u]:
            copy.wait()
        grad_normed = grad_normed + nt(grad_inner[:, cols], up[u])
        staged_up[u] = tn(normed[...], grad_inner[:, cols]).astype(BF16)
    for copy in moves[14:]:
        copy.wait()
    unit, inverse = norm_parts(mixed[...])
    grad_here, gains = norm_back(unit, inverse, vecs[base + 1 : base + 2, :], grad_normed)
    grad = grad_out[...] + grad_here
    grad_mixed[...] = grad
    grad_b = grad.astype(BF16)
    grad_att[...] = nt(grad_b, out[...]).astype(BF16)
    staged_out[...] = tn(attended[...], grad_b).astype(BF16)
    grad_gain[...] = jnp.broadcast_to(gains, grad_gain.shape)


def feed_backward(bits, base, scalars, grad_out, vecs, mixed_h, probs_h, saved,
                  keep, send, grad_mixed, grad_att, grad_gain, mixed, attended,
                  normed, active, slope, up, down, out, grad_inner, staged_up, staged_down, staged_out,
                  in_sem, sem):
    pairs = [(saved.at[pl.ds(DOWN_AT, FF)], down)]
    for u in range(4):
        pairs.append((saved.at[pl.ds(SLOPE_AT + D * u, D)], slope.at[:, pl.ds(D * u, D)]))
    for u in range(4):
        pairs.append((saved.at[pl.ds(ACTIVE_AT + D * u, D)], active.at[:, pl.ds(D * u, D)]))
    pairs.append((saved.at[pl.ds(0, SEG)], normed))
    for u in range(4):
        pairs.append((saved.at[pl.ds(UP_AT + D * u, D)], up.at[u]))
    pairs.append((saved.at[pl.ds(OUT_AT, D)], out))
    pairs.append((mixed_h, mixed))
    for b in range(2):
        pairs.append((probs_h.at[PAIRS + b, :, pl.ds(0, D)], attended.at[pl.ds(256 * b, 256)]))
    moves = [fetch(there, here, in_sem.at[index]) for index, (there, here) in enumerate(pairs)]
    feed_back(moves, base, grad_out, mixed, vecs, attended, normed, active, slope, up, down, out,
              grad_mixed, grad_att, grad_gain, grad_inner, staged_up, staged_down, staged_out)
    feed_grads_out(bits, scalars[0], scalars[1], keep, send, staged_up, staged_down, staged_out, sem)
    arrived(staged_up, sem.at[0])
    arrived(staged_down, sem.at[1])
    arrived(staged_out, sem.at[2])


def top_kernel(bits, streams, scalars, residual, attended, targets, vecs, own_low, own_high, other_low, other_high,
               keep, send, grad_mixed, grad_att, grad_gain, final_gain, loss,
               normed, active, slope, up, down, out, mixed, output, grad_out, table, final, grad_logits, staged,
               grad_inner, staged_up, staged_down, staged_out, head_sem, sem, out_sem):
    place, half, length, segment = scalars[0], scalars[1], scalars[2], scalars[3]
    both = ((half, (own_low, own_high)), (1 - half, (other_low, other_high)))
    feed_weights(bits, place, both, up, down, out, sem)
    units = [(table.at[u], 144 + 16 * u) for u in range(2)]
    for which, pieces in both:
        copies(bits, place, which, pieces, units, 16, head_sem, False)
    arrived(out, sem.at[0])
    feed_mixed(residual, attended, out, vecs[5:6, :], mixed, normed)
    arrived(up, sem.at[1])
    feed_inner(normed, up, active, slope)
    arrived(down, sem.at[2])
    feed_output(mixed, active, down, output)
    arrived(table, head_sem)
    size = length.astype(F32)
    codes = jnp.transpose(jnp.broadcast_to(targets[...].astype(F32), (BLOCK, SEG))).astype(jnp.int32)
    gain = vecs[8:9, :]
    gains = jnp.zeros((1, D), F32)
    terms = jnp.zeros((1, 1), F32)
    for b in range(2):
        rows = pl.ds(256 * b, 256)
        unit, inverse = norm_parts(output[rows, :])
        fin = (unit * gain).astype(BF16)
        final[rows, :] = fin
        logits = jnp.concatenate([nn(fin, table[0]), nn(fin, table[1])], 1)
        top = jnp.max(logits, -1, keepdims=True)
        expo = jnp.exp(logits - top)
        total = jnp.sum(expo, -1, keepdims=True)
        picks = lax.broadcasted_iota(jnp.int32, logits.shape, 1) == codes[256 * b : 256 * (b + 1), 0:1]
        picked = jnp.sum(jnp.where(picks, logits, 0.0), -1, keepdims=True)
        spot = segment * SEG + 256 * b + lax.broadcasted_iota(jnp.int32, (256, 1), 0)
        weight = jnp.where(spot < length, 1.0 / size, 0.0)
        terms = terms + jnp.sum((top + jnp.log(total) - picked) * weight, keepdims=True)
        grad = (expo * (1.0 / total) - jnp.where(picks, 1.0, 0.0)) * (weight * (1.0 / streams))
        grad_b = grad.astype(BF16)
        grad_logits[rows, :] = grad_b
        grad_final = nt(grad_b[:, 0:512], table[0]) + nt(grad_b[:, 512:1024], table[1])
        grad_here, gain_here = norm_back(unit, inverse, gain, grad_final)
        grad_out[rows, :] = grad_here
        gains = gains + gain_here
    for u in range(2):
        staged[u] = tn(final[...], grad_logits[:, 512 * u : 512 * (u + 1)]).astype(BF16)
    units = [(staged.at[u], 144 + 16 * u) for u in range(2)]
    copies(bits, place, half, (keep,), units, 16, head_sem, True)
    copies(bits, place, 1 - half, (send,), units, 16, head_sem, True)
    final_gain[...] = jnp.broadcast_to(gains, final_gain.shape)
    loss[...] = jnp.broadcast_to(terms, loss.shape)
    feed_back((), 4, grad_out, mixed, vecs, attended, normed, active, slope, up, down, out,
              grad_mixed, grad_att, grad_gain, grad_inner, staged_up, staged_down, staged_out)
    feed_grads_out(bits, place, half, keep, send, staged_up, staged_down, staged_out, out_sem)
    arrived(staged, head_sem)
    arrived(staged_up, out_sem.at[0])
    arrived(staged_down, out_sem.at[1])
    arrived(staged_out, out_sem.at[2])


def finish(counts, *refs):
    scalars, loss = refs[0], refs[1]
    total_count = sum(counts)
    sources = refs[2 : 2 + total_count]
    kept, sent, total = refs[2 + total_count : 5 + total_count]
    buffers, sem = refs[5 + total_count : -1], refs[-1]
    moves = [fetch(there.at[0], here, sem.at[index]) for index, (there, here) in enumerate(zip(sources, buffers))]
    for copy in moves:
        copy.wait()
    sums = []
    start = 0
    for count in counts:
        item = buffers[start][...].astype(F32)
        for other in buffers[start + 1 : start + count]:
            item = item + other[...].astype(F32)
        sums.append(item)
        start += count
    attn_zero, feed_zero, attn_one, feed_one, small = sums[0], sums[1], sums[2], sums[3], sums[4]
    attn_zero = attn_zero + sums[5][0:64]
    small = small + sums[5][64:80]
    first = scalars[1] == 0
    lone = jnp.zeros((1, 1), F32)
    for zero, one, rows, begin in ((attn_zero, attn_one, 64, 0), (feed_zero, feed_one[0:144], 144, 64)):
        kept[begin : begin + rows, :] = jnp.where(first, zero, one)
        sent[begin : begin + rows, :] = jnp.where(first, one, zero)
        lone = lone + jnp.sum(zero * zero + one * one, keepdims=True)
    head = feed_one[144:176]
    lone = lone + jnp.sum(head * head, keepdims=True) + jnp.sum(small * small, keepdims=True)
    for target in (kept, sent):
        target[208:240, :] = head
        target[240:256, :] = small
    column = lax.broadcasted_iota(jnp.int32, (8, 128), 1)
    total[...] = jnp.where(column == 0, lone, 0.0) + jnp.where(column == 1, loss[...], 0.0)


def adam_step(weight, grad, first, second, rate, decay, factor):
    grad = grad * factor
    first = 0.9 * first + 0.1 * grad
    second = 0.999 * second + 0.001 * grad * grad
    ratio = first / (1.0 - 0.9**STEP) / (jnp.sqrt(second / (1.0 - 0.999**STEP)) + 1e-08)
    return (weight - rate * (ratio + decay * weight), first, second)


def update(scalars, total, kept, got, *refs):
    ins, outs, small = refs[:27], refs[27:56], refs[56]
    first = scalars[1] == 0
    squares = jnp.sum(total[0:1, 0:1], keepdims=True)
    norm = jnp.sqrt(squares)
    outs[27][...] = norm
    outs[28][...] = total[0:1, 1:2]
    factor = jnp.minimum(1.0, CLIP / (norm + 1e-06))

    def half_of(half, start, rows):
        here, there = kept[start : start + rows, :], got[start : start + rows, :]
        return jnp.where(first == (half == 0), here, there)

    def apply(index, spot, grad, rate, decay):
        results = adam_step(
            ins[index][spot], grad, ins[9 + index][spot], ins[18 + index][spot], rate, decay, factor
        )
        for which, result in enumerate(results):
            outs[9 * which + index][spot] = result

    for half in range(2):
        rows = slice(16 * half, 16 * half + 16)
        for u in range(3):
            apply(0, (0, rows, slice(D * u, D * (u + 1))), half_of(half, 16 * u, 16), 0.03, 0.01)
        apply(1, (0, rows, slice(None)), half_of(half, 192, 16), 0.03, 0.01)
        apply(2, (0, rows, slice(None)), half_of(half, 48, 16), 0.03, 0.01)
        for u in range(4):
            apply(3, (0, rows, slice(D * u, D * (u + 1))), half_of(half, 64 + 16 * u, 16), 0.03, 0.01)
        apply(4, (0, slice(64 * half, 64 * half + 64), slice(None)), half_of(half, 128, 64), 0.03, 0.01)
        for u in range(2):
            apply(7, (rows, slice(D * u, D * (u + 1))), half_of(half, 208 + 16 * u, 16), 0.03, 0.01)
        small[rows, :] = half_of(half, 240, 16)[:, 0:BLOCK]
    small[32:, :] = jnp.zeros((BLOCK - 32, BLOCK), F32)
    turned = jnp.transpose(small[...])
    apply(6, (slice(None), slice(None)), small[0:32, 0:FEATS], 0.03, 0.01)
    vecs = jnp.where(first, turned[80:84, 0:32], turned[84:88, 0:32])
    apply(5, (0, slice(None), slice(None)), vecs, 0.3, 0.0)
    apply(8, (slice(None), slice(None)), turned[88:89, 0:32], 0.3, 0.0)


def pack_shards(scalars, attn, out, pos, up, down, vecs, w_in, head, gain, kept, sent, codes, small):
    half, section = scalars[1], scalars[3]
    small[...] = jnp.zeros_like(small)
    small[88:89, 0:32] = gain[...]
    small[pl.ds(FEATS + 4 * section, 4), 0:32] = vecs[0]
    turned = jnp.transpose(small[...])[0:32]
    turned = jnp.concatenate([w_in[...], turned[:, FEATS:]], 1)
    column = lax.broadcasted_iota(jnp.int32, turned.shape, 1)
    shared = (column < FEATS) | (column == 88)
    for which, target in ((half, kept), (1 - half, sent)):
        rows = pl.ds(pl.multiple_of(16 * which, 16), 16)
        for u in range(3):
            target[16 * u : 16 * u + 16, :] = attn[0, rows, D * u : D * (u + 1)].astype(BF16)
        target[48:64, :] = pos[0, rows, :].astype(BF16)
        for u in range(4):
            target[64 + 16 * u : 80 + 16 * u, :] = up[0, rows, D * u : D * (u + 1)].astype(BF16)
        target[128:192, :] = down[0, pl.ds(pl.multiple_of(64 * which, 64), 64), :].astype(BF16)
        target[192:208, :] = out[0, rows, :].astype(BF16)
        tail = jnp.where(half == 0, turned[0:16], turned[16:32])
        if target is sent:
            tail = jnp.where(half == 0, turned[16:32], turned[0:16])
            tail = jnp.where(shared[0:16], 0.0, tail)
        target[208:224, :] = jnp.zeros((16, D), BF16)
        target[208:224, 0:BLOCK] = tail.astype(BF16)
    rows = pl.ds(pl.multiple_of(16 * half, 16), 16)
    for u in range(2):
        codes[16 * u : 16 * u + 16, :] = head[rows, D * u : D * (u + 1)].astype(BF16)


VMEM = pl.BlockSpec(memory_space=pltpu.VMEM)
ANY = pl.BlockSpec(memory_space=pl.ANY)
HBM = pl.BlockSpec(memory_space=pltpu.HBM)
SMEM = pl.BlockSpec(memory_space=pltpu.SMEM)
DMA = pltpu.SemaphoreType.DMA


def shape(*dims, dtype=F32):
    return jax.ShapeDtypeStruct(dims, dtype)


def half_shape(*dims):
    return jax.ShapeDtypeStruct(dims, BF16)


def held(*dims):
    return pltpu.VMEM(dims, BF16)


def wide(*dims):
    return pltpu.VMEM(dims, F32)


def call(body, name, ins, outs, out_specs, scratch, micros, limit):
    return pl.pallas_call(
        body,
        name=name,
        in_specs=ins,
        out_shape=outs,
        out_specs=out_specs,
        scratch_shapes=scratch,
        compiler_params=pltpu.CompilerParams(vmem_limit_bytes=limit * 1024 * 1024),
        cost_estimate=pl.CostEstimate(flops=micros * 1_150_000_000, bytes_accessed=1 << 20, transcendentals=0),
    )


QUERY_KEY = (half_shape(SEG, D), half_shape(SEG, D), half_shape(ROWS, D), half_shape(ROWS, D), half_shape(ROWS, D))
PROJECT_HELD = [held(ROWS, D), held(4, D, D), DMA, DMA((12,))]
KEPT = half_shape(KEPT_ROWS, D)


def run_project_first(bits, scalars, frames, pieces, table):
    result = call(
        functools.partial(project, bits, 0),
        "project_first",
        [SMEM, VMEM, HBM, HBM, HBM, HBM, VMEM],
        QUERY_KEY + (shape(SEG, D), shape(16, D), KEPT),
        [VMEM] * 7 + [HBM],
        PROJECT_HELD + [wide(ROWS, D), held(D, BLOCK), DMA],
        6,
        40,
    )(scalars, frames, *pieces, table)
    return result[:5], result[5], result[6], result[7]


def run_project(bits, scalars, memory, hidden, vecs, pieces, table):
    result = call(
        functools.partial(project, bits, 4),
        "project",
        [SMEM, VMEM, VMEM, VMEM, HBM, HBM, HBM, HBM, VMEM],
        QUERY_KEY + (KEPT,),
        [VMEM] * 5 + [HBM],
        PROJECT_HELD,
        6,
        40,
    )(scalars, memory, hidden, vecs, *pieces, table)
    return result[:5], result[5]


def run_attend(scalars, projected):
    return call(
        attend,
        "attend",
        [SMEM] + [VMEM] * 5,
        (half_shape(SEG, D), half_shape(KEPT_PAIRS, 2 * BLOCK, WIDE)),
        [VMEM, HBM],
        [held(PAIRS, 2 * BLOCK, WIDE), DMA((PAIRS + 2,))],
        11,
        44,
    )(scalars, *projected)


HALF_HELD = [
    held(SEG, 256), held(SEG, 256), held(ROWS, 256), held(ROWS, 256), held(ROWS, 256),
    held(2, 2 * BLOCK, WIDE), held(2 * BLOCK, 2 * BLOCK),
    wide(256, ROWS), wide(256, ROWS), wide(256, ROWS), wide(SEG, 256), wide(SEG, 256), DMA((2, 6)),
]
LATE_HELD = [held(ROWS, D), held(ROWS, D), DMA((2,))]
HALF_OUT = (half_shape(SEG, 256), half_shape(ROWS, 256), half_shape(ROWS, 256))


def run_attend_back(bits, scalars, grad_att, saved, table, probs):
    result = call(
        functools.partial(attend_back, bits, False),
        "attend_back",
        [SMEM, VMEM] + [HBM] * 3,
        HALF_OUT + (half_shape(4, D, 256), shape(8, 256)),
        [VMEM] * 5,
        HALF_HELD + LATE_HELD,
        9,
        40,
    )(scalars, grad_att, table, saved, probs)
    return (*result[:3], result[4]), result[3]


def run_attend_back_rest(bits, scalars, grad_att, saved, table, probs, staged):
    result = call(
        functools.partial(attend_back, bits, True),
        "attend_back_rest",
        [SMEM, VMEM] + [HBM] * 3 + [VMEM],
        HALF_OUT + (shape(8, 256), half_shape(GROUPS, 64, D), half_shape(GROUPS, 64, D)),
        [VMEM] * 4 + [ANY] * 2,
        HALF_HELD + [held(4, D, D), DMA] + LATE_HELD,
        10,
        42,
    )(scalars, grad_att, table, saved, probs, staged)
    return result[:4], result[4], result[5]


def run_input_grads(bits, scalars, saved, grads, grad_mixed, vecs, memory, hidden):
    return call(
        functools.partial(input_grads, bits, 4),
        "input_grads",
        [SMEM, HBM] + [VMEM] * 12,
        (shape(SEG, D), shape(8, D)),
        [VMEM] * 2,
        [held(4, D, D), DMA((3,))],
        5,
        50,
    )(scalars, saved, *grads, grad_mixed, vecs, memory, hidden)


def run_input_grads_last(bits, scalars, saved, grads, grad_mixed, vecs, frames, *small_grads):
    return call(
        functools.partial(input_grads, bits, 0),
        "input_grads_last",
        [SMEM, HBM] + [VMEM] * 15,
        (half_shape(GROUPS, 16, D), half_shape(GROUPS, 16, D)),
        [ANY] * 2,
        [wide(ROWS, D), wide(BLOCK, D), held(D, D), DMA, held(D, BLOCK), DMA, held(4, D, D), DMA((3,))],
        5,
        50,
    )(scalars, saved, *grads, grad_mixed, vecs, frames, *small_grads)


FEED_HELD = [held(SEG, D), held(SEG, FF), held(SEG, FF), held(4, D, D), held(FF, D), held(D, D)]
BACK_HELD = [held(SEG, FF), held(4, D, D), held(FF, D), held(D, D)]


def run_feed_forward(bits, base, scalars, residual, attended, vecs, pieces):
    result = call(
        functools.partial(feed_forward, bits, base),
        "feed_forward",
        [SMEM, VMEM, VMEM, VMEM, HBM, HBM, HBM, HBM],
        (shape(SEG, D), shape(MEM, D), shape(SEG, D), KEPT),
        [VMEM] * 2 + [HBM] * 2,
        [wide(SEG, D)] + FEED_HELD + [DMA((3,)), DMA((16,))],
        9,
        50,
    )(scalars, residual, attended, vecs, *pieces)
    return result


def run_feed_backward(bits, base, scalars, grad_out, vecs, mixed, probs, saved):
    return call(
        functools.partial(feed_backward, bits, base),
        "feed_backward",
        [SMEM, VMEM, VMEM] + [HBM] * 3,
        (half_shape(GROUPS, 144, D), half_shape(GROUPS, 144, D), shape(SEG, D), half_shape(SEG, D), shape(8, D)),
        [ANY, ANY, VMEM, VMEM, VMEM],
        [wide(SEG, D), held(SEG, D)] + FEED_HELD + BACK_HELD + [DMA((18,)), DMA((3,))],
        13,
        50,
    )(scalars, grad_out, vecs, mixed, probs, saved)


def run_top(bits, streams, scalars, residual, attended, targets, vecs, pieces):
    return call(
        functools.partial(top_kernel, bits, streams),
        "top_kernel",
        [SMEM, VMEM, VMEM, VMEM, VMEM, HBM, HBM, HBM, HBM],
        (
            half_shape(GROUPS, 176, D), half_shape(GROUPS, 176, D),
            shape(SEG, D), half_shape(SEG, D), shape(8, D), shape(8, D), shape(8, 128),
        ),
        [ANY] * 2 + [VMEM] * 5,
        FEED_HELD
        + [wide(SEG, D), wide(SEG, D), wide(SEG, D), held(2, D, D), held(SEG, D), held(SEG, CODES), held(2, D, D)]
        + BACK_HELD
        + [DMA, DMA((3,)), DMA((3,))],
        21,
        56,
    )(scalars, residual, attended, targets, vecs, *pieces)


def run_finish(scalars, loss, *sums):
    counts = tuple((len(item) for item in sums))
    flat = [item for group in sums for item in group]
    return call(
        functools.partial(finish, counts),
        "finish",
        [SMEM, VMEM] + [ANY] * len(flat),
        (shape(256, D), shape(256, D), shape(8, 128)),
        [VMEM] * 3,
        [pltpu.VMEM(item.shape[1:], item.dtype) for item in flat] + [DMA((len(flat),))],
        3,
        56,
    )(scalars, loss, *flat)


def run_update(scalars, total, kept, got, state):
    flat = [item[None] if item.ndim == 1 else item for item in state]
    for index in (6, 15, 24):
        flat[index] = jnp.transpose(flat[index])
    result = call(
        update,
        "update",
        [SMEM] + [VMEM] * 30,
        tuple((shape(*item.shape) for item in flat)) + (shape(1, 1), shape(1, 1)),
        [VMEM] * 29,
        [wide(BLOCK, BLOCK)],
        5,
        24,
    )(scalars, total, kept, got, *flat)
    result = list(result)
    for index in (6, 15, 24):
        result[index] = jnp.transpose(result[index])
    return [item.reshape(old.shape) for item, old in zip(result, state)] + [result[27][0, 0], result[28][0, 0]]


def run_pack(scalars, w_attn, w_out, w_pos, w_up, w_down, layer_vecs, w_in, w_head, gain_final):
    return call(
        pack_shards,
        "pack_shards",
        [SMEM] + [VMEM] * 9,
        (half_shape(224, D), half_shape(224, D), half_shape(32, D)),
        [VMEM] * 3,
        [wide(BLOCK, BLOCK)],
        3,
        56,
    )(scalars, w_attn, w_out, w_pos, w_up, w_down, layer_vecs, jnp.transpose(w_in), w_head, gain_final[None])


def spread(value, bits):
    count = lax.axis_size("dp")
    pairs = [
        (half * count + i, half * count + (i ^ bit)) for half, bit in enumerate(bits) for i in range(count)
    ]
    return lax.ppermute(value, ("section", "dp"), pairs)


def swap(value):
    return lax.ppermute(value, "section", [(0, 1), (1, 0)])


def fence(*values):
    return lax.optimization_barrier(values)


def joined(low, got):
    return jnp.concatenate([low, got], 0)


def part(sources, first, last):
    total = sources[0][first:last].astype(F32)
    for item in sources[1:]:
        total = total + item[first:last].astype(F32)
    return total


def shrink(chunks, pair, merged=()):
    count = (merged or chunks[0])[-1].shape[0]
    sent, first = [], 0
    for item in chunks:
        rows = item[0].shape[1]
        total = part(item, count // 2, count)
        if merged:
            total = total + part([other[:, first : first + rows] for other in merged], count // 2, count)
        sent.append(total.astype(BF16))
        first += rows
    return spread(jnp.concatenate(sent, 1), pair)


def add_up(value, bits):
    value = value + swap(value)
    steps = [low for low, unused in zip(*bits)]
    for one, two in zip(steps[0::2], steps[1::2]):
        first, second, third = (spread(value, (step, step)) for step in (one, two, one + two))
        value = (value + first) + (second + third)
    return value


def lanes_of(block):
    return [block[:, D * u : D * (u + 1)] for u in range(block.shape[1] // D)]


def sinus_table(where_at):
    freqs = jnp.exp(-jnp.log(10000.0) * (2.0 * jnp.arange(D // 2, dtype=jnp.int32).astype(F32) / D))
    angles = where_at * freqs[None, :]
    return jnp.concatenate([jnp.sin(angles), jnp.cos(angles)], 1).astype(BF16)


def split_shards(section, scalars, params):
    kept, sent, head = run_pack(scalars, *params)
    got = swap(sent)
    first = section == 0
    zero = jnp.where(first, kept, got)
    one = jnp.where(first, got, kept)
    return (
        jnp.concatenate([zero[:64], kept[208:] + got[208:]], 0),
        zero[64:208],
        one[:64],
        jnp.concatenate([one[64:208], head], 0),
    )


def halves(whole, rows):
    return whole.reshape(GROUPS, 2, rows, whole.shape[1]).transpose(1, 0, 2, 3)


def gather_whole(section, w_attn, w_out, w_pos, w_up, w_down, layer_vecs, w_in, w_head, gain_final):
    def over(value, axis):
        return lax.all_gather(value.astype(BF16), "dp", axis=axis, tiled=True)

    def layers(value):
        return lax.all_gather(over(value[0], 0), "section", axis=0)

    attn, out, pos, up, down = (layers(item) for item in (w_attn, w_out, w_pos, w_up, w_down))
    vecs = lax.all_gather(over(layer_vecs[0], 1), "section", axis=0)
    small = jnp.concatenate(
        [over(w_in, 1), vecs[0], vecs[1], over(gain_final, 0)[None], jnp.zeros((BLOCK - 89, D), BF16)], 0
    )
    small = jnp.pad(jnp.transpose(small), ((0, 0), (0, D - BLOCK)))
    head = over(w_head, 0)

    def pieces(units):
        both = jnp.concatenate([halves(item, item.shape[0] // 32) for item in units], 2)
        own = lax.dynamic_index_in_dim(both, section, 0, keepdims=False)
        other = lax.dynamic_index_in_dim(both, 1 - section, 0, keepdims=False)
        return (own[:8], own[8:], other[:8], other[8:])

    return (
        pieces(lanes_of(attn[0]) + [pos[0], small]),
        pieces(lanes_of(up[0]) + [down[0], out[0]]),
        pieces(lanes_of(attn[1]) + [pos[1]]),
        pieces(lanes_of(up[1]) + [down[1], out[1]] + lanes_of(head)),
    )


def whole_grads(section, sums):
    count = lax.axis_size("dp")
    place = lax.axis_index("dp")
    attn_zero, feed_zero, attn_one, feed_one, small = (
        lax.all_gather(lax.psum(item, "dp"), "section", axis=0) for item in sums
    )

    def unit(both, start, rows):
        item = both[:, :, start : start + rows]
        return item.transpose(1, 0, 2, 3).reshape(GROUPS * 2 * rows, both.shape[3])

    def layer(attn, feed):
        return (
            jnp.concatenate([unit(attn, 16 * u, 16) for u in range(3)], 1),
            unit(feed, 128, 16),
            unit(attn, 48, 16),
            jnp.concatenate([unit(feed, 16 * u, 16) for u in range(4)], 1),
            unit(feed, 64, 64),
        )

    small = jnp.transpose(unit(small, 0, 16))
    zero = layer(attn_zero, feed_zero) + (small[80:84],)
    one = layer(attn_one, feed_one) + (small[84:88],)
    ends = (small[:80], jnp.concatenate([unit(feed_one, 144 + 16 * u, 16) for u in range(2)], 1), small[88])
    squares = sum((jnp.sum(item * item) for item in zero + one + ends))
    dims = (0, 0, 0, 0, 0, 1, 1, 0, 0)
    grads = tuple((jnp.where(section == 0, a, b) for a, b in zip(zero, one))) + ends
    return squares, tuple(
        (
            lax.dynamic_slice_in_dim(item, place * (item.shape[dim] // count), item.shape[dim] // count, dim)
            for item, dim in zip(grads, dims)
        )
    )


def local(frames, targets, lengths, *state):
    params, firsts, seconds = (state[:9], state[9:18], state[18:])
    section = lax.axis_index("section")
    streams = lax.axis_size("dp")
    ringed = streams == GROUPS
    place = lax.axis_index("dp") if ringed else jnp.int32(0)
    length = lengths[0]
    scalars = jnp.stack([place, section, length, section]).astype(jnp.int32)
    count_down = (ROWS - 1 - jnp.arange(ROWS, dtype=jnp.int32)).astype(F32)[:, None]
    rows = lax.dynamic_slice_in_dim(
        jnp.pad(frames[0], ((MEM, 0), (0, BLOCK - FEATS))), section * SEG, ROWS, 0
    )
    codes = lax.dynamic_slice_in_dim(targets, section * SEG, SEG, 1)
    if ringed:
        bits = ((8, 4, 1, 2), (8, 4, 2, 1))
        far, near, side, last = zip(*bits)
        zero, one, two, three = (item[None] for item in split_shards(section, scalars, params))
        zero, got, count_down = fence(zero, spread(zero, far), count_down)
        table = sinus_table(count_down)
        zero = joined(zero, got)
        zero, got, one = fence(zero, spread(zero, near), one)
        zero = joined(zero, got)
        one_got = spread(one, far)
        zero, got, two, one, one_got, rows, table, codes = fence(
            zero, spread(zero, side), two, one, one_got, rows, table, codes
        )
        zero = joined(zero, got)
        high, swapped = spread(zero, last), swap(zero)
        one = joined(one, one_got)
        one_got, two_got = spread(one, near), spread(two, far)
        zero, high, swapped, one, one_got, two, two_got = fence(
            zero, high, swapped, one, one_got, two, two_got
        )
        chunk = (zero, high, swapped, swap(high))
        one, two = joined(one, one_got), joined(two, two_got)
        one_got, two_got, three_got = spread(one, side), spread(two, near), spread(three, far)
    else:
        bits = IN_ORDER
        table = sinus_table(count_down)
        chunk, chunk_one, chunk_two, chunk_three = gather_whole(section, *params)

    projected, hidden_zero, vecs, saved_zero = run_project_first(bits, scalars, rows, chunk, table)
    if ringed:
        projected, one_got, two_got, three_got = fence(projected, one_got, two_got, three_got)
        one, two, three = joined(one, one_got), joined(two, two_got), joined(three, three_got)
        one_got, two_got, three_got, swapped = spread(one, last), spread(two, side), spread(three, near), swap(one)
    attended, probs_zero = run_attend(scalars, projected)
    if ringed:
        attended, one_got, two_got, three_got, swapped = fence(
            attended, one_got, two_got, three_got, swapped
        )
        chunk = (one, one_got, swapped, swap(one_got))
        two, three = joined(two, two_got), joined(three, three_got)
        two_got, three_got, swapped = spread(two, last), spread(three, side), swap(two)
    else:
        chunk = chunk_one
    out_zero, memory, mixed_zero, fed_zero = run_feed_forward(bits, 0, scalars, hidden_zero, attended, vecs, chunk)
    if ringed:
        out_zero, memory, two_got, three_got, swapped = fence(out_zero, memory, two_got, three_got, swapped)
        chunk = (two, two_got, swapped, swap(two_got))
        three = joined(three, three_got)
        three_got, three_swapped = spread(three, last), swap(three)
    else:
        chunk = chunk_two
    memory = lax.ppermute(memory, "section", [(0, 1)])
    projected, saved_one = run_project(bits, scalars, memory, out_zero, vecs, chunk, table)
    attended, probs_one = run_attend(scalars, projected)
    if ringed:
        attended, three_got, three_swapped = fence(attended, three_got, three_swapped)
        chunk = (three, three_got, three_swapped, swap(three_got))
    else:
        chunk = chunk_three
    keep_a, send_a, grad, grad_att, gain_one, gain_final, loss = run_top(
        bits, streams, scalars, out_zero, attended, codes, vecs, chunk
    )
    if ringed:
        grad_att, keep_a, send_a = fence(grad_att, keep_a, send_a)
        got_a = swap(send_a)
    grads_a, staged = run_attend_back(bits, scalars, grad_att, saved_one, table, probs_one)
    if ringed:
        grads_a, staged, got_a = fence(grads_a, staged, got_a)
        sum_a = [keep_a, got_a]
        got_a = shrink([sum_a], last)
    grads_b, keep_b, send_b = run_attend_back_rest(
        bits, scalars, grad_att, saved_one, table, probs_one, staged
    )
    if ringed:
        grads_b, keep_b, send_b = fence(grads_b, keep_b, send_b)
        got_b = swap(send_b)
    grad, vecs_one = run_input_grads(
        bits, scalars, saved_one, (*grads_a, *grads_b), grad, vecs, memory, out_zero
    )
    if ringed:
        grad, got_a, got_b = fence(grad, got_a, got_b)
        sum_a.append(got_a)
        sum_b = [keep_b, got_b]
        got_a, got_b = shrink([sum_a], side), shrink([sum_b], last)
    keep_c, send_c, grad, grad_att, gain_zero = run_feed_backward(
        bits, 0, scalars, grad, vecs, mixed_zero, probs_zero, fed_zero
    )
    if ringed:
        grad_att, got_a, got_b, keep_c, send_c = fence(grad_att, got_a, got_b, keep_c, send_c)
        sum_a.append(got_a)
        sum_b.append(got_b)
        got_a, got_b, got_c = shrink([sum_a], near), shrink([sum_b], side), swap(send_c)
    grads_a, staged = run_attend_back(bits, scalars, grad_att, saved_zero, table, probs_zero)
    if ringed:
        grads_a, staged, got_a, got_b, got_c = fence(grads_a, staged, got_a, got_b, got_c)
        sum_a.append(got_a)
        sum_b.append(got_b)
        sum_c = [keep_c, got_c]
        got_c, got_a, got_b = shrink([sum_c], last), shrink([sum_a], far), shrink([sum_b], near)
    grads_b, keep_d, send_d = run_attend_back_rest(
        bits, scalars, grad_att, saved_zero, table, probs_zero, staged
    )
    if ringed:
        grads_b, keep_d, send_d, got_a, got_b, got_c = fence(grads_b, keep_d, send_d, got_a, got_b, got_c)
        sum_a.append(got_a)
        sum_b.append(got_b)
        sum_c.append(got_c)
        got_d, got_c, got_b = swap(send_d), shrink([sum_c], side), shrink([sum_b], far)
    keep_e, send_e = run_input_grads_last(
        bits, scalars, saved_zero, (*grads_a, *grads_b), grad, vecs, rows,
        gain_zero, vecs_one, gain_one, gain_final,
    )
    if not ringed:
        pairs = ((keep_d, send_d), (keep_c, send_c), (keep_b, send_b), (keep_a, send_a), (keep_e, send_e))
        sums = [keep.astype(F32) + swap(send).astype(F32) for keep, send in pairs]
        squares, grads = whole_grads(section, sums)
        grad_norm = jnp.sqrt(squares)
        loss_sum = lax.psum(loss[0, 0], ("section", "dp"))
        factor = jnp.minimum(1.0, CLIP / (grad_norm + 1e-06))
        results = []
        for index in range(9):
            rate, decay = (0.3, 0.0) if index in (5, 8) else (0.03, 0.01)
            grad = grads[index][None] if index < 6 else grads[index]
            results.append(
                adam_step(params[index], grad, firsts[index], seconds[index], rate, decay, factor)
            )
        news, moms, sqs = zip(*results)
        return (*news, *moms, *sqs, grad_norm, loss_sum)
    keep_e, send_e, got_b, got_c, got_d = fence(keep_e, send_e, got_b, got_c, got_d)
    sum_b.append(got_b)
    sum_c.append(got_c)
    sum_d, sum_e, sum_de = [keep_d, got_d], [keep_e, swap(send_e)], []
    for pair in (last, side, near, far):
        got = shrink([sum_d, sum_e], pair, sum_de)
        if pair in (last, side):
            got, got_c = fence(got, shrink([sum_c], near if pair == last else far))
            sum_c.append(got_c)
        sum_de.append(got)
    kept, sent, total = run_finish(scalars, loss, sum_d, sum_c, sum_b, sum_a, sum_e, sum_de)
    got = swap(sent)
    return tuple(run_update(scalars, add_up(total, bits), kept, got, state))


def solution(mesh):
    weights = (
        P("section", "dp", None),
        P("section", "dp", None),
        P("section", "dp", None),
        P("section", "dp", None),
        P("section", "dp", None),
        P("section", None, "dp"),
        P(None, "dp"),
        P("dp", None),
        P("dp"),
    )
    return jax.shard_map(
        local,
        mesh=mesh,
        in_specs=(P("dp", None, None), P("dp", None), P("dp")) + weights * 3,
        out_specs=weights * 3 + (P(), P()),
        check_vma=False,
    )
```

```python
import functools

import jax
import jax.numpy as jnp
from jax import lax
from jax.experimental import pallas as pl
from jax.experimental.pallas import tpu as pltpu
from jax.sharding import PartitionSpec as P

D = 512
FF = 2048
CODES = 1024
FEATS = 80
MEM = 256
SEG = 512
SEGS = 2
STEP = 10
ROWS = MEM + SEG
BLOCK = 128
PAIRS = 4
WIDE = 18 * BLOCK
GROUPS = 16
QUERY_U_AT, QUERY_V_AT, KEYS_AT, VALUES_AT, REL_AT, WEIGHTS_AT, SMALL_AT = 768, 1280, 1792, 2560, 3328, 4096, 6144
ACTIVE_AT, SLOPE_AT, UP_AT, DOWN_AT, OUT_AT = 512, 2560, 4608, 6656, 8704
KEPT_ROWS = 16384
KEPT_PAIRS = 14
IN_ORDER = ((1, 2, 4, 8), (1, 2, 4, 8))
NEG = -1e30
CLIP = 0.02
SCALE = 0.125
F32 = jnp.float32
BF16 = jnp.bfloat16
SPANS = tuple((MEM + BLOCK * (b + 1) for b in range(4)))
STARTS = tuple((sum(SPANS[:b]) for b in range(4)))


def nn(left, right):
    return jnp.dot(left, right, preferred_element_type=F32)


def nt(left, right):
    return lax.dot_general(left, right, (((1,), (1,)), ((), ())), preferred_element_type=F32)


def tn(left, right):
    return lax.dot_general(left, right, (((0,), (0,)), ((), ())), preferred_element_type=F32)


def norm_parts(values):
    center = values - jnp.mean(values, -1, keepdims=True)
    spread = jnp.mean(center * center, -1, keepdims=True)
    inverse = lax.rsqrt(spread + 1e-05)
    return center * inverse, inverse


def norm_back(unit, inverse, gain, grad):
    scaled = grad * gain
    first = jnp.mean(scaled, -1, keepdims=True)
    second = jnp.mean(scaled * unit, -1, keepdims=True)
    return inverse * (scaled - first - unit * second), jnp.sum(grad * unit, 0, keepdims=True)


def group_of(bits, spot, place, half):
    if bits == IN_ORDER:
        return spot
    low, high = (sum((bit for index, bit in enumerate(each) if (spot >> index) & 1)) for each in bits)
    return jnp.bitwise_xor(place, low if low == high else jnp.where(half == 0, low, high))


def copies(bits, place, half, pieces, units, rows, sem, outward):
    count = GROUPS // len(pieces)
    for index, slab in enumerate(pieces):
        for spot in range(count):
            group = group_of(bits, index * count + spot, place, half)
            for whole, first in units:
                there = whole.at[pl.ds(pl.multiple_of((group * 2 + half) * rows, rows), rows), :]
                here = slab.at[spot, pl.ds(first, rows), pl.ds(0, whole.shape[1])]
                if outward:
                    pltpu.make_async_copy(there, here, sem).start()
                else:
                    pltpu.make_async_copy(here, there, sem).start()


def columns(ref, count):
    return [ref.at[:, pl.ds(D * u, D)] for u in range(count)]


def fetch(source, target, sem):
    copy = pltpu.make_async_copy(source, target, sem)
    copy.start()
    return copy


def arrived(buffer, sem):
    pltpu.make_async_copy(buffer, buffer, sem).wait()


def tri_mask():
    row = lax.broadcasted_iota(jnp.int32, (2 * BLOCK, BLOCK), 0)
    col = lax.broadcasted_iota(jnp.int32, (2 * BLOCK, BLOCK), 1)
    return col <= lax.rem(row, BLOCK)


def stack_heads(part):
    col = lax.broadcasted_iota(jnp.int32, part.shape, 1)
    zero = jnp.zeros_like(part)
    return jnp.concatenate(
        [jnp.where(col < 64, part, zero), jnp.where(col < 64, zero, part)], 0
    )


def pick_heads(both):
    col = lax.broadcasted_iota(jnp.int32, (BLOCK, BLOCK), 1)
    return jnp.where(col < 64, both[:BLOCK], both[BLOCK:])


def shift(both, amount):
    return jnp.concatenate(
        [pltpu.roll(part, amount, 1, stride=1, stride_axis=0) for part in (both[:BLOCK], both[BLOCK:])], 0
    )


def masked(score, triangle, first):
    if first == 0:
        return jnp.where(triangle, score, NEG)
    return jnp.concatenate([score[:, :first], jnp.where(triangle, score[:, first:], NEG)], 1)


def lanes(pair):
    return pl.ds(pl.multiple_of(pair * BLOCK, BLOCK), BLOCK)


def project(bits, base, *refs):
    first_layer = base == 0
    if first_layer:
        (scalars, frames, own_low, own_high, other_low, other_high, table) = refs[:7]
        (query_u, query_v, keys, values, rel, hidden, vecs, saved) = refs[7:15]
        (normed, weights, in_sem, out_sem, joined, small, small_sem) = refs[15:]
    else:
        (scalars, memory, hidden, vecs, own_low, own_high, other_low, other_high, table) = refs[:9]
        (query_u, query_v, keys, values, rel, saved) = refs[9:15]
        (normed, weights, in_sem, out_sem) = refs[15:]
    place, half = scalars[0], scalars[1]
    both = ((half, (own_low, own_high)), (1 - half, (other_low, other_high)))
    if first_layer:
        for which, pieces in both:
            copies(bits, place, which, pieces, [(small, 64)], 16, small_sem, False)
    units = [(weights.at[u], 16 * u) for u in range(4)]
    for which, pieces in both:
        copies(bits, place, which, pieces, units, 16, in_sem, False)
    if first_layer:
        arrived(small, small_sem)
        small_out = fetch(small, saved.at[pl.ds(SMALL_AT, D), pl.ds(0, BLOCK)], out_sem.at[7])
        vecs[...] = jnp.transpose(small[...].astype(F32))[80:96]
        for b in range(3):
            rows = pl.ds(256 * b, 256)
            joined[rows, :] = nt(frames[rows, :], small[...])
        hidden[...] = joined[MEM:, :]
        sources = [joined.at[pl.ds(256 * b, 256)] for b in range(3)]
    else:
        sources = [memory, hidden.at[pl.ds(0, 256)], hidden.at[pl.ds(256, 256)]]
    gain = vecs[base : base + 1, :]
    bias_u = vecs[base + 2 : base + 3, :]
    bias_v = vecs[base + 3 : base + 4, :]
    arrived(weights, in_sem)
    outs = [fetch(weights.at[u], saved.at[pl.ds(WEIGHTS_AT + D * u, D)], out_sem.at[8 + u]) for u in range(4)]
    rel[...] = nn(table[...], weights[3]).astype(BF16)
    outs.append(fetch(rel, saved.at[pl.ds(REL_AT, ROWS)], out_sem.at[5]))
    for b in range(3):
        unit, unused = norm_parts(sources[b][...])
        normed[pl.ds(256 * b, 256), :] = (unit * gain).astype(BF16)
    outs.append(fetch(normed, saved.at[pl.ds(0, ROWS)], out_sem.at[0]))
    keys[...] = nn(normed[...], weights[1]).astype(BF16)
    outs.append(fetch(keys, saved.at[pl.ds(KEYS_AT, ROWS)], out_sem.at[3]))
    values[...] = nn(normed[...], weights[2]).astype(BF16)
    outs.append(fetch(values, saved.at[pl.ds(VALUES_AT, ROWS)], out_sem.at[4]))
    query = nn(normed[MEM:, :], weights[0])
    query_u[...] = (query + bias_u).astype(BF16)
    query_v[...] = (query + bias_v).astype(BF16)
    outs.append(fetch(query_u, saved.at[pl.ds(QUERY_U_AT, SEG)], out_sem.at[1]))
    outs.append(fetch(query_v, saved.at[pl.ds(QUERY_V_AT, SEG)], out_sem.at[2]))
    if first_layer:
        outs.append(small_out)
    for copy in outs:
        copy.wait()


def attend(scalars, query_u, query_v, keys, values, rel, attended, probs_o, probs, out_sem):
    length, segment = scalars[2], scalars[3]
    spot = lax.broadcasted_iota(jnp.int32, (1, ROWS), 1)
    where_at = segment * SEG + spot - MEM
    allowed = (where_at < length) & ((spot >= MEM) | (segment >= 1))
    bias = jnp.where(allowed, 0.0, NEG)
    triangle = tri_mask()

    def two_pairs(first, step, carry):
        tiles = [(2 * step + one, b, SPANS[b] - first) for one in range(2) for b in range(4)]
        full = [
            nt(stack_heads(query_v[BLOCK * b : BLOCK * (b + 1), lanes(pair)]) * SCALE,
               rel[ROWS - span : ROWS, lanes(pair)])
            for pair, b, span in tiles
        ]
        content = [
            nt(stack_heads(query_u[BLOCK * b : BLOCK * (b + 1), lanes(pair)]) * SCALE,
               keys[first : first + span, lanes(pair)])
            for pair, b, span in tiles
        ]
        full = [shift(item, span - BLOCK + 1) for item, (pair, b, span) in zip(full, tiles)]
        score = [
            masked(one + two + bias[:, first : first + span], triangle, span - BLOCK)
            for one, two, (pair, b, span) in zip(content, full, tiles)
        ]
        top = [jnp.max(item, -1, keepdims=True) for item in score]
        expo = [jnp.exp(item - most) for item, most in zip(score, top)]
        total = [jnp.sum(item, -1, keepdims=True) for item in expo]
        prob = [(item * (1.0 / most)).astype(BF16) for item, most in zip(expo, total)]
        for item, (pair, b, span) in zip(prob, tiles):
            probs[pair, :, STARTS[b] + first : STARTS[b] + first + span] = item
        for one in range(2):
            pair = 2 * step + one
            pltpu.make_async_copy(probs.at[pair], probs_o.at[pair], out_sem.at[pair]).start()
        found = [
            nn(item, values[first : first + span, lanes(pair)]) for item, (pair, b, span) in zip(prob, tiles)
        ]
        for item, (pair, b, span) in zip(found, tiles):
            attended[BLOCK * b : BLOCK * (b + 1), lanes(pair)] = pick_heads(item).astype(BF16)
        return carry

    for first in (0, MEM):

        @pl.when((segment == 0) == (first > 0))
        def _():
            lax.fori_loop(0, PAIRS // 2, functools.partial(two_pairs, first), 0)

    outs = [
        fetch(attended.at[pl.ds(256 * b, 256)], probs_o.at[PAIRS + b, :, pl.ds(0, D)], out_sem.at[PAIRS + b])
        for b in range(2)
    ]
    for pair in range(PAIRS):
        pltpu.make_async_copy(probs.at[pair], probs_o.at[pair], out_sem.at[pair]).wait()
    for copy in outs:
        copy.wait()


def attend_back(bits, second, *refs):
    (scalars, grad_att, table_h, saved, probs_h) = refs[:5]
    normed, table, late_sem = refs[-3:]
    rest = refs[5:-3]
    query_u_h, query_v_h, keys_h, values_h, rel_h = (
        saved.at[pl.ds(first, rows)]
        for first, rows in (
            (QUERY_U_AT, SEG), (QUERY_V_AT, SEG), (KEYS_AT, ROWS), (VALUES_AT, ROWS), (REL_AT, ROWS)
        )
    )
    if second:
        staged_h = rest[0]
        rest = rest[1:]
        (keep, send) = rest[4:6]
        sums, rest = rest[3], rest[:3] + rest[6:]
    else:
        (staged, sums) = rest[3:5]
        rest = rest[:3] + rest[5:]
    (grad_query, grad_keys, grad_values,
     query_u, query_v, keys, values, rel, probs, flip, acc_keys, acc_values, acc_rel,
     grad_qu, grad_qv, pair_sem) = rest[:16]
    first_pair = 2 if second else 0

    def parts(pair):
        lane, here = lanes(pair + first_pair), lanes(pair)
        moves = [(probs_h.at[pair + first_pair], probs.at[pair])]
        for there, target in (
            (query_u_h, query_u), (query_v_h, query_v), (keys_h, keys), (values_h, values), (rel_h, rel)
        ):
            moves.append((there.at[:, lane], target.at[:, here]))
        return [
            pltpu.make_async_copy(there, target, pair_sem.at[pair, index])
            for index, (there, target) in enumerate(moves)
        ]

    for pair in range(2):
        for copy in parts(pair):
            copy.start()
    late = [fetch(saved.at[pl.ds(0, ROWS)], normed, late_sem.at[0]), fetch(table_h, table, late_sem.at[1])]
    if second:
        staged, sem = rest[16:]
        staged[:, :, 0:256] = staged_h[...]
    row = lax.broadcasted_iota(jnp.int32, (2 * BLOCK, 2 * BLOCK), 0)
    col = lax.broadcasted_iota(jnp.int32, (2 * BLOCK, 2 * BLOCK), 1)
    back = (row // BLOCK) * BLOCK + BLOCK - 1 - lax.rem(row, BLOCK)
    flip[...] = (col == back).astype(F32).astype(BF16)

    segment = scalars[3]

    def one_pair(first, pair, carry):
        lane = lanes(pair)
        for copy in parts(pair):
            copy.wait()
        order = (3, 2, 1, 0)
        flipped = flip[...]
        stack_g = [
            stack_heads(grad_att[BLOCK * b : BLOCK * (b + 1), lanes(pair + first_pair)]) for b in order
        ]
        stack_u = [stack_heads(query_u[BLOCK * b : BLOCK * (b + 1), lane]) * SCALE for b in order]
        stack_v = [
            nn(flipped, stack_heads(query_v[BLOCK * b : BLOCK * (b + 1), lane]) * SCALE).astype(BF16)
            for b in order
        ]
        spans = [SPANS[b] - first for b in order]
        prob_b = [
            probs[pair, :, STARTS[b] + first : STARTS[b] + first + span] for b, span in zip(order, spans)
        ]
        grad_prob = [nt(one, values[first : first + span, lane]) for one, span in zip(stack_g, spans)]
        part_values = [tn(one, two) for one, two in zip(stack_g, prob_b)]
        prob = [item.astype(F32) for item in prob_b]
        inner = [jnp.sum(one * two, -1, keepdims=True) for one, two in zip(prob, grad_prob)]
        grad_score = [
            (one * (two - three)).astype(BF16) for one, two, three in zip(prob, grad_prob, inner)
        ]
        turned = [nn(flipped, item) for item in grad_score]
        found_u = [nn(item, keys[first : first + span, lane]) for item, span in zip(grad_score, spans)]
        part_keys = [tn(one, two) for one, two in zip(stack_u, grad_score)]
        grad_full = [shift(item, 0).astype(BF16) for item in turned]
        found_v = [nn(item, rel[ROWS - span : ROWS, lane]) for item, span in zip(grad_full, spans)]
        part_rel = [tn(one, two) for one, two in zip(stack_v, grad_full)]
        for index, b in enumerate(order):
            span = spans[index]
            rows = pl.ds(BLOCK * b, BLOCK)
            grad_qu[rows, lane] = pick_heads(found_u[index]) * SCALE
            grad_qv[rows, lane] = pick_heads(found_v[index]) * SCALE
            if b == 3:
                acc_keys[lane, first:] = part_keys[index]
                acc_values[lane, first:] = part_values[index]
                acc_rel[lane, ROWS - span :] = part_rel[index]
                if first:
                    blank = jnp.zeros((BLOCK, first), F32)
                    acc_keys[lane, 0:first] = blank
                    acc_values[lane, 0:first] = blank
                    acc_rel[lane, 0 : ROWS - span] = blank
            else:
                acc_keys[lane, first : first + span] += part_keys[index]
                acc_values[lane, first : first + span] += part_values[index]
                acc_rel[lane, ROWS - span : ROWS] += part_rel[index]
        return carry

    for first in (0, MEM):

        @pl.when((segment == 0) == (first > 0))
        def _():
            lax.fori_loop(0, 2, functools.partial(one_pair, first), 0)

    grad_keys[...] = jnp.transpose(acc_keys[...]).astype(BF16)
    grad_values[...] = jnp.transpose(acc_values[...]).astype(BF16)
    grad_rel = jnp.transpose(acc_rel[...]).astype(BF16)
    sums[...] = jnp.zeros_like(sums)
    sums[2:3, :] = jnp.sum(grad_qu[...], 0, keepdims=True)
    sums[3:4, :] = jnp.sum(grad_qv[...], 0, keepdims=True)
    flip_one = flip[0:BLOCK, 0:BLOCK]
    for b in range(4):
        rows = pl.ds(BLOCK * b, BLOCK)
        part = grad_qv[rows, :]
        high = part.astype(BF16)
        low = (part - high.astype(F32)).astype(BF16)
        grad_query[rows, :] = (grad_qu[rows, :] + nn(flip_one, high) + nn(flip_one, low)).astype(BF16)
    for copy in late:
        copy.wait()
    cols = slice(256, 512) if second else slice(None)
    staged[1, :, cols] = tn(normed[...], grad_keys[...]).astype(BF16)
    staged[2, :, cols] = tn(normed[...], grad_values[...]).astype(BF16)
    staged[3, :, cols] = tn(table[...], grad_rel).astype(BF16)
    staged[0, :, cols] = tn(normed[MEM:, :], grad_query[...]).astype(BF16)
    if second:
        place, half = scalars[0], scalars[1]
        units = [(staged.at[u], 16 * u) for u in range(4)]
        copies(bits, place, half, (keep,), units, 16, sem, True)
        copies(bits, place, 1 - half, (send,), units, 16, sem, True)
        arrived(staged, sem)


def input_grads(bits, base, *refs):
    last_kernel = base == 0
    weights, weights_sem = refs[-2:]
    refs = refs[:-2]
    weights_copies = [
        fetch(refs[1].at[pl.ds(WEIGHTS_AT + D * u, D)], weights.at[u], weights_sem.at[u]) for u in range(3)
    ]
    (scalars, saved, query_a, keys_a, values_a, sums_a, query_b, keys_b, values_b, sums_b, grad_mixed, vecs) = refs[:12]
    if last_kernel:
        (frames, gain_two, vecs_one, gain_two_one, gain_final, keep, send,
         joined, smalls, staged, sem, small, small_sem) = refs[12:]
        fetch(saved.at[pl.ds(SMALL_AT, D), pl.ds(0, BLOCK)], small, small_sem).wait()
        joined[...] = nt(frames[...], small[...])
        before, here, first = joined, joined, MEM
    else:
        (memory, hidden, grad_hidden, grad_vecs) = refs[12:]
        before, here, first = memory, hidden, 0
    place, half = scalars[0], scalars[1]
    gain = vecs[base : base + 1, :]
    left, right = slice(0, 256), slice(256, 512)
    for copy in weights_copies:
        copy.wait()
    grad_keys = (
        nt(keys_a[...], weights[1, :, left])
        + nt(keys_b[...], weights[1, :, right])
        + nt(values_a[...], weights[2, :, left])
        + nt(values_b[...], weights[2, :, right])
    )
    grad_query = nt(query_a[...], weights[0, :, left]) + nt(query_b[...], weights[0, :, right])
    unit, inverse = norm_parts(before[0:MEM, :])
    grad_gain = jnp.sum(grad_keys[0:MEM] * unit, 0, keepdims=True)
    unit, inverse = norm_parts(here[first : first + SEG, :])
    grad_joined, gains = norm_back(unit, inverse, gain, grad_keys[MEM:] + grad_query)
    grad_gain = grad_gain + gains
    grad_in = grad_mixed[...] + grad_joined
    if last_kernel:
        smalls[...] = tn(frames[MEM:, :], grad_in.astype(BF16))
        smalls[80:81, :] = grad_gain
        smalls[81:82, :] = gain_two[0:1, :]
        smalls[82:84, left] = sums_a[2:4, :]
        smalls[82:84, right] = sums_b[2:4, :]
        smalls[84:88, :] = vecs_one[0:4, :]
        smalls[85:86, :] = gain_two_one[0:1, :]
        smalls[88:89, :] = gain_final[0:1, :]
        staged[...] = jnp.zeros_like(staged)
        staged[:, 0:BLOCK] = jnp.transpose(smalls[...]).astype(BF16)
        units = [(staged, 0)]
        copies(bits, place, half, (keep,), units, 16, sem, True)
        copies(bits, place, 1 - half, (send,), units, 16, sem, True)
        arrived(staged, sem)
    else:
        grad_hidden[...] = grad_in
        grad_vecs[:, left] = sums_a[...]
        grad_vecs[:, right] = sums_b[...]
        grad_vecs[0:1, :] = grad_gain


def feed_weights(bits, place, both, up, down, out, sem):
    for index, (units, rows) in enumerate(
        (
            ([(out, 128)], 16),
            ([(item, 16 * u) for u, item in enumerate(columns(up, 4))], 16),
            ([(down, 64)], 64),
        )
    ):
        for which, pieces in both:
            copies(bits, place, which, pieces, units, rows, sem.at[index], False)


def feed_mixed(residual, attended, out, gain, mixed, normed):
    mixed[...] = residual[...] + nn(attended[...], out[...])
    for b in range(2):
        rows = pl.ds(256 * b, 256)
        unit, unused = norm_parts(mixed[rows, :])
        normed[rows, :] = (unit * gain).astype(BF16)


def feed_inner(normed, up, active, slope):
    later = nn(normed[...], up[:, 0:512])
    for u in range(4):
        inner = later
        if u < 3:
            later = nn(normed[...], up[:, 512 * (u + 1) : 512 * (u + 2)])
        square = inner * inner
        bent = jnp.tanh(0.7978845608028654 * (inner + 0.044715 * (square * inner)))
        half = 0.5 * (1.0 + bent)
        active[:, 512 * u : 512 * (u + 1)] = (inner * half).astype(BF16)
        slope[:, 512 * u : 512 * (u + 1)] = (
            half
            + (0.5 * inner)
            * (1.0 - bent * bent)
            * (0.7978845608028654 * (1.0 + (3 * 0.044715) * square))
        ).astype(BF16)


def feed_output(mixed, active, down, output):
    output[...] = mixed[...] + nn(active[...], down[...])


def feed_forward(bits, base, scalars, residual, attended, vecs, own_low, own_high, other_low, other_high,
                 output, memory, mixed_o, saved,
                 mixed, normed, active, slope, up, down, out, sem, out_sem):
    place, half = scalars[0], scalars[1]
    both = ((half, (own_low, own_high)), (1 - half, (other_low, other_high)))
    feed_weights(bits, place, both, up, down, out, sem)
    arrived(out, sem.at[0])
    outs = [fetch(out, saved.at[pl.ds(OUT_AT, D)], out_sem.at[0])]
    feed_mixed(residual, attended, out, vecs[base + 1 : base + 2, :], mixed, normed)
    outs.append(fetch(normed, saved.at[pl.ds(0, SEG)], out_sem.at[1]))
    outs.append(fetch(mixed, mixed_o, out_sem.at[2]))
    arrived(up, sem.at[1])
    outs += [
        fetch(item, saved.at[pl.ds(UP_AT + D * u, D)], out_sem.at[4 + u])
        for u, item in enumerate(columns(up, 4))
    ]
    feed_inner(normed, up, active, slope)
    for u in range(4):
        cols = pl.ds(D * u, D)
        outs.append(fetch(active.at[:, cols], saved.at[pl.ds(ACTIVE_AT + D * u, D)], out_sem.at[8 + u]))
        outs.append(fetch(slope.at[:, cols], saved.at[pl.ds(SLOPE_AT + D * u, D)], out_sem.at[12 + u]))
    arrived(down, sem.at[2])
    outs.append(fetch(down, saved.at[pl.ds(DOWN_AT, FF)], out_sem.at[3]))
    feed_output(mixed, active, down, output)
    memory[...] = output[SEG - MEM :, :]
    for copy in outs:
        copy.wait()


def feed_back(moves, bits, place, half, keep, send, sem, base, grad_out, mixed, vecs, attended, normed,
              active, slope, up, down, out, grad_mixed, grad_att, grad_gain,
              grad_inner, staged_up, staged_down, staged_out):
    both = ((half, (keep,)), (1 - half, (send,)))
    grad_y = grad_out[...].astype(BF16)
    for copy in moves[:1]:
        copy.wait()
    later = nt(grad_y, down[0:512, :])
    for copy in moves[1:10]:
        copy.wait()
    for u in range(4):
        cols = slice(512 * u, 512 * (u + 1))
        part = later
        if u < 3:
            later = nt(grad_y, down[512 * (u + 1) : 512 * (u + 2), :])
        staged_down[cols, :] = tn(active[:, cols], grad_y).astype(BF16)
        grad_inner[:, cols] = (part * slope[:, cols].astype(F32)).astype(BF16)
    for copy in moves[10:]:
        copy.wait()
    grad_normed = nt(grad_inner[...], up[...])
    for which, pieces in both:
        copies(bits, place, which, pieces, [(staged_down, 64)], 64, sem.at[1], True)
    for u in range(4):
        cols = slice(512 * u, 512 * (u + 1))
        staged_up[:, cols] = tn(normed[...], grad_inner[:, cols]).astype(BF16)
    unit, inverse = norm_parts(mixed[...])
    grad_here, gains = norm_back(unit, inverse, vecs[base + 1 : base + 2, :], grad_normed)
    grad = grad_out[...] + grad_here
    grad_mixed[...] = grad
    grad_b = grad.astype(BF16)
    for which, pieces in both:
        units = [(item, 16 * u) for u, item in enumerate(columns(staged_up, 4))]
        copies(bits, place, which, pieces, units, 16, sem.at[0], True)
    grad_att[...] = nt(grad_b, out[...]).astype(BF16)
    staged_out[...] = tn(attended[...], grad_b).astype(BF16)
    for which, pieces in both:
        copies(bits, place, which, pieces, [(staged_out, 128)], 16, sem.at[2], True)
    grad_gain[...] = jnp.broadcast_to(gains, grad_gain.shape)
    arrived(staged_up, sem.at[0])
    arrived(staged_down, sem.at[1])
    arrived(staged_out, sem.at[2])


def feed_backward(bits, base, scalars, grad_out, vecs, mixed_h, probs_h, saved,
                  keep, send, grad_mixed, grad_att, grad_gain, mixed, attended,
                  normed, active, slope, up, down, out, grad_inner, staged_up, staged_down, staged_out,
                  in_sem, sem):
    pairs = [(saved.at[pl.ds(DOWN_AT, FF)], down)]
    for u in range(4):
        pairs.append((saved.at[pl.ds(SLOPE_AT + D * u, D)], slope.at[:, pl.ds(D * u, D)]))
    for u in range(4):
        pairs.append((saved.at[pl.ds(ACTIVE_AT + D * u, D)], active.at[:, pl.ds(D * u, D)]))
    pairs.append((saved.at[pl.ds(0, SEG)], normed))
    for u in range(4):
        pairs.append((saved.at[pl.ds(UP_AT + D * u, D)], columns(up, 4)[u]))
    pairs.append((saved.at[pl.ds(OUT_AT, D)], out))
    pairs.append((mixed_h, mixed))
    for b in range(2):
        pairs.append((probs_h.at[PAIRS + b, :, pl.ds(0, D)], attended.at[pl.ds(256 * b, 256)]))
    moves = [fetch(there, here, in_sem.at[index]) for index, (there, here) in enumerate(pairs)]
    feed_back(moves, bits, scalars[0], scalars[1], keep, send, sem, base, grad_out, mixed, vecs, attended, normed,
              active, slope, up, down, out, grad_mixed, grad_att, grad_gain,
              grad_inner, staged_up, staged_down, staged_out)


def top_kernel(bits, streams, scalars, residual, attended, targets, vecs, own_low, own_high, other_low, other_high,
               keep, send, grad_mixed, grad_att, grad_gain, final_gain, loss,
               normed, active, slope, up, down, out, mixed, output, grad_out, table, final, grad_logits, staged,
               grad_inner, staged_up, staged_down, staged_out, head_sem, sem, out_sem):
    place, half, length, segment = scalars[0], scalars[1], scalars[2], scalars[3]
    both = ((half, (own_low, own_high)), (1 - half, (other_low, other_high)))
    feed_weights(bits, place, both, up, down, out, sem)
    units = [(item, 144 + 16 * u) for u, item in enumerate(columns(table, 2))]
    for which, pieces in both:
        copies(bits, place, which, pieces, units, 16, head_sem, False)
    arrived(out, sem.at[0])
    feed_mixed(residual, attended, out, vecs[5:6, :], mixed, normed)
    arrived(up, sem.at[1])
    feed_inner(normed, up, active, slope)
    arrived(down, sem.at[2])
    feed_output(mixed, active, down, output)
    arrived(table, head_sem)
    size = length.astype(F32)
    codes = jnp.transpose(jnp.broadcast_to(targets[...].astype(F32), (BLOCK, SEG))).astype(jnp.int32)
    gain = vecs[8:9, :]
    gains = jnp.zeros((1, D), F32)
    terms = jnp.zeros((1, 1), F32)
    spans = (slice(0, 256), slice(256, 512))
    parts = [norm_parts(output[rows, :]) for rows in spans]
    fins = [(unit * gain).astype(BF16) for unit, unused in parts]
    logits = [nn(fin, table[...]) for fin in fins]
    for rows, fin in zip(spans, fins):
        final[rows, :] = fin
    grad_finals = []
    for b, rows in enumerate(spans):
        logit = logits[b]
        most = jnp.max(logit, -1, keepdims=True)
        expo = jnp.exp(logit - most)
        total = jnp.sum(expo, -1, keepdims=True)
        picks = lax.broadcasted_iota(jnp.int32, logit.shape, 1) == codes[rows, 0:1]
        picked = jnp.sum(jnp.where(picks, logit, 0.0), -1, keepdims=True)
        spot = segment * SEG + 256 * b + lax.broadcasted_iota(jnp.int32, (256, 1), 0)
        weight = jnp.where(spot < length, 1.0 / size, 0.0)
        terms = terms + jnp.sum((most + jnp.log(total) - picked) * weight, keepdims=True)
        grad = (expo * (1.0 / total) - jnp.where(picks, 1.0, 0.0)) * (weight * (1.0 / streams))
        grad_logits[rows, :] = grad.astype(BF16)
        grad_finals.append(nt(grad_logits[rows, :], table[...]))
    staged[...] = tn(final[...], grad_logits[...]).astype(BF16)
    for (unit, inverse), rows, grad_final in zip(parts, spans, grad_finals):
        grad_here, gain_here = norm_back(unit, inverse, gain, grad_final)
        grad_out[rows, :] = grad_here
        gains = gains + gain_here
    units = [(item, 144 + 16 * u) for u, item in enumerate(columns(staged, 2))]
    copies(bits, place, half, (keep,), units, 16, head_sem, True)
    copies(bits, place, 1 - half, (send,), units, 16, head_sem, True)
    final_gain[...] = jnp.broadcast_to(gains, final_gain.shape)
    loss[...] = jnp.broadcast_to(terms, loss.shape)
    feed_back((), bits, place, half, keep, send, out_sem, 4, grad_out, mixed, vecs, attended, normed,
              active, slope, up, down, out, grad_mixed, grad_att, grad_gain,
              grad_inner, staged_up, staged_down, staged_out)
    arrived(staged, head_sem)


def finish(counts, *refs):
    scalars, loss = refs[0], refs[1]
    total_count = sum(counts)
    sources = refs[2 : 2 + total_count]
    kept, sent, total = refs[2 + total_count : 5 + total_count]
    buffers, sem = refs[5 + total_count : -1], refs[-1]
    moves = [fetch(there.at[0], here, sem.at[index]) for index, (there, here) in enumerate(zip(sources, buffers))]
    for copy in moves:
        copy.wait()
    sums = []
    start = 0
    for count in counts:
        item = buffers[start][...].astype(F32)
        for other in buffers[start + 1 : start + count]:
            item = item + other[...].astype(F32)
        sums.append(item)
        start += count
    attn_zero, feed_zero, attn_one, feed_one, small = sums[0], sums[1], sums[2], sums[3], sums[4]
    attn_zero = attn_zero + sums[5][0:64]
    small = small + sums[5][64:80]
    first = scalars[1] == 0
    lone = jnp.zeros((1, 1), F32)
    for zero, one, rows, begin in ((attn_zero, attn_one, 64, 0), (feed_zero, feed_one[0:144], 144, 64)):
        kept[begin : begin + rows, :] = jnp.where(first, zero, one)
        sent[begin : begin + rows, :] = jnp.where(first, one, zero)
        lone = lone + jnp.sum(zero * zero + one * one, keepdims=True)
    head = feed_one[144:176]
    lone = lone + jnp.sum(head * head, keepdims=True) + jnp.sum(small * small, keepdims=True)
    for target in (kept, sent):
        target[208:240, :] = head
        target[240:256, :] = small
    column = lax.broadcasted_iota(jnp.int32, (8, 128), 1)
    total[...] = jnp.where(column == 0, lone, 0.0) + jnp.where(column == 1, loss[...], 0.0)


def adam_step(weight, grad, first, second, rate, decay, factor):
    grad = grad * factor
    first = 0.9 * first + 0.1 * grad
    second = 0.999 * second + 0.001 * grad * grad
    ratio = first / (1.0 - 0.9**STEP) / (jnp.sqrt(second / (1.0 - 0.999**STEP)) + 1e-08)
    return (weight - rate * (ratio + decay * weight), first, second)


def update(scalars, total, kept, got, *refs):
    ins, outs, small = refs[:27], refs[27:56], refs[56]
    first = scalars[1] == 0
    squares = jnp.sum(total[0:1, 0:1], keepdims=True)
    norm = jnp.sqrt(squares)
    outs[27][...] = norm
    outs[28][...] = total[0:1, 1:2]
    factor = jnp.minimum(1.0, CLIP / (norm + 1e-06))

    def half_of(half, start, rows):
        here, there = kept[start : start + rows, :], got[start : start + rows, :]
        return jnp.where(first == (half == 0), here, there)

    def apply(index, spot, grad, rate, decay):
        results = adam_step(
            ins[index][spot], grad, ins[9 + index][spot], ins[18 + index][spot], rate, decay, factor
        )
        for which, result in enumerate(results):
            outs[9 * which + index][spot] = result

    for half in range(2):
        rows = slice(16 * half, 16 * half + 16)
        for u in range(3):
            apply(0, (0, rows, slice(D * u, D * (u + 1))), half_of(half, 16 * u, 16), 0.03, 0.01)
        apply(1, (0, rows, slice(None)), half_of(half, 192, 16), 0.03, 0.01)
        apply(2, (0, rows, slice(None)), half_of(half, 48, 16), 0.03, 0.01)
        for u in range(4):
            apply(3, (0, rows, slice(D * u, D * (u + 1))), half_of(half, 64 + 16 * u, 16), 0.03, 0.01)
        apply(4, (0, slice(64 * half, 64 * half + 64), slice(None)), half_of(half, 128, 64), 0.03, 0.01)
        for u in range(2):
            apply(7, (rows, slice(D * u, D * (u + 1))), half_of(half, 208 + 16 * u, 16), 0.03, 0.01)
        small[rows, :] = half_of(half, 240, 16)[:, 0:BLOCK]
    small[32:, :] = jnp.zeros((BLOCK - 32, BLOCK), F32)
    turned = jnp.transpose(small[...])
    apply(6, (slice(None), slice(None)), small[0:32, 0:FEATS], 0.03, 0.01)
    vecs = jnp.where(first, turned[80:84, 0:32], turned[84:88, 0:32])
    apply(5, (0, slice(None), slice(None)), vecs, 0.3, 0.0)
    apply(8, (slice(None), slice(None)), turned[88:89, 0:32], 0.3, 0.0)


def pack_shards(scalars, attn, out, pos, up, down, vecs, w_in, head, gain, kept, sent, codes, small):
    half, section = scalars[1], scalars[3]
    small[...] = jnp.zeros_like(small)
    small[88:89, 0:32] = gain[...]
    small[pl.ds(FEATS + 4 * section, 4), 0:32] = vecs[0]
    turned = jnp.transpose(small[...])[0:32]
    turned = jnp.concatenate([w_in[...], turned[:, FEATS:]], 1)
    column = lax.broadcasted_iota(jnp.int32, turned.shape, 1)
    shared = (column < FEATS) | (column == 88)
    for which, target in ((half, kept), (1 - half, sent)):
        rows = pl.ds(pl.multiple_of(16 * which, 16), 16)
        for u in range(3):
            target[16 * u : 16 * u + 16, :] = attn[0, rows, D * u : D * (u + 1)].astype(BF16)
        target[48:64, :] = pos[0, rows, :].astype(BF16)
        for u in range(4):
            target[80 + 16 * u : 96 + 16 * u, :] = up[0, rows, D * u : D * (u + 1)].astype(BF16)
        target[144:208, :] = down[0, pl.ds(pl.multiple_of(64 * which, 64), 64), :].astype(BF16)
        target[208:224, :] = out[0, rows, :].astype(BF16)
        tail = jnp.where(half == 0, turned[0:16], turned[16:32])
        if target is sent:
            tail = jnp.where(half == 0, turned[16:32], turned[0:16])
            tail = jnp.where(shared[0:16], 0.0, tail)
        target[64:80, :] = jnp.zeros((16, D), BF16)
        target[64:80, 0:BLOCK] = tail.astype(BF16)
    rows = pl.ds(pl.multiple_of(16 * half, 16), 16)
    for u in range(2):
        codes[16 * u : 16 * u + 16, :] = head[rows, D * u : D * (u + 1)].astype(BF16)


VMEM = pl.BlockSpec(memory_space=pltpu.VMEM)
ANY = pl.BlockSpec(memory_space=pl.ANY)
HBM = pl.BlockSpec(memory_space=pltpu.HBM)
SMEM = pl.BlockSpec(memory_space=pltpu.SMEM)
DMA = pltpu.SemaphoreType.DMA


def shape(*dims, dtype=F32):
    return jax.ShapeDtypeStruct(dims, dtype)


def half_shape(*dims):
    return jax.ShapeDtypeStruct(dims, BF16)


def held(*dims):
    return pltpu.VMEM(dims, BF16)


def wide(*dims):
    return pltpu.VMEM(dims, F32)


def call(body, name, ins, outs, out_specs, scratch, micros, limit):
    return pl.pallas_call(
        body,
        name=name,
        in_specs=ins,
        out_shape=outs,
        out_specs=out_specs,
        scratch_shapes=scratch,
        compiler_params=pltpu.CompilerParams(vmem_limit_bytes=limit * 1024 * 1024),
        cost_estimate=pl.CostEstimate(flops=micros * 1_150_000_000, bytes_accessed=1 << 20, transcendentals=0),
    )


QUERY_KEY = (half_shape(SEG, D), half_shape(SEG, D), half_shape(ROWS, D), half_shape(ROWS, D), half_shape(ROWS, D))
PROJECT_HELD = [held(ROWS, D), held(4, D, D), DMA, DMA((12,))]
KEPT = half_shape(KEPT_ROWS, D)


def run_project_first(bits, scalars, frames, pieces, table):
    result = call(
        functools.partial(project, bits, 0),
        "project_first",
        [SMEM, VMEM, HBM, HBM, HBM, HBM, VMEM],
        QUERY_KEY + (shape(SEG, D), shape(16, D), KEPT),
        [VMEM] * 7 + [HBM],
        PROJECT_HELD + [wide(ROWS, D), held(D, BLOCK), DMA],
        6,
        40,
    )(scalars, frames, *pieces, table)
    return result[:5], result[5], result[6], result[7]


def run_project(bits, scalars, memory, hidden, vecs, pieces, table):
    result = call(
        functools.partial(project, bits, 4),
        "project",
        [SMEM, VMEM, VMEM, VMEM, HBM, HBM, HBM, HBM, VMEM],
        QUERY_KEY + (KEPT,),
        [VMEM] * 5 + [HBM],
        PROJECT_HELD,
        6,
        40,
    )(scalars, memory, hidden, vecs, *pieces, table)
    return result[:5], result[5]


def run_attend(scalars, projected):
    return call(
        attend,
        "attend",
        [SMEM] + [VMEM] * 5,
        (half_shape(SEG, D), half_shape(KEPT_PAIRS, 2 * BLOCK, WIDE)),
        [VMEM, HBM],
        [held(PAIRS, 2 * BLOCK, WIDE), DMA((PAIRS + 2,))],
        11,
        44,
    )(scalars, *projected)


HALF_HELD = [
    held(SEG, 256), held(SEG, 256), held(ROWS, 256), held(ROWS, 256), held(ROWS, 256),
    held(2, 2 * BLOCK, WIDE), held(2 * BLOCK, 2 * BLOCK),
    wide(256, ROWS), wide(256, ROWS), wide(256, ROWS), wide(SEG, 256), wide(SEG, 256), DMA((2, 6)),
]
LATE_HELD = [held(ROWS, D), held(ROWS, D), DMA((2,))]
HALF_OUT = (half_shape(SEG, 256), half_shape(ROWS, 256), half_shape(ROWS, 256))


def run_attend_back(bits, scalars, grad_att, saved, table, probs):
    result = call(
        functools.partial(attend_back, bits, False),
        "attend_back",
        [SMEM, VMEM] + [HBM] * 3,
        HALF_OUT + (half_shape(4, D, 256), shape(8, 256)),
        [VMEM] * 5,
        HALF_HELD + LATE_HELD,
        9,
        40,
    )(scalars, grad_att, table, saved, probs)
    return (*result[:3], result[4]), result[3]


def run_attend_back_rest(bits, scalars, grad_att, saved, table, probs, staged):
    result = call(
        functools.partial(attend_back, bits, True),
        "attend_back_rest",
        [SMEM, VMEM] + [HBM] * 3 + [VMEM],
        HALF_OUT + (shape(8, 256), half_shape(GROUPS, 64, D), half_shape(GROUPS, 64, D)),
        [VMEM] * 4 + [ANY] * 2,
        HALF_HELD + [held(4, D, D), DMA] + LATE_HELD,
        10,
        42,
    )(scalars, grad_att, table, saved, probs, staged)
    return result[:4], result[4], result[5]


def run_input_grads(bits, scalars, saved, grads, grad_mixed, vecs, memory, hidden):
    return call(
        functools.partial(input_grads, bits, 4),
        "input_grads",
        [SMEM, HBM] + [VMEM] * 12,
        (shape(SEG, D), shape(8, D)),
        [VMEM] * 2,
        [held(4, D, D), DMA((3,))],
        5,
        50,
    )(scalars, saved, *grads, grad_mixed, vecs, memory, hidden)


def run_input_grads_last(bits, scalars, saved, grads, grad_mixed, vecs, frames, *small_grads):
    return call(
        functools.partial(input_grads, bits, 0),
        "input_grads_last",
        [SMEM, HBM] + [VMEM] * 15,
        (half_shape(GROUPS, 16, D), half_shape(GROUPS, 16, D)),
        [ANY] * 2,
        [wide(ROWS, D), wide(BLOCK, D), held(D, D), DMA, held(D, BLOCK), DMA, held(4, D, D), DMA((3,))],
        5,
        50,
    )(scalars, saved, *grads, grad_mixed, vecs, frames, *small_grads)


FEED_HELD = [held(SEG, D), held(SEG, FF), held(SEG, FF), held(D, FF), held(FF, D), held(D, D)]
BACK_HELD = [held(SEG, FF), held(D, FF), held(FF, D), held(D, D)]


def run_feed_forward(bits, base, scalars, residual, attended, vecs, pieces):
    result = call(
        functools.partial(feed_forward, bits, base),
        "feed_forward",
        [SMEM, VMEM, VMEM, VMEM, HBM, HBM, HBM, HBM],
        (shape(SEG, D), shape(MEM, D), shape(SEG, D), KEPT),
        [VMEM] * 2 + [HBM] * 2,
        [wide(SEG, D)] + FEED_HELD + [DMA((3,)), DMA((16,))],
        9,
        50,
    )(scalars, residual, attended, vecs, *pieces)
    return result


def run_feed_backward(bits, base, scalars, grad_out, vecs, mixed, probs, saved):
    return call(
        functools.partial(feed_backward, bits, base),
        "feed_backward",
        [SMEM, VMEM, VMEM] + [HBM] * 3,
        (half_shape(GROUPS, 144, D), half_shape(GROUPS, 144, D), shape(SEG, D), half_shape(SEG, D), shape(8, D)),
        [ANY, ANY, VMEM, VMEM, VMEM],
        [wide(SEG, D), held(SEG, D)] + FEED_HELD + BACK_HELD + [DMA((18,)), DMA((3,))],
        13,
        50,
    )(scalars, grad_out, vecs, mixed, probs, saved)


def run_top(bits, streams, scalars, residual, attended, targets, vecs, pieces):
    return call(
        functools.partial(top_kernel, bits, streams),
        "top_kernel",
        [SMEM, VMEM, VMEM, VMEM, VMEM, HBM, HBM, HBM, HBM],
        (
            half_shape(GROUPS, 176, D), half_shape(GROUPS, 176, D),
            shape(SEG, D), half_shape(SEG, D), shape(8, D), shape(8, D), shape(8, 128),
        ),
        [ANY] * 2 + [VMEM] * 5,
        FEED_HELD
        + [wide(SEG, D), wide(SEG, D), wide(SEG, D), held(D, CODES), held(SEG, D), held(SEG, CODES), held(D, CODES)]
        + BACK_HELD
        + [DMA, DMA((3,)), DMA((3,))],
        21,
        56,
    )(scalars, residual, attended, targets, vecs, *pieces)


def run_finish(scalars, loss, *sums):
    counts = tuple((len(item) for item in sums))
    flat = [item for group in sums for item in group]
    return call(
        functools.partial(finish, counts),
        "finish",
        [SMEM, VMEM] + [ANY] * len(flat),
        (shape(256, D), shape(256, D), shape(8, 128)),
        [VMEM] * 3,
        [pltpu.VMEM(item.shape[1:], item.dtype) for item in flat] + [DMA((len(flat),))],
        3,
        56,
    )(scalars, loss, *flat)


def run_update(scalars, total, kept, got, state):
    flat = [item[None] if item.ndim == 1 else item for item in state]
    for index in (6, 15, 24):
        flat[index] = jnp.transpose(flat[index])
    result = call(
        update,
        "update",
        [SMEM] + [VMEM] * 30,
        tuple((shape(*item.shape) for item in flat)) + (shape(1, 1), shape(1, 1)),
        [VMEM] * 29,
        [wide(BLOCK, BLOCK)],
        5,
        24,
    )(scalars, total, kept, got, *flat)
    result = list(result)
    for index in (6, 15, 24):
        result[index] = jnp.transpose(result[index])
    return [item.reshape(old.shape) for item, old in zip(result, state)] + [result[27][0, 0], result[28][0, 0]]


def run_pack(scalars, w_attn, w_out, w_pos, w_up, w_down, layer_vecs, w_in, w_head, gain_final):
    return call(
        pack_shards,
        "pack_shards",
        [SMEM] + [VMEM] * 9,
        (half_shape(224, D), half_shape(224, D), half_shape(32, D)),
        [VMEM] * 3,
        [wide(BLOCK, BLOCK)],
        3,
        56,
    )(scalars, w_attn, w_out, w_pos, w_up, w_down, layer_vecs, jnp.transpose(w_in), w_head, gain_final[None])


def spread(value, bits):
    count = lax.axis_size("dp")
    pairs = [
        (half * count + i, half * count + (i ^ bit)) for half, bit in enumerate(bits) for i in range(count)
    ]
    return lax.ppermute(value, ("section", "dp"), pairs)


def swap(value):
    return lax.ppermute(value, "section", [(0, 1), (1, 0)])


def fence(*values):
    return lax.optimization_barrier(values)


def joined(low, got):
    return jnp.concatenate([low, got], 0)


def part(sources, first, last):
    total = sources[0][first:last].astype(F32)
    for item in sources[1:]:
        total = total + item[first:last].astype(F32)
    return total


def shrink(chunks, pair, merged=()):
    count = (merged or chunks[0])[-1].shape[0]
    sent, first = [], 0
    for item in chunks:
        rows = item[0].shape[1]
        total = part(item, count // 2, count)
        if merged:
            total = total + part([other[:, first : first + rows] for other in merged], count // 2, count)
        sent.append(total.astype(BF16))
        first += rows
    return spread(jnp.concatenate(sent, 1), pair)


def add_up(value, bits):
    value = value + swap(value)
    steps = [low for low, unused in zip(*bits)]
    for one, two in zip(steps[0::2], steps[1::2]):
        first, second, third = (spread(value, (step, step)) for step in (one, two, one + two))
        value = (value + first) + (second + third)
    return value


def lanes_of(block):
    return [block[:, D * u : D * (u + 1)] for u in range(block.shape[1] // D)]


def sinus_table(where_at):
    freqs = jnp.exp(-jnp.log(10000.0) * (2.0 * jnp.arange(D // 2, dtype=jnp.int32).astype(F32) / D))
    angles = where_at * freqs[None, :]
    return jnp.concatenate([jnp.sin(angles), jnp.cos(angles)], 1).astype(BF16)


def split_shards(section, scalars, params):
    kept, sent, head = run_pack(scalars, *params)
    got = swap(sent)
    first = section == 0
    row = lax.broadcasted_iota(jnp.int32, (80, D), 0)
    attn = jnp.where(row < 64, jnp.where(first, kept[:80], got[:80]), kept[:80] + got[:80])
    zero = jnp.where(first, kept[80:], got[80:])
    one = jnp.where(first, got, kept)
    return attn, zero, one[:64], jnp.concatenate([one[80:], head], 0)


def halves(whole, rows):
    return whole.reshape(GROUPS, 2, rows, whole.shape[1]).transpose(1, 0, 2, 3)


def gather_whole(section, w_attn, w_out, w_pos, w_up, w_down, layer_vecs, w_in, w_head, gain_final):
    def over(value, axis):
        return lax.all_gather(value.astype(BF16), "dp", axis=axis, tiled=True)

    def layers(value):
        return lax.all_gather(over(value[0], 0), "section", axis=0)

    attn, out, pos, up, down = (layers(item) for item in (w_attn, w_out, w_pos, w_up, w_down))
    vecs = lax.all_gather(over(layer_vecs[0], 1), "section", axis=0)
    small = jnp.concatenate(
        [over(w_in, 1), vecs[0], vecs[1], over(gain_final, 0)[None], jnp.zeros((BLOCK - 89, D), BF16)], 0
    )
    small = jnp.pad(jnp.transpose(small), ((0, 0), (0, D - BLOCK)))
    head = over(w_head, 0)

    def pieces(units):
        both = jnp.concatenate([halves(item, item.shape[0] // 32) for item in units], 2)
        own = lax.dynamic_index_in_dim(both, section, 0, keepdims=False)
        other = lax.dynamic_index_in_dim(both, 1 - section, 0, keepdims=False)
        return (own[:8], own[8:], other[:8], other[8:])

    return (
        pieces(lanes_of(attn[0]) + [pos[0], small]),
        pieces(lanes_of(up[0]) + [down[0], out[0]]),
        pieces(lanes_of(attn[1]) + [pos[1]]),
        pieces(lanes_of(up[1]) + [down[1], out[1]] + lanes_of(head)),
    )


def whole_grads(section, sums):
    count = lax.axis_size("dp")
    place = lax.axis_index("dp")
    attn_zero, feed_zero, attn_one, feed_one, small = (
        lax.all_gather(lax.psum(item, "dp"), "section", axis=0) for item in sums
    )

    def unit(both, start, rows):
        item = both[:, :, start : start + rows]
        return item.transpose(1, 0, 2, 3).reshape(GROUPS * 2 * rows, both.shape[3])

    def layer(attn, feed):
        return (
            jnp.concatenate([unit(attn, 16 * u, 16) for u in range(3)], 1),
            unit(feed, 128, 16),
            unit(attn, 48, 16),
            jnp.concatenate([unit(feed, 16 * u, 16) for u in range(4)], 1),
            unit(feed, 64, 64),
        )

    small = jnp.transpose(unit(small, 0, 16))
    zero = layer(attn_zero, feed_zero) + (small[80:84],)
    one = layer(attn_one, feed_one) + (small[84:88],)
    ends = (small[:80], jnp.concatenate([unit(feed_one, 144 + 16 * u, 16) for u in range(2)], 1), small[88])
    squares = sum((jnp.sum(item * item) for item in zero + one + ends))
    dims = (0, 0, 0, 0, 0, 1, 1, 0, 0)
    grads = tuple((jnp.where(section == 0, a, b) for a, b in zip(zero, one))) + ends
    return squares, tuple(
        (
            lax.dynamic_slice_in_dim(item, place * (item.shape[dim] // count), item.shape[dim] // count, dim)
            for item, dim in zip(grads, dims)
        )
    )


def local(frames, targets, lengths, *state):
    params, firsts, seconds = (state[:9], state[9:18], state[18:])
    section = lax.axis_index("section")
    streams = lax.axis_size("dp")
    ringed = streams == GROUPS
    place = lax.axis_index("dp") if ringed else jnp.int32(0)
    length = lengths[0]
    scalars = jnp.stack([place, section, length, section]).astype(jnp.int32)
    count_down = (ROWS - 1 - jnp.arange(ROWS, dtype=jnp.int32)).astype(F32)[:, None]
    rows = lax.dynamic_slice_in_dim(
        jnp.pad(frames[0], ((MEM, 0), (0, BLOCK - FEATS))), section * SEG, ROWS, 0
    )
    codes = lax.dynamic_slice_in_dim(targets, section * SEG, SEG, 1)
    if ringed:
        bits = ((8, 4, 1, 2), (8, 4, 2, 1))
        far, near, side, last = zip(*bits)
        zero, one, two, three = (item[None] for item in split_shards(section, scalars, params))
        zero, got, count_down = fence(zero, spread(zero, far), count_down)
        table = sinus_table(count_down)
        zero = joined(zero, got)
        zero, got, one = fence(zero, spread(zero, near), one)
        zero = joined(zero, got)
        one_got = spread(one, far)
        zero, got, two, one, one_got, rows, table, codes = fence(
            zero, spread(zero, side), two, one, one_got, rows, table, codes
        )
        zero = joined(zero, got)
        high = spread(zero, last)
        one = joined(one, one_got)
        one_got, two_got = spread(one, near), spread(two, far)
        zero, high, one, one_got, two, two_got = fence(zero, high, one, one_got, two, two_got)
        one, two = joined(one, one_got), joined(two, two_got)
        one_got, two_got = spread(one, side), spread(two, near)
        swapped, high_swapped = swap(zero), swap(high)
        swapped, high_swapped, one, one_got, two, two_got, three = fence(
            swapped, high_swapped, one, one_got, two, two_got, three
        )
        chunk = (zero, high, swapped, high_swapped)
        one, two = joined(one, one_got), joined(two, two_got)
        one_got, two_got, three_got, swapped = spread(one, last), spread(two, side), spread(three, far), swap(one)
    else:
        bits = IN_ORDER
        table = sinus_table(count_down)
        chunk, chunk_one, chunk_two, chunk_three = gather_whole(section, *params)

    projected, hidden_zero, vecs, saved_zero = run_project_first(bits, scalars, rows, chunk, table)
    if ringed:
        projected, two_got, three_got, swapped = fence(projected, two_got, three_got, swapped)
        two, three = joined(two, two_got), joined(three, three_got)
        two_got, three_got, two_swapped = spread(two, last), spread(three, near), swap(two)
    attended, probs_zero = run_attend(scalars, projected)
    if ringed:
        attended, one_got, two_got, three_got, two_swapped = fence(
            attended, one_got, two_got, three_got, two_swapped
        )
        chunk = (one, one_got, swapped, swap(one_got))
        two_chunk = (two, two_got, two_swapped, swap(two_got))
        three = joined(three, three_got)
        three_got = spread(three, side)
    else:
        chunk = chunk_one
    out_zero, memory, mixed_zero, fed_zero = run_feed_forward(bits, 0, scalars, hidden_zero, attended, vecs, chunk)
    if ringed:
        out_zero, memory, three_got, two_chunk = fence(out_zero, memory, three_got, two_chunk)
        chunk = two_chunk
        three = joined(three, three_got)
        three_got, three_swapped = spread(three, last), swap(three)
    else:
        chunk = chunk_two
    memory = lax.ppermute(memory, "section", [(0, 1)])
    projected, saved_one = run_project(bits, scalars, memory, out_zero, vecs, chunk, table)
    attended, probs_one = run_attend(scalars, projected)
    if ringed:
        attended, three_got, three_swapped = fence(attended, three_got, three_swapped)
        chunk = (three, three_got, three_swapped, swap(three_got))
    else:
        chunk = chunk_three
    keep_a, send_a, grad, grad_att, gain_one, gain_final, loss = run_top(
        bits, streams, scalars, out_zero, attended, codes, vecs, chunk
    )
    if ringed:
        grad_att, keep_a, send_a = fence(grad_att, keep_a, send_a)
        got_a = swap(send_a)
    grads_a, staged = run_attend_back(bits, scalars, grad_att, saved_one, table, probs_one)
    if ringed:
        grads_a, staged, got_a = fence(grads_a, staged, got_a)
        sum_a = [keep_a, got_a]
        got_a = shrink([sum_a], last)
    grads_b, keep_b, send_b = run_attend_back_rest(
        bits, scalars, grad_att, saved_one, table, probs_one, staged
    )
    if ringed:
        grads_b, keep_b, send_b = fence(grads_b, keep_b, send_b)
        got_b = swap(send_b)
    grad, vecs_one = run_input_grads(
        bits, scalars, saved_one, (*grads_a, *grads_b), grad, vecs, memory, out_zero
    )
    if ringed:
        grad, got_a, got_b = fence(grad, got_a, got_b)
        sum_a.append(got_a)
        sum_b = [keep_b, got_b]
        got_a, got_b = shrink([sum_a], side), shrink([sum_b], last)
    keep_c, send_c, grad, grad_att, gain_zero = run_feed_backward(
        bits, 0, scalars, grad, vecs, mixed_zero, probs_zero, fed_zero
    )
    if ringed:
        grad_att, got_a, got_b, keep_c, send_c = fence(grad_att, got_a, got_b, keep_c, send_c)
        sum_a.append(got_a)
        sum_b.append(got_b)
        got_a, got_b, got_c = shrink([sum_a], near), shrink([sum_b], side), swap(send_c)
    grads_a, staged = run_attend_back(bits, scalars, grad_att, saved_zero, table, probs_zero)
    if ringed:
        grads_a, staged, got_a, got_b, got_c = fence(grads_a, staged, got_a, got_b, got_c)
        sum_a.append(got_a)
        sum_b.append(got_b)
        sum_c = [keep_c, got_c]
        got_c, got_a, got_b = shrink([sum_c], last), shrink([sum_a], far), shrink([sum_b], near)
    grads_b, keep_d, send_d = run_attend_back_rest(
        bits, scalars, grad_att, saved_zero, table, probs_zero, staged
    )
    if ringed:
        grads_b, keep_d, send_d, got_a, got_b, got_c = fence(grads_b, keep_d, send_d, got_a, got_b, got_c)
        sum_a.append(got_a)
        sum_b.append(got_b)
        sum_c.append(got_c)
        got_d, got_c, got_b = swap(send_d), shrink([sum_c], side), shrink([sum_b], far)
    keep_e, send_e = run_input_grads_last(
        bits, scalars, saved_zero, (*grads_a, *grads_b), grad, vecs, rows,
        gain_zero, vecs_one, gain_one, gain_final,
    )
    if not ringed:
        pairs = ((keep_d, send_d), (keep_c, send_c), (keep_b, send_b), (keep_a, send_a), (keep_e, send_e))
        sums = [keep.astype(F32) + swap(send).astype(F32) for keep, send in pairs]
        squares, grads = whole_grads(section, sums)
        grad_norm = jnp.sqrt(squares)
        loss_sum = lax.psum(loss[0, 0], ("section", "dp"))
        factor = jnp.minimum(1.0, CLIP / (grad_norm + 1e-06))
        results = []
        for index in range(9):
            rate, decay = (0.3, 0.0) if index in (5, 8) else (0.03, 0.01)
            grad = grads[index][None] if index < 6 else grads[index]
            results.append(
                adam_step(params[index], grad, firsts[index], seconds[index], rate, decay, factor)
            )
        news, moms, sqs = zip(*results)
        return (*news, *moms, *sqs, grad_norm, loss_sum)
    keep_e, send_e, got_b, got_d = fence(keep_e, send_e, got_b, got_d)
    sum_b.append(got_b)
    sum_d, sum_e, sum_de = [keep_d, got_d], [keep_e, swap(send_e)], []
    for pair in (last, side, near, far):
        got = shrink([sum_d, sum_e], pair, sum_de)
        if pair == last:
            sum_c.append(got_c)
            got, got_c = fence(got, shrink([sum_c], near))
            sum_c.append(got_c)
            sum_c.append(shrink([sum_c], far))
        sum_de.append(got)
    kept, sent, total = run_finish(scalars, loss, sum_d, sum_c, sum_b, sum_a, sum_e, sum_de)
    got = swap(sent)
    return tuple(run_update(scalars, add_up(total, bits), kept, got, state))


def solution(mesh):
    weights = (
        P("section", "dp", None),
        P("section", "dp", None),
        P("section", "dp", None),
        P("section", "dp", None),
        P("section", "dp", None),
        P("section", None, "dp"),
        P(None, "dp"),
        P("dp", None),
        P("dp"),
    )
    return jax.shard_map(
        local,
        mesh=mesh,
        in_specs=(P("dp", None, None), P("dp", None), P("dp")) + weights * 3,
        out_specs=weights * 3 + (P(), P()),
        check_vma=False,
    )
```

```python
import functools

import jax
import jax.numpy as jnp
from jax import lax
from jax.experimental import pallas as pl
from jax.experimental.pallas import tpu as pltpu
from jax.sharding import PartitionSpec as P

D = 512
FF = 2048
CODES = 1024
FEATS = 80
MEM = 256
SEG = 512
SEGS = 2
STEP = 10
ROWS = MEM + SEG
BLOCK = 128
PAIRS = 4
WIDE = 18 * BLOCK
GROUPS = 16
QUERY_U_AT, QUERY_V_AT, KEYS_AT, VALUES_AT, REL_AT, WEIGHTS_AT, SMALL_AT = 768, 1280, 1792, 2560, 3328, 4096, 6144
ACTIVE_AT, SLOPE_AT, UP_AT, DOWN_AT, OUT_AT = 512, 2560, 4608, 6656, 8704
KEPT_ROWS = 16384
KEPT_PAIRS = 14
IN_ORDER = ((1, 2, 4, 8), (1, 2, 4, 8))
NEG = -1e30
CLIP = 0.02
SCALE = 0.125
F32 = jnp.float32
BF16 = jnp.bfloat16
SPANS = tuple((MEM + BLOCK * (b + 1) for b in range(4)))
STARTS = tuple((sum(SPANS[:b]) for b in range(4)))


def nn(left, right):
    return jnp.dot(left, right, preferred_element_type=F32)


def nt(left, right):
    return lax.dot_general(left, right, (((1,), (1,)), ((), ())), preferred_element_type=F32)


def tn(left, right):
    return lax.dot_general(left, right, (((0,), (0,)), ((), ())), preferred_element_type=F32)


def norm_parts(values):
    center = values - jnp.mean(values, -1, keepdims=True)
    spread = jnp.mean(center * center, -1, keepdims=True)
    inverse = lax.rsqrt(spread + 1e-05)
    return center * inverse, inverse


def norm_back(unit, inverse, gain, grad):
    scaled = grad * gain
    first = jnp.mean(scaled, -1, keepdims=True)
    second = jnp.mean(scaled * unit, -1, keepdims=True)
    return inverse * (scaled - first - unit * second), jnp.sum(grad * unit, 0, keepdims=True)


def group_of(bits, spot, place, half):
    if bits == IN_ORDER:
        return spot
    low, high = (sum((bit for index, bit in enumerate(each) if (spot >> index) & 1)) for each in bits)
    return jnp.bitwise_xor(place, low if low == high else jnp.where(half == 0, low, high))


def copies(bits, place, half, pieces, units, rows, sem, outward):
    count = GROUPS // len(pieces)
    for index, slab in enumerate(pieces):
        for spot in range(count):
            group = group_of(bits, index * count + spot, place, half)
            for whole, first in units:
                there = whole.at[pl.ds(pl.multiple_of((group * 2 + half) * rows, rows), rows), :]
                here = slab.at[spot, pl.ds(first, rows), pl.ds(0, whole.shape[1])]
                if outward:
                    pltpu.make_async_copy(there, here, sem).start()
                else:
                    pltpu.make_async_copy(here, there, sem).start()


def columns(ref, count):
    return [ref.at[:, pl.ds(D * u, D)] for u in range(count)]


def fetch(source, target, sem):
    copy = pltpu.make_async_copy(source, target, sem)
    copy.start()
    return copy


def arrived(buffer, sem):
    pltpu.make_async_copy(buffer, buffer, sem).wait()


def tri_mask():
    row = lax.broadcasted_iota(jnp.int32, (2 * BLOCK, BLOCK), 0)
    col = lax.broadcasted_iota(jnp.int32, (2 * BLOCK, BLOCK), 1)
    return col <= lax.rem(row, BLOCK)


def stack_heads(part):
    col = lax.broadcasted_iota(jnp.int32, part.shape, 1)
    zero = jnp.zeros_like(part)
    return jnp.concatenate(
        [jnp.where(col < 64, part, zero), jnp.where(col < 64, zero, part)], 0
    )


def pick_heads(both):
    col = lax.broadcasted_iota(jnp.int32, (BLOCK, BLOCK), 1)
    return jnp.where(col < 64, both[:BLOCK], both[BLOCK:])


def shift(both, amount):
    return jnp.concatenate(
        [pltpu.roll(part, amount, 1, stride=1, stride_axis=0) for part in (both[:BLOCK], both[BLOCK:])], 0
    )


def masked(score, triangle, first):
    if first == 0:
        return jnp.where(triangle, score, NEG)
    return jnp.concatenate([score[:, :first], jnp.where(triangle, score[:, first:], NEG)], 1)


def lanes(pair):
    return pl.ds(pl.multiple_of(pair * BLOCK, BLOCK), BLOCK)


def project(bits, base, *refs):
    first_layer = base == 0
    if first_layer:
        (scalars, frames, own_low, own_high, other_low, other_high, table) = refs[:7]
        (query_u, query_v, keys, values, rel, hidden, vecs, saved) = refs[7:15]
        (normed, weights, in_sem, out_sem, joined, small, small_sem) = refs[15:]
    else:
        (scalars, memory, hidden, vecs, own_low, own_high, other_low, other_high, table) = refs[:9]
        (query_u, query_v, keys, values, rel, saved) = refs[9:15]
        (normed, weights, in_sem, out_sem) = refs[15:]
    place, half = scalars[0], scalars[1]
    both = ((half, (own_low, own_high)), (1 - half, (other_low, other_high)))
    if first_layer:
        for which, pieces in both:
            copies(bits, place, which, pieces, [(small, 64)], 16, small_sem, False)
    units = [(weights.at[u], 16 * u) for u in range(4)]
    for which, pieces in both:
        copies(bits, place, which, pieces, units, 16, in_sem, False)
    if first_layer:
        arrived(small, small_sem)
        small_out = fetch(small, saved.at[pl.ds(SMALL_AT, D), pl.ds(0, BLOCK)], out_sem.at[7])
        vecs[...] = jnp.transpose(small[...].astype(F32))[80:96]
        for b in range(3):
            rows = pl.ds(256 * b, 256)
            joined[rows, :] = nt(frames[rows, :], small[...])
        hidden[...] = joined[MEM:, :]
        sources = [joined.at[pl.ds(256 * b, 256)] for b in range(3)]
    else:
        sources = [memory, hidden.at[pl.ds(0, 256)], hidden.at[pl.ds(256, 256)]]
    gain = vecs[base : base + 1, :]
    bias_u = vecs[base + 2 : base + 3, :]
    bias_v = vecs[base + 3 : base + 4, :]
    arrived(weights, in_sem)
    outs = [fetch(weights.at[u], saved.at[pl.ds(WEIGHTS_AT + D * u, D)], out_sem.at[8 + u]) for u in range(4)]
    rel[...] = nn(table[...], weights[3]).astype(BF16)
    outs.append(fetch(rel, saved.at[pl.ds(REL_AT, ROWS)], out_sem.at[5]))
    for b in range(3):
        unit, unused = norm_parts(sources[b][...])
        normed[pl.ds(256 * b, 256), :] = (unit * gain).astype(BF16)
    outs.append(fetch(normed, saved.at[pl.ds(0, ROWS)], out_sem.at[0]))
    keys[...] = nn(normed[...], weights[1]).astype(BF16)
    outs.append(fetch(keys, saved.at[pl.ds(KEYS_AT, ROWS)], out_sem.at[3]))
    values[...] = nn(normed[...], weights[2]).astype(BF16)
    outs.append(fetch(values, saved.at[pl.ds(VALUES_AT, ROWS)], out_sem.at[4]))
    query = nn(normed[MEM:, :], weights[0])
    query_u[...] = (query + bias_u).astype(BF16)
    query_v[...] = (query + bias_v).astype(BF16)
    outs.append(fetch(query_u, saved.at[pl.ds(QUERY_U_AT, SEG)], out_sem.at[1]))
    outs.append(fetch(query_v, saved.at[pl.ds(QUERY_V_AT, SEG)], out_sem.at[2]))
    if first_layer:
        outs.append(small_out)
    for copy in outs:
        copy.wait()


def attend(scalars, query_u, query_v, keys, values, rel, attended, probs_o, probs, out_sem):
    length, segment = scalars[2], scalars[3]
    spot = lax.broadcasted_iota(jnp.int32, (1, ROWS), 1)
    where_at = segment * SEG + spot - MEM
    allowed = (where_at < length) & ((spot >= MEM) | (segment >= 1))
    bias = jnp.where(allowed, 0.0, NEG)
    triangle = tri_mask()

    def two_pairs(first, step, carry):
        tiles = [(2 * step + one, b, SPANS[b] - first) for one in range(2) for b in range(4)]
        full = [
            nt(stack_heads(query_v[BLOCK * b : BLOCK * (b + 1), lanes(pair)]) * SCALE,
               rel[ROWS - span : ROWS, lanes(pair)])
            for pair, b, span in tiles
        ]
        content = [
            nt(stack_heads(query_u[BLOCK * b : BLOCK * (b + 1), lanes(pair)]) * SCALE,
               keys[first : first + span, lanes(pair)])
            for pair, b, span in tiles
        ]
        full = [shift(item, span - BLOCK + 1) for item, (pair, b, span) in zip(full, tiles)]
        score = [
            masked(one + two + bias[:, first : first + span], triangle, span - BLOCK)
            for one, two, (pair, b, span) in zip(content, full, tiles)
        ]
        top = [jnp.max(item, -1, keepdims=True) for item in score]
        expo = [jnp.exp(item - most) for item, most in zip(score, top)]
        total = [jnp.sum(item, -1, keepdims=True) for item in expo]
        prob = [(item * (1.0 / most)).astype(BF16) for item, most in zip(expo, total)]
        for item, (pair, b, span) in zip(prob, tiles):
            probs[pair, :, STARTS[b] + first : STARTS[b] + first + span] = item
        for one in range(2):
            pair = 2 * step + one
            pltpu.make_async_copy(probs.at[pair], probs_o.at[pair], out_sem.at[pair]).start()
        found = [
            nn(item, values[first : first + span, lanes(pair)]) for item, (pair, b, span) in zip(prob, tiles)
        ]
        for item, (pair, b, span) in zip(found, tiles):
            attended[BLOCK * b : BLOCK * (b + 1), lanes(pair)] = pick_heads(item).astype(BF16)
        return carry

    for first in (0, MEM):

        @pl.when((segment == 0) == (first > 0))
        def _():
            lax.fori_loop(0, PAIRS // 2, functools.partial(two_pairs, first), 0)

    outs = [
        fetch(attended.at[pl.ds(256 * b, 256)], probs_o.at[PAIRS + b, :, pl.ds(0, D)], out_sem.at[PAIRS + b])
        for b in range(2)
    ]
    for pair in range(PAIRS):
        pltpu.make_async_copy(probs.at[pair], probs_o.at[pair], out_sem.at[pair]).wait()
    for copy in outs:
        copy.wait()


def attend_back(bits, second, *refs):
    (scalars, grad_att, table_h, saved, probs_h) = refs[:5]
    normed, table, late_sem = refs[-3:]
    rest = refs[5:-3]
    query_u_h, query_v_h, keys_h, values_h, rel_h = (
        saved.at[pl.ds(first, rows)]
        for first, rows in (
            (QUERY_U_AT, SEG), (QUERY_V_AT, SEG), (KEYS_AT, ROWS), (VALUES_AT, ROWS), (REL_AT, ROWS)
        )
    )
    if second:
        staged_h = rest[0]
        rest = rest[1:]
        (keep, send) = rest[4:6]
        sums, rest = rest[3], rest[:3] + rest[6:]
    else:
        (staged, sums) = rest[3:5]
        rest = rest[:3] + rest[5:]
    (grad_query, grad_keys, grad_values,
     query_u, query_v, keys, values, rel, probs, flip, acc_keys, acc_values, acc_rel,
     grad_qu, grad_qv, pair_sem) = rest[:16]
    first_pair = 2 if second else 0

    def parts(pair):
        lane, here = lanes(pair + first_pair), lanes(pair)
        moves = [(probs_h.at[pair + first_pair], probs.at[pair])]
        for there, target in (
            (query_u_h, query_u), (query_v_h, query_v), (keys_h, keys), (values_h, values), (rel_h, rel)
        ):
            moves.append((there.at[:, lane], target.at[:, here]))
        return [
            pltpu.make_async_copy(there, target, pair_sem.at[pair, index])
            for index, (there, target) in enumerate(moves)
        ]

    for pair in range(2):
        for copy in parts(pair):
            copy.start()
    late = [fetch(saved.at[pl.ds(0, ROWS)], normed, late_sem.at[0]), fetch(table_h, table, late_sem.at[1])]
    if second:
        staged, sem = rest[16:]
        staged[:, :, 0:256] = staged_h[...]
    row = lax.broadcasted_iota(jnp.int32, (2 * BLOCK, 2 * BLOCK), 0)
    col = lax.broadcasted_iota(jnp.int32, (2 * BLOCK, 2 * BLOCK), 1)
    back = (row // BLOCK) * BLOCK + BLOCK - 1 - lax.rem(row, BLOCK)
    flip[...] = (col == back).astype(F32).astype(BF16)

    segment = scalars[3]

    def one_pair(first, pair, carry):
        lane = lanes(pair)
        for copy in parts(pair):
            copy.wait()
        order = (3, 2, 1, 0)
        flipped = flip[...]
        stack_g = [
            stack_heads(grad_att[BLOCK * b : BLOCK * (b + 1), lanes(pair + first_pair)]) for b in order
        ]
        stack_u = [stack_heads(query_u[BLOCK * b : BLOCK * (b + 1), lane]) * SCALE for b in order]
        stack_v = [
            nn(flipped, stack_heads(query_v[BLOCK * b : BLOCK * (b + 1), lane]) * SCALE).astype(BF16)
            for b in order
        ]
        spans = [SPANS[b] - first for b in order]
        prob_b = [
            probs[pair, :, STARTS[b] + first : STARTS[b] + first + span] for b, span in zip(order, spans)
        ]
        grad_prob = [nt(one, values[first : first + span, lane]) for one, span in zip(stack_g, spans)]
        part_values = [tn(one, two) for one, two in zip(stack_g, prob_b)]
        prob = [item.astype(F32) for item in prob_b]
        inner = [jnp.sum(one * two, -1, keepdims=True) for one, two in zip(prob, grad_prob)]
        grad_score = [
            (one * (two - three)).astype(BF16) for one, two, three in zip(prob, grad_prob, inner)
        ]
        turned = [nn(flipped, item) for item in grad_score]
        found_u = [nn(item, keys[first : first + span, lane]) for item, span in zip(grad_score, spans)]
        part_keys = [tn(one, two) for one, two in zip(stack_u, grad_score)]
        grad_full = [shift(item, 0).astype(BF16) for item in turned]
        found_v = [nn(item, rel[ROWS - span : ROWS, lane]) for item, span in zip(grad_full, spans)]
        part_rel = [tn(one, two) for one, two in zip(stack_v, grad_full)]
        for index, b in enumerate(order):
            span = spans[index]
            rows = pl.ds(BLOCK * b, BLOCK)
            grad_qu[rows, lane] = pick_heads(found_u[index]) * SCALE
            grad_qv[rows, lane] = pick_heads(found_v[index]) * SCALE
            if b == 3:
                acc_keys[lane, first:] = part_keys[index]
                acc_values[lane, first:] = part_values[index]
                acc_rel[lane, ROWS - span :] = part_rel[index]
                if first:
                    blank = jnp.zeros((BLOCK, first), F32)
                    acc_keys[lane, 0:first] = blank
                    acc_values[lane, 0:first] = blank
                    acc_rel[lane, 0 : ROWS - span] = blank
            else:
                acc_keys[lane, first : first + span] += part_keys[index]
                acc_values[lane, first : first + span] += part_values[index]
                acc_rel[lane, ROWS - span : ROWS] += part_rel[index]
        return carry

    for first in (0, MEM):

        @pl.when((segment == 0) == (first > 0))
        def _():
            lax.fori_loop(0, 2, functools.partial(one_pair, first), 0)

    grad_keys[...] = jnp.transpose(acc_keys[...]).astype(BF16)
    grad_values[...] = jnp.transpose(acc_values[...]).astype(BF16)
    grad_rel = jnp.transpose(acc_rel[...]).astype(BF16)
    sums[...] = jnp.zeros_like(sums)
    sums[2:3, :] = jnp.sum(grad_qu[...], 0, keepdims=True)
    sums[3:4, :] = jnp.sum(grad_qv[...], 0, keepdims=True)
    flip_one = flip[0:BLOCK, 0:BLOCK]
    for b in range(4):
        rows = pl.ds(BLOCK * b, BLOCK)
        part = grad_qv[rows, :]
        high = part.astype(BF16)
        low = (part - high.astype(F32)).astype(BF16)
        grad_query[rows, :] = (grad_qu[rows, :] + nn(flip_one, high) + nn(flip_one, low)).astype(BF16)
    for copy in late:
        copy.wait()
    cols = slice(256, 512) if second else slice(None)
    staged[1, :, cols] = tn(normed[...], grad_keys[...]).astype(BF16)
    staged[2, :, cols] = tn(normed[...], grad_values[...]).astype(BF16)
    staged[3, :, cols] = tn(table[...], grad_rel).astype(BF16)
    staged[0, :, cols] = tn(normed[MEM:, :], grad_query[...]).astype(BF16)
    if second:
        place, half = scalars[0], scalars[1]
        units = [(staged.at[u], 16 * u) for u in range(4)]
        copies(bits, place, half, (keep,), units, 16, sem, True)
        copies(bits, place, 1 - half, (send,), units, 16, sem, True)
        arrived(staged, sem)


def input_grads(bits, base, *refs):
    last_kernel = base == 0
    weights, weights_sem = refs[-2:]
    refs = refs[:-2]
    weights_copies = [
        fetch(refs[1].at[pl.ds(WEIGHTS_AT + D * u, D)], weights.at[u], weights_sem.at[u]) for u in range(3)
    ]
    (scalars, saved, query_a, keys_a, values_a, sums_a, query_b, keys_b, values_b, sums_b, grad_mixed, vecs) = refs[:12]
    if last_kernel:
        (frames, gain_two, vecs_one, gain_two_one, gain_final, keep, send,
         joined, smalls, staged, sem, small, small_sem) = refs[12:]
        fetch(saved.at[pl.ds(SMALL_AT, D), pl.ds(0, BLOCK)], small, small_sem).wait()
        joined[...] = nt(frames[...], small[...])
        before, here, first = joined, joined, MEM
    else:
        (memory, hidden, grad_hidden, grad_vecs) = refs[12:]
        before, here, first = memory, hidden, 0
    place, half = scalars[0], scalars[1]
    gain = vecs[base : base + 1, :]
    left, right = slice(0, 256), slice(256, 512)
    for copy in weights_copies:
        copy.wait()
    grad_keys = (
        nt(keys_a[...], weights[1, :, left])
        + nt(keys_b[...], weights[1, :, right])
        + nt(values_a[...], weights[2, :, left])
        + nt(values_b[...], weights[2, :, right])
    )
    grad_query = nt(query_a[...], weights[0, :, left]) + nt(query_b[...], weights[0, :, right])
    unit, inverse = norm_parts(before[0:MEM, :])
    grad_gain = jnp.sum(grad_keys[0:MEM] * unit, 0, keepdims=True)
    unit, inverse = norm_parts(here[first : first + SEG, :])
    grad_joined, gains = norm_back(unit, inverse, gain, grad_keys[MEM:] + grad_query)
    grad_gain = grad_gain + gains
    grad_in = grad_mixed[...] + grad_joined
    if last_kernel:
        smalls[...] = tn(frames[MEM:, :], grad_in.astype(BF16))
        smalls[80:81, :] = grad_gain
        smalls[81:82, :] = gain_two[0:1, :]
        smalls[82:84, left] = sums_a[2:4, :]
        smalls[82:84, right] = sums_b[2:4, :]
        smalls[84:88, :] = vecs_one[0:4, :]
        smalls[85:86, :] = gain_two_one[0:1, :]
        smalls[88:89, :] = gain_final[0:1, :]
        staged[...] = jnp.zeros_like(staged)
        staged[:, 0:BLOCK] = jnp.transpose(smalls[...]).astype(BF16)
        units = [(staged, 0)]
        copies(bits, place, half, (keep,), units, 16, sem, True)
        copies(bits, place, 1 - half, (send,), units, 16, sem, True)
        arrived(staged, sem)
    else:
        grad_hidden[...] = grad_in
        grad_vecs[:, left] = sums_a[...]
        grad_vecs[:, right] = sums_b[...]
        grad_vecs[0:1, :] = grad_gain


def feed_weights(bits, place, both, up, down, out, sem):
    for index, (units, rows) in enumerate(
        (
            ([(out, 128)], 16),
            ([(item, 16 * u) for u, item in enumerate(columns(up, 4))], 16),
            ([(down, 64)], 64),
        )
    ):
        for which, pieces in both:
            copies(bits, place, which, pieces, units, rows, sem.at[index], False)


def feed_mixed(residual, attended, out, gain, mixed, normed):
    mixed[...] = residual[...] + nn(attended[...], out[...])
    for b in range(2):
        rows = pl.ds(256 * b, 256)
        unit, unused = norm_parts(mixed[rows, :])
        normed[rows, :] = (unit * gain).astype(BF16)


def feed_inner(normed, up, active, slope):
    later = nn(normed[...], up[:, 0:512])
    for u in range(4):
        inner = later
        if u < 3:
            later = nn(normed[...], up[:, 512 * (u + 1) : 512 * (u + 2)])
        square = inner * inner
        bent = jnp.tanh(0.7978845608028654 * (inner + 0.044715 * (square * inner)))
        half = 0.5 * (1.0 + bent)
        active[:, 512 * u : 512 * (u + 1)] = (inner * half).astype(BF16)
        slope[:, 512 * u : 512 * (u + 1)] = (
            half
            + (0.5 * inner)
            * (1.0 - bent * bent)
            * (0.7978845608028654 * (1.0 + (3 * 0.044715) * square))
        ).astype(BF16)


def feed_output(mixed, active, down, output):
    output[...] = mixed[...] + nn(active[...], down[...])


def feed_forward(bits, base, scalars, residual, attended, vecs, own_low, own_high, other_low, other_high,
                 output, memory, mixed_o, saved,
                 mixed, normed, active, slope, up, down, out, sem, out_sem):
    place, half = scalars[0], scalars[1]
    both = ((half, (own_low, own_high)), (1 - half, (other_low, other_high)))
    feed_weights(bits, place, both, up, down, out, sem)
    arrived(out, sem.at[0])
    outs = [fetch(out, saved.at[pl.ds(OUT_AT, D)], out_sem.at[0])]
    feed_mixed(residual, attended, out, vecs[base + 1 : base + 2, :], mixed, normed)
    outs.append(fetch(normed, saved.at[pl.ds(0, SEG)], out_sem.at[1]))
    outs.append(fetch(mixed, mixed_o, out_sem.at[2]))
    arrived(up, sem.at[1])
    outs += [
        fetch(item, saved.at[pl.ds(UP_AT + D * u, D)], out_sem.at[4 + u])
        for u, item in enumerate(columns(up, 4))
    ]
    feed_inner(normed, up, active, slope)
    for u in range(4):
        cols = pl.ds(D * u, D)
        outs.append(fetch(active.at[:, cols], saved.at[pl.ds(ACTIVE_AT + D * u, D)], out_sem.at[8 + u]))
        outs.append(fetch(slope.at[:, cols], saved.at[pl.ds(SLOPE_AT + D * u, D)], out_sem.at[12 + u]))
    arrived(down, sem.at[2])
    outs.append(fetch(down, saved.at[pl.ds(DOWN_AT, FF)], out_sem.at[3]))
    feed_output(mixed, active, down, output)
    memory[...] = output[SEG - MEM :, :]
    for copy in outs:
        copy.wait()


def feed_back(moves, bits, place, half, keep, send, sem, base, grad_out, mixed, vecs, attended, normed,
              active, slope, up, down, out, grad_mixed, grad_att, grad_gain,
              grad_inner, staged_up, staged_down, staged_out):
    both = ((half, (keep,)), (1 - half, (send,)))
    grad_y = grad_out[...].astype(BF16)
    for copy in moves[:1]:
        copy.wait()
    later = nt(grad_y, down[0:512, :])
    for copy in moves[1:10]:
        copy.wait()
    for u in range(4):
        cols = slice(512 * u, 512 * (u + 1))
        part = later
        if u < 3:
            later = nt(grad_y, down[512 * (u + 1) : 512 * (u + 2), :])
        staged_down[cols, :] = tn(active[:, cols], grad_y).astype(BF16)
        grad_inner[:, cols] = (part * slope[:, cols].astype(F32)).astype(BF16)
    for copy in moves[10:]:
        copy.wait()
    grad_normed = nt(grad_inner[...], up[...])
    for which, pieces in both:
        copies(bits, place, which, pieces, [(staged_down, 64)], 64, sem.at[1], True)
    for u in range(4):
        cols = slice(512 * u, 512 * (u + 1))
        staged_up[:, cols] = tn(normed[...], grad_inner[:, cols]).astype(BF16)
    unit, inverse = norm_parts(mixed[...])
    grad_here, gains = norm_back(unit, inverse, vecs[base + 1 : base + 2, :], grad_normed)
    grad = grad_out[...] + grad_here
    grad_mixed[...] = grad
    grad_b = grad.astype(BF16)
    for which, pieces in both:
        units = [(item, 16 * u) for u, item in enumerate(columns(staged_up, 4))]
        copies(bits, place, which, pieces, units, 16, sem.at[0], True)
    grad_att[...] = nt(grad_b, out[...]).astype(BF16)
    staged_out[...] = tn(attended[...], grad_b).astype(BF16)
    for which, pieces in both:
        copies(bits, place, which, pieces, [(staged_out, 128)], 16, sem.at[2], True)
    grad_gain[...] = jnp.broadcast_to(gains, grad_gain.shape)
    arrived(staged_up, sem.at[0])
    arrived(staged_down, sem.at[1])
    arrived(staged_out, sem.at[2])


def feed_backward(bits, base, scalars, grad_out, vecs, mixed_h, probs_h, saved,
                  keep, send, grad_mixed, grad_att, grad_gain, mixed, attended,
                  normed, active, slope, up, down, out, grad_inner, staged_up, staged_down, staged_out,
                  in_sem, sem):
    pairs = [(saved.at[pl.ds(DOWN_AT, FF)], down)]
    for u in range(4):
        pairs.append((saved.at[pl.ds(SLOPE_AT + D * u, D)], slope.at[:, pl.ds(D * u, D)]))
    for u in range(4):
        pairs.append((saved.at[pl.ds(ACTIVE_AT + D * u, D)], active.at[:, pl.ds(D * u, D)]))
    pairs.append((saved.at[pl.ds(0, SEG)], normed))
    for u in range(4):
        pairs.append((saved.at[pl.ds(UP_AT + D * u, D)], columns(up, 4)[u]))
    pairs.append((saved.at[pl.ds(OUT_AT, D)], out))
    pairs.append((mixed_h, mixed))
    for b in range(2):
        pairs.append((probs_h.at[PAIRS + b, :, pl.ds(0, D)], attended.at[pl.ds(256 * b, 256)]))
    moves = [fetch(there, here, in_sem.at[index]) for index, (there, here) in enumerate(pairs)]
    feed_back(moves, bits, scalars[0], scalars[1], keep, send, sem, base, grad_out, mixed, vecs, attended, normed,
              active, slope, up, down, out, grad_mixed, grad_att, grad_gain,
              grad_inner, staged_up, staged_down, staged_out)


def top_kernel(bits, streams, scalars, residual, attended, targets, vecs, own_low, own_high, other_low, other_high,
               keep, send, grad_mixed, grad_att, grad_gain, final_gain, loss,
               normed, active, slope, up, down, out, mixed, output, grad_out, table, final, grad_logits, staged,
               grad_inner, staged_up, staged_down, staged_out, head_sem, sem, out_sem):
    place, half, length, segment = scalars[0], scalars[1], scalars[2], scalars[3]
    both = ((half, (own_low, own_high)), (1 - half, (other_low, other_high)))
    feed_weights(bits, place, both, up, down, out, sem)
    units = [(item, 144 + 16 * u) for u, item in enumerate(columns(table, 2))]
    for which, pieces in both:
        copies(bits, place, which, pieces, units, 16, head_sem, False)
    arrived(out, sem.at[0])
    feed_mixed(residual, attended, out, vecs[5:6, :], mixed, normed)
    arrived(up, sem.at[1])
    feed_inner(normed, up, active, slope)
    arrived(down, sem.at[2])
    feed_output(mixed, active, down, output)
    arrived(table, head_sem)
    size = length.astype(F32)
    codes = jnp.transpose(jnp.broadcast_to(targets[...].astype(F32), (BLOCK, SEG))).astype(jnp.int32)
    gain = vecs[8:9, :]
    gains = jnp.zeros((1, D), F32)
    terms = jnp.zeros((1, 1), F32)
    spans = (slice(0, 256), slice(256, 512))
    parts = [norm_parts(output[rows, :]) for rows in spans]
    fins = [(unit * gain).astype(BF16) for unit, unused in parts]
    logits = [nn(fin, table[...]) for fin in fins]
    for rows, fin in zip(spans, fins):
        final[rows, :] = fin
    grad_finals = []
    for b, rows in enumerate(spans):
        logit = logits[b]
        most = jnp.max(logit, -1, keepdims=True)
        expo = jnp.exp(logit - most)
        total = jnp.sum(expo, -1, keepdims=True)
        picks = lax.broadcasted_iota(jnp.int32, logit.shape, 1) == codes[rows, 0:1]
        picked = jnp.sum(jnp.where(picks, logit, 0.0), -1, keepdims=True)
        spot = segment * SEG + 256 * b + lax.broadcasted_iota(jnp.int32, (256, 1), 0)
        weight = jnp.where(spot < length, 1.0 / size, 0.0)
        terms = terms + jnp.sum((most + jnp.log(total) - picked) * weight, keepdims=True)
        grad = (expo * (1.0 / total) - jnp.where(picks, 1.0, 0.0)) * (weight * (1.0 / streams))
        grad_logits[rows, :] = grad.astype(BF16)
        grad_finals.append(nt(grad_logits[rows, :], table[...]))
    staged[...] = tn(final[...], grad_logits[...]).astype(BF16)
    for (unit, inverse), rows, grad_final in zip(parts, spans, grad_finals):
        grad_here, gain_here = norm_back(unit, inverse, gain, grad_final)
        grad_out[rows, :] = grad_here
        gains = gains + gain_here
    units = [(item, 144 + 16 * u) for u, item in enumerate(columns(staged, 2))]
    copies(bits, place, half, (keep,), units, 16, head_sem, True)
    copies(bits, place, 1 - half, (send,), units, 16, head_sem, True)
    final_gain[...] = jnp.broadcast_to(gains, final_gain.shape)
    loss[...] = jnp.broadcast_to(terms, loss.shape)
    feed_back((), bits, place, half, keep, send, out_sem, 4, grad_out, mixed, vecs, attended, normed,
              active, slope, up, down, out, grad_mixed, grad_att, grad_gain,
              grad_inner, staged_up, staged_down, staged_out)
    arrived(staged, head_sem)


def finish(counts, *refs):
    scalars, loss = refs[0], refs[1]
    total_count = sum(counts)
    sources = refs[2 : 2 + total_count]
    kept, sent, total = refs[2 + total_count : 5 + total_count]
    buffers, sem = refs[5 + total_count : -1], refs[-1]
    moves = [fetch(there.at[0], here, sem.at[index]) for index, (there, here) in enumerate(zip(sources, buffers))]
    for copy in moves:
        copy.wait()
    sums = []
    start = 0
    for count in counts:
        item = buffers[start][...].astype(F32)
        for other in buffers[start + 1 : start + count]:
            item = item + other[...].astype(F32)
        sums.append(item)
        start += count
    attn_zero, feed_zero, attn_one, feed_one, small = sums[0], sums[1], sums[2], sums[3], sums[4]
    attn_zero = attn_zero + sums[5][0:64]
    small = small + sums[5][64:80]
    first = scalars[1] == 0
    lone = jnp.zeros((1, 1), F32)
    for zero, one, rows, begin in ((attn_zero, attn_one, 64, 0), (feed_zero, feed_one[0:144], 144, 64)):
        kept[begin : begin + rows, :] = jnp.where(first, zero, one)
        sent[begin : begin + rows, :] = jnp.where(first, one, zero)
        lone = lone + jnp.sum(zero * zero + one * one, keepdims=True)
    head = feed_one[144:176]
    lone = lone + jnp.sum(head * head, keepdims=True) + jnp.sum(small * small, keepdims=True)
    for target in (kept, sent):
        target[208:240, :] = head
        target[240:256, :] = small
    column = lax.broadcasted_iota(jnp.int32, (8, 128), 1)
    total[...] = jnp.where(column == 0, lone, 0.0) + jnp.where(column == 1, loss[...], 0.0)


def adam_step(weight, grad, first, second, rate, decay, factor):
    grad = grad * factor
    first = 0.9 * first + 0.1 * grad
    second = 0.999 * second + 0.001 * grad * grad
    ratio = first / (1.0 - 0.9**STEP) / (jnp.sqrt(second / (1.0 - 0.999**STEP)) + 1e-08)
    return (weight - rate * (ratio + decay * weight), first, second)


def update(scalars, total, kept, got, *refs):
    ins, outs, small = refs[:27], refs[27:56], refs[56]
    first = scalars[1] == 0
    squares = jnp.sum(total[0:1, 0:1], keepdims=True)
    norm = jnp.sqrt(squares)
    outs[27][...] = norm
    outs[28][...] = total[0:1, 1:2]
    factor = jnp.minimum(1.0, CLIP / (norm + 1e-06))

    def half_of(half, start, rows):
        here, there = kept[start : start + rows, :], got[start : start + rows, :]
        return jnp.where(first == (half == 0), here, there)

    def apply(index, spot, grad, rate, decay):
        results = adam_step(
            ins[index][spot], grad, ins[9 + index][spot], ins[18 + index][spot], rate, decay, factor
        )
        for which, result in enumerate(results):
            outs[9 * which + index][spot] = result

    for half in range(2):
        rows = slice(16 * half, 16 * half + 16)
        for u in range(3):
            apply(0, (0, rows, slice(D * u, D * (u + 1))), half_of(half, 16 * u, 16), 0.03, 0.01)
        apply(1, (0, rows, slice(None)), half_of(half, 192, 16), 0.03, 0.01)
        apply(2, (0, rows, slice(None)), half_of(half, 48, 16), 0.03, 0.01)
        for u in range(4):
            apply(3, (0, rows, slice(D * u, D * (u + 1))), half_of(half, 64 + 16 * u, 16), 0.03, 0.01)
        apply(4, (0, slice(64 * half, 64 * half + 64), slice(None)), half_of(half, 128, 64), 0.03, 0.01)
        for u in range(2):
            apply(7, (rows, slice(D * u, D * (u + 1))), half_of(half, 208 + 16 * u, 16), 0.03, 0.01)
        small[rows, :] = half_of(half, 240, 16)[:, 0:BLOCK]
    small[32:, :] = jnp.zeros((BLOCK - 32, BLOCK), F32)
    turned = jnp.transpose(small[...])
    apply(6, (slice(None), slice(None)), small[0:32, 0:FEATS], 0.03, 0.01)
    vecs = jnp.where(first, turned[80:84, 0:32], turned[84:88, 0:32])
    apply(5, (0, slice(None), slice(None)), vecs, 0.3, 0.0)
    apply(8, (slice(None), slice(None)), turned[88:89, 0:32], 0.3, 0.0)


def pack_shards(scalars, attn, out, pos, up, down, vecs, w_in, head, gain, kept, sent, codes, small):
    half, section = scalars[1], scalars[3]
    small[...] = jnp.zeros_like(small)
    small[88:89, 0:32] = gain[...]
    small[pl.ds(FEATS + 4 * section, 4), 0:32] = vecs[0]
    turned = jnp.transpose(small[...])[0:32]
    turned = jnp.concatenate([w_in[...], turned[:, FEATS:]], 1)
    column = lax.broadcasted_iota(jnp.int32, turned.shape, 1)
    shared = (column < FEATS) | (column == 88)
    for which, target in ((half, kept), (1 - half, sent)):
        rows = pl.ds(pl.multiple_of(16 * which, 16), 16)
        for u in range(3):
            target[16 * u : 16 * u + 16, :] = attn[0, rows, D * u : D * (u + 1)].astype(BF16)
        target[48:64, :] = pos[0, rows, :].astype(BF16)
        for u in range(4):
            target[80 + 16 * u : 96 + 16 * u, :] = up[0, rows, D * u : D * (u + 1)].astype(BF16)
        target[144:208, :] = down[0, pl.ds(pl.multiple_of(64 * which, 64), 64), :].astype(BF16)
        target[208:224, :] = out[0, rows, :].astype(BF16)
        tail = jnp.where(half == 0, turned[0:16], turned[16:32])
        if target is sent:
            tail = jnp.where(half == 0, turned[16:32], turned[0:16])
            tail = jnp.where(shared[0:16], 0.0, tail)
        target[64:80, :] = jnp.zeros((16, D), BF16)
        target[64:80, 0:BLOCK] = tail.astype(BF16)
    rows = pl.ds(pl.multiple_of(16 * half, 16), 16)
    for u in range(2):
        codes[16 * u : 16 * u + 16, :] = head[rows, D * u : D * (u + 1)].astype(BF16)


VMEM = pl.BlockSpec(memory_space=pltpu.VMEM)
ANY = pl.BlockSpec(memory_space=pl.ANY)
HBM = pl.BlockSpec(memory_space=pltpu.HBM)
SMEM = pl.BlockSpec(memory_space=pltpu.SMEM)
DMA = pltpu.SemaphoreType.DMA


def shape(*dims, dtype=F32):
    return jax.ShapeDtypeStruct(dims, dtype)


def half_shape(*dims):
    return jax.ShapeDtypeStruct(dims, BF16)


def held(*dims):
    return pltpu.VMEM(dims, BF16)


def wide(*dims):
    return pltpu.VMEM(dims, F32)


def call(body, name, ins, outs, out_specs, scratch, micros, limit):
    return pl.pallas_call(
        body,
        name=name,
        in_specs=ins,
        out_shape=outs,
        out_specs=out_specs,
        scratch_shapes=scratch,
        compiler_params=pltpu.CompilerParams(vmem_limit_bytes=limit * 1024 * 1024),
        cost_estimate=pl.CostEstimate(flops=micros * 1_150_000_000, bytes_accessed=1 << 20, transcendentals=0),
    )


QUERY_KEY = (half_shape(SEG, D), half_shape(SEG, D), half_shape(ROWS, D), half_shape(ROWS, D), half_shape(ROWS, D))
PROJECT_HELD = [held(ROWS, D), held(4, D, D), DMA, DMA((12,))]
KEPT = half_shape(KEPT_ROWS, D)


def run_project_first(bits, scalars, frames, pieces, table):
    result = call(
        functools.partial(project, bits, 0),
        "project_first",
        [SMEM, VMEM, HBM, HBM, HBM, HBM, VMEM],
        QUERY_KEY + (shape(SEG, D), shape(16, D), KEPT),
        [VMEM] * 7 + [HBM],
        PROJECT_HELD + [wide(ROWS, D), held(D, BLOCK), DMA],
        6,
        40,
    )(scalars, frames, *pieces, table)
    return result[:5], result[5], result[6], result[7]


def run_project(bits, scalars, memory, hidden, vecs, pieces, table):
    result = call(
        functools.partial(project, bits, 4),
        "project",
        [SMEM, VMEM, VMEM, VMEM, HBM, HBM, HBM, HBM, VMEM],
        QUERY_KEY + (KEPT,),
        [VMEM] * 5 + [HBM],
        PROJECT_HELD,
        6,
        40,
    )(scalars, memory, hidden, vecs, *pieces, table)
    return result[:5], result[5]


def run_attend(scalars, projected):
    return call(
        attend,
        "attend",
        [SMEM] + [VMEM] * 5,
        (half_shape(SEG, D), half_shape(KEPT_PAIRS, 2 * BLOCK, WIDE)),
        [VMEM, HBM],
        [held(PAIRS, 2 * BLOCK, WIDE), DMA((PAIRS + 2,))],
        11,
        44,
    )(scalars, *projected)


HALF_HELD = [
    held(SEG, 256), held(SEG, 256), held(ROWS, 256), held(ROWS, 256), held(ROWS, 256),
    held(2, 2 * BLOCK, WIDE), held(2 * BLOCK, 2 * BLOCK),
    wide(256, ROWS), wide(256, ROWS), wide(256, ROWS), wide(SEG, 256), wide(SEG, 256), DMA((2, 6)),
]
LATE_HELD = [held(ROWS, D), held(ROWS, D), DMA((2,))]
HALF_OUT = (half_shape(SEG, 256), half_shape(ROWS, 256), half_shape(ROWS, 256))


def run_attend_back(bits, scalars, grad_att, saved, table, probs):
    result = call(
        functools.partial(attend_back, bits, False),
        "attend_back",
        [SMEM, VMEM] + [HBM] * 3,
        HALF_OUT + (half_shape(4, D, 256), shape(8, 256)),
        [VMEM] * 5,
        HALF_HELD + LATE_HELD,
        9,
        40,
    )(scalars, grad_att, table, saved, probs)
    return (*result[:3], result[4]), result[3]


def run_attend_back_rest(bits, scalars, grad_att, saved, table, probs, staged):
    result = call(
        functools.partial(attend_back, bits, True),
        "attend_back_rest",
        [SMEM, VMEM] + [HBM] * 3 + [VMEM],
        HALF_OUT + (shape(8, 256), half_shape(GROUPS, 64, D), half_shape(GROUPS, 64, D)),
        [VMEM] * 4 + [ANY] * 2,
        HALF_HELD + [held(4, D, D), DMA] + LATE_HELD,
        10,
        42,
    )(scalars, grad_att, table, saved, probs, staged)
    return result[:4], result[4], result[5]


def run_input_grads(bits, scalars, saved, grads, grad_mixed, vecs, memory, hidden):
    return call(
        functools.partial(input_grads, bits, 4),
        "input_grads",
        [SMEM, HBM] + [VMEM] * 12,
        (shape(SEG, D), shape(8, D)),
        [VMEM] * 2,
        [held(4, D, D), DMA((3,))],
        5,
        40,
    )(scalars, saved, *grads, grad_mixed, vecs, memory, hidden)


def run_input_grads_last(bits, scalars, saved, grads, grad_mixed, vecs, frames, *small_grads):
    return call(
        functools.partial(input_grads, bits, 0),
        "input_grads_last",
        [SMEM, HBM] + [VMEM] * 15,
        (half_shape(GROUPS, 16, D), half_shape(GROUPS, 16, D)),
        [ANY] * 2,
        [wide(ROWS, D), wide(BLOCK, D), held(D, D), DMA, held(D, BLOCK), DMA, held(4, D, D), DMA((3,))],
        5,
        40,
    )(scalars, saved, *grads, grad_mixed, vecs, frames, *small_grads)


FEED_HELD = [held(SEG, D), held(SEG, FF), held(SEG, FF), held(D, FF), held(FF, D), held(D, D)]
BACK_HELD = [held(SEG, FF), held(D, FF), held(FF, D), held(D, D)]


def run_feed_forward(bits, base, scalars, residual, attended, vecs, pieces):
    result = call(
        functools.partial(feed_forward, bits, base),
        "feed_forward",
        [SMEM, VMEM, VMEM, VMEM, HBM, HBM, HBM, HBM],
        (shape(SEG, D), shape(MEM, D), shape(SEG, D), KEPT),
        [VMEM] * 2 + [HBM] * 2,
        [wide(SEG, D)] + FEED_HELD + [DMA((3,)), DMA((16,))],
        9,
        50,
    )(scalars, residual, attended, vecs, *pieces)
    return result


def run_feed_backward(bits, base, scalars, grad_out, vecs, mixed, probs, saved):
    return call(
        functools.partial(feed_backward, bits, base),
        "feed_backward",
        [SMEM, VMEM, VMEM] + [HBM] * 3,
        (half_shape(GROUPS, 144, D), half_shape(GROUPS, 144, D), shape(SEG, D), half_shape(SEG, D), shape(8, D)),
        [ANY, ANY, VMEM, VMEM, VMEM],
        [wide(SEG, D), held(SEG, D)] + FEED_HELD + BACK_HELD + [DMA((18,)), DMA((3,))],
        13,
        50,
    )(scalars, grad_out, vecs, mixed, probs, saved)


def run_top(bits, streams, scalars, residual, attended, targets, vecs, pieces):
    return call(
        functools.partial(top_kernel, bits, streams),
        "top_kernel",
        [SMEM, VMEM, VMEM, VMEM, VMEM, HBM, HBM, HBM, HBM],
        (
            half_shape(GROUPS, 176, D), half_shape(GROUPS, 176, D),
            shape(SEG, D), half_shape(SEG, D), shape(8, D), shape(8, D), shape(8, 128),
        ),
        [ANY] * 2 + [VMEM] * 5,
        FEED_HELD
        + [wide(SEG, D), wide(SEG, D), wide(SEG, D), held(D, CODES), held(SEG, D), held(SEG, CODES), held(D, CODES)]
        + BACK_HELD
        + [DMA, DMA((3,)), DMA((3,))],
        21,
        55,
    )(scalars, residual, attended, targets, vecs, *pieces)


def run_finish(scalars, loss, *sums):
    counts = tuple((len(item) for item in sums))
    flat = [item for group in sums for item in group]
    return call(
        functools.partial(finish, counts),
        "finish",
        [SMEM, VMEM] + [ANY] * len(flat),
        (shape(256, D), shape(256, D), shape(8, 128)),
        [VMEM] * 3,
        [pltpu.VMEM(item.shape[1:], item.dtype) for item in flat] + [DMA((len(flat),))],
        3,
        40,
    )(scalars, loss, *flat)


def run_update(scalars, total, kept, got, state):
    flat = [item[None] if item.ndim == 1 else item for item in state]
    for index in (6, 15, 24):
        flat[index] = jnp.transpose(flat[index])
    result = call(
        update,
        "update",
        [SMEM] + [VMEM] * 30,
        tuple((shape(*item.shape) for item in flat)) + (shape(1, 1), shape(1, 1)),
        [VMEM] * 29,
        [wide(BLOCK, BLOCK)],
        5,
        24,
    )(scalars, total, kept, got, *flat)
    result = list(result)
    for index in (6, 15, 24):
        result[index] = jnp.transpose(result[index])
    return [item.reshape(old.shape) for item, old in zip(result, state)] + [result[27][0, 0], result[28][0, 0]]


def run_pack(scalars, w_attn, w_out, w_pos, w_up, w_down, layer_vecs, w_in, w_head, gain_final):
    return call(
        pack_shards,
        "pack_shards",
        [SMEM] + [VMEM] * 9,
        (half_shape(224, D), half_shape(224, D), half_shape(32, D)),
        [VMEM] * 3,
        [wide(BLOCK, BLOCK)],
        3,
        56,
    )(scalars, w_attn, w_out, w_pos, w_up, w_down, layer_vecs, jnp.transpose(w_in), w_head, gain_final[None])


def spread(value, bits):
    count = lax.axis_size("dp")
    pairs = [
        (half * count + i, half * count + (i ^ bit)) for half, bit in enumerate(bits) for i in range(count)
    ]
    return lax.ppermute(value, ("section", "dp"), pairs)


def swap(value):
    return lax.ppermute(value, "section", [(0, 1), (1, 0)])


def fence(*values):
    return lax.optimization_barrier(values)


def joined(low, got):
    return jnp.concatenate([low, got], 0)


def part(sources, first, last):
    total = sources[0][first:last].astype(F32)
    for item in sources[1:]:
        total = total + item[first:last].astype(F32)
    return total


def shrink(chunks, pair, merged=()):
    count = (merged or chunks[0])[-1].shape[0]
    sent, first = [], 0
    for item in chunks:
        rows = item[0].shape[1]
        total = part(item, count // 2, count)
        if merged:
            total = total + part([other[:, first : first + rows] for other in merged], count // 2, count)
        sent.append(total.astype(BF16))
        first += rows
    return spread(jnp.concatenate(sent, 1), pair)


def add_up(value, bits):
    value = value + swap(value)
    steps = [low for low, unused in zip(*bits)]
    for one, two in zip(steps[0::2], steps[1::2]):
        first, second, third = (spread(value, (step, step)) for step in (one, two, one + two))
        value = (value + first) + (second + third)
    return value


def lanes_of(block):
    return [block[:, D * u : D * (u + 1)] for u in range(block.shape[1] // D)]


def sinus_table(where_at):
    freqs = jnp.exp(-jnp.log(10000.0) * (2.0 * jnp.arange(D // 2, dtype=jnp.int32).astype(F32) / D))
    angles = where_at * freqs[None, :]
    return jnp.concatenate([jnp.sin(angles), jnp.cos(angles)], 1).astype(BF16)


def split_shards(section, scalars, params):
    kept, sent, head = run_pack(scalars, *params)
    got = swap(sent)
    first = section == 0
    row = lax.broadcasted_iota(jnp.int32, (80, D), 0)
    attn = jnp.where(row < 64, jnp.where(first, kept[:80], got[:80]), kept[:80] + got[:80])
    zero = jnp.where(first, kept[80:], got[80:])
    one = jnp.where(first, got, kept)
    return attn, zero, one[:64], jnp.concatenate([one[80:], head], 0)


def halves(whole, rows):
    return whole.reshape(GROUPS, 2, rows, whole.shape[1]).transpose(1, 0, 2, 3)


def gather_whole(section, w_attn, w_out, w_pos, w_up, w_down, layer_vecs, w_in, w_head, gain_final):
    def over(value, axis):
        return lax.all_gather(value.astype(BF16), "dp", axis=axis, tiled=True)

    def layers(value):
        return lax.all_gather(over(value[0], 0), "section", axis=0)

    attn, out, pos, up, down = (layers(item) for item in (w_attn, w_out, w_pos, w_up, w_down))
    vecs = lax.all_gather(over(layer_vecs[0], 1), "section", axis=0)
    small = jnp.concatenate(
        [over(w_in, 1), vecs[0], vecs[1], over(gain_final, 0)[None], jnp.zeros((BLOCK - 89, D), BF16)], 0
    )
    small = jnp.pad(jnp.transpose(small), ((0, 0), (0, D - BLOCK)))
    head = over(w_head, 0)

    def pieces(units):
        both = jnp.concatenate([halves(item, item.shape[0] // 32) for item in units], 2)
        own = lax.dynamic_index_in_dim(both, section, 0, keepdims=False)
        other = lax.dynamic_index_in_dim(both, 1 - section, 0, keepdims=False)
        return (own[:8], own[8:], other[:8], other[8:])

    return (
        pieces(lanes_of(attn[0]) + [pos[0], small]),
        pieces(lanes_of(up[0]) + [down[0], out[0]]),
        pieces(lanes_of(attn[1]) + [pos[1]]),
        pieces(lanes_of(up[1]) + [down[1], out[1]] + lanes_of(head)),
    )


def whole_grads(section, sums):
    count = lax.axis_size("dp")
    place = lax.axis_index("dp")
    attn_zero, feed_zero, attn_one, feed_one, small = (
        lax.all_gather(lax.psum(item, "dp"), "section", axis=0) for item in sums
    )

    def unit(both, start, rows):
        item = both[:, :, start : start + rows]
        return item.transpose(1, 0, 2, 3).reshape(GROUPS * 2 * rows, both.shape[3])

    def layer(attn, feed):
        return (
            jnp.concatenate([unit(attn, 16 * u, 16) for u in range(3)], 1),
            unit(feed, 128, 16),
            unit(attn, 48, 16),
            jnp.concatenate([unit(feed, 16 * u, 16) for u in range(4)], 1),
            unit(feed, 64, 64),
        )

    small = jnp.transpose(unit(small, 0, 16))
    zero = layer(attn_zero, feed_zero) + (small[80:84],)
    one = layer(attn_one, feed_one) + (small[84:88],)
    ends = (small[:80], jnp.concatenate([unit(feed_one, 144 + 16 * u, 16) for u in range(2)], 1), small[88])
    squares = sum((jnp.sum(item * item) for item in zero + one + ends))
    dims = (0, 0, 0, 0, 0, 1, 1, 0, 0)
    grads = tuple((jnp.where(section == 0, a, b) for a, b in zip(zero, one))) + ends
    return squares, tuple(
        (
            lax.dynamic_slice_in_dim(item, place * (item.shape[dim] // count), item.shape[dim] // count, dim)
            for item, dim in zip(grads, dims)
        )
    )


def local(frames, targets, lengths, *state):
    params, firsts, seconds = (state[:9], state[9:18], state[18:])
    section = lax.axis_index("section")
    streams = lax.axis_size("dp")
    ringed = streams == GROUPS
    place = lax.axis_index("dp") if ringed else jnp.int32(0)
    length = lengths[0]
    scalars = jnp.stack([place, section, length, section]).astype(jnp.int32)
    count_down = (ROWS - 1 - jnp.arange(ROWS, dtype=jnp.int32)).astype(F32)[:, None]
    rows = lax.dynamic_slice_in_dim(
        jnp.pad(frames[0], ((MEM, 0), (0, BLOCK - FEATS))), section * SEG, ROWS, 0
    )
    codes = lax.dynamic_slice_in_dim(targets, section * SEG, SEG, 1)
    if ringed:
        bits = ((8, 4, 1, 2), (8, 4, 2, 1))
        far, near, side, last = zip(*bits)
        zero, one, two, three = (item[None] for item in split_shards(section, scalars, params))
        zero, got, count_down = fence(zero, spread(zero, far), count_down)
        table = sinus_table(count_down)
        zero = joined(zero, got)
        zero, got, one = fence(zero, spread(zero, near), one)
        zero = joined(zero, got)
        one_got = spread(one, far)
        zero, got, two, one, one_got, rows, table, codes = fence(
            zero, spread(zero, side), two, one, one_got, rows, table, codes
        )
        zero = joined(zero, got)
        high = spread(zero, last)
        one = joined(one, one_got)
        one_got, two_got = spread(one, near), spread(two, far)
        zero, high, one, one_got, two, two_got = fence(zero, high, one, one_got, two, two_got)
        one, two = joined(one, one_got), joined(two, two_got)
        one_got, two_got = spread(one, side), spread(two, near)
        swapped, high_swapped = swap(zero), swap(high)
        swapped, high_swapped, one, one_got, two, two_got, three = fence(
            swapped, high_swapped, one, one_got, two, two_got, three
        )
        chunk = (zero, high, swapped, high_swapped)
        one, two = joined(one, one_got), joined(two, two_got)
        one_got, two_got, three_got, swapped = spread(one, last), spread(two, side), spread(three, far), swap(one)
    else:
        bits = IN_ORDER
        table = sinus_table(count_down)
        chunk, chunk_one, chunk_two, chunk_three = gather_whole(section, *params)

    projected, hidden_zero, vecs, saved_zero = run_project_first(bits, scalars, rows, chunk, table)
    if ringed:
        projected, two_got, three_got, swapped = fence(projected, two_got, three_got, swapped)
        two, three = joined(two, two_got), joined(three, three_got)
        two_got, three_got, two_swapped = spread(two, last), spread(three, near), swap(two)
    attended, probs_zero = run_attend(scalars, projected)
    if ringed:
        attended, one_got, two_got, three_got, two_swapped = fence(
            attended, one_got, two_got, three_got, two_swapped
        )
        chunk = (one, one_got, swapped, swap(one_got))
        two_chunk = (two, two_got, two_swapped, swap(two_got))
        three = joined(three, three_got)
        three_got = spread(three, side)
    else:
        chunk = chunk_one
    out_zero, memory, mixed_zero, fed_zero = run_feed_forward(bits, 0, scalars, hidden_zero, attended, vecs, chunk)
    if ringed:
        out_zero, memory, three_got, two_chunk = fence(out_zero, memory, three_got, two_chunk)
        chunk = two_chunk
        three = joined(three, three_got)
        three_got, three_swapped = spread(three, last), swap(three)
    else:
        chunk = chunk_two
    memory = lax.ppermute(memory, "section", [(0, 1)])
    projected, saved_one = run_project(bits, scalars, memory, out_zero, vecs, chunk, table)
    attended, probs_one = run_attend(scalars, projected)
    if ringed:
        attended, three_got, three_swapped = fence(attended, three_got, three_swapped)
        chunk = (three, three_got, three_swapped, swap(three_got))
    else:
        chunk = chunk_three
    keep_a, send_a, grad, grad_att, gain_one, gain_final, loss = run_top(
        bits, streams, scalars, out_zero, attended, codes, vecs, chunk
    )
    if ringed:
        grad_att, keep_a, send_a = fence(grad_att, keep_a, send_a)
        got_a = swap(send_a)
    grads_a, staged = run_attend_back(bits, scalars, grad_att, saved_one, table, probs_one)
    if ringed:
        grads_a, staged, got_a = fence(grads_a, staged, got_a)
        sum_a = [keep_a, got_a]
        got_a = shrink([sum_a], last)
    grads_b, keep_b, send_b = run_attend_back_rest(
        bits, scalars, grad_att, saved_one, table, probs_one, staged
    )
    if ringed:
        grads_b, keep_b, send_b = fence(grads_b, keep_b, send_b)
        got_b = swap(send_b)
    grad, vecs_one = run_input_grads(
        bits, scalars, saved_one, (*grads_a, *grads_b), grad, vecs, memory, out_zero
    )
    if ringed:
        grad, got_a, got_b = fence(grad, got_a, got_b)
        sum_a.append(got_a)
        sum_b = [keep_b, got_b]
        got_a, got_b = shrink([sum_a], side), shrink([sum_b], last)
    keep_c, send_c, grad, grad_att, gain_zero = run_feed_backward(
        bits, 0, scalars, grad, vecs, mixed_zero, probs_zero, fed_zero
    )
    if ringed:
        grad_att, got_a, got_b, keep_c, send_c = fence(grad_att, got_a, got_b, keep_c, send_c)
        sum_a.append(got_a)
        sum_b.append(got_b)
        got_a, got_b, got_c = shrink([sum_a], near), shrink([sum_b], side), swap(send_c)
    grads_a, staged = run_attend_back(bits, scalars, grad_att, saved_zero, table, probs_zero)
    if ringed:
        grads_a, staged, got_a, got_b, got_c = fence(grads_a, staged, got_a, got_b, got_c)
        sum_a.append(got_a)
        sum_b.append(got_b)
        sum_c = [keep_c, got_c]
        got_c, got_a, got_b = shrink([sum_c], last), shrink([sum_a], far), shrink([sum_b], near)
    grads_b, keep_d, send_d = run_attend_back_rest(
        bits, scalars, grad_att, saved_zero, table, probs_zero, staged
    )
    if ringed:
        grads_b, keep_d, send_d, got_a, got_b, got_c = fence(grads_b, keep_d, send_d, got_a, got_b, got_c)
        sum_a.append(got_a)
        sum_b.append(got_b)
        sum_c.append(got_c)
        got_d, got_c, got_b = swap(send_d), shrink([sum_c], side), shrink([sum_b], far)
    keep_e, send_e = run_input_grads_last(
        bits, scalars, saved_zero, (*grads_a, *grads_b), grad, vecs, rows,
        gain_zero, vecs_one, gain_one, gain_final,
    )
    if not ringed:
        pairs = ((keep_d, send_d), (keep_c, send_c), (keep_b, send_b), (keep_a, send_a), (keep_e, send_e))
        sums = [keep.astype(F32) + swap(send).astype(F32) for keep, send in pairs]
        squares, grads = whole_grads(section, sums)
        grad_norm = jnp.sqrt(squares)
        loss_sum = lax.psum(loss[0, 0], ("section", "dp"))
        factor = jnp.minimum(1.0, CLIP / (grad_norm + 1e-06))
        results = []
        for index in range(9):
            rate, decay = (0.3, 0.0) if index in (5, 8) else (0.03, 0.01)
            grad = grads[index][None] if index < 6 else grads[index]
            results.append(
                adam_step(params[index], grad, firsts[index], seconds[index], rate, decay, factor)
            )
        news, moms, sqs = zip(*results)
        return (*news, *moms, *sqs, grad_norm, loss_sum)
    keep_e, send_e, got_b, got_d = fence(keep_e, send_e, got_b, got_d)
    sum_b.append(got_b)
    sum_d, sum_e, sum_de = [keep_d, got_d], [keep_e, swap(send_e)], []
    for pair in (last, side, near, far):
        got = shrink([sum_d, sum_e], pair, sum_de)
        if pair == last:
            sum_c.append(got_c)
            got, got_c, one_a, one_b = fence(got, shrink([sum_c], near), part(sum_a, 0, 1), part(sum_b, 0, 1))
            sum_c.append(got_c)
            got_c = shrink([sum_c], far)
        if pair == near:
            one_d = part(sum_d + [item[:, :64] for item in sum_de], 0, 1)
            one_e = part(sum_e + [item[:, 64:] for item in sum_de], 0, 1)
            got, one_c, one_d, one_e = fence(got, part(sum_c, 0, 1), one_d, one_e)
            one_d, one_e = one_d + got[:1, :64].astype(F32), one_e + got[:1, 64:].astype(F32)
        sum_de.append(got)
    kept, sent, total = run_finish(
        scalars, loss, [one_d], [one_c, got_c], [one_b], [one_a], [one_e], sum_de[3:]
    )
    got = swap(sent)
    return tuple(run_update(scalars, add_up(total, bits), kept, got, state))


def solution(mesh):
    weights = (
        P("section", "dp", None),
        P("section", "dp", None),
        P("section", "dp", None),
        P("section", "dp", None),
        P("section", "dp", None),
        P("section", None, "dp"),
        P(None, "dp"),
        P("dp", None),
        P("dp"),
    )
    return jax.shard_map(
        local,
        mesh=mesh,
        in_specs=(P("dp", None, None), P("dp", None), P("dp")) + weights * 3,
        out_specs=weights * 3 + (P(), P()),
        check_vma=False,
    )
```

```python
import functools

import jax
import jax.numpy as jnp
from jax import lax
from jax.experimental import pallas as pl
from jax.experimental.pallas import tpu as pltpu
from jax.sharding import PartitionSpec as P

D = 512
FF = 2048
CODES = 1024
FEATS = 80
MEM = 256
SEG = 512
SEGS = 2
STEP = 10
ROWS = MEM + SEG
BLOCK = 128
PAIRS = 4
WIDE = 18 * BLOCK
GROUPS = 16
QUERY_U_AT, QUERY_V_AT, KEYS_AT, VALUES_AT, REL_AT, WEIGHTS_AT, SMALL_AT = 768, 1280, 1792, 2560, 3328, 4096, 6144
ACTIVE_AT, SLOPE_AT, UP_AT, DOWN_AT, OUT_AT = 512, 2560, 4608, 6656, 8704
KEPT_ROWS = 16384
KEPT_PAIRS = 14
IN_ORDER = ((1, 2, 4, 8), (1, 2, 4, 8))
NEG = -1e30
CLIP = 0.02
SCALE = 0.125
F32 = jnp.float32
BF16 = jnp.bfloat16
SPANS = tuple((MEM + BLOCK * (b + 1) for b in range(4)))
STARTS = tuple((sum(SPANS[:b]) for b in range(4)))


def nn(left, right):
    return jnp.dot(left, right, preferred_element_type=F32)


def nt(left, right):
    return lax.dot_general(left, right, (((1,), (1,)), ((), ())), preferred_element_type=F32)


def tn(left, right):
    return lax.dot_general(left, right, (((0,), (0,)), ((), ())), preferred_element_type=F32)


def norm_parts(values):
    center = values - jnp.mean(values, -1, keepdims=True)
    spread = jnp.mean(center * center, -1, keepdims=True)
    inverse = lax.rsqrt(spread + 1e-05)
    return center * inverse, inverse


def norm_back(unit, inverse, gain, grad):
    scaled = grad * gain
    first = jnp.mean(scaled, -1, keepdims=True)
    second = jnp.mean(scaled * unit, -1, keepdims=True)
    return inverse * (scaled - first - unit * second), jnp.sum(grad * unit, 0, keepdims=True)


def group_of(bits, spot, place, half):
    if bits == IN_ORDER:
        return spot
    low, high = (sum((bit for index, bit in enumerate(each) if (spot >> index) & 1)) for each in bits)
    return jnp.bitwise_xor(place, low if low == high else jnp.where(half == 0, low, high))


def copies(bits, place, half, pieces, units, rows, sem, outward):
    count = GROUPS // len(pieces)
    for index, slab in enumerate(pieces):
        for spot in range(count):
            group = group_of(bits, index * count + spot, place, half)
            for whole, first in units:
                there = whole.at[pl.ds(pl.multiple_of((group * 2 + half) * rows, rows), rows), :]
                here = slab.at[spot, pl.ds(first, rows), pl.ds(0, whole.shape[1])]
                if outward:
                    pltpu.make_async_copy(there, here, sem).start()
                else:
                    pltpu.make_async_copy(here, there, sem).start()


def gather_units(bits, place, half, pieces, units, rows):
    count = GROUPS // len(pieces)
    for index, slab in enumerate(pieces):
        for spot in range(count):
            group = group_of(bits, index * count + spot, place, half)
            start = pl.multiple_of((group * 2 + half) * rows, rows)
            for whole, first in units:
                whole[pl.ds(start, rows), :] = slab[spot, first : first + rows, 0 : whole.shape[1]]


def scatter_units(bits, place, half, slab, units, rows):
    for spot in range(GROUPS):
        group = group_of(bits, spot, place, half)
        start = pl.multiple_of((group * 2 + half) * rows, rows)
        for whole, first in units:
            slab[spot, first : first + rows, 0 : whole.shape[1]] = whole[pl.ds(start, rows), :]


def columns(ref, count):
    return [ref.at[:, pl.ds(D * u, D)] for u in range(count)]


def fetch(source, target, sem):
    copy = pltpu.make_async_copy(source, target, sem)
    copy.start()
    return copy


def arrived(buffer, sem):
    pltpu.make_async_copy(buffer, buffer, sem).wait()


def tri_mask():
    row = lax.broadcasted_iota(jnp.int32, (2 * BLOCK, BLOCK), 0)
    col = lax.broadcasted_iota(jnp.int32, (2 * BLOCK, BLOCK), 1)
    return col <= lax.rem(row, BLOCK)


def stack_heads(part):
    col = lax.broadcasted_iota(jnp.int32, part.shape, 1)
    zero = jnp.zeros_like(part)
    return jnp.concatenate(
        [jnp.where(col < 64, part, zero), jnp.where(col < 64, zero, part)], 0
    )


def pick_heads(both):
    col = lax.broadcasted_iota(jnp.int32, (BLOCK, BLOCK), 1)
    return jnp.where(col < 64, both[:BLOCK], both[BLOCK:])


def shift(both, amount):
    return jnp.concatenate(
        [pltpu.roll(part, amount, 1, stride=1, stride_axis=0) for part in (both[:BLOCK], both[BLOCK:])], 0
    )


def masked(score, triangle, first):
    if first == 0:
        return jnp.where(triangle, score, NEG)
    return jnp.concatenate([score[:, :first], jnp.where(triangle, score[:, first:], NEG)], 1)


def lanes(pair):
    return pl.ds(pl.multiple_of(pair * BLOCK, BLOCK), BLOCK)


def project(bits, base, *refs):
    first_layer = base == 0
    if first_layer:
        (scalars, frames, own_low, own_high, other_low, other_high, table) = refs[:7]
        (query_u, query_v, keys, values, rel, hidden, vecs, saved) = refs[7:15]
        (normed, weights, in_sem, out_sem, joined, small, small_sem) = refs[15:]
    else:
        (scalars, memory, hidden, vecs, own_low, own_high, other_low, other_high, table) = refs[:9]
        (query_u, query_v, keys, values, rel, saved) = refs[9:15]
        (normed, weights, in_sem, out_sem) = refs[15:]
    place, half = scalars[0], scalars[1]
    both = ((half, (own_low, own_high)), (1 - half, (other_low, other_high)))
    if first_layer:
        for which, pieces in both:
            gather_units(bits, place, which, pieces, [(small, 64)], 16)
    units = [(weights.at[u], 16 * u) for u in range(4)]
    for which, pieces in both:
        gather_units(bits, place, which, pieces, units, 16)
    if first_layer:
        small_out = fetch(small, saved.at[pl.ds(SMALL_AT, D), pl.ds(0, BLOCK)], out_sem.at[7])
        vecs[...] = jnp.transpose(small[...].astype(F32))[80:96]
        for b in range(3):
            rows = pl.ds(256 * b, 256)
            joined[rows, :] = nt(frames[rows, :], small[...])
        hidden[...] = joined[MEM:, :]
        sources = [joined.at[pl.ds(256 * b, 256)] for b in range(3)]
    else:
        sources = [memory, hidden.at[pl.ds(0, 256)], hidden.at[pl.ds(256, 256)]]
    gain = vecs[base : base + 1, :]
    bias_u = vecs[base + 2 : base + 3, :]
    bias_v = vecs[base + 3 : base + 4, :]
    outs = [fetch(weights.at[u], saved.at[pl.ds(WEIGHTS_AT + D * u, D)], out_sem.at[8 + u]) for u in range(4)]
    rel[...] = nn(table[...], weights[3]).astype(BF16)
    outs.append(fetch(rel, saved.at[pl.ds(REL_AT, ROWS)], out_sem.at[5]))
    for b in range(3):
        unit, unused = norm_parts(sources[b][...])
        normed[pl.ds(256 * b, 256), :] = (unit * gain).astype(BF16)
    outs.append(fetch(normed, saved.at[pl.ds(0, ROWS)], out_sem.at[0]))
    keys[...] = nn(normed[...], weights[1]).astype(BF16)
    outs.append(fetch(keys, saved.at[pl.ds(KEYS_AT, ROWS)], out_sem.at[3]))
    values[...] = nn(normed[...], weights[2]).astype(BF16)
    outs.append(fetch(values, saved.at[pl.ds(VALUES_AT, ROWS)], out_sem.at[4]))
    query = nn(normed[MEM:, :], weights[0])
    query_u[...] = (query + bias_u).astype(BF16)
    query_v[...] = (query + bias_v).astype(BF16)
    outs.append(fetch(query_u, saved.at[pl.ds(QUERY_U_AT, SEG)], out_sem.at[1]))
    outs.append(fetch(query_v, saved.at[pl.ds(QUERY_V_AT, SEG)], out_sem.at[2]))
    if first_layer:
        outs.append(small_out)
    for copy in outs:
        copy.wait()


def attend(scalars, query_u, query_v, keys, values, rel, attended, probs_o, probs, out_sem):
    length, segment = scalars[2], scalars[3]
    spot = lax.broadcasted_iota(jnp.int32, (1, ROWS), 1)
    where_at = segment * SEG + spot - MEM
    allowed = (where_at < length) & ((spot >= MEM) | (segment >= 1))
    bias = jnp.where(allowed, 0.0, NEG)
    triangle = tri_mask()

    def two_pairs(first, step, carry):
        tiles = [(2 * step + one, b, SPANS[b] - first) for one in range(2) for b in range(4)]
        full = [
            nt(stack_heads(query_v[BLOCK * b : BLOCK * (b + 1), lanes(pair)]) * SCALE,
               rel[ROWS - span : ROWS, lanes(pair)])
            for pair, b, span in tiles
        ]
        content = [
            nt(stack_heads(query_u[BLOCK * b : BLOCK * (b + 1), lanes(pair)]) * SCALE,
               keys[first : first + span, lanes(pair)])
            for pair, b, span in tiles
        ]
        full = [shift(item, span - BLOCK + 1) for item, (pair, b, span) in zip(full, tiles)]
        score = [
            masked(one + two + bias[:, first : first + span], triangle, span - BLOCK)
            for one, two, (pair, b, span) in zip(content, full, tiles)
        ]
        top = [jnp.max(item, -1, keepdims=True) for item in score]
        expo = [jnp.exp(item - most) for item, most in zip(score, top)]
        total = [jnp.sum(item, -1, keepdims=True) for item in expo]
        prob = [(item * (1.0 / most)).astype(BF16) for item, most in zip(expo, total)]
        for item, (pair, b, span) in zip(prob, tiles):
            probs[pair, :, STARTS[b] + first : STARTS[b] + first + span] = item
        for one in range(2):
            pair = 2 * step + one
            pltpu.make_async_copy(probs.at[pair], probs_o.at[pair], out_sem.at[pair]).start()
        found = [
            nn(item, values[first : first + span, lanes(pair)]) for item, (pair, b, span) in zip(prob, tiles)
        ]
        for item, (pair, b, span) in zip(found, tiles):
            attended[BLOCK * b : BLOCK * (b + 1), lanes(pair)] = pick_heads(item).astype(BF16)
        return carry

    for first in (0, MEM):

        @pl.when((segment == 0) == (first > 0))
        def _():
            lax.fori_loop(0, PAIRS // 2, functools.partial(two_pairs, first), 0)

    outs = [
        fetch(attended.at[pl.ds(256 * b, 256)], probs_o.at[PAIRS + b, :, pl.ds(0, D)], out_sem.at[PAIRS + b])
        for b in range(2)
    ]
    for pair in range(PAIRS):
        pltpu.make_async_copy(probs.at[pair], probs_o.at[pair], out_sem.at[pair]).wait()
    for copy in outs:
        copy.wait()


def attend_back(bits, second, *refs):
    (scalars, grad_att, table_h, saved, probs_h) = refs[:5]
    normed, table, late_sem = refs[-3:]
    rest = refs[5:-3]
    query_u_h, query_v_h, keys_h, values_h, rel_h = (
        saved.at[pl.ds(first, rows)]
        for first, rows in (
            (QUERY_U_AT, SEG), (QUERY_V_AT, SEG), (KEYS_AT, ROWS), (VALUES_AT, ROWS), (REL_AT, ROWS)
        )
    )
    if second:
        staged_h = rest[0]
        rest = rest[1:]
        (keep, send) = rest[4:6]
        sums, rest = rest[3], rest[:3] + rest[6:]
    else:
        (staged, sums) = rest[3:5]
        rest = rest[:3] + rest[5:]
    (grad_query, grad_keys, grad_values,
     query_u, query_v, keys, values, rel, probs, flip, acc_keys, acc_values, acc_rel,
     grad_qu, grad_qv, pair_sem) = rest[:16]
    first_pair = 2 if second else 0

    def parts(pair):
        lane, here = lanes(pair + first_pair), lanes(pair)
        moves = [(probs_h.at[pair + first_pair], probs.at[pair])]
        for there, target in (
            (query_u_h, query_u), (query_v_h, query_v), (keys_h, keys), (values_h, values), (rel_h, rel)
        ):
            moves.append((there.at[:, lane], target.at[:, here]))
        return [
            pltpu.make_async_copy(there, target, pair_sem.at[pair, index])
            for index, (there, target) in enumerate(moves)
        ]

    for pair in range(2):
        for copy in parts(pair):
            copy.start()
    late = [fetch(saved.at[pl.ds(0, ROWS)], normed, late_sem.at[0]), fetch(table_h, table, late_sem.at[1])]
    if second:
        staged, sem = rest[16:]
        staged[:, :, 0:256] = staged_h[...]
    row = lax.broadcasted_iota(jnp.int32, (2 * BLOCK, 2 * BLOCK), 0)
    col = lax.broadcasted_iota(jnp.int32, (2 * BLOCK, 2 * BLOCK), 1)
    back = (row // BLOCK) * BLOCK + BLOCK - 1 - lax.rem(row, BLOCK)
    flip[...] = (col == back).astype(F32).astype(BF16)

    segment = scalars[3]

    def one_pair(first, pair, carry):
        lane = lanes(pair)
        for copy in parts(pair):
            copy.wait()
        order = (3, 2, 1, 0)
        flipped = flip[...]
        stack_g = [
            stack_heads(grad_att[BLOCK * b : BLOCK * (b + 1), lanes(pair + first_pair)]) for b in order
        ]
        stack_u = [stack_heads(query_u[BLOCK * b : BLOCK * (b + 1), lane]) * SCALE for b in order]
        stack_v = [
            nn(flipped, stack_heads(query_v[BLOCK * b : BLOCK * (b + 1), lane]) * SCALE).astype(BF16)
            for b in order
        ]
        spans = [SPANS[b] - first for b in order]
        prob_b = [
            probs[pair, :, STARTS[b] + first : STARTS[b] + first + span] for b, span in zip(order, spans)
        ]
        grad_prob = [nt(one, values[first : first + span, lane]) for one, span in zip(stack_g, spans)]
        part_values = [tn(one, two) for one, two in zip(stack_g, prob_b)]
        prob = [item.astype(F32) for item in prob_b]
        inner = [jnp.sum(one * two, -1, keepdims=True) for one, two in zip(prob, grad_prob)]
        grad_score = [
            (one * (two - three)).astype(BF16) for one, two, three in zip(prob, grad_prob, inner)
        ]
        turned = [nn(flipped, item) for item in grad_score]
        found_u = [nn(item, keys[first : first + span, lane]) for item, span in zip(grad_score, spans)]
        part_keys = [tn(one, two) for one, two in zip(stack_u, grad_score)]
        grad_full = [shift(item, 0).astype(BF16) for item in turned]
        found_v = [nn(item, rel[ROWS - span : ROWS, lane]) for item, span in zip(grad_full, spans)]
        part_rel = [tn(one, two) for one, two in zip(stack_v, grad_full)]
        for index, b in enumerate(order):
            span = spans[index]
            rows = pl.ds(BLOCK * b, BLOCK)
            grad_qu[rows, lane] = pick_heads(found_u[index]) * SCALE
            grad_qv[rows, lane] = pick_heads(found_v[index]) * SCALE
            if b == 3:
                acc_keys[lane, first:] = part_keys[index]
                acc_values[lane, first:] = part_values[index]
                acc_rel[lane, ROWS - span :] = part_rel[index]
                if first:
                    blank = jnp.zeros((BLOCK, first), F32)
                    acc_keys[lane, 0:first] = blank
                    acc_values[lane, 0:first] = blank
                    acc_rel[lane, 0 : ROWS - span] = blank
            else:
                acc_keys[lane, first : first + span] += part_keys[index]
                acc_values[lane, first : first + span] += part_values[index]
                acc_rel[lane, ROWS - span : ROWS] += part_rel[index]
        return carry

    for first in (0, MEM):

        @pl.when((segment == 0) == (first > 0))
        def _():
            lax.fori_loop(0, 2, functools.partial(one_pair, first), 0)

    grad_keys[...] = jnp.transpose(acc_keys[...]).astype(BF16)
    grad_values[...] = jnp.transpose(acc_values[...]).astype(BF16)
    grad_rel = jnp.transpose(acc_rel[...]).astype(BF16)
    sums[...] = jnp.zeros_like(sums)
    sums[2:3, :] = jnp.sum(grad_qu[...], 0, keepdims=True)
    sums[3:4, :] = jnp.sum(grad_qv[...], 0, keepdims=True)
    flip_one = flip[0:BLOCK, 0:BLOCK]
    for b in range(4):
        rows = pl.ds(BLOCK * b, BLOCK)
        part = grad_qv[rows, :]
        high = part.astype(BF16)
        low = (part - high.astype(F32)).astype(BF16)
        grad_query[rows, :] = (grad_qu[rows, :] + nn(flip_one, high) + nn(flip_one, low)).astype(BF16)
    for copy in late:
        copy.wait()
    cols = slice(256, 512) if second else slice(None)
    staged[1, :, cols] = tn(normed[...], grad_keys[...]).astype(BF16)
    staged[2, :, cols] = tn(normed[...], grad_values[...]).astype(BF16)
    staged[3, :, cols] = tn(table[...], grad_rel).astype(BF16)
    staged[0, :, cols] = tn(normed[MEM:, :], grad_query[...]).astype(BF16)
    if second:
        place, half = scalars[0], scalars[1]
        units = [(staged.at[u], 16 * u) for u in range(4)]
        scatter_units(bits, place, half, keep, units, 16)
        scatter_units(bits, place, 1 - half, send, units, 16)


def input_grads(bits, base, *refs):
    last_kernel = base == 0
    weights, weights_sem = refs[-2:]
    refs = refs[:-2]
    weights_copies = [
        fetch(refs[1].at[pl.ds(WEIGHTS_AT + D * u, D)], weights.at[u], weights_sem.at[u]) for u in range(3)
    ]
    (scalars, saved, query_a, keys_a, values_a, sums_a, query_b, keys_b, values_b, sums_b, grad_mixed, vecs) = refs[:12]
    if last_kernel:
        (frames, gain_two, vecs_one, gain_two_one, gain_final, keep, send,
         joined, smalls, staged, sem, small, small_sem) = refs[12:]
        fetch(saved.at[pl.ds(SMALL_AT, D), pl.ds(0, BLOCK)], small, small_sem).wait()
        joined[...] = nt(frames[...], small[...])
        before, here, first = joined, joined, MEM
    else:
        (memory, hidden, grad_hidden, grad_vecs) = refs[12:]
        before, here, first = memory, hidden, 0
    place, half = scalars[0], scalars[1]
    gain = vecs[base : base + 1, :]
    left, right = slice(0, 256), slice(256, 512)
    for copy in weights_copies:
        copy.wait()
    grad_keys = (
        nt(keys_a[...], weights[1, :, left])
        + nt(keys_b[...], weights[1, :, right])
        + nt(values_a[...], weights[2, :, left])
        + nt(values_b[...], weights[2, :, right])
    )
    grad_query = nt(query_a[...], weights[0, :, left]) + nt(query_b[...], weights[0, :, right])
    unit, inverse = norm_parts(before[0:MEM, :])
    grad_gain = jnp.sum(grad_keys[0:MEM] * unit, 0, keepdims=True)
    unit, inverse = norm_parts(here[first : first + SEG, :])
    grad_joined, gains = norm_back(unit, inverse, gain, grad_keys[MEM:] + grad_query)
    grad_gain = grad_gain + gains
    grad_in = grad_mixed[...] + grad_joined
    if last_kernel:
        smalls[...] = tn(frames[MEM:, :], grad_in.astype(BF16))
        smalls[80:81, :] = grad_gain
        smalls[81:82, :] = gain_two[0:1, :]
        smalls[82:84, left] = sums_a[2:4, :]
        smalls[82:84, right] = sums_b[2:4, :]
        smalls[84:88, :] = vecs_one[0:4, :]
        smalls[85:86, :] = gain_two_one[0:1, :]
        smalls[88:89, :] = gain_final[0:1, :]
        staged[...] = jnp.zeros_like(staged)
        staged[:, 0:BLOCK] = jnp.transpose(smalls[...]).astype(BF16)
        units = [(staged, 0)]
        scatter_units(bits, place, half, keep, units, 16)
        scatter_units(bits, place, 1 - half, send, units, 16)
    else:
        grad_hidden[...] = grad_in
        grad_vecs[:, left] = sums_a[...]
        grad_vecs[:, right] = sums_b[...]
        grad_vecs[0:1, :] = grad_gain


def feed_weights(bits, place, both, up, down, out):
    for units, rows in (
        ([(out, 128)], 16),
        ([(item, 16 * u) for u, item in enumerate(columns(up, 4))], 16),
        ([(down, 64)], 64),
    ):
        for which, pieces in both:
            gather_units(bits, place, which, pieces, units, rows)


def feed_mixed(residual, attended, out, gain, mixed, normed):
    mixed[...] = residual[...] + nn(attended[...], out[...])
    for b in range(2):
        rows = pl.ds(256 * b, 256)
        unit, unused = norm_parts(mixed[rows, :])
        normed[rows, :] = (unit * gain).astype(BF16)


def feed_inner(normed, up, active, slope):
    later = nn(normed[...], up[:, 0:512])
    for u in range(4):
        inner = later
        if u < 3:
            later = nn(normed[...], up[:, 512 * (u + 1) : 512 * (u + 2)])
        square = inner * inner
        bent = jnp.tanh(0.7978845608028654 * (inner + 0.044715 * (square * inner)))
        half = 0.5 * (1.0 + bent)
        active[:, 512 * u : 512 * (u + 1)] = (inner * half).astype(BF16)
        slope[:, 512 * u : 512 * (u + 1)] = (
            half
            + (0.5 * inner)
            * (1.0 - bent * bent)
            * (0.7978845608028654 * (1.0 + (3 * 0.044715) * square))
        ).astype(BF16)


def feed_output(mixed, active, down, output):
    output[...] = mixed[...] + nn(active[...], down[...])


def feed_forward(bits, base, scalars, residual, attended, vecs, own_low, own_high, other_low, other_high,
                 output, memory, mixed_o, saved,
                 mixed, normed, active, slope, up, down, out, sem, out_sem):
    place, half = scalars[0], scalars[1]
    both = ((half, (own_low, own_high)), (1 - half, (other_low, other_high)))
    feed_weights(bits, place, both, up, down, out)
    outs = [fetch(out, saved.at[pl.ds(OUT_AT, D)], out_sem.at[0])]
    feed_mixed(residual, attended, out, vecs[base + 1 : base + 2, :], mixed, normed)
    outs.append(fetch(normed, saved.at[pl.ds(0, SEG)], out_sem.at[1]))
    outs.append(fetch(mixed, mixed_o, out_sem.at[2]))
    outs += [
        fetch(item, saved.at[pl.ds(UP_AT + D * u, D)], out_sem.at[4 + u])
        for u, item in enumerate(columns(up, 4))
    ]
    feed_inner(normed, up, active, slope)
    for u in range(4):
        cols = pl.ds(D * u, D)
        outs.append(fetch(active.at[:, cols], saved.at[pl.ds(ACTIVE_AT + D * u, D)], out_sem.at[8 + u]))
        outs.append(fetch(slope.at[:, cols], saved.at[pl.ds(SLOPE_AT + D * u, D)], out_sem.at[12 + u]))
    outs.append(fetch(down, saved.at[pl.ds(DOWN_AT, FF)], out_sem.at[3]))
    feed_output(mixed, active, down, output)
    memory[...] = output[SEG - MEM :, :]
    for copy in outs:
        copy.wait()


def feed_back(moves, bits, place, half, keep, send, sem, base, grad_out, mixed, vecs, attended, normed,
              active, slope, up, down, out, grad_mixed, grad_att, grad_gain,
              grad_inner, staged_up, staged_down, staged_out):
    both = ((half, keep), (1 - half, send))
    grad_y = grad_out[...].astype(BF16)
    for copy in moves[:1]:
        copy.wait()
    later = nt(grad_y, down[0:512, :])
    for copy in moves[1:10]:
        copy.wait()
    for u in range(4):
        cols = slice(512 * u, 512 * (u + 1))
        part = later
        if u < 3:
            later = nt(grad_y, down[512 * (u + 1) : 512 * (u + 2), :])
        staged_down[cols, :] = tn(active[:, cols], grad_y).astype(BF16)
        grad_inner[:, cols] = (part * slope[:, cols].astype(F32)).astype(BF16)
    for copy in moves[10:]:
        copy.wait()
    grad_normed = nt(grad_inner[...], up[...])
    for which, pieces in both:
        scatter_units(bits, place, which, pieces, [(staged_down, 64)], 64)
    for u in range(4):
        cols = slice(512 * u, 512 * (u + 1))
        staged_up[:, cols] = tn(normed[...], grad_inner[:, cols]).astype(BF16)
    unit, inverse = norm_parts(mixed[...])
    grad_here, gains = norm_back(unit, inverse, vecs[base + 1 : base + 2, :], grad_normed)
    grad = grad_out[...] + grad_here
    grad_mixed[...] = grad
    grad_b = grad.astype(BF16)
    for which, pieces in both:
        units = [(item, 16 * u) for u, item in enumerate(columns(staged_up, 4))]
        scatter_units(bits, place, which, pieces, units, 16)
    grad_att[...] = nt(grad_b, out[...]).astype(BF16)
    staged_out[...] = tn(attended[...], grad_b).astype(BF16)
    for which, pieces in both:
        scatter_units(bits, place, which, pieces, [(staged_out, 128)], 16)
    grad_gain[...] = jnp.broadcast_to(gains, grad_gain.shape)


def feed_backward(bits, base, scalars, grad_out, vecs, mixed_h, probs_h, saved,
                  keep, send, grad_mixed, grad_att, grad_gain, mixed, attended,
                  normed, active, slope, up, down, out, grad_inner, staged_up, staged_down, staged_out,
                  in_sem, sem):
    pairs = [(saved.at[pl.ds(DOWN_AT, FF)], down)]
    for u in range(4):
        pairs.append((saved.at[pl.ds(SLOPE_AT + D * u, D)], slope.at[:, pl.ds(D * u, D)]))
    for u in range(4):
        pairs.append((saved.at[pl.ds(ACTIVE_AT + D * u, D)], active.at[:, pl.ds(D * u, D)]))
    pairs.append((saved.at[pl.ds(0, SEG)], normed))
    for u in range(4):
        pairs.append((saved.at[pl.ds(UP_AT + D * u, D)], columns(up, 4)[u]))
    pairs.append((saved.at[pl.ds(OUT_AT, D)], out))
    pairs.append((mixed_h, mixed))
    for b in range(2):
        pairs.append((probs_h.at[PAIRS + b, :, pl.ds(0, D)], attended.at[pl.ds(256 * b, 256)]))
    moves = [fetch(there, here, in_sem.at[index]) for index, (there, here) in enumerate(pairs)]
    feed_back(moves, bits, scalars[0], scalars[1], keep, send, sem, base, grad_out, mixed, vecs, attended, normed,
              active, slope, up, down, out, grad_mixed, grad_att, grad_gain,
              grad_inner, staged_up, staged_down, staged_out)


def top_kernel(bits, streams, scalars, residual, attended, targets, vecs, own_low, own_high, other_low, other_high,
               keep, send, grad_mixed, grad_att, grad_gain, final_gain, loss,
               normed, active, slope, up, down, out, mixed, output, grad_out, table, final, grad_logits, staged,
               grad_inner, staged_up, staged_down, staged_out, head_sem, sem, out_sem):
    place, half, length, segment = scalars[0], scalars[1], scalars[2], scalars[3]
    both = ((half, (own_low, own_high)), (1 - half, (other_low, other_high)))
    feed_weights(bits, place, both, up, down, out)
    units = [(item, 144 + 16 * u) for u, item in enumerate(columns(table, 2))]
    for which, pieces in both:
        gather_units(bits, place, which, pieces, units, 16)
    feed_mixed(residual, attended, out, vecs[5:6, :], mixed, normed)
    feed_inner(normed, up, active, slope)
    feed_output(mixed, active, down, output)
    size = length.astype(F32)
    codes = jnp.transpose(jnp.broadcast_to(targets[...].astype(F32), (BLOCK, SEG))).astype(jnp.int32)
    gain = vecs[8:9, :]
    gains = jnp.zeros((1, D), F32)
    terms = jnp.zeros((1, 1), F32)
    spans = (slice(0, 256), slice(256, 512))
    parts = [norm_parts(output[rows, :]) for rows in spans]
    fins = [(unit * gain).astype(BF16) for unit, unused in parts]
    logits = [nn(fin, table[...]) for fin in fins]
    for rows, fin in zip(spans, fins):
        final[rows, :] = fin
    grad_finals = []
    for b, rows in enumerate(spans):
        logit = logits[b]
        most = jnp.max(logit, -1, keepdims=True)
        expo = jnp.exp(logit - most)
        total = jnp.sum(expo, -1, keepdims=True)
        picks = lax.broadcasted_iota(jnp.int32, logit.shape, 1) == codes[rows, 0:1]
        picked = jnp.sum(jnp.where(picks, logit, 0.0), -1, keepdims=True)
        spot = segment * SEG + 256 * b + lax.broadcasted_iota(jnp.int32, (256, 1), 0)
        weight = jnp.where(spot < length, 1.0 / size, 0.0)
        terms = terms + jnp.sum((most + jnp.log(total) - picked) * weight, keepdims=True)
        grad = (expo * (1.0 / total) - jnp.where(picks, 1.0, 0.0)) * (weight * (1.0 / streams))
        grad_logits[rows, :] = grad.astype(BF16)
        grad_finals.append(nt(grad_logits[rows, :], table[...]))
    staged[...] = tn(final[...], grad_logits[...]).astype(BF16)
    for (unit, inverse), rows, grad_final in zip(parts, spans, grad_finals):
        grad_here, gain_here = norm_back(unit, inverse, gain, grad_final)
        grad_out[rows, :] = grad_here
        gains = gains + gain_here
    units = [(item, 144 + 16 * u) for u, item in enumerate(columns(staged, 2))]
    scatter_units(bits, place, half, keep, units, 16)
    scatter_units(bits, place, 1 - half, send, units, 16)
    final_gain[...] = jnp.broadcast_to(gains, final_gain.shape)
    loss[...] = jnp.broadcast_to(terms, loss.shape)
    feed_back((), bits, place, half, keep, send, out_sem, 4, grad_out, mixed, vecs, attended, normed,
              active, slope, up, down, out, grad_mixed, grad_att, grad_gain,
              grad_inner, staged_up, staged_down, staged_out)


def finish(counts, *refs):
    scalars, loss = refs[0], refs[1]
    total_count = sum(counts)
    sources = refs[2 : 2 + total_count]
    kept, sent, total = refs[2 + total_count : 5 + total_count]
    buffers, sem = refs[5 + total_count : -1], refs[-1]
    moves = [fetch(there.at[0], here, sem.at[index]) for index, (there, here) in enumerate(zip(sources, buffers))]
    for copy in moves:
        copy.wait()
    sums = []
    start = 0
    for count in counts:
        item = buffers[start][...].astype(F32)
        for other in buffers[start + 1 : start + count]:
            item = item + other[...].astype(F32)
        sums.append(item)
        start += count
    attn_zero, feed_zero, attn_one, feed_one, small = sums[0], sums[1], sums[2], sums[3], sums[4]
    attn_zero = attn_zero + sums[5][0:64]
    small = small + sums[5][64:80]
    first = scalars[1] == 0
    lone = jnp.zeros((1, 1), F32)
    for zero, one, rows, begin in ((attn_zero, attn_one, 64, 0), (feed_zero, feed_one[0:144], 144, 64)):
        kept[begin : begin + rows, :] = jnp.where(first, zero, one)
        sent[begin : begin + rows, :] = jnp.where(first, one, zero)
        lone = lone + jnp.sum(zero * zero + one * one, keepdims=True)
    head = feed_one[144:176]
    lone = lone + jnp.sum(head * head, keepdims=True) + jnp.sum(small * small, keepdims=True)
    for target in (kept, sent):
        target[208:240, :] = head
        target[240:256, :] = small
    column = lax.broadcasted_iota(jnp.int32, (8, 128), 1)
    total[...] = jnp.where(column == 0, lone, 0.0) + jnp.where(column == 1, loss[...], 0.0)


def adam_step(weight, grad, first, second, rate, decay, factor):
    grad = grad * factor
    first = 0.9 * first + 0.1 * grad
    second = 0.999 * second + 0.001 * grad * grad
    ratio = first / (1.0 - 0.9**STEP) / (jnp.sqrt(second / (1.0 - 0.999**STEP)) + 1e-08)
    return (weight - rate * (ratio + decay * weight), first, second)


def update(scalars, total, kept, got, *refs):
    ins, outs, small = refs[:27], refs[27:56], refs[56]
    first = scalars[1] == 0
    squares = jnp.sum(total[0:1, 0:1], keepdims=True)
    norm = jnp.sqrt(squares)
    outs[27][...] = norm
    outs[28][...] = total[0:1, 1:2]
    factor = jnp.minimum(1.0, CLIP / (norm + 1e-06))

    def half_of(half, start, rows):
        here, there = kept[start : start + rows, :], got[start : start + rows, :]
        return jnp.where(first == (half == 0), here, there)

    def apply(index, spot, grad, rate, decay):
        results = adam_step(
            ins[index][spot], grad, ins[9 + index][spot], ins[18 + index][spot], rate, decay, factor
        )
        for which, result in enumerate(results):
            outs[9 * which + index][spot] = result

    for half in range(2):
        rows = slice(16 * half, 16 * half + 16)
        for u in range(3):
            apply(0, (0, rows, slice(D * u, D * (u + 1))), half_of(half, 16 * u, 16), 0.03, 0.01)
        apply(1, (0, rows, slice(None)), half_of(half, 192, 16), 0.03, 0.01)
        apply(2, (0, rows, slice(None)), half_of(half, 48, 16), 0.03, 0.01)
        for u in range(4):
            apply(3, (0, rows, slice(D * u, D * (u + 1))), half_of(half, 64 + 16 * u, 16), 0.03, 0.01)
        apply(4, (0, slice(64 * half, 64 * half + 64), slice(None)), half_of(half, 128, 64), 0.03, 0.01)
        for u in range(2):
            apply(7, (rows, slice(D * u, D * (u + 1))), half_of(half, 208 + 16 * u, 16), 0.03, 0.01)
        small[rows, :] = half_of(half, 240, 16)[:, 0:BLOCK]
    small[32:, :] = jnp.zeros((BLOCK - 32, BLOCK), F32)
    turned = jnp.transpose(small[...])
    apply(6, (slice(None), slice(None)), small[0:32, 0:FEATS], 0.03, 0.01)
    vecs = jnp.where(first, turned[80:84, 0:32], turned[84:88, 0:32])
    apply(5, (0, slice(None), slice(None)), vecs, 0.3, 0.0)
    apply(8, (slice(None), slice(None)), turned[88:89, 0:32], 0.3, 0.0)


def pack_shards(scalars, attn, out, pos, up, down, vecs, w_in, head, gain, kept, sent, codes, small):
    half, section = scalars[1], scalars[3]
    small[...] = jnp.zeros_like(small)
    small[88:89, 0:32] = gain[...]
    small[pl.ds(FEATS + 4 * section, 4), 0:32] = vecs[0]
    turned = jnp.transpose(small[...])[0:32]
    turned = jnp.concatenate([w_in[...], turned[:, FEATS:]], 1)
    column = lax.broadcasted_iota(jnp.int32, turned.shape, 1)
    shared = (column < FEATS) | (column == 88)
    for which, target in ((half, kept), (1 - half, sent)):
        rows = pl.ds(pl.multiple_of(16 * which, 16), 16)
        for u in range(3):
            target[16 * u : 16 * u + 16, :] = attn[0, rows, D * u : D * (u + 1)].astype(BF16)
        target[48:64, :] = pos[0, rows, :].astype(BF16)
        for u in range(4):
            target[80 + 16 * u : 96 + 16 * u, :] = up[0, rows, D * u : D * (u + 1)].astype(BF16)
        target[144:208, :] = down[0, pl.ds(pl.multiple_of(64 * which, 64), 64), :].astype(BF16)
        target[208:224, :] = out[0, rows, :].astype(BF16)
        tail = jnp.where(half == 0, turned[0:16], turned[16:32])
        if target is sent:
            tail = jnp.where(half == 0, turned[16:32], turned[0:16])
            tail = jnp.where(shared[0:16], 0.0, tail)
        target[64:80, :] = jnp.zeros((16, D), BF16)
        target[64:80, 0:BLOCK] = tail.astype(BF16)
    rows = pl.ds(pl.multiple_of(16 * half, 16), 16)
    for u in range(2):
        codes[16 * u : 16 * u + 16, :] = head[rows, D * u : D * (u + 1)].astype(BF16)


VMEM = pl.BlockSpec(memory_space=pltpu.VMEM)
ANY = pl.BlockSpec(memory_space=pl.ANY)
HBM = pl.BlockSpec(memory_space=pltpu.HBM)
SMEM = pl.BlockSpec(memory_space=pltpu.SMEM)
DMA = pltpu.SemaphoreType.DMA


def shape(*dims, dtype=F32):
    return jax.ShapeDtypeStruct(dims, dtype)


def half_shape(*dims):
    return jax.ShapeDtypeStruct(dims, BF16)


def held(*dims):
    return pltpu.VMEM(dims, BF16)


def wide(*dims):
    return pltpu.VMEM(dims, F32)


def call(body, name, ins, outs, out_specs, scratch, micros, limit):
    return pl.pallas_call(
        body,
        name=name,
        in_specs=ins,
        out_shape=outs,
        out_specs=out_specs,
        scratch_shapes=scratch,
        compiler_params=pltpu.CompilerParams(vmem_limit_bytes=limit * 1024 * 1024),
        cost_estimate=pl.CostEstimate(flops=micros * 1_150_000_000, bytes_accessed=1 << 20, transcendentals=0),
    )


QUERY_KEY = (half_shape(SEG, D), half_shape(SEG, D), half_shape(ROWS, D), half_shape(ROWS, D), half_shape(ROWS, D))
PROJECT_HELD = [held(ROWS, D), held(4, D, D), DMA, DMA((12,))]
KEPT = half_shape(KEPT_ROWS, D)


def run_project_first(bits, scalars, frames, pieces, table):
    result = call(
        functools.partial(project, bits, 0),
        "project_first",
        [SMEM] + [VMEM] * 6,
        QUERY_KEY + (shape(SEG, D), shape(16, D), KEPT),
        [VMEM] * 7 + [HBM],
        PROJECT_HELD + [wide(ROWS, D), held(D, BLOCK), DMA],
        6,
        40,
    )(scalars, frames, *pieces, table)
    return result[:5], result[5], result[6], result[7]


def run_project(bits, scalars, memory, hidden, vecs, pieces, table):
    result = call(
        functools.partial(project, bits, 4),
        "project",
        [SMEM] + [VMEM] * 8,
        QUERY_KEY + (KEPT,),
        [VMEM] * 5 + [HBM],
        PROJECT_HELD,
        6,
        40,
    )(scalars, memory, hidden, vecs, *pieces, table)
    return result[:5], result[5]


def run_attend(scalars, projected):
    return call(
        attend,
        "attend",
        [SMEM] + [VMEM] * 5,
        (half_shape(SEG, D), half_shape(KEPT_PAIRS, 2 * BLOCK, WIDE)),
        [VMEM, HBM],
        [held(PAIRS, 2 * BLOCK, WIDE), DMA((PAIRS + 2,))],
        11,
        44,
    )(scalars, *projected)


HALF_HELD = [
    held(SEG, 256), held(SEG, 256), held(ROWS, 256), held(ROWS, 256), held(ROWS, 256),
    held(2, 2 * BLOCK, WIDE), held(2 * BLOCK, 2 * BLOCK),
    wide(256, ROWS), wide(256, ROWS), wide(256, ROWS), wide(SEG, 256), wide(SEG, 256), DMA((2, 6)),
]
LATE_HELD = [held(ROWS, D), held(ROWS, D), DMA((2,))]
HALF_OUT = (half_shape(SEG, 256), half_shape(ROWS, 256), half_shape(ROWS, 256))


def run_attend_back(bits, scalars, grad_att, saved, table, probs):
    result = call(
        functools.partial(attend_back, bits, False),
        "attend_back",
        [SMEM, VMEM] + [HBM] * 3,
        HALF_OUT + (half_shape(4, D, 256), shape(8, 256)),
        [VMEM] * 5,
        HALF_HELD + LATE_HELD,
        9,
        40,
    )(scalars, grad_att, table, saved, probs)
    return (*result[:3], result[4]), result[3]


def run_attend_back_rest(bits, scalars, grad_att, saved, table, probs, staged):
    result = call(
        functools.partial(attend_back, bits, True),
        "attend_back_rest",
        [SMEM, VMEM] + [HBM] * 3 + [VMEM],
        HALF_OUT + (shape(8, 256), half_shape(GROUPS, 64, D), half_shape(GROUPS, 64, D)),
        [VMEM] * 6,
        HALF_HELD + [held(4, D, D), DMA] + LATE_HELD,
        10,
        42,
    )(scalars, grad_att, table, saved, probs, staged)
    return result[:4], result[4], result[5]


def run_input_grads(bits, scalars, saved, grads, grad_mixed, vecs, memory, hidden):
    return call(
        functools.partial(input_grads, bits, 4),
        "input_grads",
        [SMEM, HBM] + [VMEM] * 12,
        (shape(SEG, D), shape(8, D)),
        [VMEM] * 2,
        [held(4, D, D), DMA((3,))],
        5,
        40,
    )(scalars, saved, *grads, grad_mixed, vecs, memory, hidden)


def run_input_grads_last(bits, scalars, saved, grads, grad_mixed, vecs, frames, *small_grads):
    return call(
        functools.partial(input_grads, bits, 0),
        "input_grads_last",
        [SMEM, HBM] + [VMEM] * 15,
        (half_shape(GROUPS, 16, D), half_shape(GROUPS, 16, D)),
        [VMEM] * 2,
        [wide(ROWS, D), wide(BLOCK, D), held(D, D), DMA, held(D, BLOCK), DMA, held(4, D, D), DMA((3,))],
        5,
        40,
    )(scalars, saved, *grads, grad_mixed, vecs, frames, *small_grads)


FEED_HELD = [held(SEG, D), held(SEG, FF), held(SEG, FF), held(D, FF), held(FF, D), held(D, D)]
BACK_HELD = [held(SEG, FF), held(D, FF), held(FF, D), held(D, D)]


def run_feed_forward(bits, base, scalars, residual, attended, vecs, pieces):
    result = call(
        functools.partial(feed_forward, bits, base),
        "feed_forward",
        [SMEM] + [VMEM] * 7,
        (shape(SEG, D), shape(MEM, D), shape(SEG, D), KEPT),
        [VMEM] * 2 + [HBM] * 2,
        [wide(SEG, D)] + FEED_HELD + [DMA((3,)), DMA((16,))],
        9,
        46,
    )(scalars, residual, attended, vecs, *pieces)
    return result


def run_feed_backward(bits, base, scalars, grad_out, vecs, mixed, probs, saved):
    return call(
        functools.partial(feed_backward, bits, base),
        "feed_backward",
        [SMEM, VMEM, VMEM] + [HBM] * 3,
        (half_shape(GROUPS, 144, D), half_shape(GROUPS, 144, D), shape(SEG, D), half_shape(SEG, D), shape(8, D)),
        [VMEM] * 5,
        [wide(SEG, D), held(SEG, D)] + FEED_HELD + BACK_HELD + [DMA((18,)), DMA((3,))],
        13,
        44,
    )(scalars, grad_out, vecs, mixed, probs, saved)


def run_top(bits, streams, scalars, residual, attended, targets, vecs, pieces):
    return call(
        functools.partial(top_kernel, bits, streams),
        "top_kernel",
        [SMEM] + [VMEM] * 8,
        (
            half_shape(GROUPS, 176, D), half_shape(GROUPS, 176, D),
            shape(SEG, D), half_shape(SEG, D), shape(8, D), shape(8, D), shape(8, 128),
        ),
        [VMEM] * 7,
        FEED_HELD
        + [wide(SEG, D), wide(SEG, D), wide(SEG, D), held(D, CODES), held(SEG, D), held(SEG, CODES), held(D, CODES)]
        + BACK_HELD
        + [DMA, DMA((3,)), DMA((3,))],
        21,
        42,
    )(scalars, residual, attended, targets, vecs, *pieces)


def run_finish(scalars, loss, *sums):
    counts = tuple((len(item) for item in sums))
    flat = [item for group in sums for item in group]
    return call(
        functools.partial(finish, counts),
        "finish",
        [SMEM, VMEM] + [ANY] * len(flat),
        (shape(256, D), shape(256, D), shape(8, 128)),
        [VMEM] * 3,
        [pltpu.VMEM(item.shape[1:], item.dtype) for item in flat] + [DMA((len(flat),))],
        3,
        40,
    )(scalars, loss, *flat)


def run_update(scalars, total, kept, got, state):
    flat = [item[None] if item.ndim == 1 else item for item in state]
    for index in (6, 15, 24):
        flat[index] = jnp.transpose(flat[index])
    result = call(
        update,
        "update",
        [SMEM] + [VMEM] * 30,
        tuple((shape(*item.shape) for item in flat)) + (shape(1, 1), shape(1, 1)),
        [VMEM] * 29,
        [wide(BLOCK, BLOCK)],
        5,
        24,
    )(scalars, total, kept, got, *flat)
    result = list(result)
    for index in (6, 15, 24):
        result[index] = jnp.transpose(result[index])
    return [item.reshape(old.shape) for item, old in zip(result, state)] + [result[27][0, 0], result[28][0, 0]]


def run_pack(scalars, w_attn, w_out, w_pos, w_up, w_down, layer_vecs, w_in, w_head, gain_final):
    return call(
        pack_shards,
        "pack_shards",
        [SMEM] + [VMEM] * 9,
        (half_shape(224, D), half_shape(224, D), half_shape(32, D)),
        [VMEM] * 3,
        [wide(BLOCK, BLOCK)],
        3,
        56,
    )(scalars, w_attn, w_out, w_pos, w_up, w_down, layer_vecs, jnp.transpose(w_in), w_head, gain_final[None])


def swap_parts(value):
    half = value.shape[0] // 2
    return jnp.concatenate([swap(value[:half]), swap(value[half:])], 0)


def spread(value, bits):
    count = lax.axis_size("dp")
    pairs = [
        (half * count + i, half * count + (i ^ bit)) for half, bit in enumerate(bits) for i in range(count)
    ]
    return lax.ppermute(value, ("section", "dp"), pairs)


def swap(value):
    return lax.ppermute(value, "section", [(0, 1), (1, 0)])


def fence(*values):
    return lax.optimization_barrier(values)


def joined(low, got):
    return jnp.concatenate([low, got], 0)


def part(sources, first, last):
    total = sources[0][first:last].astype(F32)
    for item in sources[1:]:
        total = total + item[first:last].astype(F32)
    return total


def shrink(chunks, pair, merged=()):
    count = (merged or chunks[0])[-1].shape[0]
    sent, first = [], 0
    for item in chunks:
        rows = item[0].shape[1]
        total = part(item, count // 2, count)
        if merged:
            total = total + part([other[:, first : first + rows] for other in merged], count // 2, count)
        sent.append(total.astype(BF16))
        first += rows
    return spread(jnp.concatenate(sent, 1), pair)


def add_up(value, bits):
    value = value + swap(value)
    steps = [low for low, unused in zip(*bits)]
    for one, two in zip(steps[0::2], steps[1::2]):
        first, second, third = (spread(value, (step, step)) for step in (one, two, one + two))
        value = (value + first) + (second + third)
    return value


def lanes_of(block):
    return [block[:, D * u : D * (u + 1)] for u in range(block.shape[1] // D)]


def sinus_table(where_at):
    freqs = jnp.exp(-jnp.log(10000.0) * (2.0 * jnp.arange(D // 2, dtype=jnp.int32).astype(F32) / D))
    angles = where_at * freqs[None, :]
    return jnp.concatenate([jnp.sin(angles), jnp.cos(angles)], 1).astype(BF16)


def split_shards(section, scalars, params):
    kept, sent, head = run_pack(scalars, *params)
    got = swap(sent)
    first = section == 0
    row = lax.broadcasted_iota(jnp.int32, (80, D), 0)
    attn = jnp.where(row < 64, jnp.where(first, kept[:80], got[:80]), kept[:80] + got[:80])
    zero = jnp.where(first, kept[80:], got[80:])
    one = jnp.where(first, got, kept)
    return attn, zero, one[:64], jnp.concatenate([one[80:], head], 0)


def halves(whole, rows):
    return whole.reshape(GROUPS, 2, rows, whole.shape[1]).transpose(1, 0, 2, 3)


def gather_whole(section, w_attn, w_out, w_pos, w_up, w_down, layer_vecs, w_in, w_head, gain_final):
    def over(value, axis):
        return lax.all_gather(value.astype(BF16), "dp", axis=axis, tiled=True)

    def layers(value):
        return lax.all_gather(over(value[0], 0), "section", axis=0)

    attn, out, pos, up, down = (layers(item) for item in (w_attn, w_out, w_pos, w_up, w_down))
    vecs = lax.all_gather(over(layer_vecs[0], 1), "section", axis=0)
    small = jnp.concatenate(
        [over(w_in, 1), vecs[0], vecs[1], over(gain_final, 0)[None], jnp.zeros((BLOCK - 89, D), BF16)], 0
    )
    small = jnp.pad(jnp.transpose(small), ((0, 0), (0, D - BLOCK)))
    head = over(w_head, 0)

    def pieces(units):
        both = jnp.concatenate([halves(item, item.shape[0] // 32) for item in units], 2)
        own = lax.dynamic_index_in_dim(both, section, 0, keepdims=False)
        other = lax.dynamic_index_in_dim(both, 1 - section, 0, keepdims=False)
        return (own[:8], own[8:], other[:8], other[8:])

    return (
        pieces(lanes_of(attn[0]) + [pos[0], small]),
        pieces(lanes_of(up[0]) + [down[0], out[0]]),
        pieces(lanes_of(attn[1]) + [pos[1]]),
        pieces(lanes_of(up[1]) + [down[1], out[1]] + lanes_of(head)),
    )


def whole_grads(section, sums):
    count = lax.axis_size("dp")
    place = lax.axis_index("dp")
    attn_zero, feed_zero, attn_one, feed_one, small = (
        lax.all_gather(lax.psum(item, "dp"), "section", axis=0) for item in sums
    )

    def unit(both, start, rows):
        item = both[:, :, start : start + rows]
        return item.transpose(1, 0, 2, 3).reshape(GROUPS * 2 * rows, both.shape[3])

    def layer(attn, feed):
        return (
            jnp.concatenate([unit(attn, 16 * u, 16) for u in range(3)], 1),
            unit(feed, 128, 16),
            unit(attn, 48, 16),
            jnp.concatenate([unit(feed, 16 * u, 16) for u in range(4)], 1),
            unit(feed, 64, 64),
        )

    small = jnp.transpose(unit(small, 0, 16))
    zero = layer(attn_zero, feed_zero) + (small[80:84],)
    one = layer(attn_one, feed_one) + (small[84:88],)
    ends = (small[:80], jnp.concatenate([unit(feed_one, 144 + 16 * u, 16) for u in range(2)], 1), small[88])
    squares = sum((jnp.sum(item * item) for item in zero + one + ends))
    dims = (0, 0, 0, 0, 0, 1, 1, 0, 0)
    grads = tuple((jnp.where(section == 0, a, b) for a, b in zip(zero, one))) + ends
    return squares, tuple(
        (
            lax.dynamic_slice_in_dim(item, place * (item.shape[dim] // count), item.shape[dim] // count, dim)
            for item, dim in zip(grads, dims)
        )
    )


def local(frames, targets, lengths, *state):
    params, firsts, seconds = (state[:9], state[9:18], state[18:])
    section = lax.axis_index("section")
    streams = lax.axis_size("dp")
    ringed = streams == GROUPS
    place = lax.axis_index("dp") if ringed else jnp.int32(0)
    length = lengths[0]
    scalars = jnp.stack([place, section, length, section]).astype(jnp.int32)
    count_down = (ROWS - 1 - jnp.arange(ROWS, dtype=jnp.int32)).astype(F32)[:, None]
    rows = lax.dynamic_slice_in_dim(
        jnp.pad(frames[0], ((MEM, 0), (0, BLOCK - FEATS))), section * SEG, ROWS, 0
    )
    codes = lax.dynamic_slice_in_dim(targets, section * SEG, SEG, 1)
    if ringed:
        bits = ((8, 4, 1, 2), (8, 4, 2, 1))
        far, near, side, last = zip(*bits)
        zero, one, two, three = (item[None] for item in split_shards(section, scalars, params))
        zero, got, count_down = fence(zero, spread(zero, far), count_down)
        table = sinus_table(count_down)
        zero = joined(zero, got)
        zero, got, one = fence(zero, spread(zero, near), one)
        zero = joined(zero, got)
        one_got = spread(one, far)
        zero, got, two, one, one_got, rows, table, codes = fence(
            zero, spread(zero, side), two, one, one_got, rows, table, codes
        )
        zero = joined(zero, got)
        high = spread(zero, last)
        one = joined(one, one_got)
        one_got, two_got = spread(one, near), spread(two, far)
        zero, high, one, one_got, two, two_got = fence(zero, high, one, one_got, two, two_got)
        one, two = joined(one, one_got), joined(two, two_got)
        one_got, two_got = spread(one, side), spread(two, near)
        swapped, high_swapped = swap_parts(zero), swap_parts(high)
        swapped, high_swapped, one, one_got, two, two_got, three = fence(
            swapped, high_swapped, one, one_got, two, two_got, three
        )
        chunk = (zero, high, swapped, high_swapped)
        one, two = joined(one, one_got), joined(two, two_got)
        one_got, two_got, three_got, swapped = spread(one, last), spread(two, side), spread(three, far), swap(one)
    else:
        bits = IN_ORDER
        table = sinus_table(count_down)
        chunk, chunk_one, chunk_two, chunk_three = gather_whole(section, *params)

    projected, hidden_zero, vecs, saved_zero = run_project_first(bits, scalars, rows, chunk, table)
    if ringed:
        projected, two_got, three_got, swapped = fence(projected, two_got, three_got, swapped)
        two, three = joined(two, two_got), joined(three, three_got)
        two_got, three_got, two_swapped = spread(two, last), spread(three, near), swap(two)
    attended, probs_zero = run_attend(scalars, projected)
    if ringed:
        attended, one_got, two_got, three_got, two_swapped = fence(
            attended, one_got, two_got, three_got, two_swapped
        )
        chunk = (one, one_got, swapped, swap(one_got))
        two_chunk = (two, two_got, two_swapped, swap(two_got))
        three = joined(three, three_got)
        three_got = spread(three, side)
    else:
        chunk = chunk_one
    out_zero, memory, mixed_zero, fed_zero = run_feed_forward(bits, 0, scalars, hidden_zero, attended, vecs, chunk)
    if ringed:
        out_zero, memory, three_got, two_chunk = fence(out_zero, memory, three_got, two_chunk)
        chunk = two_chunk
        three = joined(three, three_got)
        three_got, three_swapped = spread(three, last), swap(three)
    else:
        chunk = chunk_two
    memory = lax.ppermute(memory, "section", [(0, 1)])
    projected, saved_one = run_project(bits, scalars, memory, out_zero, vecs, chunk, table)
    attended, probs_one = run_attend(scalars, projected)
    if ringed:
        attended, three_got, three_swapped = fence(attended, three_got, three_swapped)
        chunk = (three, three_got, three_swapped, swap(three_got))
    else:
        chunk = chunk_three
    keep_a, send_a, grad, grad_att, gain_one, gain_final, loss = run_top(
        bits, streams, scalars, out_zero, attended, codes, vecs, chunk
    )
    if ringed:
        grad_att, keep_a, send_a = fence(grad_att, keep_a, send_a)
        got_a = swap(send_a)
    grads_a, staged = run_attend_back(bits, scalars, grad_att, saved_one, table, probs_one)
    if ringed:
        grads_a, staged, got_a = fence(grads_a, staged, got_a)
        sum_a = [keep_a, got_a]
        got_a = shrink([sum_a], last)
    grads_b, keep_b, send_b = run_attend_back_rest(
        bits, scalars, grad_att, saved_one, table, probs_one, staged
    )
    if ringed:
        grads_b, keep_b, send_b = fence(grads_b, keep_b, send_b)
        got_b = swap(send_b)
    grad, vecs_one = run_input_grads(
        bits, scalars, saved_one, (*grads_a, *grads_b), grad, vecs, memory, out_zero
    )
    if ringed:
        grad, got_a, got_b = fence(grad, got_a, got_b)
        sum_a.append(got_a)
        sum_b = [keep_b, got_b]
        got_a, got_b = shrink([sum_a], side), shrink([sum_b], last)
    keep_c, send_c, grad, grad_att, gain_zero = run_feed_backward(
        bits, 0, scalars, grad, vecs, mixed_zero, probs_zero, fed_zero
    )
    if ringed:
        grad_att, got_a, got_b, keep_c, send_c = fence(grad_att, got_a, got_b, keep_c, send_c)
        sum_a.append(got_a)
        sum_b.append(got_b)
        got_a, got_b, got_c = shrink([sum_a], near), shrink([sum_b], side), swap(send_c)
    grads_a, staged = run_attend_back(bits, scalars, grad_att, saved_zero, table, probs_zero)
    if ringed:
        grads_a, staged, got_a, got_b, got_c = fence(grads_a, staged, got_a, got_b, got_c)
        sum_a.append(got_a)
        sum_b.append(got_b)
        sum_c = [keep_c, got_c]
        got_c, got_a, got_b = shrink([sum_c], last), shrink([sum_a], far), shrink([sum_b], near)
    grads_b, keep_d, send_d = run_attend_back_rest(
        bits, scalars, grad_att, saved_zero, table, probs_zero, staged
    )
    if ringed:
        grads_b, keep_d, send_d, got_a, got_b, got_c = fence(grads_b, keep_d, send_d, got_a, got_b, got_c)
        sum_a.append(got_a)
        sum_b.append(got_b)
        sum_c.append(got_c)
        got_d, got_c, got_b = swap(send_d), shrink([sum_c], side), shrink([sum_b], far)
    keep_e, send_e = run_input_grads_last(
        bits, scalars, saved_zero, (*grads_a, *grads_b), grad, vecs, rows,
        gain_zero, vecs_one, gain_one, gain_final,
    )
    if not ringed:
        pairs = ((keep_d, send_d), (keep_c, send_c), (keep_b, send_b), (keep_a, send_a), (keep_e, send_e))
        sums = [keep.astype(F32) + swap(send).astype(F32) for keep, send in pairs]
        squares, grads = whole_grads(section, sums)
        grad_norm = jnp.sqrt(squares)
        loss_sum = lax.psum(loss[0, 0], ("section", "dp"))
        factor = jnp.minimum(1.0, CLIP / (grad_norm + 1e-06))
        results = []
        for index in range(9):
            rate, decay = (0.3, 0.0) if index in (5, 8) else (0.03, 0.01)
            grad = grads[index][None] if index < 6 else grads[index]
            results.append(
                adam_step(params[index], grad, firsts[index], seconds[index], rate, decay, factor)
            )
        news, moms, sqs = zip(*results)
        return (*news, *moms, *sqs, grad_norm, loss_sum)
    keep_e, send_e, got_b, got_d = fence(keep_e, send_e, got_b, got_d)
    sum_b.append(got_b)
    sum_d, sum_e, sum_de = [keep_d, got_d], [keep_e, swap(send_e)], []
    for pair in (last, side, near, far):
        got = shrink([sum_d, sum_e], pair, sum_de)
        if pair == last:
            sum_c.append(got_c)
            got, got_c, one_a, one_b = fence(got, shrink([sum_c], near), part(sum_a, 0, 1), part(sum_b, 0, 1))
            sum_c.append(got_c)
            got_c = shrink([sum_c], far)
        if pair == near:
            one_d = part(sum_d + [item[:, :64] for item in sum_de], 0, 1)
            one_e = part(sum_e + [item[:, 64:] for item in sum_de], 0, 1)
            got, one_c, one_d, one_e = fence(got, part(sum_c, 0, 1), one_d, one_e)
            one_d, one_e = one_d + got[:1, :64].astype(F32), one_e + got[:1, 64:].astype(F32)
        sum_de.append(got)
    kept, sent, total = run_finish(
        scalars, loss, [one_d], [one_c, got_c], [one_b], [one_a], [one_e], sum_de[3:]
    )
    got = swap(sent)
    return tuple(run_update(scalars, add_up(total, bits), kept, got, state))


def solution(mesh):
    weights = (
        P("section", "dp", None),
        P("section", "dp", None),
        P("section", "dp", None),
        P("section", "dp", None),
        P("section", "dp", None),
        P("section", None, "dp"),
        P(None, "dp"),
        P("dp", None),
        P("dp"),
    )
    return jax.shard_map(
        local,
        mesh=mesh,
        in_specs=(P("dp", None, None), P("dp", None), P("dp")) + weights * 3,
        out_specs=weights * 3 + (P(), P()),
        check_vma=False,
    )
```

```python
import functools

import jax
import jax.numpy as jnp
from jax import lax
from jax.experimental import pallas as pl
from jax.experimental.pallas import tpu as pltpu
from jax.sharding import PartitionSpec as P

D = 512
FF = 2048
CODES = 1024
FEATS = 80
MEM = 256
SEG = 512
SEGS = 2
STEP = 10
ROWS = MEM + SEG
BLOCK = 128
PAIRS = 4
WIDE = 18 * BLOCK
GROUPS = 16
QUERY_U_AT, QUERY_V_AT, KEYS_AT, VALUES_AT, REL_AT, WEIGHTS_AT, SMALL_AT = 768, 1280, 1792, 2560, 3328, 4096, 6144
ACTIVE_AT, SLOPE_AT, UP_AT, DOWN_AT, OUT_AT = 512, 2560, 4608, 6656, 8704
KEPT_ROWS = 16384
KEPT_PAIRS = 14
IN_ORDER = ((1, 2, 4, 8), (1, 2, 4, 8))
NEG = -1e30
CLIP = 0.02
SCALE = 0.125
F32 = jnp.float32
BF16 = jnp.bfloat16
SPANS = tuple((MEM + BLOCK * (b + 1) for b in range(4)))
STARTS = tuple((sum(SPANS[:b]) for b in range(4)))


def nn(left, right):
    return jnp.dot(left, right, preferred_element_type=F32)


def nt(left, right):
    return lax.dot_general(left, right, (((1,), (1,)), ((), ())), preferred_element_type=F32)


def tn(left, right):
    return lax.dot_general(left, right, (((0,), (0,)), ((), ())), preferred_element_type=F32)


def norm_parts(values):
    center = values - jnp.mean(values, -1, keepdims=True)
    spread = jnp.mean(center * center, -1, keepdims=True)
    inverse = lax.rsqrt(spread + 1e-05)
    return center * inverse, inverse


def norm_back(unit, inverse, gain, grad):
    scaled = grad * gain
    first = jnp.mean(scaled, -1, keepdims=True)
    second = jnp.mean(scaled * unit, -1, keepdims=True)
    return inverse * (scaled - first - unit * second), jnp.sum(grad * unit, 0, keepdims=True)


def group_of(bits, spot, place, half):
    if bits == IN_ORDER:
        return spot
    low, high = (sum((bit for index, bit in enumerate(each) if (spot >> index) & 1)) for each in bits)
    return jnp.bitwise_xor(place, low if low == high else jnp.where(half == 0, low, high))


def copies(bits, place, half, pieces, units, rows, sem, outward):
    count = GROUPS // len(pieces)
    for index, slab in enumerate(pieces):
        for spot in range(count):
            group = group_of(bits, index * count + spot, place, half)
            for whole, first in units:
                there = whole.at[pl.ds(pl.multiple_of((group * 2 + half) * rows, rows), rows), :]
                here = slab.at[spot, pl.ds(first, rows), pl.ds(0, whole.shape[1])]
                if outward:
                    pltpu.make_async_copy(there, here, sem).start()
                else:
                    pltpu.make_async_copy(here, there, sem).start()


def gather_units(bits, place, half, pieces, units, rows):
    count = GROUPS // len(pieces)
    for index, slab in enumerate(pieces):
        for spot in range(count):
            group = group_of(bits, index * count + spot, place, half)
            start = pl.multiple_of((group * 2 + half) * rows, rows)
            for whole, first in units:
                whole[pl.ds(start, rows), :] = slab[spot, first : first + rows, 0 : whole.shape[1]]


def scatter_units(bits, place, half, slab, units, rows):
    for spot in range(GROUPS):
        group = group_of(bits, spot, place, half)
        start = pl.multiple_of((group * 2 + half) * rows, rows)
        for whole, first in units:
            slab[spot, first : first + rows, 0 : whole.shape[1]] = whole[pl.ds(start, rows), :]


def columns(ref, count):
    return [ref.at[:, pl.ds(D * u, D)] for u in range(count)]


def fetch(source, target, sem):
    copy = pltpu.make_async_copy(source, target, sem)
    copy.start()
    return copy


def arrived(buffer, sem):
    pltpu.make_async_copy(buffer, buffer, sem).wait()


def tri_mask():
    row = lax.broadcasted_iota(jnp.int32, (2 * BLOCK, BLOCK), 0)
    col = lax.broadcasted_iota(jnp.int32, (2 * BLOCK, BLOCK), 1)
    return col <= lax.rem(row, BLOCK)


def stack_heads(part):
    col = lax.broadcasted_iota(jnp.int32, part.shape, 1)
    zero = jnp.zeros_like(part)
    return jnp.concatenate(
        [jnp.where(col < 64, part, zero), jnp.where(col < 64, zero, part)], 0
    )


def pick_heads(both):
    col = lax.broadcasted_iota(jnp.int32, (BLOCK, BLOCK), 1)
    return jnp.where(col < 64, both[:BLOCK], both[BLOCK:])


def shift(both, amount):
    return jnp.concatenate(
        [pltpu.roll(part, amount, 1, stride=1, stride_axis=0) for part in (both[:BLOCK], both[BLOCK:])], 0
    )


def masked(score, triangle, first):
    if first == 0:
        return jnp.where(triangle, score, NEG)
    return jnp.concatenate([score[:, :first], jnp.where(triangle, score[:, first:], NEG)], 1)


def lanes(pair):
    return pl.ds(pl.multiple_of(pair * BLOCK, BLOCK), BLOCK)


def project(bits, base, *refs):
    first_layer = base == 0
    if first_layer:
        (scalars, frames, own_low, own_high, other_low, other_high, table) = refs[:7]
        (query_u, query_v, keys, values, rel, hidden, vecs, saved) = refs[7:15]
        (normed, weights, in_sem, out_sem, joined, small, small_sem) = refs[15:]
    else:
        (scalars, memory, hidden, vecs, own_low, own_high, other_low, other_high, table) = refs[:9]
        (query_u, query_v, keys, values, rel, saved) = refs[9:15]
        (normed, weights, in_sem, out_sem) = refs[15:]
    place, half = scalars[0], scalars[1]
    both = ((half, (own_low, own_high)), (1 - half, (other_low, other_high)))
    if first_layer:
        for which, pieces in both:
            gather_units(bits, place, which, pieces, [(small, 64)], 16)
    units = [(weights.at[u], 16 * u) for u in range(4)]
    for which, pieces in both:
        gather_units(bits, place, which, pieces, units, 16)
    if first_layer:
        small_out = fetch(small, saved.at[pl.ds(SMALL_AT, D), pl.ds(0, BLOCK)], out_sem.at[7])
        vecs[...] = jnp.transpose(small[...].astype(F32))[80:96]
        for b in range(3):
            rows = pl.ds(256 * b, 256)
            joined[rows, :] = nt(frames[rows, :], small[...])
        hidden[...] = joined[MEM:, :]
        sources = [joined.at[pl.ds(256 * b, 256)] for b in range(3)]
    else:
        sources = [memory, hidden.at[pl.ds(0, 256)], hidden.at[pl.ds(256, 256)]]
    gain = vecs[base : base + 1, :]
    bias_u = vecs[base + 2 : base + 3, :]
    bias_v = vecs[base + 3 : base + 4, :]
    outs = [fetch(weights.at[u], saved.at[pl.ds(WEIGHTS_AT + D * u, D)], out_sem.at[8 + u]) for u in range(4)]
    rel[...] = nn(table[...], weights[3]).astype(BF16)
    outs.append(fetch(rel, saved.at[pl.ds(REL_AT, ROWS)], out_sem.at[5]))
    for b in range(3):
        unit, unused = norm_parts(sources[b][...])
        normed[pl.ds(256 * b, 256), :] = (unit * gain).astype(BF16)
    outs.append(fetch(normed, saved.at[pl.ds(0, ROWS)], out_sem.at[0]))
    keys[...] = nn(normed[...], weights[1]).astype(BF16)
    outs.append(fetch(keys, saved.at[pl.ds(KEYS_AT, ROWS)], out_sem.at[3]))
    values[...] = nn(normed[...], weights[2]).astype(BF16)
    outs.append(fetch(values, saved.at[pl.ds(VALUES_AT, ROWS)], out_sem.at[4]))
    query = nn(normed[MEM:, :], weights[0])
    query_u[...] = (query + bias_u).astype(BF16)
    query_v[...] = (query + bias_v).astype(BF16)
    outs.append(fetch(query_u, saved.at[pl.ds(QUERY_U_AT, SEG)], out_sem.at[1]))
    outs.append(fetch(query_v, saved.at[pl.ds(QUERY_V_AT, SEG)], out_sem.at[2]))
    if first_layer:
        outs.append(small_out)
    for copy in outs:
        copy.wait()


def attend(scalars, query_u, query_v, keys, values, rel, attended, probs_o, probs, out_sem):
    length, segment = scalars[2], scalars[3]
    spot = lax.broadcasted_iota(jnp.int32, (1, ROWS), 1)
    where_at = segment * SEG + spot - MEM
    allowed = (where_at < length) & ((spot >= MEM) | (segment >= 1))
    bias = jnp.where(allowed, 0.0, NEG)
    triangle = tri_mask()

    def two_pairs(first, step, carry):
        tiles = [(2 * step + one, b, SPANS[b] - first) for one in range(2) for b in range(4)]
        full = [
            nt(stack_heads(query_v[BLOCK * b : BLOCK * (b + 1), lanes(pair)]) * SCALE,
               rel[ROWS - span : ROWS, lanes(pair)])
            for pair, b, span in tiles
        ]
        content = [
            nt(stack_heads(query_u[BLOCK * b : BLOCK * (b + 1), lanes(pair)]) * SCALE,
               keys[first : first + span, lanes(pair)])
            for pair, b, span in tiles
        ]
        full = [shift(item, span - BLOCK + 1) for item, (pair, b, span) in zip(full, tiles)]
        score = [
            masked(one + two + bias[:, first : first + span], triangle, span - BLOCK)
            for one, two, (pair, b, span) in zip(content, full, tiles)
        ]
        top = [jnp.max(item, -1, keepdims=True) for item in score]
        expo = [jnp.exp(item - most) for item, most in zip(score, top)]
        total = [jnp.sum(item, -1, keepdims=True) for item in expo]
        prob = [(item * (1.0 / most)).astype(BF16) for item, most in zip(expo, total)]
        for item, (pair, b, span) in zip(prob, tiles):
            probs[pair, :, STARTS[b] + first : STARTS[b] + first + span] = item
        for one in range(2):
            pair = 2 * step + one
            pltpu.make_async_copy(probs.at[pair], probs_o.at[pair], out_sem.at[pair]).start()
        found = [
            nn(item, values[first : first + span, lanes(pair)]) for item, (pair, b, span) in zip(prob, tiles)
        ]
        for item, (pair, b, span) in zip(found, tiles):
            attended[BLOCK * b : BLOCK * (b + 1), lanes(pair)] = pick_heads(item).astype(BF16)
        return carry

    for first in (0, MEM):

        @pl.when((segment == 0) == (first > 0))
        def _():
            lax.fori_loop(0, PAIRS // 2, functools.partial(two_pairs, first), 0)

    outs = [
        fetch(attended.at[pl.ds(256 * b, 256)], probs_o.at[PAIRS + b, :, pl.ds(0, D)], out_sem.at[PAIRS + b])
        for b in range(2)
    ]
    for pair in range(PAIRS):
        pltpu.make_async_copy(probs.at[pair], probs_o.at[pair], out_sem.at[pair]).wait()
    for copy in outs:
        copy.wait()


def attend_back(bits, second, *refs):
    (scalars, grad_att, table_h, saved, probs_h) = refs[:5]
    normed, table, late_sem = refs[-3:]
    rest = refs[5:-3]
    query_u_h, query_v_h, keys_h, values_h, rel_h = (
        saved.at[pl.ds(first, rows)]
        for first, rows in (
            (QUERY_U_AT, SEG), (QUERY_V_AT, SEG), (KEYS_AT, ROWS), (VALUES_AT, ROWS), (REL_AT, ROWS)
        )
    )
    if second:
        staged_h = rest[0]
        rest = rest[1:]
        (keep, send) = rest[4:6]
        sums, rest = rest[3], rest[:3] + rest[6:]
    else:
        (staged, sums) = rest[3:5]
        rest = rest[:3] + rest[5:]
    (grad_query, grad_keys, grad_values,
     query_u, query_v, keys, values, rel, probs, flip, acc_keys, acc_values, acc_rel,
     grad_qu, grad_qv, pair_sem) = rest[:16]
    first_pair = 2 if second else 0

    def parts(pair):
        lane, here = lanes(pair + first_pair), lanes(pair)
        moves = [(probs_h.at[pair + first_pair], probs.at[pair])]
        for there, target in (
            (query_u_h, query_u), (query_v_h, query_v), (keys_h, keys), (values_h, values), (rel_h, rel)
        ):
            moves.append((there.at[:, lane], target.at[:, here]))
        return [
            pltpu.make_async_copy(there, target, pair_sem.at[pair, index])
            for index, (there, target) in enumerate(moves)
        ]

    for pair in range(2):
        for copy in parts(pair):
            copy.start()
    late = [fetch(saved.at[pl.ds(0, ROWS)], normed, late_sem.at[0]), fetch(table_h, table, late_sem.at[1])]
    if second:
        staged, sem = rest[16:]
        staged[:, :, 0:256] = staged_h[...]
    row = lax.broadcasted_iota(jnp.int32, (2 * BLOCK, 2 * BLOCK), 0)
    col = lax.broadcasted_iota(jnp.int32, (2 * BLOCK, 2 * BLOCK), 1)
    back = (row // BLOCK) * BLOCK + BLOCK - 1 - lax.rem(row, BLOCK)
    flip[...] = (col == back).astype(F32).astype(BF16)

    segment = scalars[3]

    def one_pair(first, pair, carry):
        lane = lanes(pair)
        for copy in parts(pair):
            copy.wait()
        order = (3, 2, 1, 0)
        flipped = flip[...]
        stack_g = [
            stack_heads(grad_att[BLOCK * b : BLOCK * (b + 1), lanes(pair + first_pair)]) for b in order
        ]
        stack_u = [stack_heads(query_u[BLOCK * b : BLOCK * (b + 1), lane]) * SCALE for b in order]
        stack_v = [
            nn(flipped, stack_heads(query_v[BLOCK * b : BLOCK * (b + 1), lane]) * SCALE).astype(BF16)
            for b in order
        ]
        spans = [SPANS[b] - first for b in order]
        prob_b = [
            probs[pair, :, STARTS[b] + first : STARTS[b] + first + span] for b, span in zip(order, spans)
        ]
        grad_prob = [nt(one, values[first : first + span, lane]) for one, span in zip(stack_g, spans)]
        part_values = [tn(one, two) for one, two in zip(stack_g, prob_b)]
        prob = [item.astype(F32) for item in prob_b]
        inner = [jnp.sum(one * two, -1, keepdims=True) for one, two in zip(prob, grad_prob)]
        grad_score = [
            (one * (two - three)).astype(BF16) for one, two, three in zip(prob, grad_prob, inner)
        ]
        turned = [nn(flipped, item) for item in grad_score]
        found_u = [nn(item, keys[first : first + span, lane]) for item, span in zip(grad_score, spans)]
        part_keys = [tn(one, two) for one, two in zip(stack_u, grad_score)]
        grad_full = [shift(item, 0).astype(BF16) for item in turned]
        found_v = [nn(item, rel[ROWS - span : ROWS, lane]) for item, span in zip(grad_full, spans)]
        part_rel = [tn(one, two) for one, two in zip(stack_v, grad_full)]
        for index, b in enumerate(order):
            span = spans[index]
            rows = pl.ds(BLOCK * b, BLOCK)
            grad_qu[rows, lane] = pick_heads(found_u[index]) * SCALE
            grad_qv[rows, lane] = pick_heads(found_v[index]) * SCALE
            if b == 3:
                acc_keys[lane, first:] = part_keys[index]
                acc_values[lane, first:] = part_values[index]
                acc_rel[lane, ROWS - span :] = part_rel[index]
                if first:
                    blank = jnp.zeros((BLOCK, first), F32)
                    acc_keys[lane, 0:first] = blank
                    acc_values[lane, 0:first] = blank
                    acc_rel[lane, 0 : ROWS - span] = blank
            else:
                acc_keys[lane, first : first + span] += part_keys[index]
                acc_values[lane, first : first + span] += part_values[index]
                acc_rel[lane, ROWS - span : ROWS] += part_rel[index]
        return carry

    for first in (0, MEM):

        @pl.when((segment == 0) == (first > 0))
        def _():
            lax.fori_loop(0, 2, functools.partial(one_pair, first), 0)

    grad_keys[...] = jnp.transpose(acc_keys[...]).astype(BF16)
    grad_values[...] = jnp.transpose(acc_values[...]).astype(BF16)
    grad_rel = jnp.transpose(acc_rel[...]).astype(BF16)
    sums[...] = jnp.zeros_like(sums)
    sums[2:3, :] = jnp.sum(grad_qu[...], 0, keepdims=True)
    sums[3:4, :] = jnp.sum(grad_qv[...], 0, keepdims=True)
    flip_one = flip[0:BLOCK, 0:BLOCK]
    for b in range(4):
        rows = pl.ds(BLOCK * b, BLOCK)
        part = grad_qv[rows, :]
        high = part.astype(BF16)
        low = (part - high.astype(F32)).astype(BF16)
        grad_query[rows, :] = (grad_qu[rows, :] + nn(flip_one, high) + nn(flip_one, low)).astype(BF16)
    for copy in late:
        copy.wait()
    cols = slice(256, 512) if second else slice(None)
    staged[1, :, cols] = tn(normed[...], grad_keys[...]).astype(BF16)
    staged[2, :, cols] = tn(normed[...], grad_values[...]).astype(BF16)
    staged[3, :, cols] = tn(table[...], grad_rel).astype(BF16)
    staged[0, :, cols] = tn(normed[MEM:, :], grad_query[...]).astype(BF16)
    if second:
        place, half = scalars[0], scalars[1]
        units = [(staged.at[u], 16 * u) for u in range(4)]
        scatter_units(bits, place, half, keep, units, 16)
        scatter_units(bits, place, 1 - half, send, units, 16)


def input_grads(bits, base, *refs):
    last_kernel = base == 0
    weights, weights_sem = refs[-2:]
    refs = refs[:-2]
    weights_copies = [
        fetch(refs[1].at[pl.ds(WEIGHTS_AT + D * u, D)], weights.at[u], weights_sem.at[u]) for u in range(3)
    ]
    (scalars, saved, query_a, keys_a, values_a, sums_a, query_b, keys_b, values_b, sums_b, grad_mixed, vecs) = refs[:12]
    if last_kernel:
        (frames, gain_two, vecs_one, gain_two_one, gain_final, keep, send,
         joined, smalls, staged, sem, small, small_sem) = refs[12:]
        fetch(saved.at[pl.ds(SMALL_AT, D), pl.ds(0, BLOCK)], small, small_sem).wait()
        joined[...] = nt(frames[...], small[...])
        before, here, first = joined, joined, MEM
    else:
        (memory, hidden, grad_hidden, grad_vecs) = refs[12:]
        before, here, first = memory, hidden, 0
    place, half = scalars[0], scalars[1]
    gain = vecs[base : base + 1, :]
    left, right = slice(0, 256), slice(256, 512)
    for copy in weights_copies:
        copy.wait()
    grad_keys = (
        nt(keys_a[...], weights[1, :, left])
        + nt(keys_b[...], weights[1, :, right])
        + nt(values_a[...], weights[2, :, left])
        + nt(values_b[...], weights[2, :, right])
    )
    grad_query = nt(query_a[...], weights[0, :, left]) + nt(query_b[...], weights[0, :, right])
    unit, inverse = norm_parts(before[0:MEM, :])
    grad_gain = jnp.sum(grad_keys[0:MEM] * unit, 0, keepdims=True)
    unit, inverse = norm_parts(here[first : first + SEG, :])
    grad_joined, gains = norm_back(unit, inverse, gain, grad_keys[MEM:] + grad_query)
    grad_gain = grad_gain + gains
    grad_in = grad_mixed[...] + grad_joined
    if last_kernel:
        smalls[...] = tn(frames[MEM:, :], grad_in.astype(BF16))
        smalls[80:81, :] = grad_gain
        smalls[81:82, :] = gain_two[0:1, :]
        smalls[82:84, left] = sums_a[2:4, :]
        smalls[82:84, right] = sums_b[2:4, :]
        smalls[84:88, :] = vecs_one[0:4, :]
        smalls[85:86, :] = gain_two_one[0:1, :]
        smalls[88:89, :] = gain_final[0:1, :]
        staged[...] = jnp.zeros_like(staged)
        staged[:, 0:BLOCK] = jnp.transpose(smalls[...]).astype(BF16)
        units = [(staged, 0)]
        scatter_units(bits, place, half, keep, units, 16)
        scatter_units(bits, place, 1 - half, send, units, 16)
    else:
        grad_hidden[...] = grad_in
        grad_vecs[:, left] = sums_a[...]
        grad_vecs[:, right] = sums_b[...]
        grad_vecs[0:1, :] = grad_gain


def feed_weights(bits, place, both, up, down, out):
    for units, rows in (
        ([(out, 128)], 16),
        ([(item, 16 * u) for u, item in enumerate(columns(up, 4))], 16),
        ([(down, 64)], 64),
    ):
        for which, pieces in both:
            gather_units(bits, place, which, pieces, units, rows)


def feed_mixed(residual, attended, out, gain, mixed, normed):
    mixed[...] = residual[...] + nn(attended[...], out[...])
    for b in range(2):
        rows = pl.ds(256 * b, 256)
        unit, unused = norm_parts(mixed[rows, :])
        normed[rows, :] = (unit * gain).astype(BF16)


def feed_inner(normed, up, active, slope):
    later = nn(normed[...], up[:, 0:512])
    for u in range(4):
        inner = later
        if u < 3:
            later = nn(normed[...], up[:, 512 * (u + 1) : 512 * (u + 2)])
        square = inner * inner
        bent = jnp.tanh(0.7978845608028654 * (inner + 0.044715 * (square * inner)))
        half = 0.5 * (1.0 + bent)
        active[:, 512 * u : 512 * (u + 1)] = (inner * half).astype(BF16)
        slope[:, 512 * u : 512 * (u + 1)] = (
            half
            + (0.5 * inner)
            * (1.0 - bent * bent)
            * (0.7978845608028654 * (1.0 + (3 * 0.044715) * square))
        ).astype(BF16)


def feed_output(mixed, active, down, output):
    output[...] = mixed[...] + nn(active[...], down[...])


def feed_forward(bits, base, scalars, residual, attended, vecs, own_low, own_high, other_low, other_high,
                 output, memory, mixed_o, saved,
                 mixed, normed, active, slope, up, down, out, sem, out_sem):
    place, half = scalars[0], scalars[1]
    both = ((half, (own_low, own_high)), (1 - half, (other_low, other_high)))
    feed_weights(bits, place, both, up, down, out)
    outs = [fetch(out, saved.at[pl.ds(OUT_AT, D)], out_sem.at[0])]
    feed_mixed(residual, attended, out, vecs[base + 1 : base + 2, :], mixed, normed)
    outs.append(fetch(normed, saved.at[pl.ds(0, SEG)], out_sem.at[1]))
    outs.append(fetch(mixed, mixed_o, out_sem.at[2]))
    outs += [
        fetch(item, saved.at[pl.ds(UP_AT + D * u, D)], out_sem.at[4 + u])
        for u, item in enumerate(columns(up, 4))
    ]
    feed_inner(normed, up, active, slope)
    for u in range(4):
        cols = pl.ds(D * u, D)
        outs.append(fetch(active.at[:, cols], saved.at[pl.ds(ACTIVE_AT + D * u, D)], out_sem.at[8 + u]))
        outs.append(fetch(slope.at[:, cols], saved.at[pl.ds(SLOPE_AT + D * u, D)], out_sem.at[12 + u]))
    outs.append(fetch(down, saved.at[pl.ds(DOWN_AT, FF)], out_sem.at[3]))
    feed_output(mixed, active, down, output)
    memory[...] = output[SEG - MEM :, :]
    for copy in outs:
        copy.wait()


def feed_back(moves, bits, place, half, keep, send, sem, base, grad_out, mixed, vecs, attended, normed,
              active, slope, up, down, out, grad_mixed, grad_att, grad_gain,
              grad_inner, staged_up, staged_down, staged_out):
    both = ((half, keep), (1 - half, send))
    grad_y = grad_out[...].astype(BF16)
    for copy in moves[:1]:
        copy.wait()
    later = nt(grad_y, down[0:512, :])
    for copy in moves[1:10]:
        copy.wait()
    for u in range(4):
        cols = slice(512 * u, 512 * (u + 1))
        part = later
        if u < 3:
            later = nt(grad_y, down[512 * (u + 1) : 512 * (u + 2), :])
        staged_down[cols, :] = tn(active[:, cols], grad_y).astype(BF16)
        grad_inner[:, cols] = (part * slope[:, cols].astype(F32)).astype(BF16)
    for copy in moves[10:]:
        copy.wait()
    grad_normed = nt(grad_inner[...], up[...])
    for which, pieces in both:
        scatter_units(bits, place, which, pieces, [(staged_down, 64)], 64)
    for u in range(4):
        cols = slice(512 * u, 512 * (u + 1))
        staged_up[:, cols] = tn(normed[...], grad_inner[:, cols]).astype(BF16)
    unit, inverse = norm_parts(mixed[...])
    grad_here, gains = norm_back(unit, inverse, vecs[base + 1 : base + 2, :], grad_normed)
    grad = grad_out[...] + grad_here
    grad_mixed[...] = grad
    grad_b = grad.astype(BF16)
    for which, pieces in both:
        units = [(item, 16 * u) for u, item in enumerate(columns(staged_up, 4))]
        scatter_units(bits, place, which, pieces, units, 16)
    grad_att[...] = nt(grad_b, out[...]).astype(BF16)
    staged_out[...] = tn(attended[...], grad_b).astype(BF16)
    for which, pieces in both:
        scatter_units(bits, place, which, pieces, [(staged_out, 128)], 16)
    grad_gain[...] = jnp.broadcast_to(gains, grad_gain.shape)


def feed_backward(bits, base, scalars, grad_out, vecs, mixed_h, probs_h, saved,
                  keep, send, grad_mixed, grad_att, grad_gain, mixed, attended,
                  normed, active, slope, up, down, out, grad_inner, staged_up, staged_down, staged_out,
                  in_sem, sem):
    pairs = [(saved.at[pl.ds(DOWN_AT, FF)], down)]
    for u in range(4):
        pairs.append((saved.at[pl.ds(SLOPE_AT + D * u, D)], slope.at[:, pl.ds(D * u, D)]))
    for u in range(4):
        pairs.append((saved.at[pl.ds(ACTIVE_AT + D * u, D)], active.at[:, pl.ds(D * u, D)]))
    pairs.append((saved.at[pl.ds(0, SEG)], normed))
    for u in range(4):
        pairs.append((saved.at[pl.ds(UP_AT + D * u, D)], columns(up, 4)[u]))
    pairs.append((saved.at[pl.ds(OUT_AT, D)], out))
    pairs.append((mixed_h, mixed))
    for b in range(2):
        pairs.append((probs_h.at[PAIRS + b, :, pl.ds(0, D)], attended.at[pl.ds(256 * b, 256)]))
    moves = [fetch(there, here, in_sem.at[index]) for index, (there, here) in enumerate(pairs)]
    feed_back(moves, bits, scalars[0], scalars[1], keep, send, sem, base, grad_out, mixed, vecs, attended, normed,
              active, slope, up, down, out, grad_mixed, grad_att, grad_gain,
              grad_inner, staged_up, staged_down, staged_out)


def top_kernel(bits, streams, scalars, residual, attended, targets, vecs, own_low, own_high, other_low, other_high,
               keep, send, grad_mixed, grad_att, grad_gain, final_gain, loss,
               normed, active, slope, up, down, out, mixed, output, grad_out, table, final, grad_logits, staged,
               grad_inner, staged_up, staged_down, staged_out, head_sem, sem, out_sem):
    place, half, length, segment = scalars[0], scalars[1], scalars[2], scalars[3]
    both = ((half, (own_low, own_high)), (1 - half, (other_low, other_high)))
    feed_weights(bits, place, both, up, down, out)
    units = [(item, 144 + 16 * u) for u, item in enumerate(columns(table, 2))]
    for which, pieces in both:
        gather_units(bits, place, which, pieces, units, 16)
    feed_mixed(residual, attended, out, vecs[5:6, :], mixed, normed)
    feed_inner(normed, up, active, slope)
    feed_output(mixed, active, down, output)
    size = length.astype(F32)
    codes = jnp.transpose(jnp.broadcast_to(targets[...].astype(F32), (BLOCK, SEG))).astype(jnp.int32)
    gain = vecs[8:9, :]
    gains = jnp.zeros((1, D), F32)
    terms = jnp.zeros((1, 1), F32)
    spans = (slice(0, 256), slice(256, 512))
    parts = [norm_parts(output[rows, :]) for rows in spans]
    fins = [(unit * gain).astype(BF16) for unit, unused in parts]
    logits = [nn(fin, table[...]) for fin in fins]
    for rows, fin in zip(spans, fins):
        final[rows, :] = fin
    grad_finals = []
    for b, rows in enumerate(spans):
        logit = logits[b]
        most = jnp.max(logit, -1, keepdims=True)
        expo = jnp.exp(logit - most)
        total = jnp.sum(expo, -1, keepdims=True)
        picks = lax.broadcasted_iota(jnp.int32, logit.shape, 1) == codes[rows, 0:1]
        picked = jnp.sum(jnp.where(picks, logit, 0.0), -1, keepdims=True)
        spot = segment * SEG + 256 * b + lax.broadcasted_iota(jnp.int32, (256, 1), 0)
        weight = jnp.where(spot < length, 1.0 / size, 0.0)
        terms = terms + jnp.sum((most + jnp.log(total) - picked) * weight, keepdims=True)
        grad = (expo * (1.0 / total) - jnp.where(picks, 1.0, 0.0)) * (weight * (1.0 / streams))
        grad_logits[rows, :] = grad.astype(BF16)
        grad_finals.append(nt(grad_logits[rows, :], table[...]))
    staged[...] = tn(final[...], grad_logits[...]).astype(BF16)
    for (unit, inverse), rows, grad_final in zip(parts, spans, grad_finals):
        grad_here, gain_here = norm_back(unit, inverse, gain, grad_final)
        grad_out[rows, :] = grad_here
        gains = gains + gain_here
    units = [(item, 144 + 16 * u) for u, item in enumerate(columns(staged, 2))]
    scatter_units(bits, place, half, keep, units, 16)
    scatter_units(bits, place, 1 - half, send, units, 16)
    final_gain[...] = jnp.broadcast_to(gains, final_gain.shape)
    loss[...] = jnp.broadcast_to(terms, loss.shape)
    feed_back((), bits, place, half, keep, send, out_sem, 4, grad_out, mixed, vecs, attended, normed,
              active, slope, up, down, out, grad_mixed, grad_att, grad_gain,
              grad_inner, staged_up, staged_down, staged_out)


def finish(counts, *refs):
    scalars, loss = refs[0], refs[1]
    total_count = sum(counts)
    sources = refs[2 : 2 + total_count]
    kept, sent, total = refs[2 + total_count : 5 + total_count]
    buffers, sem = refs[5 + total_count : -1], refs[-1]
    moves = [fetch(there.at[0], here, sem.at[index]) for index, (there, here) in enumerate(zip(sources, buffers))]
    for copy in moves:
        copy.wait()
    sums = []
    start = 0
    for count in counts:
        item = buffers[start][...].astype(F32)
        for other in buffers[start + 1 : start + count]:
            item = item + other[...].astype(F32)
        sums.append(item)
        start += count
    attn_zero, feed_zero, attn_one, feed_one, small = sums[0], sums[1], sums[2], sums[3], sums[4]
    attn_zero = attn_zero + sums[5][0:64]
    small = small + sums[5][64:80]
    first = scalars[1] == 0
    lone = jnp.zeros((1, 1), F32)
    for zero, one, rows, begin in ((attn_zero, attn_one, 64, 0), (feed_zero, feed_one[0:144], 144, 64)):
        kept[begin : begin + rows, :] = jnp.where(first, zero, one)
        sent[begin : begin + rows, :] = jnp.where(first, one, zero)
        lone = lone + jnp.sum(zero * zero + one * one, keepdims=True)
    head = feed_one[144:176]
    lone = lone + jnp.sum(head * head, keepdims=True) + jnp.sum(small * small, keepdims=True)
    for target in (kept, sent):
        target[208:240, :] = head
        target[240:256, :] = small
    column = lax.broadcasted_iota(jnp.int32, (8, 128), 1)
    total[...] = jnp.where(column == 0, lone, 0.0) + jnp.where(column == 1, loss[...], 0.0)


def adam_step(weight, grad, first, second, rate, decay, factor):
    grad = grad * factor
    first = 0.9 * first + 0.1 * grad
    second = 0.999 * second + 0.001 * grad * grad
    ratio = first / (1.0 - 0.9**STEP) / (jnp.sqrt(second / (1.0 - 0.999**STEP)) + 1e-08)
    return (weight - rate * (ratio + decay * weight), first, second)


def update(scalars, total, kept, got, *refs):
    ins, outs, small = refs[:27], refs[27:56], refs[56]
    first = scalars[1] == 0
    squares = jnp.sum(total[0:1, 0:1], keepdims=True)
    norm = jnp.sqrt(squares)
    outs[27][...] = norm
    outs[28][...] = total[0:1, 1:2]
    factor = jnp.minimum(1.0, CLIP / (norm + 1e-06))

    def half_of(half, start, rows):
        here, there = kept[start : start + rows, :], got[start : start + rows, :]
        return jnp.where(first == (half == 0), here, there)

    def apply(index, spot, grad, rate, decay):
        results = adam_step(
            ins[index][spot], grad, ins[9 + index][spot], ins[18 + index][spot], rate, decay, factor
        )
        for which, result in enumerate(results):
            outs[9 * which + index][spot] = result

    for half in range(2):
        rows = slice(16 * half, 16 * half + 16)
        for u in range(3):
            apply(0, (0, rows, slice(D * u, D * (u + 1))), half_of(half, 16 * u, 16), 0.03, 0.01)
        apply(1, (0, rows, slice(None)), half_of(half, 192, 16), 0.03, 0.01)
        apply(2, (0, rows, slice(None)), half_of(half, 48, 16), 0.03, 0.01)
        for u in range(4):
            apply(3, (0, rows, slice(D * u, D * (u + 1))), half_of(half, 64 + 16 * u, 16), 0.03, 0.01)
        apply(4, (0, slice(64 * half, 64 * half + 64), slice(None)), half_of(half, 128, 64), 0.03, 0.01)
        for u in range(2):
            apply(7, (rows, slice(D * u, D * (u + 1))), half_of(half, 208 + 16 * u, 16), 0.03, 0.01)
        small[rows, :] = half_of(half, 240, 16)[:, 0:BLOCK]
    small[32:, :] = jnp.zeros((BLOCK - 32, BLOCK), F32)
    turned = jnp.transpose(small[...])
    apply(6, (slice(None), slice(None)), small[0:32, 0:FEATS], 0.03, 0.01)
    vecs = jnp.where(first, turned[80:84, 0:32], turned[84:88, 0:32])
    apply(5, (0, slice(None), slice(None)), vecs, 0.3, 0.0)
    apply(8, (slice(None), slice(None)), turned[88:89, 0:32], 0.3, 0.0)


def pack_shards(scalars, attn, out, pos, up, down, vecs, w_in, head, gain, kept, sent, codes, small):
    half, section = scalars[1], scalars[3]
    small[...] = jnp.zeros_like(small)
    small[88:89, 0:32] = gain[...]
    small[pl.ds(FEATS + 4 * section, 4), 0:32] = vecs[0]
    turned = jnp.transpose(small[...])[0:32]
    turned = jnp.concatenate([w_in[...], turned[:, FEATS:]], 1)
    column = lax.broadcasted_iota(jnp.int32, turned.shape, 1)
    shared = (column < FEATS) | (column == 88)
    for which, target in ((half, kept), (1 - half, sent)):
        rows = pl.ds(pl.multiple_of(16 * which, 16), 16)
        for u in range(3):
            target[16 * u : 16 * u + 16, :] = attn[0, rows, D * u : D * (u + 1)].astype(BF16)
        target[48:64, :] = pos[0, rows, :].astype(BF16)
        for u in range(4):
            target[80 + 16 * u : 96 + 16 * u, :] = up[0, rows, D * u : D * (u + 1)].astype(BF16)
        target[144:208, :] = down[0, pl.ds(pl.multiple_of(64 * which, 64), 64), :].astype(BF16)
        target[208:224, :] = out[0, rows, :].astype(BF16)
        tail = jnp.where(half == 0, turned[0:16], turned[16:32])
        if target is sent:
            tail = jnp.where(half == 0, turned[16:32], turned[0:16])
            tail = jnp.where(shared[0:16], 0.0, tail)
        target[64:80, :] = jnp.zeros((16, D), BF16)
        target[64:80, 0:BLOCK] = tail.astype(BF16)
    rows = pl.ds(pl.multiple_of(16 * half, 16), 16)
    for u in range(2):
        codes[16 * u : 16 * u + 16, :] = head[rows, D * u : D * (u + 1)].astype(BF16)


VMEM = pl.BlockSpec(memory_space=pltpu.VMEM)
ANY = pl.BlockSpec(memory_space=pl.ANY)
HBM = pl.BlockSpec(memory_space=pltpu.HBM)
SMEM = pl.BlockSpec(memory_space=pltpu.SMEM)
DMA = pltpu.SemaphoreType.DMA


def shape(*dims, dtype=F32):
    return jax.ShapeDtypeStruct(dims, dtype)


def half_shape(*dims):
    return jax.ShapeDtypeStruct(dims, BF16)


def held(*dims):
    return pltpu.VMEM(dims, BF16)


def wide(*dims):
    return pltpu.VMEM(dims, F32)


def call(body, name, ins, outs, out_specs, scratch, micros, limit):
    return pl.pallas_call(
        body,
        name=name,
        in_specs=ins,
        out_shape=outs,
        out_specs=out_specs,
        scratch_shapes=scratch,
        compiler_params=pltpu.CompilerParams(vmem_limit_bytes=limit * 1024 * 1024),
        cost_estimate=pl.CostEstimate(flops=micros * 1_150_000_000, bytes_accessed=1 << 20, transcendentals=0),
    )


QUERY_KEY = (half_shape(SEG, D), half_shape(SEG, D), half_shape(ROWS, D), half_shape(ROWS, D), half_shape(ROWS, D))
PROJECT_HELD = [held(ROWS, D), held(4, D, D), DMA, DMA((12,))]
KEPT = half_shape(KEPT_ROWS, D)


def run_project_first(bits, scalars, frames, pieces, table):
    result = call(
        functools.partial(project, bits, 0),
        "project_first",
        [SMEM] + [VMEM] * 6,
        QUERY_KEY + (shape(SEG, D), shape(16, D), KEPT),
        [VMEM] * 7 + [HBM],
        PROJECT_HELD + [wide(ROWS, D), held(D, BLOCK), DMA],
        6,
        40,
    )(scalars, frames, *pieces, table)
    return result[:5], result[5], result[6], result[7]


def run_project(bits, scalars, memory, hidden, vecs, pieces, table):
    result = call(
        functools.partial(project, bits, 4),
        "project",
        [SMEM] + [VMEM] * 8,
        QUERY_KEY + (KEPT,),
        [VMEM] * 5 + [HBM],
        PROJECT_HELD,
        6,
        40,
    )(scalars, memory, hidden, vecs, *pieces, table)
    return result[:5], result[5]


def run_attend(scalars, projected):
    return call(
        attend,
        "attend",
        [SMEM] + [VMEM] * 5,
        (half_shape(SEG, D), half_shape(KEPT_PAIRS, 2 * BLOCK, WIDE)),
        [VMEM, HBM],
        [held(PAIRS, 2 * BLOCK, WIDE), DMA((PAIRS + 2,))],
        11,
        44,
    )(scalars, *projected)


HALF_HELD = [
    held(SEG, 256), held(SEG, 256), held(ROWS, 256), held(ROWS, 256), held(ROWS, 256),
    held(2, 2 * BLOCK, WIDE), held(2 * BLOCK, 2 * BLOCK),
    wide(256, ROWS), wide(256, ROWS), wide(256, ROWS), wide(SEG, 256), wide(SEG, 256), DMA((2, 6)),
]
LATE_HELD = [held(ROWS, D), held(ROWS, D), DMA((2,))]
HALF_OUT = (half_shape(SEG, 256), half_shape(ROWS, 256), half_shape(ROWS, 256))


def run_attend_back(bits, scalars, grad_att, saved, table, probs):
    result = call(
        functools.partial(attend_back, bits, False),
        "attend_back",
        [SMEM, VMEM] + [HBM] * 3,
        HALF_OUT + (half_shape(4, D, 256), shape(8, 256)),
        [VMEM] * 5,
        HALF_HELD + LATE_HELD,
        9,
        40,
    )(scalars, grad_att, table, saved, probs)
    return (*result[:3], result[4]), result[3]


def run_attend_back_rest(bits, scalars, grad_att, saved, table, probs, staged):
    result = call(
        functools.partial(attend_back, bits, True),
        "attend_back_rest",
        [SMEM, VMEM] + [HBM] * 3 + [VMEM],
        HALF_OUT + (shape(8, 256), half_shape(GROUPS, 64, D), half_shape(GROUPS, 64, D)),
        [VMEM] * 6,
        HALF_HELD + [held(4, D, D), DMA] + LATE_HELD,
        10,
        42,
    )(scalars, grad_att, table, saved, probs, staged)
    return result[:4], result[4], result[5]


def run_input_grads(bits, scalars, saved, grads, grad_mixed, vecs, memory, hidden):
    return call(
        functools.partial(input_grads, bits, 4),
        "input_grads",
        [SMEM, HBM] + [VMEM] * 12,
        (shape(SEG, D), shape(8, D)),
        [VMEM] * 2,
        [held(4, D, D), DMA((3,))],
        5,
        40,
    )(scalars, saved, *grads, grad_mixed, vecs, memory, hidden)


def run_input_grads_last(bits, scalars, saved, grads, grad_mixed, vecs, frames, *small_grads):
    return call(
        functools.partial(input_grads, bits, 0),
        "input_grads_last",
        [SMEM, HBM] + [VMEM] * 15,
        (half_shape(GROUPS, 16, D), half_shape(GROUPS, 16, D)),
        [VMEM] * 2,
        [wide(ROWS, D), wide(BLOCK, D), held(D, D), DMA, held(D, BLOCK), DMA, held(4, D, D), DMA((3,))],
        5,
        40,
    )(scalars, saved, *grads, grad_mixed, vecs, frames, *small_grads)


FEED_HELD = [held(SEG, D), held(SEG, FF), held(SEG, FF), held(D, FF), held(FF, D), held(D, D)]
BACK_HELD = [held(SEG, FF), held(D, FF), held(FF, D), held(D, D)]


def run_feed_forward(bits, base, scalars, residual, attended, vecs, pieces):
    result = call(
        functools.partial(feed_forward, bits, base),
        "feed_forward",
        [SMEM] + [VMEM] * 7,
        (shape(SEG, D), shape(MEM, D), shape(SEG, D), KEPT),
        [VMEM] * 2 + [HBM] * 2,
        [wide(SEG, D)] + FEED_HELD + [DMA((3,)), DMA((16,))],
        9,
        36,
    )(scalars, residual, attended, vecs, *pieces)
    return result


def run_feed_backward(bits, base, scalars, grad_out, vecs, mixed, probs, saved):
    return call(
        functools.partial(feed_backward, bits, base),
        "feed_backward",
        [SMEM, VMEM, VMEM] + [HBM] * 3,
        (half_shape(GROUPS, 144, D), half_shape(GROUPS, 144, D), shape(SEG, D), half_shape(SEG, D), shape(8, D)),
        [VMEM] * 5,
        [wide(SEG, D), held(SEG, D)] + FEED_HELD + BACK_HELD + [DMA((18,)), DMA((3,))],
        13,
        38,
    )(scalars, grad_out, vecs, mixed, probs, saved)


def run_top(bits, streams, scalars, residual, attended, targets, vecs, pieces):
    return call(
        functools.partial(top_kernel, bits, streams),
        "top_kernel",
        [SMEM] + [VMEM] * 8,
        (
            half_shape(GROUPS, 176, D), half_shape(GROUPS, 176, D),
            shape(SEG, D), half_shape(SEG, D), shape(8, D), shape(8, D), shape(8, 128),
        ),
        [VMEM] * 7,
        FEED_HELD
        + [wide(SEG, D), wide(SEG, D), wide(SEG, D), held(D, CODES), held(SEG, D), held(SEG, CODES), held(D, CODES)]
        + BACK_HELD
        + [DMA, DMA((3,)), DMA((3,))],
        21,
        42,
    )(scalars, residual, attended, targets, vecs, *pieces)


def run_finish(scalars, loss, *sums):
    counts = tuple((len(item) for item in sums))
    flat = [item for group in sums for item in group]
    return call(
        functools.partial(finish, counts),
        "finish",
        [SMEM, VMEM] + [ANY] * len(flat),
        (shape(256, D), shape(256, D), shape(8, 128)),
        [VMEM] * 3,
        [pltpu.VMEM(item.shape[1:], item.dtype) for item in flat] + [DMA((len(flat),))],
        3,
        40,
    )(scalars, loss, *flat)


def run_update(scalars, total, kept, got, state):
    flat = [item[None] if item.ndim == 1 else item for item in state]
    for index in (6, 15, 24):
        flat[index] = jnp.transpose(flat[index])
    result = call(
        update,
        "update",
        [SMEM] + [VMEM] * 30,
        tuple((shape(*item.shape) for item in flat)) + (shape(1, 1), shape(1, 1)),
        [VMEM] * 29,
        [wide(BLOCK, BLOCK)],
        5,
        24,
    )(scalars, total, kept, got, *flat)
    result = list(result)
    for index in (6, 15, 24):
        result[index] = jnp.transpose(result[index])
    return [item.reshape(old.shape) for item, old in zip(result, state)] + [result[27][0, 0], result[28][0, 0]]


def run_pack(scalars, w_attn, w_out, w_pos, w_up, w_down, layer_vecs, w_in, w_head, gain_final):
    return call(
        pack_shards,
        "pack_shards",
        [SMEM] + [VMEM] * 9,
        (half_shape(224, D), half_shape(224, D), half_shape(32, D)),
        [VMEM] * 3,
        [wide(BLOCK, BLOCK)],
        3,
        56,
    )(scalars, w_attn, w_out, w_pos, w_up, w_down, layer_vecs, jnp.transpose(w_in), w_head, gain_final[None])


def swap_parts(value):
    half = value.shape[0] // 2
    return jnp.concatenate([swap(value[:half]), swap(value[half:])], 0)


def spread(value, bits):
    count = lax.axis_size("dp")
    pairs = [
        (half * count + i, half * count + (i ^ bit)) for half, bit in enumerate(bits) for i in range(count)
    ]
    return lax.ppermute(value, ("section", "dp"), pairs)


def swap(value):
    return lax.ppermute(value, "section", [(0, 1), (1, 0)])


def fence(*values):
    return lax.optimization_barrier(values)


def joined(low, got):
    return jnp.concatenate([low, got], 0)


def part(sources, first, last):
    total = sources[0][first:last].astype(F32)
    for item in sources[1:]:
        total = total + item[first:last].astype(F32)
    return total


def shrink(chunks, pair, merged=()):
    count = (merged or chunks[0])[-1].shape[0]
    sent, first = [], 0
    for item in chunks:
        rows = item[0].shape[1]
        total = part(item, count // 2, count)
        if merged:
            total = total + part([other[:, first : first + rows] for other in merged], count // 2, count)
        sent.append(total.astype(BF16))
        first += rows
    return spread(jnp.concatenate(sent, 1), pair)


def add_up(value, bits):
    value = value + swap(value)
    steps = [low for low, unused in zip(*bits)]
    for one, two in zip(steps[0::2], steps[1::2]):
        first, second, third = (spread(value, (step, step)) for step in (one, two, one + two))
        value = (value + first) + (second + third)
    return value


def lanes_of(block):
    return [block[:, D * u : D * (u + 1)] for u in range(block.shape[1] // D)]


def sinus_table(where_at):
    freqs = jnp.exp(-jnp.log(10000.0) * (2.0 * jnp.arange(D // 2, dtype=jnp.int32).astype(F32) / D))
    angles = where_at * freqs[None, :]
    return jnp.concatenate([jnp.sin(angles), jnp.cos(angles)], 1).astype(BF16)


def split_shards(section, scalars, params):
    kept, sent, head = run_pack(scalars, *params)
    got = swap(sent)
    first = section == 0
    row = lax.broadcasted_iota(jnp.int32, (80, D), 0)
    attn = jnp.where(row < 64, jnp.where(first, kept[:80], got[:80]), kept[:80] + got[:80])
    zero = jnp.where(first, kept[80:], got[80:])
    one = jnp.where(first, got, kept)
    return attn, zero, one[:64], jnp.concatenate([one[80:], head], 0)


def halves(whole, rows):
    return whole.reshape(GROUPS, 2, rows, whole.shape[1]).transpose(1, 0, 2, 3)


def gather_whole(section, w_attn, w_out, w_pos, w_up, w_down, layer_vecs, w_in, w_head, gain_final):
    def over(value, axis):
        return lax.all_gather(value.astype(BF16), "dp", axis=axis, tiled=True)

    def layers(value):
        return lax.all_gather(over(value[0], 0), "section", axis=0)

    attn, out, pos, up, down = (layers(item) for item in (w_attn, w_out, w_pos, w_up, w_down))
    vecs = lax.all_gather(over(layer_vecs[0], 1), "section", axis=0)
    small = jnp.concatenate(
        [over(w_in, 1), vecs[0], vecs[1], over(gain_final, 0)[None], jnp.zeros((BLOCK - 89, D), BF16)], 0
    )
    small = jnp.pad(jnp.transpose(small), ((0, 0), (0, D - BLOCK)))
    head = over(w_head, 0)

    def pieces(units):
        both = jnp.concatenate([halves(item, item.shape[0] // 32) for item in units], 2)
        own = lax.dynamic_index_in_dim(both, section, 0, keepdims=False)
        other = lax.dynamic_index_in_dim(both, 1 - section, 0, keepdims=False)
        return (own[:8], own[8:], other[:8], other[8:])

    return (
        pieces(lanes_of(attn[0]) + [pos[0], small]),
        pieces(lanes_of(up[0]) + [down[0], out[0]]),
        pieces(lanes_of(attn[1]) + [pos[1]]),
        pieces(lanes_of(up[1]) + [down[1], out[1]] + lanes_of(head)),
    )


def whole_grads(section, sums):
    count = lax.axis_size("dp")
    place = lax.axis_index("dp")
    attn_zero, feed_zero, attn_one, feed_one, small = (
        lax.all_gather(lax.psum(item, "dp"), "section", axis=0) for item in sums
    )

    def unit(both, start, rows):
        item = both[:, :, start : start + rows]
        return item.transpose(1, 0, 2, 3).reshape(GROUPS * 2 * rows, both.shape[3])

    def layer(attn, feed):
        return (
            jnp.concatenate([unit(attn, 16 * u, 16) for u in range(3)], 1),
            unit(feed, 128, 16),
            unit(attn, 48, 16),
            jnp.concatenate([unit(feed, 16 * u, 16) for u in range(4)], 1),
            unit(feed, 64, 64),
        )

    small = jnp.transpose(unit(small, 0, 16))
    zero = layer(attn_zero, feed_zero) + (small[80:84],)
    one = layer(attn_one, feed_one) + (small[84:88],)
    ends = (small[:80], jnp.concatenate([unit(feed_one, 144 + 16 * u, 16) for u in range(2)], 1), small[88])
    squares = sum((jnp.sum(item * item) for item in zero + one + ends))
    dims = (0, 0, 0, 0, 0, 1, 1, 0, 0)
    grads = tuple((jnp.where(section == 0, a, b) for a, b in zip(zero, one))) + ends
    return squares, tuple(
        (
            lax.dynamic_slice_in_dim(item, place * (item.shape[dim] // count), item.shape[dim] // count, dim)
            for item, dim in zip(grads, dims)
        )
    )


def local(frames, targets, lengths, *state):
    params, firsts, seconds = (state[:9], state[9:18], state[18:])
    section = lax.axis_index("section")
    streams = lax.axis_size("dp")
    ringed = streams == GROUPS
    place = lax.axis_index("dp") if ringed else jnp.int32(0)
    length = lengths[0]
    scalars = jnp.stack([place, section, length, section]).astype(jnp.int32)
    count_down = (ROWS - 1 - jnp.arange(ROWS, dtype=jnp.int32)).astype(F32)[:, None]
    rows = lax.dynamic_slice_in_dim(
        jnp.pad(frames[0], ((MEM, 0), (0, BLOCK - FEATS))), section * SEG, ROWS, 0
    )
    codes = lax.dynamic_slice_in_dim(targets, section * SEG, SEG, 1)
    if ringed:
        bits = ((8, 4, 1, 2), (8, 4, 2, 1))
        far, near, side, last = zip(*bits)
        zero, one, two, three = (item[None] for item in split_shards(section, scalars, params))
        zero, got, count_down = fence(zero, spread(zero, far), count_down)
        table = sinus_table(count_down)
        zero = joined(zero, got)
        zero, got, one = fence(zero, spread(zero, near), one)
        zero = joined(zero, got)
        one_got = spread(one, far)
        zero, got, two, one, one_got, rows, table, codes = fence(
            zero, spread(zero, side), two, one, one_got, rows, table, codes
        )
        zero = joined(zero, got)
        high = spread(zero, last)
        one = joined(one, one_got)
        one_got, two_got = spread(one, near), spread(two, far)
        zero, high, one, one_got, two, two_got = fence(zero, high, one, one_got, two, two_got)
        one, two = joined(one, one_got), joined(two, two_got)
        one_got, two_got = spread(one, side), spread(two, near)
        swapped, high_swapped = swap_parts(zero), swap_parts(high)
        swapped, high_swapped, one, one_got, two, two_got, three = fence(
            swapped, high_swapped, one, one_got, two, two_got, three
        )
        chunk = (zero, high, swapped, high_swapped)
        one, two = joined(one, one_got), joined(two, two_got)
        one_got, two_got, three_got, swapped = spread(one, last), spread(two, side), spread(three, far), swap(one)
    else:
        bits = IN_ORDER
        table = sinus_table(count_down)
        chunk, chunk_one, chunk_two, chunk_three = gather_whole(section, *params)

    projected, hidden_zero, vecs, saved_zero = run_project_first(bits, scalars, rows, chunk, table)
    if ringed:
        projected, two_got, three_got, swapped = fence(projected, two_got, three_got, swapped)
        two, three = joined(two, two_got), joined(three, three_got)
        two_got, three_got, two_swapped = spread(two, last), spread(three, near), swap(two)
    attended, probs_zero = run_attend(scalars, projected)
    if ringed:
        attended, one_got, two_got, three_got, two_swapped = fence(
            attended, one_got, two_got, three_got, two_swapped
        )
        chunk = (one, one_got, swapped, swap(one_got))
        two_chunk = (two, two_got, two_swapped, swap(two_got))
        three = joined(three, three_got)
        three_got = spread(three, side)
    else:
        chunk = chunk_one
    out_zero, memory, mixed_zero, fed_zero = run_feed_forward(bits, 0, scalars, hidden_zero, attended, vecs, chunk)
    if ringed:
        out_zero, memory, three_got, two_chunk = fence(out_zero, memory, three_got, two_chunk)
        chunk = two_chunk
        three = joined(three, three_got)
        three_got, three_swapped = spread(three, last), swap(three)
    else:
        chunk = chunk_two
    memory = lax.ppermute(memory, "section", [(0, 1)])
    projected, saved_one = run_project(bits, scalars, memory, out_zero, vecs, chunk, table)
    attended, probs_one = run_attend(scalars, projected)
    if ringed:
        attended, three_got, three_swapped = fence(attended, three_got, three_swapped)
        chunk = (three, three_got, three_swapped, swap(three_got))
    else:
        chunk = chunk_three
    keep_a, send_a, grad, grad_att, gain_one, gain_final, loss = run_top(
        bits, streams, scalars, out_zero, attended, codes, vecs, chunk
    )
    if ringed:
        grad_att, keep_a, send_a = fence(grad_att, keep_a, send_a)
        got_a = swap(send_a)
    grads_a, staged = run_attend_back(bits, scalars, grad_att, saved_one, table, probs_one)
    if ringed:
        grads_a, staged, got_a = fence(grads_a, staged, got_a)
        sum_a = [keep_a, got_a]
        got_a = shrink([sum_a], last)
    grads_b, keep_b, send_b = run_attend_back_rest(
        bits, scalars, grad_att, saved_one, table, probs_one, staged
    )
    if ringed:
        grads_b, keep_b, send_b = fence(grads_b, keep_b, send_b)
        got_b = swap(send_b)
    grad, vecs_one = run_input_grads(
        bits, scalars, saved_one, (*grads_a, *grads_b), grad, vecs, memory, out_zero
    )
    if ringed:
        grad, got_a, got_b = fence(grad, got_a, got_b)
        sum_a.append(got_a)
        sum_b = [keep_b, got_b]
        got_a, got_b = shrink([sum_a], side), shrink([sum_b], last)
    keep_c, send_c, grad, grad_att, gain_zero = run_feed_backward(
        bits, 0, scalars, grad, vecs, mixed_zero, probs_zero, fed_zero
    )
    if ringed:
        grad_att, got_a, got_b, keep_c, send_c = fence(grad_att, got_a, got_b, keep_c, send_c)
        sum_a.append(got_a)
        sum_b.append(got_b)
        got_a, got_b, got_c = shrink([sum_a], near), shrink([sum_b], side), swap(send_c)
    grads_a, staged = run_attend_back(bits, scalars, grad_att, saved_zero, table, probs_zero)
    if ringed:
        grads_a, staged, got_a, got_b, got_c = fence(grads_a, staged, got_a, got_b, got_c)
        sum_a.append(got_a)
        sum_b.append(got_b)
        sum_c = [keep_c, got_c]
        got_c, got_a, got_b = shrink([sum_c], last), shrink([sum_a], far), shrink([sum_b], near)
    grads_b, keep_d, send_d = run_attend_back_rest(
        bits, scalars, grad_att, saved_zero, table, probs_zero, staged
    )
    if ringed:
        grads_b, keep_d, send_d, got_a, got_b, got_c = fence(grads_b, keep_d, send_d, got_a, got_b, got_c)
        sum_a.append(got_a)
        sum_b.append(got_b)
        sum_c.append(got_c)
        got_d, got_c, got_b = swap(send_d), shrink([sum_c], side), shrink([sum_b], far)
    keep_e, send_e = run_input_grads_last(
        bits, scalars, saved_zero, (*grads_a, *grads_b), grad, vecs, rows,
        gain_zero, vecs_one, gain_one, gain_final,
    )
    if not ringed:
        pairs = ((keep_d, send_d), (keep_c, send_c), (keep_b, send_b), (keep_a, send_a), (keep_e, send_e))
        sums = [keep.astype(F32) + swap(send).astype(F32) for keep, send in pairs]
        squares, grads = whole_grads(section, sums)
        grad_norm = jnp.sqrt(squares)
        loss_sum = lax.psum(loss[0, 0], ("section", "dp"))
        factor = jnp.minimum(1.0, CLIP / (grad_norm + 1e-06))
        results = []
        for index in range(9):
            rate, decay = (0.3, 0.0) if index in (5, 8) else (0.03, 0.01)
            grad = grads[index][None] if index < 6 else grads[index]
            results.append(
                adam_step(params[index], grad, firsts[index], seconds[index], rate, decay, factor)
            )
        news, moms, sqs = zip(*results)
        return (*news, *moms, *sqs, grad_norm, loss_sum)
    keep_e, send_e, got_b, got_d = fence(keep_e, send_e, got_b, got_d)
    sum_b.append(got_b)
    sum_d, sum_e, sum_de = [keep_d, got_d], [keep_e, swap(send_e)], []
    for pair in (last, side, near, far):
        got = shrink([sum_d, sum_e], pair, sum_de)
        if pair == last:
            sum_c.append(got_c)
            got, got_c, one_a, one_b = fence(got, shrink([sum_c], near), part(sum_a, 0, 1), part(sum_b, 0, 1))
            sum_c.append(got_c)
            got_c = shrink([sum_c], far)
        if pair == near:
            one_d = part(sum_d + [item[:, :64] for item in sum_de], 0, 1)
            one_e = part(sum_e + [item[:, 64:] for item in sum_de], 0, 1)
            got, one_c, one_d, one_e = fence(got, part(sum_c, 0, 1), one_d, one_e)
            one_d, one_e = one_d + got[:1, :64].astype(F32), one_e + got[:1, 64:].astype(F32)
        sum_de.append(got)
    kept, sent, total = run_finish(
        scalars, loss, [one_d], [one_c, got_c], [one_b], [one_a], [one_e], sum_de[3:]
    )
    got = swap(sent)
    return tuple(run_update(scalars, add_up(total, bits), kept, got, state))


def solution(mesh):
    weights = (
        P("section", "dp", None),
        P("section", "dp", None),
        P("section", "dp", None),
        P("section", "dp", None),
        P("section", "dp", None),
        P("section", None, "dp"),
        P(None, "dp"),
        P("dp", None),
        P("dp"),
    )
    return jax.shard_map(
        local,
        mesh=mesh,
        in_specs=(P("dp", None, None), P("dp", None), P("dp")) + weights * 3,
        out_specs=weights * 3 + (P(), P()),
        check_vma=False,
    )
```
